32 devices in a mesh: comp: 4 (over y, core), patch: 8 (over z, x).
Axes of the slice: x: 2, y: 2, z: 4, core: 2. Of those that a mesh axis runs over, the one named last changes fastest.
Arguments:
- load_cases: float32 [32, 98304], P(None, ('comp', 'patch')), may hold values from -6 to 6
- mass_diag: float32 [98304], P(('comp', 'patch')), may hold values from 0.5 to 2
- stiffness: float32 [1536, 64, 256], P(('comp', 'patch')), may hold values from -0.375 to 0.375
- block_cols: int32 [1536, 4], P(('comp', 'patch')), may hold values from 0 to 47
- trace_dofs: int32 [32768], P(('comp', 'patch')), may hold values from 0 to 3071
- penalty: float32 [32768], P(('comp', 'patch')), may hold values from 0.5 to 2
- cell_partials: float32 [32, 16384], P(None, ('comp', 'patch')), may hold values from -6 to 6
- cell_owner: int32 [16384, 1], P(('comp', 'patch')), may hold values from 0 to 7; in each aligned block of 512 rows (0 to 511, 512 to 1023, ...) at most 256 rows name the same one
- cell_dof: int32 [16384], P(('comp', 'patch')), may hold values from 0 to 3071
Outputs:
- solution: float32 [32, 98304], P(None, ('comp', 'patch'))
- residual: float32 [32, 98304], P(None, ('comp', 'patch'))
The draws below stay inside these ranges and needn't reach their ends.
Inputs may be any that keep to these rules, and one draw needn't show every extreme that they name: `cell_owner`: no more than 256 trimmed cells of one patch name the same owner, a bound that some block reaches of them.
All inputs are finite; a program needn't handle non-finite values.
Results may differ from the reference program's by a relative error of at most 0.0003.
Values sent between devices are 32-bit elements; how exact they have to be, the bound alone decides.
No kernel may reach another device: no remote copies, remote signals or barrier semaphores. Data moves between devices by JAX's collectives and lax.ppermute only.
A program may use at most 64 MiB of HBM per device.

```python
import math
import jax
import jax.numpy as jnp
import numpy as np
from jax import lax

CASES = 32
BLK = 64
KNB = 4
NB = 48
TR = 1024
NCELL = 512
ITERS = 2
CAP = 256
DOFS = 98304
N_PATCH = 8
DEVICES = 32


def touch_ends(array, key, low, largest):
    shape = array.shape
    place = [jax.random.randint(jax.random.fold_in(key, axis), (), 0, shape[axis]) for axis in range(len(shape))]
    array = array.at[tuple(place)].set(low)
    longest = shape.index(max(shape))
    place[longest] = (place[longest] + 1) % shape[longest]
    return array.at[tuple(place)].set(largest)


def shard_levels(stream_key, shape, cuts, least, largest):
    def one(position, parts):
        steps = jax.random.uniform(jax.random.fold_in(jax.random.fold_in(stream_key, 6), position), (parts,), jnp.float32, least / len(cuts), largest / len(cuts))
        return jnp.repeat(jnp.exp(steps), shape[position] // parts).reshape((-1,) + (1,) * (len(shape) - position - 1))

    factor_of = one(*cuts[0])
    for cut in cuts[1:]:
        factor_of = factor_of * one(*cut)
    return factor_of


def deal_out(own_key, own, number, rows, number_of, top, limit, lean):
    order = jax.random.permutation(own_key, number_of)
    heavy_load, usual = portions_of(number_of, rows * top, limit, lean, True), portions_of(number_of, rows * top, limit, lean, False)
    places = jnp.arange(number_of)

    def named(tallies, offset_by):
        used = int((tallies > 0).sum())
        fixed = max(1, used // 4)
        passed = fixed + (places - fixed + offset_by * (used - fixed)) % max(1, number_of - fixed)
        return jnp.zeros((number_of,), jnp.int32).at[order[jnp.where(places < fixed, places, passed)]].set(jnp.asarray(tallies, jnp.int32))

    tallies = jnp.where(number % 4 == 0, named(heavy_load, number // 4), named(usual, number - number // 4 - 1))
    mixed = jax.random.permutation(jax.random.fold_in(own, 3), number_of)
    donor, receiver = mixed[0:number_of // 2 * 2:2], mixed[1:number_of // 2 * 2:2]
    room = jnp.minimum(tallies[donor] - 1, limit - tallies[receiver]) // 2
    room = jnp.where((donor == order[0]) | (receiver == order[0]) | (tallies[receiver] == 0), 0, jnp.maximum(room, 0))
    passed = jax.random.randint(jax.random.fold_in(own, 4), (number_of // 2,), 0, 1 << 20) % (room + 1)
    tallies = tallies.at[donor].add(-passed).at[receiver].add(passed)
    labels = jnp.searchsorted(jnp.cumsum(tallies), jnp.arange(rows * top), side="right").astype(jnp.int32)
    listing = labels.reshape(top, rows).T
    listing = listing[jax.random.permutation(jax.random.fold_in(own, 1), rows)]
    offset_by = jax.random.randint(jax.random.fold_in(own, 2), (rows, 1), 0, top)
    return jnp.take_along_axis(listing, (jnp.arange(top)[None, :] + offset_by) % top, axis=1)


def portions_of(number_of, total, bound, lean, full):
    portions = [(1 << 20) // math.isqrt(grade ** lean) + 1 for grade in range(1, number_of + 1)]
    largest = bound if full else min(bound, max(-(-total // number_of), total * portions[0] // sum(portions)))
    least = 1 if total - largest >= number_of - 1 else 0
    holding, surplus = [largest] + [least] * (number_of - 1), total - largest - least * (number_of - 1)
    while surplus > 0:
        candidates = [i for i in range(1, number_of) if holding[i] < largest] or [i for i in range(1, number_of) if holding[i] < bound]
        mass, budget = sum([portions[i] for i in candidates]), surplus
        for i in candidates:
            extra = min(bound - holding[i], max(1, budget * portions[i] // mass), surplus)
            holding[i] = holding[i] + extra
            surplus = surplus - extra
    return np.array(holding)


def normal_values(stream_key, extent, spread, bound, pieces=(), kind=jnp.bfloat16):
    array = jax.random.normal(stream_key, extent, jnp.float32) * spread
    if len(pieces) > 0:
        array = shard_levels(stream_key, extent, pieces, -0.22, 0.18) * array
    return jnp.clip(array, min=-bound, max=bound).astype(kind)


def setup_inputs(seed: int = 0) -> dict:
    key_list = jax.random.split(jax.random.key(seed), 10)
    load_cases = normal_values(key_list[0], (CASES, DOFS), 1.0, 6.0, ((1, 32),), jnp.float32)
    mass_diag = jnp.clip(0.5 + 1.5 * jax.random.uniform(key_list[1], (DOFS,), jnp.float32) ** shard_levels(key_list[1], (DOFS,), ((0, 32),), -0.2, 0.2), 0.5, 2.0)
    stiffness = normal_values(key_list[2], (DEVICES * NB, BLK, KNB * BLK), (KNB * BLK) ** -0.5, 0.375, ((0, 32),), jnp.float32)
    block_cols = touch_ends(jax.random.randint(key_list[3], (DEVICES * NB, KNB), 0, NB), jax.random.fold_in(key_list[3], 1), 0, NB - 1).astype(jnp.int32)
    trace_dofs = touch_ends(jax.random.randint(key_list[4], (DEVICES * TR,), 0, NB * BLK), jax.random.fold_in(key_list[4], 1), 0, (NB * BLK) - 1).astype(jnp.int32)
    penalty = jnp.clip(jnp.exp(math.log(2.0) - 1.3862944 * jax.random.uniform(key_list[5], (DEVICES * TR,), jnp.float32) ** shard_levels(key_list[5], (DEVICES * TR,), ((0, 32),), -0.2, 0.2)), 0.5, 2.0)
    cell_partials = normal_values(key_list[6], (CASES, DEVICES * NCELL), 1.0, 6.0, ((1, 32),), jnp.float32)
    cell_owner_keys = jax.random.split(jax.random.fold_in(key_list[7], 1), (DEVICES * NCELL) // NCELL)
    cell_owner_turns = jax.random.permutation(jax.random.fold_in(key_list[7], 3), (DEVICES * NCELL) // NCELL)
    cell_owner = jax.vmap(lambda own, number: deal_out(jax.random.fold_in(key_list[7], 2), own, number, NCELL, N_PATCH, 1, CAP, 2))(cell_owner_keys, cell_owner_turns).reshape((DEVICES * NCELL, 1))
    cell_dof = touch_ends(jax.random.randint(key_list[8], (DEVICES * NCELL,), 0, NB * BLK), jax.random.fold_in(key_list[8], 1), 0, (NB * BLK) - 1).astype(jnp.int32)
    return dict(load_cases=load_cases, mass_diag=mass_diag, stiffness=stiffness, block_cols=block_cols, trace_dofs=trace_dofs, penalty=penalty, cell_partials=cell_partials, cell_owner=cell_owner, cell_dof=cell_dof)


def gram_matrix(first, second):
    return jnp.dot(first.astype(jnp.float32), second.T.astype(jnp.float32), precision=lax.Precision.HIGHEST, preferred_element_type=jnp.float32)

def small_solve(matrix, target):
    factor = jnp.linalg.cholesky(matrix)
    return jax.scipy.linalg.cho_solve((factor, True), target)

def local_blocks(inputs):
    field_dev, stiff_dev, cols_dev = inputs
    blocks = field_dev.reshape(CASES, NB, BLK)
    neighbour_vals = blocks[:, cols_dev, :].reshape(CASES, NB, KNB * BLK)
    strain = jnp.einsum('cnk,nrk->cnr', neighbour_vals, stiff_dev, precision=lax.Precision.HIGHEST)
    transposed = jnp.einsum('cnr,nrk->cnk', strain, stiff_dev, precision=lax.Precision.HIGHEST)
    transposed = transposed.reshape(CASES, NB * KNB, BLK)
    folded = jnp.zeros((CASES, NB, BLK), jnp.float32).at[:, cols_dev.reshape(-1), :].add(transposed)
    return folded.reshape(CASES, NB * BLK)

def add_jump(totals, indices, jump_term):
    return totals.at[:, indices].add(jump_term)

def apply_operator(field, mass_diag, stiff_all, cols_all, trace_all, pen_all):
    per_device = field.reshape(CASES, DEVICES, NB * BLK).transpose(1, 0, 2)
    folded = lax.map(local_blocks, (per_device, stiff_all, cols_all))
    own_trace = jnp.take_along_axis(per_device, trace_all[:, None, :], axis=2)
    device_ids = jnp.arange(DEVICES, dtype=jnp.int32)
    partner_ids = device_ids // N_PATCH * N_PATCH + (device_ids % N_PATCH + N_PATCH // 2) % N_PATCH
    weight = pen_all * pen_all[partner_ids]
    jump_term = weight[:, None, :] * (own_trace - own_trace[partner_ids])
    folded = jax.vmap(add_jump)(folded, trace_all, jump_term)
    return mass_diag[None, :] * field + folded.transpose(1, 0, 2).reshape(CASES, DEVICES * NB * BLK)

def reference(load_cases, mass_diag, stiffness, block_cols, trace_dofs, penalty, cell_partials, cell_owner, cell_dof):
    cell_device = jnp.arange(DEVICES * NCELL, dtype=jnp.int32) // NCELL
    target_device = cell_device // N_PATCH * N_PATCH + cell_owner[:, 0].astype(jnp.int32)
    flat_target = target_device * (NB * BLK) + cell_dof.astype(jnp.int32)
    right_side = load_cases.at[:, flat_target].add(cell_partials)
    stiff_all = stiffness.reshape(DEVICES, NB, BLK, KNB * BLK)
    cols_all = block_cols.reshape(DEVICES, NB, KNB)
    trace_all = trace_dofs.reshape(DEVICES, TR)
    pen_all = penalty.reshape(DEVICES, TR)
    solution = jnp.zeros_like(right_side)
    residual = right_side
    direction = right_side
    norm_now = gram_matrix(residual, residual)
    for turn_index in range(ITERS):
        image_field = apply_operator(direction, mass_diag, stiff_all, cols_all, trace_all, pen_all)
        curvature = gram_matrix(direction, image_field)
        step_size = small_solve(curvature, norm_now)
        solution = solution + jnp.dot(step_size.T.astype(jnp.float32), direction.astype(jnp.float32), precision=lax.Precision.HIGHEST, preferred_element_type=jnp.float32)
        residual = residual - jnp.dot(step_size.T.astype(jnp.float32), image_field.astype(jnp.float32), precision=lax.Precision.HIGHEST, preferred_element_type=jnp.float32)
        if turn_index + 1 < ITERS:
            norm_next = gram_matrix(residual, residual)
            correction = small_solve(norm_now, norm_next)
            direction = residual + jnp.dot(correction.T.astype(jnp.float32), direction.astype(jnp.float32), precision=lax.Precision.HIGHEST, preferred_element_type=jnp.float32)
            norm_now = norm_next
    return (solution, residual)
```

```python
import jax
import jax.numpy as jnp
from jax import lax
from jax.experimental import pallas as pl
from jax.experimental.pallas import tpu as pltpu
from jax.sharding import PartitionSpec as P

F32 = jnp.float32
BF16 = jnp.bfloat16
WIDE = 256
LANES = 128
VMEM_BYTES = 48 * 1024 * 1024


def split2(x):
    high = x.astype(BF16)
    low = (x - high.astype(F32)).astype(BF16)
    return high, low


def stack2(x):
    return jnp.concatenate(split2(x), axis=0)


def dot_nn(a, b):
    return lax.dot_general(a, b, (((1,), (0,)), ((), ())), preferred_element_type=F32)


def dot_nt(a, b):
    return lax.dot_general(a, b, (((1,), (1,)), ((), ())), preferred_element_type=F32)


def iota(shape, axis):
    return lax.broadcasted_iota(jnp.int32, shape, axis)


def one_hot_low(low, width):
    return (iota((WIDE, width), 0) == low).astype(F32).astype(BF16)


def masked_groups(stacked, group, count):
    parts = []
    for g in range(count):
        mask = (group == g).astype(F32).astype(BF16)
        parts.append(stacked * jnp.broadcast_to(mask, stacked.shape))
    return jnp.concatenate(parts, axis=0)


def gather_slots(field, one_hot, group, groups):
    cases = field.shape[0]
    rows = jnp.concatenate(
        [stack2(field[:, g * WIDE:(g + 1) * WIDE]) for g in range(groups)], axis=0
    )
    found = dot_nn(rows, one_hot)
    total = jnp.zeros((cases, group.shape[1]), F32)
    for g in range(groups):
        base = g * 2 * cases
        both = found[base:base + cases] + found[base + cases:base + 2 * cases]
        total = jnp.where(group == g, both, total)
    return total


def pack_cells(partials_ref, owner_ref, dof_ref, out_ref):
    patches, rows, cap = out_ref.shape
    cases, cells = partials_ref.shape
    owner = owner_ref[...]
    mine = (iota((patches, cells), 0) == owner).astype(F32)
    before = (iota((cells, cells), 0) < iota((cells, cells), 1)).astype(F32).astype(BF16)
    counts = dot_nn(mine.astype(BF16), before)
    rank = jnp.sum(mine * counts, axis=0, keepdims=True).astype(jnp.int32)
    extra = jnp.where(iota((rows - cases, cells), 0) == 0, dof_ref[...] + 1, 0).astype(F32)
    body = stack2(jnp.concatenate([partials_ref[...], extra], axis=0))
    for o in range(patches):
        key = jnp.where(owner == o, rank, -1)
        pick = (iota((cap, cells), 0) == key).astype(F32).astype(BF16)
        packed = dot_nt(body, pick)
        out_ref[o] = packed[:rows] + packed[rows:]


def split_stiffness(stiff_ref, out_ref):
    blk = stiff_ref.shape[1]
    high, low = split2(stiff_ref[...])
    out_ref[:, :blk, :] = high
    out_ref[:, blk:, :] = low


def assemble(recv_ref, load_ref, trace_ref, field_ref, own_ref):
    patches = recv_ref.shape[0]
    cases, dofs = load_ref.shape
    groups = dofs // WIDE
    cells = jnp.concatenate([recv_ref[p] for p in range(patches)], axis=1)
    slots = cells.shape[1]
    dof = cells[cases:cases + 1].astype(jnp.int32) - 1
    rows = masked_groups(stack2(cells[:cases]), dof >> 8, groups)
    sums = dot_nt(rows, one_hot_low(jnp.where(dof < 0, -1, dof & (WIDE - 1)), slots))
    pieces = []
    for g in range(groups):
        base = g * 2 * cases
        pieces.append(
            load_ref[:, g * WIDE:(g + 1) * WIDE]
            + (sums[base:base + cases] + sums[base + cases:base + 2 * cases])
        )
    field = jnp.concatenate(pieces, axis=1)
    field_ref[...] = field
    trace = trace_ref[...]
    own_ref[...] = gather_slots(
        field, one_hot_low(trace & (WIDE - 1), trace.shape[1]), trace >> 8, groups
    )


def spread_blocks(field_ref, low_ref, high_ref):
    cases, dofs = field_ref.shape
    in_low = iota((cases, LANES), 1) < LANES // 2
    for j in range(dofs // LANES):
        tile = field_ref[:, j * LANES:(j + 1) * LANES]
        turned = pltpu.roll(tile, LANES // 2, 1)
        low_ref[2 * j] = stack2(jnp.where(in_low, tile, 0.0))
        high_ref[2 * j + 1] = stack2(jnp.where(in_low, 0.0, tile))
        low_ref[2 * j + 1] = stack2(jnp.where(in_low, turned, 0.0))
        high_ref[2 * j] = stack2(jnp.where(in_low, 0.0, turned))


def strain_rows(cols_ref, stiff_ref, low_ref, high_ref, strain_ref):
    count = stiff_ref.shape[0]
    cases = strain_ref.shape[1] // 2
    for n in range(count):
        c = [cols_ref[4 * n + k] for k in range(4)]
        near = jnp.concatenate(
            [low_ref[c[0]] + high_ref[c[1]], low_ref[c[2]] + high_ref[c[3]]], axis=1
        )
        both = dot_nt(near, stiff_ref[n])
        both = both[:cases] + both[cases:]
        strain_ref[n] = stack2(both + pltpu.roll(both, LANES // 2, 1))


def transposed_sums(cols_ref, stiff_ref, strain_ref, sums):
    count = stiff_ref.shape[0]
    cases = strain_ref.shape[1] // 2
    for ref in sums:
        ref[...] = jnp.zeros_like(ref)
    for n in range(count):
        c = [cols_ref[4 * n + k] for k in range(4)]
        both = dot_nn(strain_ref[n], stiff_ref[n])
        both = both[:cases] + both[cases:]
        left, right = both[:, :LANES], both[:, LANES:]
        sums[0][c[0]] += left
        sums[1][c[1]] += left
        sums[2][c[2]] += right
        sums[3][c[3]] += right


def folded_tile(sums, j):
    cases = sums[0].shape[1]
    in_low = iota((cases, LANES), 1) < LANES // 2
    even, odd = 2 * j, 2 * j + 1
    straight = jnp.where(in_low, sums[0][even] + sums[2][even], sums[1][odd] + sums[3][odd])
    crossed = jnp.where(in_low, sums[0][odd] + sums[2][odd], sums[1][even] + sums[3][even])
    return straight + pltpu.roll(crossed, LANES // 2, 1)


def operator_body(cols_ref, field_ref, mass_ref, stiff_ref, out_ref, low_ref, high_ref, strain_ref, *sums):
    spread_blocks(field_ref, low_ref, high_ref)
    strain_rows(cols_ref, stiff_ref, low_ref, high_ref, strain_ref)
    transposed_sums(cols_ref, stiff_ref, strain_ref, sums)
    for j in range(field_ref.shape[1] // LANES):
        at = slice(j * LANES, (j + 1) * LANES)
        out_ref[:, at] = field_ref[:, at] * mass_ref[:, at] + folded_tile(sums, j)


def add_jump(base, jump, one_hot, group):
    cases, dofs = base.shape
    groups = dofs // WIDE
    sums = dot_nt(masked_groups(stack2(jump), group, groups), one_hot)
    pieces = []
    for g in range(groups):
        row = g * 2 * cases
        pieces.append(
            base[:, g * WIDE:(g + 1) * WIDE]
            + (sums[row:row + cases] + sums[row + cases:row + 2 * cases])
        )
    return jnp.concatenate(pieces, axis=1)


def first_image(part_ref, own_ref, match_ref, pen_ref, match_pen_ref, trace_ref, image_ref, trace_out_ref):
    trace = trace_ref[...]
    one_hot = one_hot_low(trace & (WIDE - 1), trace.shape[1])
    weight = pen_ref[...] * match_pen_ref[...]
    jump = weight * (own_ref[...] - match_ref[...])
    image = add_jump(part_ref[...], jump, one_hot, trace >> 8)
    image_ref[...] = image
    trace_out_ref[...] = gather_slots(image, one_hot, trace >> 8, image.shape[1] // WIDE)


def gram_body(cols_ref, field_ref, image_ref, mass_ref, stiff_ref, gram_ref, strain_ref, low_ref, high_ref):
    cases, dofs = field_ref.shape
    spread_blocks(image_ref, low_ref, high_ref)
    strain_rows(cols_ref, stiff_ref, low_ref, high_ref, strain_ref)
    in_low = iota((2 * cases, LANES), 1) < LANES // 2
    strain = jnp.concatenate(
        [
            jnp.where(in_low, strain_ref[2 * j].astype(F32), strain_ref[2 * j + 1].astype(F32)).astype(BF16)
            for j in range(strain_ref.shape[0] // 2)
        ],
        axis=1,
    )
    image = image_ref[...]
    image_rows = stack2(image)
    rows = jnp.concatenate([stack2(field_ref[...]), image_rows], axis=0)
    every = dot_nt(rows, image_rows)
    every = every[:, :cases] + every[:, cases:]
    cross = every[:cases] + every[cases:2 * cases]
    square = every[2 * cases:3 * cases] + every[3 * cases:]
    start = dot_nt(rows[:2 * cases], rows[:2 * cases])
    start = start[:, :cases] + start[:, cases:]
    start = start[:cases] + start[cases:]
    last = dot_nt(image_rows, stack2(image * mass_ref[...])) + dot_nt(strain, strain)
    last = last[:, :cases] + last[:, cases:]
    last = last[:cases] + last[cases:]
    gram_ref[...] = jnp.concatenate([cross, start, square, last], axis=1)


def gram_trace(gram_ref, own_ref, match_ref, pen_ref, match_pen_ref, out_ref, jump_ref):
    cases = gram_ref.shape[0]
    jump = (pen_ref[...] * match_pen_ref[...]) * (own_ref[...] - match_ref[...])
    jump_ref[...] = jump
    more = dot_nt(stack2(own_ref[...]), stack2(jump))
    more = more[:, :cases] + more[:, cases:]
    more = more[:cases] + more[cases:]
    zeros = jnp.zeros((cases, 3 * cases), F32)
    out_ref[...] = gram_ref[...] + jnp.concatenate([zeros, more], axis=1)


def second_image(cols_ref, image_ref, mass_ref, stiff_ref, strain_ref, jump_ref, trace_ref, out_ref, *sums):
    transposed_sums(cols_ref, stiff_ref, strain_ref, sums)
    trace = trace_ref[...]
    one_hot = one_hot_low(trace & (WIDE - 1), trace.shape[1])
    folded = jnp.concatenate(
        [folded_tile(sums, j) for j in range(image_ref.shape[1] // LANES)], axis=1
    )
    base = image_ref[...] * mass_ref[...] + folded
    out_ref[...] = add_jump(base, jump_ref[...], one_hot, trace >> 8)


def eliminate(matrix, size):
    rows = iota(matrix.shape, 0)
    for p in range(size):
        row = matrix[p:p + 1, :] / matrix[p:p + 1, p:p + 1]
        column = matrix[:, p:p + 1]
        matrix = jnp.where(rows == p, row, matrix - column * row)
    return matrix


def small_dot(a, b):
    return jnp.dot(a, b, precision=lax.Precision.HIGHEST, preferred_element_type=F32)


def square_transpose(a):
    size = a.shape[0]
    wide = jnp.concatenate([a, jnp.zeros((size, LANES - size), F32)], axis=1)
    tall = jnp.concatenate([wide, jnp.zeros((LANES - size, LANES), F32)], axis=0)
    return tall.T[:size, :size]


def finish(gram_ref, field_ref, image_ref, second_ref, solution_ref, residual_ref):
    cases = field_ref.shape[0]
    gram = gram_ref[...]
    cross, start = gram[:, :cases], gram[:, cases:2 * cases]
    square, last = gram[:, 2 * cases:3 * cases], gram[:, 3 * cases:]
    solved = eliminate(gram, cases)
    alpha = solved[:, cases:2 * cases]
    mixed = small_dot(solved[:, 2 * cases:3 * cases], alpha)
    eye = (iota((cases, cases), 0) == iota((cases, cases), 1)).astype(F32)
    norm = small_dot(start, mixed - eye)
    alpha_t, mixed_t = square_transpose(alpha), square_transpose(mixed)
    cross_mixed = small_dot(cross, mixed)
    curvature = small_dot(mixed_t, cross_mixed - small_dot(square, alpha)) + small_dot(
        alpha_t, small_dot(last, alpha) - small_dot(square, mixed)
    )
    stacked = jnp.concatenate([curvature, norm, jnp.zeros((cases, 2 * cases), F32)], axis=1)
    alpha_next = eliminate(stacked, cases)[:, cases:2 * cases]
    one = alpha + small_dot(mixed, alpha_next)
    two = small_dot(alpha, alpha_next)
    zero = jnp.zeros((cases, cases), F32)
    weights = jnp.concatenate(
        [
            jnp.concatenate([one, zero, zero, zero], axis=1),
            jnp.concatenate([-two, -one, zero, zero], axis=1),
            jnp.concatenate([zero, two, zero, zero], axis=1),
            jnp.concatenate([zero, zero, zero, zero], axis=1),
        ],
        axis=0,
    ).T[:2 * cases]
    high, low = split2(weights)
    coefs = jnp.concatenate(
        [jnp.concatenate([high, high], axis=1), jnp.concatenate([low, low], axis=1)], axis=0
    )
    field = field_ref[...]
    pad = jnp.zeros_like(field)
    rows = stack2(jnp.concatenate([field, image_ref[...], second_ref[...], pad], axis=0))
    out = dot_nn(coefs, rows)
    out = out[:2 * cases] + out[2 * cases:]
    solution_ref[...] = out[:cases]
    residual_ref[...] = field + out[cases:]


def run(body, outs, args, scratch=(), scalars=0):
    whole = pl.BlockSpec(memory_space=pltpu.VMEM)
    return pl.pallas_call(
        body,
        out_shape=outs,
        in_specs=[pl.BlockSpec(memory_space=pltpu.SMEM)] * scalars + [whole] * (len(args) - scalars),
        out_specs=jax.tree.map(lambda _: whole, outs),
        scratch_shapes=list(scratch),
        compiler_params=pltpu.CompilerParams(vmem_limit_bytes=VMEM_BYTES),
    )(*args)


def shards(
    load_cases,
    mass_diag,
    stiffness,
    block_cols,
    trace_dofs,
    penalty,
    cell_partials,
    cell_owner,
    cell_dof,
):
    cases, dofs = load_cases.shape
    count, blk, width = stiffness.shape
    cells = cell_partials.shape[1]
    slots = trace_dofs.shape[0]
    patches = lax.axis_size("patch")
    cap = 4 * cells // patches
    rows = cases + 8
    shape = jax.ShapeDtypeStruct
    field_shape = shape((cases, dofs), F32)
    slot_shape = shape((cases, slots), F32)
    mass = mass_diag.reshape(1, dofs)
    trace = trace_dofs.reshape(1, slots)
    pen = penalty.reshape(1, slots)
    cols = block_cols.reshape(-1)

    half = patches // 2
    pairs = [(i, (i + half) % patches) for i in range(patches)]
    match_pen = lax.ppermute(pen, "patch", pairs)
    packed = run(
        pack_cells,
        shape((patches, rows, cap), F32),
        (cell_partials, cell_owner.reshape(1, cells), cell_dof.reshape(1, cells)),
    )
    received = lax.all_to_all(packed, "patch", 0, 0)
    stiff = run(split_stiffness, shape((count, 2 * blk, width), BF16), (stiffness,))

    spread = [pltpu.VMEM((dofs // blk, 2 * cases, LANES), BF16)] * 2
    strain_scratch = pltpu.VMEM((count, 2 * cases, LANES), BF16)
    sums = [pltpu.VMEM((dofs // blk, cases, LANES), F32)] * 4

    field, own = run(assemble, (field_shape, slot_shape), (received, load_cases, trace))
    match = lax.ppermute(own, "patch", pairs)
    part = run(
        operator_body,
        field_shape,
        (cols, field, mass, stiff),
        scratch=[*spread, strain_scratch, *sums],
        scalars=1,
    )
    image, own = run(
        first_image, (field_shape, slot_shape), (part, own, match, pen, match_pen, trace)
    )
    match = lax.ppermute(own, "patch", pairs)
    gram, strain = run(
        gram_body,
        (shape((cases, 4 * cases), F32), shape((count, 2 * cases, LANES), BF16)),
        (cols, field, image, mass, stiff),
        scratch=spread,
        scalars=1,
    )
    gram, jump = run(
        gram_trace,
        (shape((cases, 4 * cases), F32), slot_shape),
        (gram, own, match, pen, match_pen),
    )
    gram = lax.psum(gram, ("comp", "patch"))
    second = run(
        second_image,
        field_shape,
        (cols, image, mass, stiff, strain, jump, trace),
        scratch=sums,
        scalars=1,
    )
    return run(finish, (field_shape, field_shape), (gram, field, image, second))


def solution(mesh):
    return jax.shard_map(
        shards,
        mesh=mesh,
        in_specs=(
            P(None, ("comp", "patch")),
            P(("comp", "patch")),
            P(("comp", "patch"), None, None),
            P(("comp", "patch"), None),
            P(("comp", "patch")),
            P(("comp", "patch")),
            P(None, ("comp", "patch")),
            P(("comp", "patch"), None),
            P(("comp", "patch")),
        ),
        out_specs=(P(None, ("comp", "patch")), P(None, ("comp", "patch"))),
        check_vma=False,
    )
```

```python
import jax
import jax.numpy as jnp
from jax import lax
from jax.experimental import pallas as pl
from jax.experimental.pallas import tpu as pltpu
from jax.sharding import PartitionSpec as P

F32 = jnp.float32
BF16 = jnp.bfloat16
WIDE = 256
LANES = 128
VMEM_BYTES = 48 * 1024 * 1024


def split2(x):
    high = x.astype(BF16)
    low = (x - high.astype(F32)).astype(BF16)
    return high, low


def stack2(x):
    return jnp.concatenate(split2(x), axis=0)


def dot_nn(a, b):
    return lax.dot_general(a, b, (((1,), (0,)), ((), ())), preferred_element_type=F32)


def dot_nt(a, b):
    return lax.dot_general(a, b, (((1,), (1,)), ((), ())), preferred_element_type=F32)


def iota(shape, axis):
    return lax.broadcasted_iota(jnp.int32, shape, axis)


def one_hot_low(low, width):
    return (iota((WIDE, width), 0) == low).astype(F32).astype(BF16)


def masked_groups(stacked, group, count):
    parts = []
    for g in range(count):
        mask = (group == g).astype(F32).astype(BF16)
        parts.append(stacked * jnp.broadcast_to(mask, stacked.shape))
    return jnp.concatenate(parts, axis=0)


def gather_slots(field, one_hot, group, groups):
    cases = field.shape[0]
    rows = jnp.concatenate(
        [stack2(field[:, g * WIDE:(g + 1) * WIDE]) for g in range(groups)], axis=0
    )
    found = dot_nn(rows, one_hot)
    total = jnp.zeros((cases, group.shape[1]), F32)
    for g in range(groups):
        base = g * 2 * cases
        both = found[base:base + cases] + found[base + cases:base + 2 * cases]
        total = jnp.where(group == g, both, total)
    return total


def pack_cells(partials_ref, owner_ref, dof_ref, out_ref):
    patches, rows, cap = out_ref.shape
    cases, cells = partials_ref.shape
    owner = owner_ref[...]
    mine = (iota((patches, cells), 0) == owner).astype(F32)
    before = (iota((cells, cells), 0) < iota((cells, cells), 1)).astype(F32).astype(BF16)
    counts = dot_nn(mine.astype(BF16), before)
    rank = jnp.sum(mine * counts, axis=0, keepdims=True).astype(jnp.int32)
    extra = jnp.where(iota((rows - cases, cells), 0) == 0, dof_ref[...] + 1, 0).astype(F32)
    body = stack2(jnp.concatenate([partials_ref[...], extra], axis=0))
    for o in range(patches):
        key = jnp.where(owner == o, rank, -1)
        pick = (iota((cap, cells), 0) == key).astype(F32).astype(BF16)
        packed = dot_nt(body, pick)
        out_ref[o] = packed[:rows] + packed[rows:]


def split_stiffness(stiff_ref, out_ref):
    blk = stiff_ref.shape[1]
    high, low = split2(stiff_ref[...])
    out_ref[:, :blk, :] = high
    out_ref[:, blk:, :] = low


def assemble(recv_ref, load_ref, trace_ref, field_ref, own_ref):
    patches = recv_ref.shape[0]
    cases, dofs = load_ref.shape
    groups = dofs // WIDE
    cells = jnp.concatenate([recv_ref[p] for p in range(patches)], axis=1)
    slots = cells.shape[1]
    dof = cells[cases:cases + 1].astype(jnp.int32) - 1
    rows = masked_groups(stack2(cells[:cases]), dof >> 8, groups)
    sums = dot_nt(rows, one_hot_low(jnp.where(dof < 0, -1, dof & (WIDE - 1)), slots))
    pieces = []
    for g in range(groups):
        base = g * 2 * cases
        pieces.append(
            load_ref[:, g * WIDE:(g + 1) * WIDE]
            + (sums[base:base + cases] + sums[base + cases:base + 2 * cases])
        )
    field = jnp.concatenate(pieces, axis=1)
    field_ref[...] = field
    trace = trace_ref[...]
    own_ref[...] = gather_slots(
        field, one_hot_low(trace & (WIDE - 1), trace.shape[1]), trace >> 8, groups
    )


def spread_blocks(field_ref, low_ref, high_ref):
    cases, dofs = field_ref.shape
    in_low = iota((cases, LANES), 1) < LANES // 2
    for j in range(dofs // LANES):
        tile = field_ref[:, j * LANES:(j + 1) * LANES]
        turned = pltpu.roll(tile, LANES // 2, 1)
        low_ref[2 * j] = stack2(jnp.where(in_low, tile, 0.0))
        high_ref[2 * j + 1] = stack2(jnp.where(in_low, 0.0, tile))
        low_ref[2 * j + 1] = stack2(jnp.where(in_low, turned, 0.0))
        high_ref[2 * j] = stack2(jnp.where(in_low, 0.0, turned))


def strain_rows(cols_ref, stiff_ref, low_ref, high_ref, strain_ref):
    count = stiff_ref.shape[0]
    cases = strain_ref.shape[1] // 2
    for n in range(count):
        c = [cols_ref[4 * n + k] for k in range(4)]
        near = jnp.concatenate(
            [low_ref[c[0]] + high_ref[c[1]], low_ref[c[2]] + high_ref[c[3]]], axis=1
        )
        both = dot_nt(near, stiff_ref[n])
        both = both[:cases] + both[cases:]
        strain_ref[n] = stack2(both + pltpu.roll(both, LANES // 2, 1))


def transposed_sums(cols_ref, stiff_ref, strain_ref, sums):
    count = stiff_ref.shape[0]
    cases = strain_ref.shape[1] // 2
    for ref in sums:
        ref[...] = jnp.zeros_like(ref)
    for n in range(count):
        c = [cols_ref[4 * n + k] for k in range(4)]
        both = dot_nn(strain_ref[n], stiff_ref[n])
        both = both[:cases] + both[cases:]
        left, right = both[:, :LANES], both[:, LANES:]
        sums[0][c[0]] += left
        sums[1][c[1]] += left
        sums[2][c[2]] += right
        sums[3][c[3]] += right


def folded_tile(sums, j):
    cases = sums[0].shape[1]
    in_low = iota((cases, LANES), 1) < LANES // 2
    even, odd = 2 * j, 2 * j + 1
    straight = jnp.where(in_low, sums[0][even] + sums[2][even], sums[1][odd] + sums[3][odd])
    crossed = jnp.where(in_low, sums[0][odd] + sums[2][odd], sums[1][even] + sums[3][even])
    return straight + pltpu.roll(crossed, LANES // 2, 1)


def operator_body(cols_ref, field_ref, mass_ref, stiff_ref, out_ref, low_ref, high_ref, strain_ref, *sums):
    spread_blocks(field_ref, low_ref, high_ref)
    strain_rows(cols_ref, stiff_ref, low_ref, high_ref, strain_ref)
    transposed_sums(cols_ref, stiff_ref, strain_ref, sums)
    for j in range(field_ref.shape[1] // LANES):
        at = slice(j * LANES, (j + 1) * LANES)
        out_ref[:, at] = field_ref[:, at] * mass_ref[:, at] + folded_tile(sums, j)


def add_jump(base, jump, one_hot, group):
    cases, dofs = base.shape
    groups = dofs // WIDE
    sums = dot_nt(masked_groups(stack2(jump), group, groups), one_hot)
    pieces = []
    for g in range(groups):
        row = g * 2 * cases
        pieces.append(
            base[:, g * WIDE:(g + 1) * WIDE]
            + (sums[row:row + cases] + sums[row + cases:row + 2 * cases])
        )
    return jnp.concatenate(pieces, axis=1)


def first_image(part_ref, own_ref, match_ref, pen_ref, match_pen_ref, trace_ref, image_ref, trace_out_ref):
    trace = trace_ref[...]
    one_hot = one_hot_low(trace & (WIDE - 1), trace.shape[1])
    weight = pen_ref[...] * match_pen_ref[...]
    jump = weight * (own_ref[...] - match_ref[...])
    image = add_jump(part_ref[...], jump, one_hot, trace >> 8)
    image_ref[...] = image
    trace_out_ref[...] = gather_slots(image, one_hot, trace >> 8, image.shape[1] // WIDE)


def gram_body(cols_ref, field_ref, image_ref, mass_ref, stiff_ref, gram_ref, strain_ref, low_ref, high_ref):
    cases, dofs = field_ref.shape
    spread_blocks(image_ref, low_ref, high_ref)
    strain_rows(cols_ref, stiff_ref, low_ref, high_ref, strain_ref)
    in_low = iota((2 * cases, LANES), 1) < LANES // 2
    strain = jnp.concatenate(
        [
            jnp.where(in_low, strain_ref[2 * j].astype(F32), strain_ref[2 * j + 1].astype(F32)).astype(BF16)
            for j in range(strain_ref.shape[0] // 2)
        ],
        axis=1,
    )
    image = image_ref[...]
    image_rows = stack2(image)
    rows = jnp.concatenate([stack2(field_ref[...]), image_rows], axis=0)
    every = dot_nt(rows, image_rows)
    every = every[:, :cases] + every[:, cases:]
    cross = every[:cases] + every[cases:2 * cases]
    square = every[2 * cases:3 * cases] + every[3 * cases:]
    start = dot_nt(rows[:2 * cases], rows[:2 * cases])
    start = start[:, :cases] + start[:, cases:]
    start = start[:cases] + start[cases:]
    last = dot_nt(image_rows, stack2(image * mass_ref[...])) + dot_nt(strain, strain)
    last = last[:, :cases] + last[:, cases:]
    last = last[:cases] + last[cases:]
    gram_ref[...] = jnp.concatenate([cross, start, square, last], axis=1)


def gram_trace(gram_ref, own_ref, match_ref, pen_ref, match_pen_ref, out_ref, jump_ref):
    cases = gram_ref.shape[0]
    jump = (pen_ref[...] * match_pen_ref[...]) * (own_ref[...] - match_ref[...])
    jump_ref[...] = jump
    more = dot_nt(stack2(own_ref[...]), stack2(jump))
    more = more[:, :cases] + more[:, cases:]
    more = more[:cases] + more[cases:]
    zeros = jnp.zeros((cases, 3 * cases), F32)
    out_ref[...] = gram_ref[...] + jnp.concatenate([zeros, more], axis=1)


def second_image(cols_ref, image_ref, mass_ref, stiff_ref, strain_ref, jump_ref, trace_ref, out_ref, *sums):
    transposed_sums(cols_ref, stiff_ref, strain_ref, sums)
    trace = trace_ref[...]
    one_hot = one_hot_low(trace & (WIDE - 1), trace.shape[1])
    folded = jnp.concatenate(
        [folded_tile(sums, j) for j in range(image_ref.shape[1] // LANES)], axis=1
    )
    base = image_ref[...] * mass_ref[...] + folded
    out_ref[...] = add_jump(base, jump_ref[...], one_hot, trace >> 8)


def eliminate(matrix, size):
    rows = iota(matrix.shape, 0)
    for p in range(size):
        row = matrix[p:p + 1, :] / matrix[p:p + 1, p:p + 1]
        column = matrix[:, p:p + 1]
        matrix = jnp.where(rows == p, row, matrix - column * row)
    return matrix


def small_dot(a, b):
    return jnp.dot(a, b, precision=lax.Precision.HIGHEST, preferred_element_type=F32)


def square_transpose(a):
    size = a.shape[0]
    wide = jnp.concatenate([a, jnp.zeros((size, LANES - size), F32)], axis=1)
    tall = jnp.concatenate([wide, jnp.zeros((LANES - size, LANES), F32)], axis=0)
    return tall.T[:size, :size]


def finish(*refs):
    *gram_refs, field_ref, image_ref, second_ref, solution_ref, residual_ref = refs
    cases = field_ref.shape[0]
    gram = sum_of([ref[...] for ref in gram_refs])
    cross, start = gram[:, :cases], gram[:, cases:2 * cases]
    square, last = gram[:, 2 * cases:3 * cases], gram[:, 3 * cases:]
    solved = eliminate(gram, cases)
    alpha = solved[:, cases:2 * cases]
    mixed = small_dot(solved[:, 2 * cases:3 * cases], alpha)
    eye = (iota((cases, cases), 0) == iota((cases, cases), 1)).astype(F32)
    norm = small_dot(start, mixed - eye)
    alpha_t, mixed_t = square_transpose(alpha), square_transpose(mixed)
    cross_mixed = small_dot(cross, mixed)
    curvature = small_dot(mixed_t, cross_mixed - small_dot(square, alpha)) + small_dot(
        alpha_t, small_dot(last, alpha) - small_dot(square, mixed)
    )
    stacked = jnp.concatenate([curvature, norm, jnp.zeros((cases, 2 * cases), F32)], axis=1)
    alpha_next = eliminate(stacked, cases)[:, cases:2 * cases]
    one = alpha + small_dot(mixed, alpha_next)
    two = small_dot(alpha, alpha_next)
    zero = jnp.zeros((cases, cases), F32)
    weights = jnp.concatenate(
        [
            jnp.concatenate([one, zero, zero, zero], axis=1),
            jnp.concatenate([-two, -one, zero, zero], axis=1),
            jnp.concatenate([zero, two, zero, zero], axis=1),
            jnp.concatenate([zero, zero, zero, zero], axis=1),
        ],
        axis=0,
    ).T[:2 * cases]
    high, low = split2(weights)
    coefs = jnp.concatenate(
        [jnp.concatenate([high, high], axis=1), jnp.concatenate([low, low], axis=1)], axis=0
    )
    field = field_ref[...]
    pad = jnp.zeros_like(field)
    rows = stack2(jnp.concatenate([field, image_ref[...], second_ref[...], pad], axis=0))
    out = dot_nn(coefs, rows)
    out = out[:2 * cases] + out[2 * cases:]
    solution_ref[...] = out[:cases]
    residual_ref[...] = field + out[cases:]


def sum_of(terms):
    while len(terms) > 1:
        terms = [sum(terms[i:i + 2][1:], terms[i]) for i in range(0, len(terms), 2)]
    return terms[0]


def from_all(array, axis):
    count = lax.axis_size(axis)
    return [array] + [
        lax.ppermute(array, axis, [(i, (i + by) % count) for i in range(count)])
        for by in range(1, count)
    ]


def run(body, outs, args, scratch=(), scalars=0):
    whole = pl.BlockSpec(memory_space=pltpu.VMEM)
    return pl.pallas_call(
        body,
        out_shape=outs,
        in_specs=[pl.BlockSpec(memory_space=pltpu.SMEM)] * scalars + [whole] * (len(args) - scalars),
        out_specs=jax.tree.map(lambda _: whole, outs),
        scratch_shapes=list(scratch),
        compiler_params=pltpu.CompilerParams(vmem_limit_bytes=VMEM_BYTES),
    )(*args)


def shards(
    load_cases,
    mass_diag,
    stiffness,
    block_cols,
    trace_dofs,
    penalty,
    cell_partials,
    cell_owner,
    cell_dof,
):
    cases, dofs = load_cases.shape
    count, blk, width = stiffness.shape
    cells = cell_partials.shape[1]
    slots = trace_dofs.shape[0]
    patches = lax.axis_size("patch")
    cap = 4 * cells // patches
    rows = cases + 8
    shape = jax.ShapeDtypeStruct
    field_shape = shape((cases, dofs), F32)
    slot_shape = shape((cases, slots), F32)
    mass = mass_diag.reshape(1, dofs)
    trace = trace_dofs.reshape(1, slots)
    pen = penalty.reshape(1, slots)
    cols = block_cols.reshape(-1)

    half = patches // 2
    pairs = [(i, (i + half) % patches) for i in range(patches)]
    match_pen = lax.ppermute(pen, "patch", pairs)
    packed = run(
        pack_cells,
        shape((patches, rows, cap), F32),
        (cell_partials, cell_owner.reshape(1, cells), cell_dof.reshape(1, cells)),
    )
    received = lax.all_to_all(packed, "patch", 0, 0)
    stiff = run(split_stiffness, shape((count, 2 * blk, width), BF16), (stiffness,))

    spread = [pltpu.VMEM((dofs // blk, 2 * cases, LANES), BF16)] * 2
    strain_scratch = pltpu.VMEM((count, 2 * cases, LANES), BF16)
    sums = [pltpu.VMEM((dofs // blk, cases, LANES), F32)] * 4

    field, own = run(assemble, (field_shape, slot_shape), (received, load_cases, trace))
    match = lax.ppermute(own, "patch", pairs)
    part = run(
        operator_body,
        field_shape,
        (cols, field, mass, stiff),
        scratch=[*spread, strain_scratch, *sums],
        scalars=1,
    )
    image, own = run(
        first_image, (field_shape, slot_shape), (part, own, match, pen, match_pen, trace)
    )
    match = lax.ppermute(own, "patch", pairs)
    gram, strain = run(
        gram_body,
        (shape((cases, 4 * cases), F32), shape((count, 2 * cases, LANES), BF16)),
        (cols, field, image, mass, stiff),
        scratch=spread,
        scalars=1,
    )
    gram, jump = run(
        gram_trace,
        (shape((cases, 4 * cases), F32), slot_shape),
        (gram, own, match, pen, match_pen),
    )
    grams = from_all(sum_of(from_all(gram, "comp")), "patch")
    second = run(
        second_image,
        field_shape,
        (cols, image, mass, stiff, strain, jump, trace),
        scratch=sums,
        scalars=1,
    )
    return run(finish, (field_shape, field_shape), (*grams, field, image, second))


def solution(mesh):
    return jax.shard_map(
        shards,
        mesh=mesh,
        in_specs=(
            P(None, ("comp", "patch")),
            P(("comp", "patch")),
            P(("comp", "patch"), None, None),
            P(("comp", "patch"), None),
            P(("comp", "patch")),
            P(("comp", "patch")),
            P(None, ("comp", "patch")),
            P(("comp", "patch"), None),
            P(("comp", "patch")),
        ),
        out_specs=(P(None, ("comp", "patch")), P(None, ("comp", "patch"))),
        check_vma=False,
    )
```

```python
import jax
import jax.numpy as jnp
from jax import lax
from jax.experimental import pallas as pl
from jax.experimental.pallas import tpu as pltpu
from jax.sharding import PartitionSpec as P

F32 = jnp.float32
BF16 = jnp.bfloat16
WIDE = 256
LANES = 128
VMEM_BYTES = 48 * 1024 * 1024


def split2(x):
    high = x.astype(BF16)
    low = (x - high.astype(F32)).astype(BF16)
    return high, low


def stack2(x):
    return jnp.concatenate(split2(x), axis=0)


def dot_nn(a, b):
    return lax.dot_general(a, b, (((1,), (0,)), ((), ())), preferred_element_type=F32)


def dot_nt(a, b):
    return lax.dot_general(a, b, (((1,), (1,)), ((), ())), preferred_element_type=F32)


def iota(shape, axis):
    return lax.broadcasted_iota(jnp.int32, shape, axis)


def one_hot_low(low, width):
    return (iota((WIDE, width), 0) == low).astype(F32).astype(BF16)


def masked_groups(stacked, group, count):
    parts = []
    for g in range(count):
        mask = (group == g).astype(F32).astype(BF16)
        parts.append(stacked * jnp.broadcast_to(mask, stacked.shape))
    return jnp.concatenate(parts, axis=0)


def gather_slots(field, one_hot, group, groups):
    cases = field.shape[0]
    rows = jnp.concatenate(
        [stack2(field[:, g * WIDE:(g + 1) * WIDE]) for g in range(groups)], axis=0
    )
    found = dot_nn(rows, one_hot)
    total = jnp.zeros((cases, group.shape[1]), F32)
    for g in range(groups):
        base = g * 2 * cases
        both = found[base:base + cases] + found[base + cases:base + 2 * cases]
        total = jnp.where(group == g, both, total)
    return total


def pack_cells(partials_ref, owner_ref, dof_ref, pen_ref, *out_refs):
    patches = len(out_refs)
    rows, cap = out_refs[0].shape
    cases, cells = partials_ref.shape
    me = lax.axis_index("patch")
    shift = owner_ref[...] - me
    shift = jnp.where(shift < 0, shift + patches, shift)
    mine = (iota((patches, cells), 0) == shift).astype(F32)
    before = (iota((cells, cells), 0) < iota((cells, cells), 1)).astype(F32).astype(BF16)
    counts = dot_nn(mine.astype(BF16), before)
    rank = jnp.sum(mine * counts, axis=0, keepdims=True).astype(jnp.int32)
    extra = jnp.where(iota((rows - cases, cells), 0) == 0, dof_ref[...] + 1, 0).astype(F32)
    body = stack2(jnp.concatenate([partials_ref[...], extra], axis=0))
    for by, out_ref in enumerate(out_refs):
        key = jnp.where(shift == by, rank, -1)
        pick = (iota((cap, cells), 0) == key).astype(F32).astype(BF16)
        packed = dot_nt(body, pick)
        out_ref[...] = packed[:rows] + packed[rows:]
        if by == patches // 2:
            for i in range(pen_ref.shape[1] // cap):
                at = cases + 1 + i
                out_ref[at:at + 1, :] = pen_ref[:, i * cap:(i + 1) * cap]


def split_stiffness(stiff_ref, out_ref):
    blk = stiff_ref.shape[1]
    high, low = split2(stiff_ref[...])
    out_ref[:, :blk, :] = high
    out_ref[:, blk:, :] = low


def assemble(load_ref, trace_ref, *refs):
    *recv_refs, field_ref, own_ref, pen_ref = refs
    patches = len(recv_refs)
    cases, dofs = load_ref.shape
    groups = dofs // WIDE
    cells = jnp.concatenate([ref[...] for ref in recv_refs], axis=1)
    cap = recv_refs[0].shape[1]
    for i in range(pen_ref.shape[1] // cap):
        at = cases + 1 + i
        pen_ref[:, i * cap:(i + 1) * cap] = recv_refs[patches // 2][at:at + 1, :]
    slots = cells.shape[1]
    dof = cells[cases:cases + 1].astype(jnp.int32) - 1
    rows = masked_groups(stack2(cells[:cases]), dof >> 8, groups)
    sums = dot_nt(rows, one_hot_low(jnp.where(dof < 0, -1, dof & (WIDE - 1)), slots))
    pieces = []
    for g in range(groups):
        base = g * 2 * cases
        pieces.append(
            load_ref[:, g * WIDE:(g + 1) * WIDE]
            + (sums[base:base + cases] + sums[base + cases:base + 2 * cases])
        )
    field = jnp.concatenate(pieces, axis=1)
    field_ref[...] = field
    trace = trace_ref[...]
    own_ref[...] = gather_slots(
        field, one_hot_low(trace & (WIDE - 1), trace.shape[1]), trace >> 8, groups
    )


def spread_blocks(field_ref, low_ref, high_ref):
    cases, dofs = field_ref.shape
    in_low = iota((cases, LANES), 1) < LANES // 2
    for j in range(dofs // LANES):
        tile = field_ref[:, j * LANES:(j + 1) * LANES]
        turned = pltpu.roll(tile, LANES // 2, 1)
        low_ref[2 * j] = stack2(jnp.where(in_low, tile, 0.0))
        high_ref[2 * j + 1] = stack2(jnp.where(in_low, 0.0, tile))
        low_ref[2 * j + 1] = stack2(jnp.where(in_low, turned, 0.0))
        high_ref[2 * j] = stack2(jnp.where(in_low, 0.0, turned))


def strain_rows(cols_ref, stiff_ref, low_ref, high_ref, strain_ref):
    count = stiff_ref.shape[0]
    cases = strain_ref.shape[1] // 2
    for n in range(count):
        c = [cols_ref[4 * n + k] for k in range(4)]
        near = jnp.concatenate(
            [low_ref[c[0]] + high_ref[c[1]], low_ref[c[2]] + high_ref[c[3]]], axis=1
        )
        both = dot_nt(near, stiff_ref[n])
        both = both[:cases] + both[cases:]
        strain_ref[n] = stack2(both + pltpu.roll(both, LANES // 2, 1))


def transposed_sums(cols_ref, stiff_ref, strain_ref, sums):
    count = stiff_ref.shape[0]
    cases = strain_ref.shape[1] // 2
    for ref in sums:
        ref[...] = jnp.zeros_like(ref)
    for n in range(count):
        c = [cols_ref[4 * n + k] for k in range(4)]
        both = dot_nn(strain_ref[n], stiff_ref[n])
        both = both[:cases] + both[cases:]
        left, right = both[:, :LANES], both[:, LANES:]
        sums[0][c[0]] += left
        sums[1][c[1]] += left
        sums[2][c[2]] += right
        sums[3][c[3]] += right


def folded_tile(sums, j):
    cases = sums[0].shape[1]
    in_low = iota((cases, LANES), 1) < LANES // 2
    even, odd = 2 * j, 2 * j + 1
    straight = jnp.where(in_low, sums[0][even] + sums[2][even], sums[1][odd] + sums[3][odd])
    crossed = jnp.where(in_low, sums[0][odd] + sums[2][odd], sums[1][even] + sums[3][even])
    return straight + pltpu.roll(crossed, LANES // 2, 1)


def operator_body(cols_ref, field_ref, mass_ref, stiff_ref, out_ref, low_ref, high_ref, strain_ref, *sums):
    spread_blocks(field_ref, low_ref, high_ref)
    strain_rows(cols_ref, stiff_ref, low_ref, high_ref, strain_ref)
    transposed_sums(cols_ref, stiff_ref, strain_ref, sums)
    for j in range(field_ref.shape[1] // LANES):
        at = slice(j * LANES, (j + 1) * LANES)
        out_ref[:, at] = field_ref[:, at] * mass_ref[:, at] + folded_tile(sums, j)


def add_jump(base, jump, one_hot, group):
    cases, dofs = base.shape
    groups = dofs // WIDE
    sums = dot_nt(masked_groups(stack2(jump), group, groups), one_hot)
    pieces = []
    for g in range(groups):
        row = g * 2 * cases
        pieces.append(
            base[:, g * WIDE:(g + 1) * WIDE]
            + (sums[row:row + cases] + sums[row + cases:row + 2 * cases])
        )
    return jnp.concatenate(pieces, axis=1)


def first_image(part_ref, own_ref, match_ref, pen_ref, match_pen_ref, trace_ref, image_ref, trace_out_ref):
    trace = trace_ref[...]
    one_hot = one_hot_low(trace & (WIDE - 1), trace.shape[1])
    weight = pen_ref[...] * match_pen_ref[...]
    jump = weight * (own_ref[...] - match_ref[...])
    image = add_jump(part_ref[...], jump, one_hot, trace >> 8)
    image_ref[...] = image
    trace_out_ref[...] = gather_slots(image, one_hot, trace >> 8, image.shape[1] // WIDE)


def gram_body(cols_ref, field_ref, image_ref, mass_ref, stiff_ref, gram_ref, strain_ref, low_ref, high_ref):
    cases, dofs = field_ref.shape
    spread_blocks(image_ref, low_ref, high_ref)
    strain_rows(cols_ref, stiff_ref, low_ref, high_ref, strain_ref)
    in_low = iota((2 * cases, LANES), 1) < LANES // 2
    strain = jnp.concatenate(
        [
            jnp.where(in_low, strain_ref[2 * j].astype(F32), strain_ref[2 * j + 1].astype(F32)).astype(BF16)
            for j in range(strain_ref.shape[0] // 2)
        ],
        axis=1,
    )
    image = image_ref[...]
    image_rows = stack2(image)
    rows = jnp.concatenate([stack2(field_ref[...]), image_rows], axis=0)
    every = dot_nt(rows, image_rows)
    every = every[:, :cases] + every[:, cases:]
    cross = every[:cases] + every[cases:2 * cases]
    square = every[2 * cases:3 * cases] + every[3 * cases:]
    start = dot_nt(rows[:2 * cases], rows[:2 * cases])
    start = start[:, :cases] + start[:, cases:]
    start = start[:cases] + start[cases:]
    last = dot_nt(image_rows, stack2(image * mass_ref[...])) + dot_nt(strain, strain)
    last = last[:, :cases] + last[:, cases:]
    last = last[:cases] + last[cases:]
    gram_ref[...] = jnp.concatenate([cross, start, square, last], axis=1)


def gram_trace(gram_ref, own_ref, match_ref, pen_ref, match_pen_ref, out_ref, jump_ref):
    cases = gram_ref.shape[0]
    jump = (pen_ref[...] * match_pen_ref[...]) * (own_ref[...] - match_ref[...])
    jump_ref[...] = jump
    more = dot_nt(stack2(own_ref[...]), stack2(jump))
    more = more[:, :cases] + more[:, cases:]
    more = more[:cases] + more[cases:]
    zeros = jnp.zeros((cases, 3 * cases), F32)
    out_ref[...] = gram_ref[...] + jnp.concatenate([zeros, more], axis=1)


def second_image(cols_ref, image_ref, mass_ref, stiff_ref, strain_ref, jump_ref, trace_ref, out_ref, *sums):
    transposed_sums(cols_ref, stiff_ref, strain_ref, sums)
    trace = trace_ref[...]
    one_hot = one_hot_low(trace & (WIDE - 1), trace.shape[1])
    folded = jnp.concatenate(
        [folded_tile(sums, j) for j in range(image_ref.shape[1] // LANES)], axis=1
    )
    base = image_ref[...] * mass_ref[...] + folded
    out_ref[...] = add_jump(base, jump_ref[...], one_hot, trace >> 8)


def eliminate(matrix, size, group=4):
    rows = iota(matrix.shape, 0)
    for first in range(0, size, group):
        columns = [
            jnp.broadcast_to(matrix[:, p:p + 1], matrix.shape) for p in range(first, first + group)
        ]
        for q in range(group):
            p = first + q
            column = columns[q]
            inverse = 1.0 / column[p:p + 1]
            row = matrix[p:p + 1] * inverse
            here = rows == p
            matrix = jnp.where(here, row, matrix - column * row)
            for r in range(q + 1, group):
                entry = column[first + r:first + r + 1] * inverse
                columns[r] = jnp.where(here, entry, columns[r] - column * entry)
    return matrix


def small_dot(a, b):
    return jnp.dot(a, b, precision=lax.Precision.HIGHEST, preferred_element_type=F32)


def finish(*refs):
    *gram_refs, field_ref, image_ref, second_ref, solution_ref, residual_ref = refs
    cases = field_ref.shape[0]
    gram = sum_of([ref[...] for ref in gram_refs])
    square = gram[:, 2 * cases:3 * cases]
    solved = eliminate(gram, cases)
    zeros = jnp.zeros((cases, 2 * cases), F32)
    given = jnp.concatenate([gram[:, 3 * cases:], gram[:, :cases]], axis=1)
    both = jnp.concatenate([solved[:, 2 * cases:3 * cases], solved[:, cases:2 * cases]], axis=1)
    second_part = eliminate(
        jnp.concatenate([given - small_dot(square, both), zeros], axis=1), cases
    )[:, cases:2 * cases]
    first_part = both[:, cases:] - small_dot(both[:, :cases], second_part)
    zero = jnp.zeros((cases, cases), F32)
    weights = jnp.concatenate(
        [
            jnp.concatenate([first_part, zero, zero, zero], axis=1),
            jnp.concatenate([second_part, -first_part, zero, zero], axis=1),
            jnp.concatenate([zero, -second_part, zero, zero], axis=1),
            jnp.concatenate([zero, zero, zero, zero], axis=1),
        ],
        axis=0,
    ).T[:2 * cases]
    high, low = split2(weights)
    coefs = jnp.concatenate(
        [jnp.concatenate([high, high], axis=1), jnp.concatenate([low, low], axis=1)], axis=0
    )
    field = field_ref[...]
    pad = jnp.zeros_like(field)
    rows = stack2(jnp.concatenate([field, image_ref[...], second_ref[...], pad], axis=0))
    out = dot_nn(coefs, rows)
    out = out[:2 * cases] + out[2 * cases:]
    solution_ref[...] = out[:cases]
    residual_ref[...] = field + out[cases:]


def sum_of(terms):
    while len(terms) > 1:
        terms = [sum(terms[i:i + 2][1:], terms[i]) for i in range(0, len(terms), 2)]
    return terms[0]


def from_all(array, axis):
    count = lax.axis_size(axis)
    return [array] + [
        lax.ppermute(array, axis, [(i, (i + by) % count) for i in range(count)])
        for by in range(1, count)
    ]


def run(body, outs, args, scratch=(), scalars=0, cost=None):
    whole = pl.BlockSpec(memory_space=pltpu.VMEM)
    return pl.pallas_call(
        body,
        out_shape=outs,
        in_specs=[pl.BlockSpec(memory_space=pltpu.SMEM)] * scalars + [whole] * (len(args) - scalars),
        out_specs=jax.tree.map(lambda _: whole, outs),
        scratch_shapes=list(scratch),
        compiler_params=pltpu.CompilerParams(vmem_limit_bytes=VMEM_BYTES),
        cost_estimate=cost,
    )(*args)


def shards(
    load_cases,
    mass_diag,
    stiffness,
    block_cols,
    trace_dofs,
    penalty,
    cell_partials,
    cell_owner,
    cell_dof,
):
    cases, dofs = load_cases.shape
    count, blk, width = stiffness.shape
    cells = cell_partials.shape[1]
    slots = trace_dofs.shape[0]
    patches = lax.axis_size("patch")
    cap = 4 * cells // patches
    rows = cases + -(-(1 + slots // cap) // 8) * 8
    shape = jax.ShapeDtypeStruct
    field_shape = shape((cases, dofs), F32)
    slot_shape = shape((cases, slots), F32)
    mass = mass_diag.reshape(1, dofs)
    trace = trace_dofs.reshape(1, slots)
    pen = penalty.reshape(1, slots)
    cols = block_cols.reshape(-1)

    half = patches // 2
    pairs = [(i, (i + half) % patches) for i in range(patches)]
    packets = run(
        pack_cells,
        [shape((rows, cap), F32)] * patches,
        (cell_partials, cell_owner.reshape(1, cells), cell_dof.reshape(1, cells), pen),
    )
    received = [packets[0]] + [
        lax.ppermute(packets[by], "patch", [(i, (i + by) % patches) for i in range(patches)])
        for by in range(1, patches)
    ]
    stiff = run(
        split_stiffness,
        shape((count, 2 * blk, width), BF16),
        (stiffness,),
        cost=pl.CostEstimate(flops=4 * stiffness.size, bytes_accessed=8 * stiffness.size, transcendentals=0),
    )

    received, stiff, cols, mass, load_cases, trace = lax.optimization_barrier(
        (received, stiff, cols, mass, load_cases, trace)
    )

    spread = [pltpu.VMEM((dofs // blk, 2 * cases, LANES), BF16)] * 2
    strain_scratch = pltpu.VMEM((count, 2 * cases, LANES), BF16)
    sums = [pltpu.VMEM((dofs // blk, cases, LANES), F32)] * 4

    field, own, match_pen = run(
        assemble, (field_shape, slot_shape, shape((1, slots), F32)), (load_cases, trace, *received)
    )
    match = lax.ppermute(own, "patch", pairs)
    part = run(
        operator_body,
        field_shape,
        (cols, field, mass, stiff),
        scratch=[*spread, strain_scratch, *sums],
        scalars=1,
    )
    image, own = run(
        first_image, (field_shape, slot_shape), (part, own, match, pen, match_pen, trace)
    )
    match = lax.ppermute(own, "patch", pairs)
    gram, strain = run(
        gram_body,
        (shape((cases, 4 * cases), F32), shape((count, 2 * cases, LANES), BF16)),
        (cols, field, image, mass, stiff),
        scratch=spread,
        scalars=1,
    )
    gram, jump = run(
        gram_trace,
        (shape((cases, 4 * cases), F32), slot_shape),
        (gram, own, match, pen, match_pen),
    )
    grams = from_all(sum_of(from_all(gram, "comp")), "patch")
    second = run(
        second_image,
        field_shape,
        (cols, image, mass, stiff, strain, jump, trace),
        scratch=sums,
        scalars=1,
    )
    return run(finish, (field_shape, field_shape), (*grams, field, image, second))


def solution(mesh):
    return jax.shard_map(
        shards,
        mesh=mesh,
        in_specs=(
            P(None, ("comp", "patch")),
            P(("comp", "patch")),
            P(("comp", "patch"), None, None),
            P(("comp", "patch"), None),
            P(("comp", "patch")),
            P(("comp", "patch")),
            P(None, ("comp", "patch")),
            P(("comp", "patch"), None),
            P(("comp", "patch")),
        ),
        out_specs=(P(None, ("comp", "patch")), P(None, ("comp", "patch"))),
        check_vma=False,
    )
```

```python
import jax
import jax.numpy as jnp
from jax import lax
from jax.experimental import pallas as pl
from jax.experimental.pallas import tpu as pltpu
from jax.sharding import PartitionSpec as P

F32 = jnp.float32
BF16 = jnp.bfloat16
WIDE = 256
LANES = 128
VMEM_BYTES = 48 * 1024 * 1024


def split2(x):
    high = x.astype(BF16)
    low = (x - high.astype(F32)).astype(BF16)
    return high, low


def stack2(x):
    return jnp.concatenate(split2(x), axis=0)


def dot_nn(a, b):
    return lax.dot_general(a, b, (((1,), (0,)), ((), ())), preferred_element_type=F32)


def dot_nt(a, b):
    return lax.dot_general(a, b, (((1,), (1,)), ((), ())), preferred_element_type=F32)


def iota(shape, axis):
    return lax.broadcasted_iota(jnp.int32, shape, axis)


def one_hot_low(low, width):
    return (iota((WIDE, width), 0) == low).astype(F32).astype(BF16)


def masked_groups(stacked, group, count):
    parts = []
    for g in range(count):
        mask = (group == g).astype(F32).astype(BF16)
        parts.append(stacked * jnp.broadcast_to(mask, stacked.shape))
    return jnp.concatenate(parts, axis=0)


def gather_slots(field, one_hot, group, groups):
    cases = field.shape[0]
    rows = jnp.concatenate(
        [stack2(field[:, g * WIDE:(g + 1) * WIDE]) for g in range(groups)], axis=0
    )
    found = dot_nn(rows, one_hot)
    total = jnp.zeros((cases, group.shape[1]), F32)
    for g in range(groups):
        base = g * 2 * cases
        both = found[base:base + cases] + found[base + cases:base + 2 * cases]
        total = jnp.where(group == g, both, total)
    return total


def fetch(sources, targets, sems):
    copies = [
        pltpu.make_async_copy(source, target, sems.at[i])
        for i, (source, target) in enumerate(zip(sources, targets))
    ]
    for copy in copies:
        copy.start()
    for copy in copies:
        copy.wait()


def pack_cells(*refs):
    sources, out_refs, targets, sems = refs[:4], refs[4:-5], refs[-5:-1], refs[-1]
    fetch(sources, targets, sems)
    partials_ref, owner_ref, dof_ref, pen_ref = targets
    patches = len(out_refs)
    rows, cap = out_refs[0].shape
    cases, cells = partials_ref.shape
    me = lax.axis_index("patch")
    shift = owner_ref[...] - me
    shift = jnp.where(shift < 0, shift + patches, shift)
    mine = (iota((patches, cells), 0) == shift).astype(F32)
    before = (iota((cells, cells), 0) < iota((cells, cells), 1)).astype(F32).astype(BF16)
    counts = dot_nn(mine.astype(BF16), before)
    rank = jnp.sum(mine * counts, axis=0, keepdims=True).astype(jnp.int32)
    extra = jnp.where(iota((rows - cases, cells), 0) == 0, dof_ref[...] + 1, 0).astype(F32)
    body = stack2(jnp.concatenate([partials_ref[...], extra], axis=0))
    for by, out_ref in enumerate(out_refs):
        key = jnp.where(shift == by, rank, -1)
        pick = (iota((cap, cells), 0) == key).astype(F32).astype(BF16)
        packed = dot_nt(body, pick)
        out_ref[...] = packed[:rows] + packed[rows:]
        if by == patches // 2:
            for i in range(pen_ref.shape[1] // cap):
                at = cases + 1 + i
                out_ref[at:at + 1, :] = pen_ref[:, i * cap:(i + 1) * cap]


def split_stiffness(stiff_ref, out_ref):
    blk = stiff_ref.shape[1]
    high, low = split2(stiff_ref[...])
    out_ref[:, :blk, :] = high
    out_ref[:, blk:, :] = low


def assemble(load_ref, trace_ref, *refs):
    *recv_refs, field_ref, own_ref, pen_ref = refs
    patches = len(recv_refs)
    cases, dofs = load_ref.shape
    groups = dofs // WIDE
    cells = jnp.concatenate([ref[...] for ref in recv_refs], axis=1)
    cap = recv_refs[0].shape[1]
    for i in range(pen_ref.shape[1] // cap):
        at = cases + 1 + i
        pen_ref[:, i * cap:(i + 1) * cap] = recv_refs[patches // 2][at:at + 1, :]
    slots = cells.shape[1]
    dof = cells[cases:cases + 1].astype(jnp.int32) - 1
    rows = masked_groups(stack2(cells[:cases]), dof >> 8, groups)
    sums = dot_nt(rows, one_hot_low(jnp.where(dof < 0, -1, dof & (WIDE - 1)), slots))
    pieces = []
    for g in range(groups):
        base = g * 2 * cases
        pieces.append(
            load_ref[:, g * WIDE:(g + 1) * WIDE]
            + (sums[base:base + cases] + sums[base + cases:base + 2 * cases])
        )
    field = jnp.concatenate(pieces, axis=1)
    field_ref[...] = field
    trace = trace_ref[...]
    own_ref[...] = gather_slots(
        field, one_hot_low(trace & (WIDE - 1), trace.shape[1]), trace >> 8, groups
    )


def spread_blocks(field_ref, low_ref, high_ref):
    cases, dofs = field_ref.shape
    in_low = iota((cases, LANES), 1) < LANES // 2
    for j in range(dofs // LANES):
        tile = field_ref[:, j * LANES:(j + 1) * LANES]
        turned = pltpu.roll(tile, LANES // 2, 1)
        low_ref[2 * j] = stack2(jnp.where(in_low, tile, 0.0))
        high_ref[2 * j + 1] = stack2(jnp.where(in_low, 0.0, tile))
        low_ref[2 * j + 1] = stack2(jnp.where(in_low, turned, 0.0))
        high_ref[2 * j] = stack2(jnp.where(in_low, 0.0, turned))


def strain_rows(cols_ref, stiff_ref, low_ref, high_ref, strain_ref):
    count = stiff_ref.shape[0]
    cases = strain_ref.shape[1] // 2
    for n in range(count):
        c = [cols_ref[4 * n + k] for k in range(4)]
        near = jnp.concatenate(
            [low_ref[c[0]] + high_ref[c[1]], low_ref[c[2]] + high_ref[c[3]]], axis=1
        )
        both = dot_nt(near, stiff_ref[n])
        both = both[:cases] + both[cases:]
        strain_ref[n] = stack2(both + pltpu.roll(both, LANES // 2, 1))


def transposed_sums(cols_ref, stiff_ref, strain_ref, sums):
    count = stiff_ref.shape[0]
    cases = strain_ref.shape[1] // 2
    for ref in sums:
        ref[...] = jnp.zeros_like(ref)
    for n in range(count):
        c = [cols_ref[4 * n + k] for k in range(4)]
        both = dot_nn(strain_ref[n], stiff_ref[n])
        both = both[:cases] + both[cases:]
        left, right = both[:, :LANES], both[:, LANES:]
        sums[0][c[0]] += left
        sums[1][c[1]] += left
        sums[2][c[2]] += right
        sums[3][c[3]] += right


def folded_tile(sums, j):
    cases = sums[0].shape[1]
    in_low = iota((cases, LANES), 1) < LANES // 2
    even, odd = 2 * j, 2 * j + 1
    straight = jnp.where(in_low, sums[0][even] + sums[2][even], sums[1][odd] + sums[3][odd])
    crossed = jnp.where(in_low, sums[0][odd] + sums[2][odd], sums[1][even] + sums[3][even])
    return straight + pltpu.roll(crossed, LANES // 2, 1)


def operator_body(cols_ref, field_ref, mass_ref, stiff_ref, out_ref, low_ref, high_ref, strain_ref, *sums):
    spread_blocks(field_ref, low_ref, high_ref)
    strain_rows(cols_ref, stiff_ref, low_ref, high_ref, strain_ref)
    transposed_sums(cols_ref, stiff_ref, strain_ref, sums)
    for j in range(field_ref.shape[1] // LANES):
        at = slice(j * LANES, (j + 1) * LANES)
        out_ref[:, at] = field_ref[:, at] * mass_ref[:, at] + folded_tile(sums, j)


def add_jump(base, jump, one_hot, group):
    cases, dofs = base.shape
    groups = dofs // WIDE
    sums = dot_nt(masked_groups(stack2(jump), group, groups), one_hot)
    pieces = []
    for g in range(groups):
        row = g * 2 * cases
        pieces.append(
            base[:, g * WIDE:(g + 1) * WIDE]
            + (sums[row:row + cases] + sums[row + cases:row + 2 * cases])
        )
    return jnp.concatenate(pieces, axis=1)


def first_image(part_ref, own_ref, match_ref, pen_ref, match_pen_ref, trace_ref, image_ref, trace_out_ref):
    trace = trace_ref[...]
    one_hot = one_hot_low(trace & (WIDE - 1), trace.shape[1])
    weight = pen_ref[...] * match_pen_ref[...]
    jump = weight * (own_ref[...] - match_ref[...])
    image = add_jump(part_ref[...], jump, one_hot, trace >> 8)
    image_ref[...] = image
    trace_out_ref[...] = gather_slots(image, one_hot, trace >> 8, image.shape[1] // WIDE)


def gram_body(cols_ref, field_ref, image_ref, mass_ref, stiff_ref, gram_ref, strain_ref, low_ref, high_ref):
    cases, dofs = field_ref.shape
    spread_blocks(image_ref, low_ref, high_ref)
    strain_rows(cols_ref, stiff_ref, low_ref, high_ref, strain_ref)
    in_low = iota((2 * cases, LANES), 1) < LANES // 2
    strain = jnp.concatenate(
        [
            jnp.where(in_low, strain_ref[2 * j].astype(F32), strain_ref[2 * j + 1].astype(F32)).astype(BF16)
            for j in range(strain_ref.shape[0] // 2)
        ],
        axis=1,
    )
    image = image_ref[...]
    image_rows = stack2(image)
    rows = jnp.concatenate([stack2(field_ref[...]), image_rows], axis=0)
    every = dot_nt(rows, image_rows)
    every = every[:, :cases] + every[:, cases:]
    cross = every[:cases] + every[cases:2 * cases]
    square = every[2 * cases:3 * cases] + every[3 * cases:]
    start = dot_nt(rows[:2 * cases], rows[:2 * cases])
    start = start[:, :cases] + start[:, cases:]
    start = start[:cases] + start[cases:]
    last = dot_nt(image_rows, stack2(image * mass_ref[...])) + dot_nt(strain, strain)
    last = last[:, :cases] + last[:, cases:]
    last = last[:cases] + last[cases:]
    gram_ref[...] = jnp.concatenate([cross, start, square, last], axis=1)


def gram_trace(gram_ref, own_ref, match_ref, pen_ref, match_pen_ref, out_ref, jump_ref):
    cases = gram_ref.shape[0]
    jump = (pen_ref[...] * match_pen_ref[...]) * (own_ref[...] - match_ref[...])
    jump_ref[...] = jump
    more = dot_nt(stack2(own_ref[...]), stack2(jump))
    more = more[:, :cases] + more[:, cases:]
    more = more[:cases] + more[cases:]
    zeros = jnp.zeros((cases, 3 * cases), F32)
    out_ref[...] = gram_ref[...] + jnp.concatenate([zeros, more], axis=1)


def second_image(cols_ref, image_ref, mass_ref, stiff_ref, strain_ref, jump_ref, trace_ref, out_ref, *sums):
    transposed_sums(cols_ref, stiff_ref, strain_ref, sums)
    trace = trace_ref[...]
    one_hot = one_hot_low(trace & (WIDE - 1), trace.shape[1])
    folded = jnp.concatenate(
        [folded_tile(sums, j) for j in range(image_ref.shape[1] // LANES)], axis=1
    )
    base = image_ref[...] * mass_ref[...] + folded
    out_ref[...] = add_jump(base, jump_ref[...], one_hot, trace >> 8)


def eliminate(matrix, size, group=4):
    rows = iota(matrix.shape, 0)
    for first in range(0, size, group):
        columns = [
            jnp.broadcast_to(matrix[:, p:p + 1], matrix.shape) for p in range(first, first + group)
        ]
        for q in range(group):
            p = first + q
            column = columns[q]
            inverse = 1.0 / column[p:p + 1]
            row = matrix[p:p + 1] * inverse
            here = rows == p
            matrix = jnp.where(here, row, matrix - column * row)
            for r in range(q + 1, group):
                entry = column[first + r:first + r + 1] * inverse
                columns[r] = jnp.where(here, entry, columns[r] - column * entry)
    return matrix


def small_dot(a, b):
    return jnp.dot(a, b, precision=lax.Precision.HIGHEST, preferred_element_type=F32)


def finish(*refs):
    *gram_refs, field_ref, image_ref, second_ref, solution_ref, residual_ref = refs
    cases = field_ref.shape[0]
    gram = sum_of([ref[...] for ref in gram_refs])
    square = gram[:, 2 * cases:3 * cases]
    solved = eliminate(gram, cases)
    zeros = jnp.zeros((cases, 2 * cases), F32)
    given = jnp.concatenate([gram[:, 3 * cases:], gram[:, :cases]], axis=1)
    both = jnp.concatenate([solved[:, 2 * cases:3 * cases], solved[:, cases:2 * cases]], axis=1)
    second_part = eliminate(
        jnp.concatenate([given - small_dot(square, both), zeros], axis=1), cases
    )[:, cases:2 * cases]
    first_part = both[:, cases:] - small_dot(both[:, :cases], second_part)
    zero = jnp.zeros((cases, cases), F32)
    weights = jnp.concatenate(
        [
            jnp.concatenate([first_part, zero, zero, zero], axis=1),
            jnp.concatenate([second_part, -first_part, zero, zero], axis=1),
            jnp.concatenate([zero, -second_part, zero, zero], axis=1),
            jnp.concatenate([zero, zero, zero, zero], axis=1),
        ],
        axis=0,
    ).T[:2 * cases]
    high, low = split2(weights)
    coefs = jnp.concatenate(
        [jnp.concatenate([high, high], axis=1), jnp.concatenate([low, low], axis=1)], axis=0
    )
    field = field_ref[...]
    pad = jnp.zeros_like(field)
    rows = stack2(jnp.concatenate([field, image_ref[...], second_ref[...], pad], axis=0))
    out = dot_nn(coefs, rows)
    out = out[:2 * cases] + out[2 * cases:]
    solution_ref[...] = out[:cases]
    residual_ref[...] = field + out[cases:]


def sum_of(terms):
    while len(terms) > 1:
        terms = [sum(terms[i:i + 2][1:], terms[i]) for i in range(0, len(terms), 2)]
    return terms[0]


def from_all(array, axis, stride=1, radix=None):
    count = lax.axis_size(axis)
    radix = radix or count
    span = stride * radix

    def target(i, by):
        digit = i // stride % radix
        return i // span * span + (digit + by) % radix * stride + i % stride

    return [array] + [
        lax.ppermute(array, axis, [(i, target(i, by)) for i in range(count)])
        for by in range(1, radix)
    ]


def digits(count):
    stages, stride = [], 1
    while stride < count:
        left = count // stride
        radix = 2 if stride == 1 and left % 2 == 0 else 4 if left % 4 == 0 else left
        stages.append((stride, radix))
        stride *= radix
    return stages


def run(body, outs, args, scratch=(), scalars=0, cost=None, far=0):
    whole = pl.BlockSpec(memory_space=pltpu.VMEM)
    args = [
        pltpu.with_memory_space_constraint(arg, pltpu.HBM) if scalars <= i < scalars + far else arg
        for i, arg in enumerate(args)
    ]
    return pl.pallas_call(
        body,
        out_shape=outs,
        in_specs=[pl.BlockSpec(memory_space=pltpu.SMEM)] * scalars
        + [pl.BlockSpec(memory_space=pltpu.HBM)] * far
        + [whole] * (len(args) - scalars - far),
        out_specs=jax.tree.map(lambda _: whole, outs),
        scratch_shapes=list(scratch),
        compiler_params=pltpu.CompilerParams(vmem_limit_bytes=VMEM_BYTES),
        cost_estimate=cost,
    )(*args)


def shards(
    load_cases,
    mass_diag,
    stiffness,
    block_cols,
    trace_dofs,
    penalty,
    cell_partials,
    cell_owner,
    cell_dof,
):
    cases, dofs = load_cases.shape
    count, blk, width = stiffness.shape
    cells = cell_partials.shape[1]
    slots = trace_dofs.shape[0]
    patches = lax.axis_size("patch")
    cap = 4 * cells // patches
    rows = cases + -(-(1 + slots // cap) // 8) * 8
    shape = jax.ShapeDtypeStruct
    field_shape = shape((cases, dofs), F32)
    slot_shape = shape((cases, slots), F32)
    mass = mass_diag.reshape(1, dofs)
    trace = trace_dofs.reshape(1, slots)
    pen = penalty.reshape(1, slots)
    cols = block_cols.reshape(-1)

    half = patches // 2
    pairs = [(i, (i + half) % patches) for i in range(patches)]
    packets = run(
        pack_cells,
        [shape((rows, cap), F32)] * patches,
        (cell_partials, cell_owner.reshape(1, cells), cell_dof.reshape(1, cells), pen),
        scratch=[
            pltpu.VMEM((cases, cells), F32),
            pltpu.VMEM((1, cells), jnp.int32),
            pltpu.VMEM((1, cells), jnp.int32),
            pltpu.VMEM((1, slots), F32),
            pltpu.SemaphoreType.DMA((4,)),
        ],
        far=4,
    )
    received = [packets[0]] + [
        lax.ppermute(packets[by], "patch", [(i, (i + by) % patches) for i in range(patches)])
        for by in range(1, patches)
    ]
    stiff = run(
        split_stiffness,
        shape((count, 2 * blk, width), BF16),
        (stiffness,),
        cost=pl.CostEstimate(flops=4 * stiffness.size, bytes_accessed=8 * stiffness.size, transcendentals=0),
    )

    received, stiff, cols, mass, load_cases, trace = lax.optimization_barrier(
        (received, stiff, cols, mass, load_cases, trace)
    )

    spread = [pltpu.VMEM((dofs // blk, 2 * cases, LANES), BF16)] * 2
    strain_scratch = pltpu.VMEM((count, 2 * cases, LANES), BF16)
    sums = [pltpu.VMEM((dofs // blk, cases, LANES), F32)] * 4

    field, own, match_pen = run(
        assemble, (field_shape, slot_shape, shape((1, slots), F32)), (load_cases, trace, *received)
    )
    match = lax.ppermute(own, "patch", pairs)
    part = run(
        operator_body,
        field_shape,
        (cols, field, mass, stiff),
        scratch=[*spread, strain_scratch, *sums],
        scalars=1,
    )
    image, own = run(
        first_image, (field_shape, slot_shape), (part, own, match, pen, match_pen, trace)
    )
    match = lax.ppermute(own, "patch", pairs)
    gram, strain = run(
        gram_body,
        (shape((cases, 4 * cases), F32), shape((count, 2 * cases, LANES), BF16)),
        (cols, field, image, mass, stiff),
        scratch=spread,
        scalars=1,
    )
    gram, jump = run(
        gram_trace,
        (shape((cases, 4 * cases), F32), slot_shape),
        (gram, own, match, pen, match_pen),
    )
    gram = sum_of(from_all(gram, "comp"))
    *early, last = digits(patches)
    for stride, radix in early:
        gram = sum_of(from_all(gram, "patch", stride, radix))
    grams = from_all(gram, "patch", *last)
    second = run(
        second_image,
        field_shape,
        (cols, image, mass, stiff, strain, jump, trace),
        scratch=sums,
        scalars=1,
    )
    return run(finish, (field_shape, field_shape), (*grams, field, image, second))


def solution(mesh):
    return jax.shard_map(
        shards,
        mesh=mesh,
        in_specs=(
            P(None, ("comp", "patch")),
            P(("comp", "patch")),
            P(("comp", "patch"), None, None),
            P(("comp", "patch"), None),
            P(("comp", "patch")),
            P(("comp", "patch")),
            P(None, ("comp", "patch")),
            P(("comp", "patch"), None),
            P(("comp", "patch")),
        ),
        out_specs=(P(None, ("comp", "patch")), P(None, ("comp", "patch"))),
        check_vma=False,
    )
```

```python
import jax
import jax.numpy as jnp
from jax import lax
from jax.experimental import pallas as pl
from jax.experimental.pallas import tpu as pltpu
from jax.sharding import PartitionSpec as P

F32 = jnp.float32
BF16 = jnp.bfloat16
WIDE = 256
LANES = 128
VMEM_BYTES = 32 * 1024 * 1024


def split2(x):
    high = x.astype(BF16)
    low = (x - high.astype(F32)).astype(BF16)
    return high, low


def stack2(x):
    return jnp.concatenate(split2(x), axis=0)


def dot_nn(a, b):
    return lax.dot_general(a, b, (((1,), (0,)), ((), ())), preferred_element_type=F32)


def dot_nt(a, b):
    return lax.dot_general(a, b, (((1,), (1,)), ((), ())), preferred_element_type=F32)


def iota(shape, axis):
    return lax.broadcasted_iota(jnp.int32, shape, axis)


def one_hot_low(low, width):
    return (iota((WIDE, width), 0) == low).astype(F32).astype(BF16)


def masked_groups(stacked, group, count):
    parts = []
    for g in range(count):
        mask = (group == g).astype(F32).astype(BF16)
        parts.append(stacked * jnp.broadcast_to(mask, stacked.shape))
    return jnp.concatenate(parts, axis=0)


def gather_slots(field, one_hot, group, groups):
    cases = field.shape[0]
    rows = jnp.concatenate(
        [stack2(field[:, g * WIDE:(g + 1) * WIDE]) for g in range(groups)], axis=0
    )
    found = dot_nn(rows, one_hot)
    total = jnp.zeros((cases, group.shape[1]), F32)
    for g in range(groups):
        base = g * 2 * cases
        both = found[base:base + cases] + found[base + cases:base + 2 * cases]
        total = jnp.where(group == g, both, total)
    return total


def fetch(sources, targets, sems):
    copies = [
        pltpu.make_async_copy(source, target, sems.at[i])
        for i, (source, target) in enumerate(zip(sources, targets))
    ]
    for copy in copies:
        copy.start()
    for copy in copies:
        copy.wait()


def pack_cells(*refs):
    sources, out_refs, targets, sems = refs[:5], refs[5:-6], refs[-6:-1], refs[-1]
    fetch(sources, targets, sems)
    partials_ref, owner_ref, dof_ref, pen_ref, trace_ref = targets
    patches = len(out_refs)
    rows, cap = out_refs[0].shape
    cases, cells = partials_ref.shape
    me = lax.axis_index("patch")
    shift = owner_ref[...] - me
    shift = jnp.where(shift < 0, shift + patches, shift)
    mine = (iota((patches, cells), 0) == shift).astype(F32)
    before = (iota((cells, cells), 0) < iota((cells, cells), 1)).astype(F32).astype(BF16)
    counts = dot_nn(mine.astype(BF16), before)
    rank = jnp.sum(mine * counts, axis=0, keepdims=True).astype(jnp.int32)
    extra = jnp.where(iota((rows - cases, cells), 0) == 0, dof_ref[...] + 1, 0).astype(F32)
    body = stack2(jnp.concatenate([partials_ref[...], extra], axis=0))
    for by, out_ref in enumerate(out_refs):
        key = jnp.where(shift == by, rank, -1)
        pick = (iota((cap, cells), 0) == key).astype(F32).astype(BF16)
        packed = dot_nt(body, pick)
        out_ref[:rows, :] = packed[:rows] + packed[rows:]
        if by == patches // 2:
            more = pen_ref.shape[1] // cap
            for i in range(more):
                at = cases + 1 + i
                out_ref[at:at + 1, :] = pen_ref[:, i * cap:(i + 1) * cap]
                out_ref[at + more:at + more + 1, :] = trace_ref[:, i * cap:(i + 1) * cap].astype(F32)


def split_stiffness(stiff_ref, out_ref):
    blk = stiff_ref.shape[1]
    high, low = split2(stiff_ref[...])
    out_ref[:, :blk, :] = high
    out_ref[:, blk:, :] = low


def assemble(load_ref, trace_ref, *refs):
    *recv_refs, field_ref, own_ref, pen_ref, match_trace_ref = refs
    patches = len(recv_refs)
    cases, dofs = load_ref.shape
    groups = dofs // WIDE
    rows, cap = recv_refs[0].shape
    cells = jnp.concatenate([ref[:rows, :] for ref in recv_refs], axis=1)
    far_ref = recv_refs[patches // 2]
    more = pen_ref.shape[1] // cap
    for i in range(more):
        at = cases + 1 + i
        pen_ref[:, i * cap:(i + 1) * cap] = far_ref[at:at + 1, :]
        match_trace_ref[:, i * cap:(i + 1) * cap] = far_ref[at + more:at + more + 1, :]
    slots = cells.shape[1]
    dof = cells[cases:cases + 1].astype(jnp.int32) - 1
    rows = masked_groups(stack2(cells[:cases]), dof >> 8, groups)
    sums = dot_nt(rows, one_hot_low(jnp.where(dof < 0, -1, dof & (WIDE - 1)), slots))
    pieces = []
    for g in range(groups):
        base = g * 2 * cases
        pieces.append(
            load_ref[:, g * WIDE:(g + 1) * WIDE]
            + (sums[base:base + cases] + sums[base + cases:base + 2 * cases])
        )
    field = jnp.concatenate(pieces, axis=1)
    field_ref[...] = field
    trace = trace_ref[...]
    own_ref[...] = gather_slots(
        field, one_hot_low(trace & (WIDE - 1), trace.shape[1]), trace >> 8, groups
    )


def spread_blocks(field_ref, low_ref, high_ref):
    cases, dofs = field_ref.shape
    in_low = iota((cases, LANES), 1) < LANES // 2
    for j in range(dofs // LANES):
        tile = field_ref[:, j * LANES:(j + 1) * LANES]
        turned = pltpu.roll(tile, LANES // 2, 1)
        low_ref[2 * j] = stack2(jnp.where(in_low, tile, 0.0))
        high_ref[2 * j + 1] = stack2(jnp.where(in_low, 0.0, tile))
        low_ref[2 * j + 1] = stack2(jnp.where(in_low, turned, 0.0))
        high_ref[2 * j] = stack2(jnp.where(in_low, 0.0, turned))


def strain_rows(cols_ref, stiff_ref, low_ref, high_ref, strain_ref):
    count = stiff_ref.shape[0]
    cases = strain_ref.shape[1] // 2
    for n in range(count):
        c = [cols_ref[4 * n + k] for k in range(4)]
        near = jnp.concatenate(
            [low_ref[c[0]] + high_ref[c[1]], low_ref[c[2]] + high_ref[c[3]]], axis=1
        )
        both = dot_nt(near, stiff_ref[n])
        both = both[:cases] + both[cases:]
        strain_ref[n] = stack2(both + pltpu.roll(both, LANES // 2, 1))


def transposed_sums(cols_ref, stiff_ref, strain_ref, sums):
    count = stiff_ref.shape[0]
    cases = strain_ref.shape[1] // 2
    for ref in sums:
        ref[...] = jnp.zeros_like(ref)
    for n in range(count):
        c = [cols_ref[4 * n + k] for k in range(4)]
        both = dot_nn(strain_ref[n], stiff_ref[n])
        both = both[:cases] + both[cases:]
        left, right = both[:, :LANES], both[:, LANES:]
        sums[0][c[0]] += left
        sums[1][c[1]] += left
        sums[2][c[2]] += right
        sums[3][c[3]] += right


def folded_tile(sums, j):
    cases = sums[0].shape[1]
    in_low = iota((cases, LANES), 1) < LANES // 2
    even, odd = 2 * j, 2 * j + 1
    straight = jnp.where(in_low, sums[0][even] + sums[2][even], sums[1][odd] + sums[3][odd])
    crossed = jnp.where(in_low, sums[0][odd] + sums[2][odd], sums[1][even] + sums[3][even])
    return straight + pltpu.roll(crossed, LANES // 2, 1)


def operator_body(
    cols_ref, field_ref, mass_ref, trace_ref, stiff_ref, out_ref, own_ref, low_ref, high_ref, strain_ref, *sums
):
    spread_blocks(field_ref, low_ref, high_ref)
    strain_rows(cols_ref, stiff_ref, low_ref, high_ref, strain_ref)
    transposed_sums(cols_ref, stiff_ref, strain_ref, sums)
    dofs = field_ref.shape[1]
    for j in range(dofs // LANES):
        at = slice(j * LANES, (j + 1) * LANES)
        out_ref[:, at] = field_ref[:, at] * mass_ref[:, at] + folded_tile(sums, j)
    trace = trace_ref[...]
    own_ref[...] = gather_slots(
        out_ref[...], one_hot_low(trace & (WIDE - 1), trace.shape[1]), trace >> 8, dofs // WIDE
    )


def coincidence(trace_ref, match_trace_ref, out_ref):
    slots = trace_ref.shape[1]
    rows = [trace_ref[...].astype(F32), match_trace_ref[...]]
    for i in range(slots // LANES):
        at = slice(i * LANES, (i + 1) * LANES)
        total = jnp.zeros((LANES, slots), F32)
        for row in rows:
            column = jnp.broadcast_to(row[:, at], (LANES, LANES)).T
            total += (jnp.broadcast_to(column[:, :1], (LANES, slots)) == row).astype(F32)
        out_ref[at, :] = total.astype(BF16)


def add_jump(base, jump, one_hot, group):
    cases, dofs = base.shape
    groups = dofs // WIDE
    sums = dot_nt(masked_groups(stack2(jump), group, groups), one_hot)
    pieces = []
    for g in range(groups):
        row = g * 2 * cases
        pieces.append(
            base[:, g * WIDE:(g + 1) * WIDE]
            + (sums[row:row + cases] + sums[row + cases:row + 2 * cases])
        )
    return jnp.concatenate(pieces, axis=1)


def first_image(
    cols_ref, field_ref, part_ref, own_ref, match_ref, pen_ref, match_pen_ref, trace_ref, mass_ref, same_ref, stiff_ref,
    image_ref, shift_ref, gram_ref, strain_ref, low_ref, high_ref,
):
    cases, dofs = field_ref.shape
    trace = trace_ref[...]
    weight = pen_ref[...] * match_pen_ref[...]
    jump = weight * (own_ref[...] - match_ref[...])
    image_ref[...] = add_jump(
        part_ref[...], jump, one_hot_low(trace & (WIDE - 1), trace.shape[1]), trace >> 8
    )
    moved = dot_nn(stack2(jump), same_ref[...])
    shift_ref[...] = moved[:cases] + moved[cases:]
    spread_blocks(image_ref, low_ref, high_ref)
    strain_rows(cols_ref, stiff_ref, low_ref, high_ref, strain_ref)
    in_low = iota((2 * cases, LANES), 1) < LANES // 2
    strain = jnp.concatenate(
        [
            jnp.where(in_low, strain_ref[2 * j].astype(F32), strain_ref[2 * j + 1].astype(F32)).astype(BF16)
            for j in range(strain_ref.shape[0] // 2)
        ],
        axis=1,
    )
    image = image_ref[...]
    image_rows = stack2(image)
    rows = jnp.concatenate([stack2(field_ref[...]), image_rows], axis=0)
    every = dot_nt(rows, image_rows)
    every = every[:, :cases] + every[:, cases:]
    cross = every[:cases] + every[cases:2 * cases]
    square = every[2 * cases:3 * cases] + every[3 * cases:]
    start = dot_nt(rows[:2 * cases], rows[:2 * cases])
    start = start[:, :cases] + start[:, cases:]
    start = start[:cases] + start[cases:]
    last = dot_nt(image_rows, stack2(image * mass_ref[...])) + dot_nt(strain, strain)
    last = last[:, :cases] + last[:, cases:]
    last = last[:cases] + last[cases:]
    gram_ref[...] = jnp.concatenate([cross, start, square, last], axis=1)


def gram_trace(gram_ref, own_ref, match_ref, shift_ref, pen_ref, match_pen_ref, out_ref, jump_ref):
    cases = gram_ref.shape[0]
    apart = (own_ref[...] - match_ref[...]) + shift_ref[...]
    jump = (pen_ref[...] * match_pen_ref[...]) * apart
    jump_ref[...] = jump
    more = dot_nt(stack2(0.5 * apart), stack2(jump))
    more = more[:, :cases] + more[:, cases:]
    more = more[:cases] + more[cases:]
    zeros = jnp.zeros((cases, 3 * cases), F32)
    out_ref[...] = gram_ref[...] + jnp.concatenate([zeros, more], axis=1)


def second_image(
    cols_ref, field_ref, image_ref, mass_ref, stiff_ref, strain_ref, jump_ref, trace_ref, out_ref, *sums
):
    transposed_sums(cols_ref, stiff_ref, strain_ref, sums)
    trace = trace_ref[...]
    one_hot = one_hot_low(trace & (WIDE - 1), trace.shape[1])
    folded = jnp.concatenate(
        [folded_tile(sums, j) for j in range(image_ref.shape[1] // LANES)], axis=1
    )
    image = image_ref[...]
    rows = 2 * image.shape[0]
    second = add_jump(image * mass_ref[...] + folded, jump_ref[...], one_hot, trace >> 8)
    for i, part in enumerate((field_ref[...], image, second)):
        out_ref[i * rows:(i + 1) * rows, :] = stack2(part)
    out_ref[3 * rows:, :] = jnp.zeros((out_ref.shape[0] - 3 * rows, out_ref.shape[1]), BF16)


def eliminate(matrix, size, group=8):
    rows = iota(matrix.shape, 0)
    for first in range(0, size, group):
        columns = [
            jnp.broadcast_to(matrix[:, p:p + 1], matrix.shape) for p in range(first, first + group)
        ]
        for q in range(group):
            p = first + q
            column = columns[q]
            inverse = 1.0 / column[p:p + 1]
            row = matrix[p:p + 1] * inverse
            here = rows == p
            matrix = jnp.where(here, row, matrix - column * row)
            for r in range(q + 1, group):
                entry = column[first + r:first + r + 1] * inverse
                columns[r] = jnp.where(here, entry, columns[r] - column * entry)
    return matrix


def small_dot(a, b):
    return jnp.dot(a, b, precision=lax.Precision.HIGHEST, preferred_element_type=F32)


def finish(*refs):
    *gram_refs, field_ref, rows_ref, solution_ref, residual_ref = refs
    cases = field_ref.shape[0]
    gram = sum_of([ref[...] for ref in gram_refs])
    square = gram[:, 2 * cases:3 * cases]
    solved = eliminate(gram, cases)
    zeros = jnp.zeros((cases, 2 * cases), F32)
    given = jnp.concatenate([gram[:, 3 * cases:], gram[:, :cases]], axis=1)
    both = jnp.concatenate([solved[:, 2 * cases:3 * cases], solved[:, cases:2 * cases]], axis=1)
    second_part = eliminate(
        jnp.concatenate([given - small_dot(square, both), zeros], axis=1), cases
    )[:, cases:2 * cases]
    first_part = both[:, cases:] - small_dot(both[:, :cases], second_part)
    zero = jnp.zeros((cases, cases), F32)
    blocks = [[first_part, zero], [second_part, -first_part], [zero, -second_part], [zero, zero]]
    weights = [jnp.concatenate(block + [zero, zero], axis=1) for block in blocks]
    weights = jnp.concatenate([weights[i // 2] for i in range(8)], axis=0)
    weights = jnp.concatenate([weights[:LANES].T, weights[LANES:].T], axis=1)[:2 * cases]
    out = dot_nn(stack2(weights), rows_ref[...])
    out = out[:2 * cases] + out[2 * cases:]
    solution_ref[...] = out[:cases]
    residual_ref[...] = field_ref[...] + out[cases:]


def sum_of(terms):
    while len(terms) > 1:
        terms = [sum(terms[i:i + 2][1:], terms[i]) for i in range(0, len(terms), 2)]
    return terms[0]


def from_all(array, axis, stride=1, radix=None):
    count = lax.axis_size(axis)
    radix = radix or count
    span = stride * radix

    def target(i, by):
        digit = i // stride % radix
        return i // span * span + (digit + by) % radix * stride + i % stride

    return [array] + [
        lax.ppermute(array, axis, [(i, target(i, by)) for i in range(count)])
        for by in range(1, radix)
    ]


def digits(count):
    stages, stride = [], 1
    while stride < count:
        left = count // stride
        radix = 2 if stride == 1 and left % 2 == 0 else 4 if left % 4 == 0 else left
        stages.append((stride, radix))
        stride *= radix
    return stages


def run(body, outs, args, scratch=(), scalars=0, cost=None, far=0):
    whole = pl.BlockSpec(memory_space=pltpu.VMEM)
    args = [
        pltpu.with_memory_space_constraint(arg, pltpu.HBM) if scalars <= i < scalars + far else arg
        for i, arg in enumerate(args)
    ]
    return pl.pallas_call(
        body,
        out_shape=outs,
        in_specs=[pl.BlockSpec(memory_space=pltpu.SMEM)] * scalars
        + [pl.BlockSpec(memory_space=pltpu.HBM)] * far
        + [whole] * (len(args) - scalars - far),
        out_specs=jax.tree.map(lambda _: whole, outs),
        scratch_shapes=list(scratch),
        compiler_params=pltpu.CompilerParams(vmem_limit_bytes=VMEM_BYTES),
        cost_estimate=cost,
    )(*args)


def shards(
    load_cases,
    mass_diag,
    stiffness,
    block_cols,
    trace_dofs,
    penalty,
    cell_partials,
    cell_owner,
    cell_dof,
):
    cases, dofs = load_cases.shape
    count, blk, width = stiffness.shape
    cells = cell_partials.shape[1]
    slots = trace_dofs.shape[0]
    patches = lax.axis_size("patch")
    cap = 4 * cells // patches
    rows = cases + 8
    far_rows = cases + -(-(1 + 2 * (slots // cap)) // 8) * 8
    shape = jax.ShapeDtypeStruct
    field_shape = shape((cases, dofs), F32)
    slot_shape = shape((cases, slots), F32)
    mass = mass_diag.reshape(1, dofs)
    trace = trace_dofs.reshape(1, slots)
    pen = penalty.reshape(1, slots)
    cols = block_cols.reshape(-1)

    half = patches // 2
    pairs = [(i, (i + half) % patches) for i in range(patches)]
    packets = run(
        pack_cells,
        [shape((far_rows if by == half else rows, cap), F32) for by in range(patches)],
        (cell_partials, cell_owner.reshape(1, cells), cell_dof.reshape(1, cells), pen, trace),
        scratch=[
            pltpu.VMEM((cases, cells), F32),
            pltpu.VMEM((1, cells), jnp.int32),
            pltpu.VMEM((1, cells), jnp.int32),
            pltpu.VMEM((1, slots), F32),
            pltpu.VMEM((1, slots), jnp.int32),
            pltpu.SemaphoreType.DMA((5,)),
        ],
        far=5,
    )
    received = [packets[0]] + [
        lax.ppermute(packets[by], "patch", [(i, (i + by) % patches) for i in range(patches)])
        for by in range(1, patches)
    ]
    stiff = run(
        split_stiffness,
        shape((count, 2 * blk, width), BF16),
        (stiffness,),
        cost=pl.CostEstimate(flops=4 * stiffness.size, bytes_accessed=8 * stiffness.size, transcendentals=0),
    )

    received, stiff, cols, mass, load_cases, trace = lax.optimization_barrier(
        (received, stiff, cols, mass, load_cases, trace)
    )

    spread = [pltpu.VMEM((dofs // blk, 2 * cases, LANES), BF16)] * 2
    strain_scratch = pltpu.VMEM((count, 2 * cases, LANES), BF16)
    sums = [pltpu.VMEM((dofs // blk, cases, LANES), F32)] * 4

    row_shape = shape((1, slots), F32)
    field, own, match_pen, match_trace = run(
        assemble, (field_shape, slot_shape, row_shape, row_shape), (load_cases, trace, *received)
    )
    match = lax.ppermute(own, "patch", pairs)
    part, part_own = run(
        operator_body,
        (field_shape, slot_shape),
        (cols, field, mass, trace, stiff),
        scratch=[*spread, strain_scratch, *sums],
        scalars=1,
    )
    part_match = lax.ppermute(part_own, "patch", pairs)
    same = run(coincidence, shape((slots, slots), BF16), (trace, match_trace))
    image, shift, gram, strain = run(
        first_image,
        (
            field_shape,
            slot_shape,
            shape((cases, 4 * cases), F32),
            shape((count, 2 * cases, LANES), BF16),
        ),
        (cols, field, part, own, match, pen, match_pen, trace, mass, same, stiff),
        scratch=spread,
        scalars=1,
    )
    gram, jump = run(
        gram_trace,
        (shape((cases, 4 * cases), F32), slot_shape),
        (gram, part_own, part_match, shift, pen, match_pen),
    )
    gram = sum_of(from_all(gram, "comp"))
    *early, last = digits(patches)
    for stride, radix in early:
        gram = sum_of(from_all(gram, "patch", stride, radix))
    grams = from_all(gram, "patch", *last)
    stacked = run(
        second_image,
        shape((-(-6 * cases // LANES) * LANES, dofs), BF16),
        (cols, field, image, mass, stiff, strain, jump, trace),
        scratch=sums,
        scalars=1,
    )
    return run(finish, (field_shape, field_shape), (*grams, field, stacked))


def solution(mesh):
    return jax.shard_map(
        shards,
        mesh=mesh,
        in_specs=(
            P(None, ("comp", "patch")),
            P(("comp", "patch")),
            P(("comp", "patch"), None, None),
            P(("comp", "patch"), None),
            P(("comp", "patch")),
            P(("comp", "patch")),
            P(None, ("comp", "patch")),
            P(("comp", "patch"), None),
            P(("comp", "patch")),
        ),
        out_specs=(P(None, ("comp", "patch")), P(None, ("comp", "patch"))),
        check_vma=False,
    )
```

```python
import jax
import jax.numpy as jnp
from jax import lax
from jax.experimental import pallas as pl
from jax.experimental.pallas import tpu as pltpu
from jax.sharding import PartitionSpec as P

F32 = jnp.float32
BF16 = jnp.bfloat16
WIDE = 256
LANES = 128
VMEM_BYTES = 32 * 1024 * 1024


def split2(x):
    high = x.astype(BF16)
    low = (x - high.astype(F32)).astype(BF16)
    return high, low


def stack2(x):
    return jnp.concatenate(split2(x), axis=0)


def dot_nn(a, b):
    return lax.dot_general(a, b, (((1,), (0,)), ((), ())), preferred_element_type=F32)


def dot_nt(a, b):
    return lax.dot_general(a, b, (((1,), (1,)), ((), ())), preferred_element_type=F32)


def iota(shape, axis):
    return lax.broadcasted_iota(jnp.int32, shape, axis)


def one_hot_low(low, width):
    return (iota((WIDE, width), 0) == low).astype(F32).astype(BF16)


def masked_groups(stacked, group, count):
    parts = []
    for g in range(count):
        mask = (group == g).astype(F32).astype(BF16)
        parts.append(stacked * jnp.broadcast_to(mask, stacked.shape))
    return jnp.concatenate(parts, axis=0)


def gather_slots(field, one_hot, group, groups):
    cases = field.shape[0]
    rows = jnp.concatenate(
        [stack2(field[:, g * WIDE:(g + 1) * WIDE]) for g in range(groups)], axis=0
    )
    found = dot_nn(rows, one_hot)
    total = jnp.zeros((cases, group.shape[1]), F32)
    for g in range(groups):
        base = g * 2 * cases
        both = found[base:base + cases] + found[base + cases:base + 2 * cases]
        total = jnp.where(group == g, both, total)
    return total


def pack_cells(*refs):
    sources, out_refs, stiff_ref, targets, sems = refs[:6], refs[6:-7], refs[-7], refs[-6:-1], refs[-1]
    copies = [
        pltpu.make_async_copy(source, target, sems.at[i])
        for i, (source, target) in enumerate(zip(sources, [*targets, stiff_ref]))
    ]
    for copy in copies:
        copy.start()
    for copy in copies[:-1]:
        copy.wait()
    partials_ref, owner_ref, dof_ref, pen_ref, trace_ref = targets
    patches = len(out_refs)
    rows, cap = out_refs[0].shape
    cases, cells = partials_ref.shape
    me = lax.axis_index("patch")
    shift = owner_ref[...] - me
    shift = jnp.where(shift < 0, shift + patches, shift)
    mine = (iota((patches, cells), 0) == shift).astype(F32)
    before = (iota((cells, cells), 0) < iota((cells, cells), 1)).astype(F32).astype(BF16)
    counts = dot_nn(mine.astype(BF16), before)
    rank = jnp.sum(mine * counts, axis=0, keepdims=True).astype(jnp.int32)
    extra = jnp.where(iota((rows - cases, cells), 0) == 0, dof_ref[...] + 1, 0).astype(F32)
    body = stack2(jnp.concatenate([partials_ref[...], extra], axis=0))
    for by, out_ref in enumerate(out_refs):
        key = jnp.where(shift == by, rank, -1)
        pick = (iota((cap, cells), 0) == key).astype(F32).astype(BF16)
        packed = dot_nt(body, pick)
        out_ref[:rows, :] = packed[:rows] + packed[rows:]
        if by == patches // 2:
            more = pen_ref.shape[1] // cap
            for i in range(more):
                at = cases + 1 + i
                out_ref[at:at + 1, :] = pen_ref[:, i * cap:(i + 1) * cap]
                out_ref[at + more:at + more + 1, :] = trace_ref[:, i * cap:(i + 1) * cap].astype(F32)
    copies[-1].wait()


def split_stiffness(stiff_ref, out_ref):
    blk = stiff_ref.shape[1]
    high, low = split2(stiff_ref[...])
    out_ref[:, :blk, :] = high
    out_ref[:, blk:, :] = low


def assemble(load_ref, trace_ref, stiff_ref, *refs):
    *recv_refs, field_ref, own_ref, pen_ref, match_trace_ref, split_ref = refs
    split_stiffness(stiff_ref, split_ref)
    patches = len(recv_refs)
    cases, dofs = load_ref.shape
    groups = dofs // WIDE
    rows, cap = recv_refs[0].shape
    cells = jnp.concatenate([ref[:rows, :] for ref in recv_refs], axis=1)
    far_ref = recv_refs[patches // 2]
    more = pen_ref.shape[1] // cap
    for i in range(more):
        at = cases + 1 + i
        pen_ref[:, i * cap:(i + 1) * cap] = far_ref[at:at + 1, :]
        match_trace_ref[:, i * cap:(i + 1) * cap] = far_ref[at + more:at + more + 1, :]
    slots = cells.shape[1]
    dof = cells[cases:cases + 1].astype(jnp.int32) - 1
    rows = masked_groups(stack2(cells[:cases]), dof >> 8, groups)
    sums = dot_nt(rows, one_hot_low(jnp.where(dof < 0, -1, dof & (WIDE - 1)), slots))
    pieces = []
    for g in range(groups):
        base = g * 2 * cases
        pieces.append(
            load_ref[:, g * WIDE:(g + 1) * WIDE]
            + (sums[base:base + cases] + sums[base + cases:base + 2 * cases])
        )
    field = jnp.concatenate(pieces, axis=1)
    field_ref[...] = field
    trace = trace_ref[...]
    own_ref[...] = gather_slots(
        field, one_hot_low(trace & (WIDE - 1), trace.shape[1]), trace >> 8, groups
    )


def spread_blocks(field_ref, low_ref, high_ref):
    cases, dofs = field_ref.shape
    in_low = iota((cases, LANES), 1) < LANES // 2
    for j in range(dofs // LANES):
        tile = field_ref[:, j * LANES:(j + 1) * LANES]
        turned = pltpu.roll(tile, LANES // 2, 1)
        low_ref[2 * j] = stack2(jnp.where(in_low, tile, 0.0))
        high_ref[2 * j + 1] = stack2(jnp.where(in_low, 0.0, tile))
        low_ref[2 * j + 1] = stack2(jnp.where(in_low, turned, 0.0))
        high_ref[2 * j] = stack2(jnp.where(in_low, 0.0, turned))


def strain_rows(cols_ref, stiff_ref, low_ref, high_ref, strain_ref):
    count = stiff_ref.shape[0]
    cases = strain_ref.shape[1] // 2
    for n in range(count):
        c = [cols_ref[k, n] for k in range(4)]
        near = jnp.concatenate(
            [low_ref[c[0]] + high_ref[c[1]], low_ref[c[2]] + high_ref[c[3]]], axis=1
        )
        both = dot_nt(near, stiff_ref[n])
        both = both[:cases] + both[cases:]
        strain_ref[n] = stack2(both + pltpu.roll(both, LANES // 2, 1))


def transposed_sums(cols_ref, stiff_ref, strain_ref, sums):
    count = stiff_ref.shape[0]
    cases = strain_ref.shape[1] // 2
    for ref in sums:
        ref[...] = jnp.zeros_like(ref)
    for n in range(count):
        c = [cols_ref[k, n] for k in range(4)]
        both = dot_nn(strain_ref[n], stiff_ref[n])
        both = both[:cases] + both[cases:]
        left, right = both[:, :LANES], both[:, LANES:]
        sums[0][c[0]] += left
        sums[1][c[1]] += left
        sums[2][c[2]] += right
        sums[3][c[3]] += right


def folded_tile(sums, j):
    cases = sums[0].shape[1]
    in_low = iota((cases, LANES), 1) < LANES // 2
    even, odd = 2 * j, 2 * j + 1
    straight = jnp.where(in_low, sums[0][even] + sums[2][even], sums[1][odd] + sums[3][odd])
    crossed = jnp.where(in_low, sums[0][odd] + sums[2][odd], sums[1][even] + sums[3][even])
    return straight + pltpu.roll(crossed, LANES // 2, 1)


def operator_body(
    cols_ref, field_ref, mass_ref, trace_ref, stiff_ref, out_ref, own_ref, low_ref, high_ref, strain_ref, *sums
):
    spread_blocks(field_ref, low_ref, high_ref)
    strain_rows(cols_ref, stiff_ref, low_ref, high_ref, strain_ref)
    transposed_sums(cols_ref, stiff_ref, strain_ref, sums)
    dofs = field_ref.shape[1]
    for j in range(dofs // LANES):
        at = slice(j * LANES, (j + 1) * LANES)
        out_ref[:, at] = field_ref[:, at] * mass_ref[:, at] + folded_tile(sums, j)
    trace = trace_ref[...]
    own_ref[...] = gather_slots(
        out_ref[...], one_hot_low(trace & (WIDE - 1), trace.shape[1]), trace >> 8, dofs // WIDE
    )


def coincidence(trace_ref, match_trace_ref, out_ref):
    slots = trace_ref.shape[1]
    rows = [trace_ref[...].astype(F32), match_trace_ref[...]]
    for i in range(slots // LANES):
        at = slice(i * LANES, (i + 1) * LANES)
        total = jnp.zeros((LANES, slots), F32)
        for row in rows:
            column = jnp.broadcast_to(row[:, at], (LANES, LANES)).T
            total += (jnp.broadcast_to(column[:, :1], (LANES, slots)) == row).astype(F32)
        out_ref[at, :] = total.astype(BF16)


def add_jump(base, jump, one_hot, group):
    cases, dofs = base.shape
    groups = dofs // WIDE
    sums = dot_nt(masked_groups(stack2(jump), group, groups), one_hot)
    pieces = []
    for g in range(groups):
        row = g * 2 * cases
        pieces.append(
            base[:, g * WIDE:(g + 1) * WIDE]
            + (sums[row:row + cases] + sums[row + cases:row + 2 * cases])
        )
    return jnp.concatenate(pieces, axis=1)


def first_image(
    cols_ref, field_ref, part_ref, own_ref, match_ref, pen_ref, match_pen_ref, trace_ref, mass_ref, same_ref, stiff_ref,
    image_ref, shift_ref, gram_ref, strain_ref, low_ref, high_ref,
):
    cases, dofs = field_ref.shape
    trace = trace_ref[...]
    weight = pen_ref[...] * match_pen_ref[...]
    jump = weight * (own_ref[...] - match_ref[...])
    image_ref[...] = add_jump(
        part_ref[...], jump, one_hot_low(trace & (WIDE - 1), trace.shape[1]), trace >> 8
    )
    moved = dot_nn(stack2(jump), same_ref[...])
    shift_ref[...] = moved[:cases] + moved[cases:]
    spread_blocks(image_ref, low_ref, high_ref)
    strain_rows(cols_ref, stiff_ref, low_ref, high_ref, strain_ref)
    in_low = iota((2 * cases, LANES), 1) < LANES // 2
    strain = jnp.concatenate(
        [
            jnp.where(in_low, strain_ref[2 * j].astype(F32), strain_ref[2 * j + 1].astype(F32)).astype(BF16)
            for j in range(strain_ref.shape[0] // 2)
        ],
        axis=1,
    )
    image = image_ref[...]
    image_rows = stack2(image)
    rows = jnp.concatenate([stack2(field_ref[...]), image_rows], axis=0)
    every = dot_nt(rows, image_rows)
    every = every[:, :cases] + every[:, cases:]
    cross = every[:cases] + every[cases:2 * cases]
    square = every[2 * cases:3 * cases] + every[3 * cases:]
    start = dot_nt(rows[:2 * cases], rows[:2 * cases])
    start = start[:, :cases] + start[:, cases:]
    start = start[:cases] + start[cases:]
    last = dot_nt(image_rows, stack2(image * mass_ref[...])) + dot_nt(strain, strain)
    last = last[:, :cases] + last[:, cases:]
    last = last[:cases] + last[cases:]
    gram_ref[...] = jnp.concatenate([cross, start, square, last], axis=1)


def gram_trace(gram_ref, match_gram_ref, own_ref, match_ref, shift_ref, pen_ref, match_pen_ref, out_ref, jump_ref):
    cases = gram_ref.shape[0]
    apart = (own_ref[...] - match_ref[...]) + shift_ref[...]
    jump = (pen_ref[...] * match_pen_ref[...]) * apart
    jump_ref[...] = jump
    more = dot_nt(stack2(apart), stack2(jump))
    more = more[:, :cases] + more[:, cases:]
    more = more[:cases] + more[cases:]
    zeros = jnp.zeros((cases, 3 * cases), F32)
    out_ref[...] = (gram_ref[...] + match_gram_ref[...]) + jnp.concatenate([zeros, more], axis=1)


def second_image(
    cols_ref, field_ref, image_ref, mass_ref, stiff_ref, strain_ref, jump_ref, trace_ref, out_ref, *sums
):
    transposed_sums(cols_ref, stiff_ref, strain_ref, sums)
    trace = trace_ref[...]
    one_hot = one_hot_low(trace & (WIDE - 1), trace.shape[1])
    folded = jnp.concatenate(
        [folded_tile(sums, j) for j in range(image_ref.shape[1] // LANES)], axis=1
    )
    image = image_ref[...]
    rows = 2 * image.shape[0]
    second = add_jump(image * mass_ref[...] + folded, jump_ref[...], one_hot, trace >> 8)
    for i, part in enumerate((field_ref[...], image, second)):
        out_ref[i * rows:(i + 1) * rows, :] = stack2(part)
    out_ref[3 * rows:, :] = jnp.zeros((out_ref.shape[0] - 3 * rows, out_ref.shape[1]), BF16)


def eliminate(matrix, size, group=8):
    rows = iota(matrix.shape, 0)
    for first in range(0, size, group):
        columns = [
            jnp.broadcast_to(matrix[:, p:p + 1], matrix.shape) for p in range(first, first + group)
        ]
        for q in range(group):
            p = first + q
            column = columns[q]
            inverse = 1.0 / column[p:p + 1]
            row = matrix[p:p + 1] * inverse
            here = rows == p
            matrix = jnp.where(here, row, matrix - column * row)
            for r in range(q + 1, group):
                entry = column[first + r:first + r + 1] * inverse
                columns[r] = jnp.where(here, entry, columns[r] - column * entry)
    return matrix


def small_dot(a, b):
    return jnp.dot(a, b, precision=lax.Precision.HIGHEST, preferred_element_type=F32)


def finish(*refs):
    *gram_refs, field_ref, rows_ref, solution_ref, residual_ref = refs
    cases = field_ref.shape[0]
    gram = sum_of([ref[...] for ref in gram_refs])
    square = gram[:, 2 * cases:3 * cases]
    solved = eliminate(gram, cases)
    zeros = jnp.zeros((cases, 2 * cases), F32)
    given = jnp.concatenate([gram[:, 3 * cases:], gram[:, :cases]], axis=1)
    both = jnp.concatenate([solved[:, 2 * cases:3 * cases], solved[:, cases:2 * cases]], axis=1)
    second_part = eliminate(
        jnp.concatenate([given - small_dot(square, both), zeros], axis=1), cases
    )[:, cases:2 * cases]
    first_part = both[:, cases:] - small_dot(both[:, :cases], second_part)
    zero = jnp.zeros((cases, cases), F32)
    blocks = [[first_part, zero], [second_part, -first_part], [zero, -second_part], [zero, zero]]
    weights = [jnp.concatenate(block + [zero, zero], axis=1) for block in blocks]
    weights = jnp.concatenate([weights[i // 2] for i in range(8)], axis=0)
    weights = jnp.concatenate([weights[:LANES].T, weights[LANES:].T], axis=1)[:2 * cases]
    out = dot_nn(stack2(weights), rows_ref[...])
    out = out[:2 * cases] + out[2 * cases:]
    solution_ref[...] = out[:cases]
    residual_ref[...] = field_ref[...] + out[cases:]


def sum_of(terms):
    while len(terms) > 1:
        terms = [sum(terms[i:i + 2][1:], terms[i]) for i in range(0, len(terms), 2)]
    return terms[0]


def from_all(array, axis, stride=1, radix=None):
    count = lax.axis_size(axis)
    radix = radix or count
    span = stride * radix

    def target(i, by):
        digit = i // stride % radix
        return i // span * span + (digit + by) % radix * stride + i % stride

    return [array] + [
        lax.ppermute(array, axis, [(i, target(i, by)) for i in range(count)])
        for by in range(1, radix)
    ]


def digits(count):
    stages, stride = [], 1
    while stride < count:
        left = count // stride
        radix = 4 if left % 4 == 0 else left
        stages.append((stride, radix))
        stride *= radix
    return stages


def run(body, outs, args, scratch=(), scalars=0, cost=None, far=0):
    whole = pl.BlockSpec(memory_space=pltpu.VMEM)
    args = [
        pltpu.with_memory_space_constraint(arg, pltpu.HBM) if scalars <= i < scalars + far else arg
        for i, arg in enumerate(args)
    ]
    return pl.pallas_call(
        body,
        out_shape=outs,
        in_specs=[pl.BlockSpec(memory_space=pltpu.SMEM)] * scalars
        + [pl.BlockSpec(memory_space=pltpu.HBM)] * far
        + [whole] * (len(args) - scalars - far),
        out_specs=jax.tree.map(lambda _: whole, outs),
        scratch_shapes=list(scratch),
        compiler_params=pltpu.CompilerParams(vmem_limit_bytes=VMEM_BYTES),
        cost_estimate=cost,
    )(*args)


def shards(
    load_cases,
    mass_diag,
    stiffness,
    block_cols,
    trace_dofs,
    penalty,
    cell_partials,
    cell_owner,
    cell_dof,
):
    cases, dofs = load_cases.shape
    count, blk, width = stiffness.shape
    cells = cell_partials.shape[1]
    slots = trace_dofs.shape[0]
    patches = lax.axis_size("patch")
    cap = 4 * cells // patches
    rows = cases + 8
    far_rows = cases + -(-(1 + 2 * (slots // cap)) // 8) * 8
    shape = jax.ShapeDtypeStruct
    field_shape = shape((cases, dofs), F32)
    slot_shape = shape((cases, slots), F32)
    mass = mass_diag.reshape(1, dofs)
    trace = trace_dofs.reshape(1, slots)
    pen = penalty.reshape(1, slots)
    cols = block_cols.T

    half = patches // 2
    pairs = [(i, (i + half) % patches) for i in range(patches)]
    *packets, stiff = run(
        pack_cells,
        [
            *[shape((far_rows if by == half else rows, cap), F32) for by in range(patches)],
            shape(stiffness.shape, F32),
        ],
        (cell_partials, cell_owner.reshape(1, cells), cell_dof.reshape(1, cells), pen, trace, stiffness),
        scratch=[
            pltpu.VMEM((cases, cells), F32),
            pltpu.VMEM((1, cells), jnp.int32),
            pltpu.VMEM((1, cells), jnp.int32),
            pltpu.VMEM((1, slots), F32),
            pltpu.VMEM((1, slots), jnp.int32),
            pltpu.SemaphoreType.DMA((6,)),
        ],
        far=6,
    )
    received = [packets[0]] + [
        lax.ppermute(packets[by], "patch", [(i, (i + by) % patches) for i in range(patches)])
        for by in range(1, patches)
    ]
    received, cols, mass, load_cases, trace = lax.optimization_barrier(
        (received, cols, mass, load_cases, trace)
    )

    spread = [pltpu.VMEM((dofs // blk, 2 * cases, LANES), BF16)] * 2
    strain_scratch = pltpu.VMEM((count, 2 * cases, LANES), BF16)
    sums = [pltpu.VMEM((dofs // blk, cases, LANES), F32)] * 4

    row_shape = shape((1, slots), F32)
    field, own, match_pen, match_trace, stiff = run(
        assemble,
        (field_shape, slot_shape, row_shape, row_shape, shape((count, 2 * blk, width), BF16)),
        (load_cases, trace, stiff, *received),
    )
    match = lax.ppermute(own, "patch", pairs)
    part, part_own = run(
        operator_body,
        (field_shape, slot_shape),
        (cols, field, mass, trace, stiff),
        scratch=[*spread, strain_scratch, *sums],
        scalars=1,
    )
    part_match = lax.ppermute(part_own, "patch", pairs)
    same = run(coincidence, shape((slots, slots), BF16), (trace, match_trace))
    image, shift, gram, strain = run(
        first_image,
        (
            field_shape,
            slot_shape,
            shape((cases, 4 * cases), F32),
            shape((count, 2 * cases, LANES), BF16),
        ),
        (cols, field, part, own, match, pen, match_pen, trace, mass, same, stiff),
        scratch=spread,
        scalars=1,
    )
    match_gram = lax.ppermute(gram, "patch", pairs)
    gram, jump = run(
        gram_trace,
        (shape((cases, 4 * cases), F32), slot_shape),
        (gram, match_gram, part_own, part_match, shift, pen, match_pen),
    )
    gram = sum_of(from_all(gram, "comp"))
    *early, last = digits(half)
    for stride, radix in early:
        gram = sum_of(from_all(gram, "patch", stride, radix))
    grams = from_all(gram, "patch", *last)
    stacked = run(
        second_image,
        shape((-(-6 * cases // LANES) * LANES, dofs), BF16),
        (cols, field, image, mass, stiff, strain, jump, trace),
        scratch=sums,
        scalars=1,
    )
    return run(finish, (field_shape, field_shape), (*grams, field, stacked))


def solution(mesh):
    return jax.shard_map(
        shards,
        mesh=mesh,
        in_specs=(
            P(None, ("comp", "patch")),
            P(("comp", "patch")),
            P(("comp", "patch"), None, None),
            P(("comp", "patch"), None),
            P(("comp", "patch")),
            P(("comp", "patch")),
            P(None, ("comp", "patch")),
            P(("comp", "patch"), None),
            P(("comp", "patch")),
        ),
        out_specs=(P(None, ("comp", "patch")), P(None, ("comp", "patch"))),
        check_vma=False,
    )
```

```python
import jax
import jax.numpy as jnp
from jax import lax
from jax.experimental import pallas as pl
from jax.experimental.pallas import tpu as pltpu
from jax.sharding import PartitionSpec as P

F32 = jnp.float32
BF16 = jnp.bfloat16
WIDE = 256
LANES = 128
VMEM_BYTES = 32 * 1024 * 1024


def split2(x):
    high = x.astype(BF16)
    low = (x - high.astype(F32)).astype(BF16)
    return high, low


def stack2(x):
    return jnp.concatenate(split2(x), axis=0)


def dot_nn(a, b):
    return lax.dot_general(a, b, (((1,), (0,)), ((), ())), preferred_element_type=F32)


def dot_nt(a, b):
    return lax.dot_general(a, b, (((1,), (1,)), ((), ())), preferred_element_type=F32)


def iota(shape, axis):
    return lax.broadcasted_iota(jnp.int32, shape, axis)


def one_hot_low(low, width):
    return (iota((WIDE, width), 0) == low).astype(F32).astype(BF16)


def masked_groups(stacked, group, count):
    parts = []
    for g in range(count):
        mask = (group == g).astype(F32).astype(BF16)
        parts.append(stacked * jnp.broadcast_to(mask, stacked.shape))
    return jnp.concatenate(parts, axis=0)


def gather_slots(field, one_hot, group, groups):
    cases = field.shape[0]
    rows = jnp.concatenate(
        [stack2(field[:, g * WIDE:(g + 1) * WIDE]) for g in range(groups)], axis=0
    )
    found = dot_nn(rows, one_hot)
    total = jnp.zeros((cases, group.shape[1]), F32)
    for g in range(groups):
        base = g * 2 * cases
        both = found[base:base + cases] + found[base + cases:base + 2 * cases]
        total = jnp.where(group == g, both, total)
    return total


def fetch(sources, targets, sems):
    copies = [
        pltpu.make_async_copy(source, target, sems.at[i])
        for i, (source, target) in enumerate(zip(sources, targets))
    ]
    for copy in copies:
        copy.start()
    for copy in copies:
        copy.wait()


def pack_cells(*refs):
    sources, out_refs, targets, sems = refs[:5], refs[5:-6], refs[-6:-1], refs[-1]
    fetch(sources, targets, sems)
    partials_ref, owner_ref, dof_ref, pen_ref, trace_ref = targets
    patches = len(out_refs)
    rows, cap = out_refs[0].shape
    cases, cells = partials_ref.shape
    me = lax.axis_index("patch")
    shift = owner_ref[...] ^ me
    mine = (iota((patches, cells), 0) == shift).astype(F32)
    before = (iota((cells, cells), 0) < iota((cells, cells), 1)).astype(F32).astype(BF16)
    counts = dot_nn(mine.astype(BF16), before)
    rank = jnp.sum(mine * counts, axis=0, keepdims=True).astype(jnp.int32)
    extra = jnp.where(iota((rows - cases, cells), 0) == 0, dof_ref[...] + 1, 0).astype(F32)
    body = stack2(jnp.concatenate([partials_ref[...], extra], axis=0))
    for by, out_ref in enumerate(out_refs):
        key = jnp.where(shift == by, rank, -1)
        pick = (iota((cap, cells), 0) == key).astype(F32).astype(BF16)
        packed = dot_nt(body, pick)
        out_ref[:rows, :] = packed[:rows] + packed[rows:]
        if by == patches // 2:
            more = pen_ref.shape[1] // cap
            for i in range(more):
                at = cases + 1 + i
                out_ref[at:at + 1, :] = pen_ref[:, i * cap:(i + 1) * cap]
                out_ref[at + more:at + more + 1, :] = trace_ref[:, i * cap:(i + 1) * cap].astype(F32)


def split_stiffness(stiff_ref, out_ref):
    blk = stiff_ref.shape[1]
    high, low = split2(stiff_ref[...])
    out_ref[:, :blk, :] = high
    out_ref[:, blk:, :] = low


def assemble(load_ref, trace_ref, *refs):
    *recv_refs, field_ref, own_ref, pen_ref, match_trace_ref = refs
    cases, dofs = load_ref.shape
    groups = dofs // WIDE
    rows, cap = recv_refs[0].shape
    cells = jnp.concatenate([ref[:rows, :] for ref in recv_refs], axis=1)
    far_ref = recv_refs[1]
    more = pen_ref.shape[1] // cap
    for i in range(more):
        at = cases + 1 + i
        pen_ref[:, i * cap:(i + 1) * cap] = far_ref[at:at + 1, :]
        match_trace_ref[:, i * cap:(i + 1) * cap] = far_ref[at + more:at + more + 1, :]
    slots = cells.shape[1]
    dof = cells[cases:cases + 1].astype(jnp.int32) - 1
    rows = masked_groups(stack2(cells[:cases]), dof >> 8, groups)
    sums = dot_nt(rows, one_hot_low(jnp.where(dof < 0, -1, dof & (WIDE - 1)), slots))
    pieces = []
    for g in range(groups):
        base = g * 2 * cases
        pieces.append(
            load_ref[:, g * WIDE:(g + 1) * WIDE]
            + (sums[base:base + cases] + sums[base + cases:base + 2 * cases])
        )
    field = jnp.concatenate(pieces, axis=1)
    field_ref[...] = field
    trace = trace_ref[...]
    own_ref[...] = gather_slots(
        field, one_hot_low(trace & (WIDE - 1), trace.shape[1]), trace >> 8, groups
    )


def spread_blocks(field_ref, low_ref, high_ref):
    cases, dofs = field_ref.shape
    in_low = iota((cases, LANES), 1) < LANES // 2
    for j in range(dofs // LANES):
        tile = field_ref[:, j * LANES:(j + 1) * LANES]
        turned = pltpu.roll(tile, LANES // 2, 1)
        low_ref[2 * j] = stack2(jnp.where(in_low, tile, 0.0))
        high_ref[2 * j + 1] = stack2(jnp.where(in_low, 0.0, tile))
        low_ref[2 * j + 1] = stack2(jnp.where(in_low, turned, 0.0))
        high_ref[2 * j] = stack2(jnp.where(in_low, 0.0, turned))


def strain_rows(cols_ref, stiff_ref, low_ref, high_ref, strain_ref):
    count = stiff_ref.shape[0]
    cases = strain_ref.shape[1] // 2
    for n in range(count):
        c = [cols_ref[k, n] for k in range(4)]
        near = jnp.concatenate(
            [low_ref[c[0]] + high_ref[c[1]], low_ref[c[2]] + high_ref[c[3]]], axis=1
        )
        both = dot_nt(near, stiff_ref[n])
        both = both[:cases] + both[cases:]
        strain_ref[n] = stack2(both + pltpu.roll(both, LANES // 2, 1))


def transposed_sums(cols_ref, stiff_ref, strain_ref, sums):
    count = stiff_ref.shape[0]
    cases = strain_ref.shape[1] // 2
    for ref in sums:
        ref[...] = jnp.zeros_like(ref)
    for n in range(count):
        c = [cols_ref[k, n] for k in range(4)]
        both = dot_nn(strain_ref[n], stiff_ref[n])
        both = both[:cases] + both[cases:]
        left, right = both[:, :LANES], both[:, LANES:]
        sums[0][c[0]] += left
        sums[1][c[1]] += left
        sums[0][c[2]] += right
        sums[1][c[3]] += right


def folded_tile(sums, j):
    cases = sums[0].shape[1]
    in_low = iota((cases, LANES), 1) < LANES // 2
    even, odd = 2 * j, 2 * j + 1
    straight = jnp.where(in_low, sums[0][even], sums[1][odd])
    crossed = jnp.where(in_low, sums[0][odd], sums[1][even])
    return straight + pltpu.roll(crossed, LANES // 2, 1)


def operator_body(
    cols_ref, field_ref, mass_ref, trace_ref, stiff_ref, out_ref, own_ref, low_ref, high_ref, strain_ref, *sums
):
    spread_blocks(field_ref, low_ref, high_ref)
    strain_rows(cols_ref, stiff_ref, low_ref, high_ref, strain_ref)
    transposed_sums(cols_ref, stiff_ref, strain_ref, sums)
    dofs = field_ref.shape[1]
    for j in range(dofs // LANES):
        at = slice(j * LANES, (j + 1) * LANES)
        out_ref[:, at] = field_ref[:, at] * mass_ref[:, at] + folded_tile(sums, j)
    trace = trace_ref[...]
    own_ref[...] = gather_slots(
        out_ref[...], one_hot_low(trace & (WIDE - 1), trace.shape[1]), trace >> 8, dofs // WIDE
    )


def coincidence(trace_ref, match_trace_ref, out_ref):
    slots = trace_ref.shape[1]
    rows = [trace_ref[...].astype(F32), match_trace_ref[...]]
    for i in range(slots // LANES):
        at = slice(i * LANES, (i + 1) * LANES)
        total = jnp.zeros((LANES, slots), F32)
        for row in rows:
            column = jnp.broadcast_to(row[:, at], (LANES, LANES)).T
            total += (jnp.broadcast_to(column[:, :1], (LANES, slots)) == row).astype(F32)
        out_ref[at, :] = total.astype(BF16)


def add_jump(base, jump, one_hot, group):
    cases, dofs = base.shape
    groups = dofs // WIDE
    sums = dot_nt(masked_groups(stack2(jump), group, groups), one_hot)
    pieces = []
    for g in range(groups):
        row = g * 2 * cases
        pieces.append(
            base[:, g * WIDE:(g + 1) * WIDE]
            + (sums[row:row + cases] + sums[row + cases:row + 2 * cases])
        )
    return jnp.concatenate(pieces, axis=1)


def first_image(
    cols_ref, field_ref, part_ref, own_ref, match_ref, pen_ref, match_pen_ref, trace_ref, mass_ref, same_ref, stiff_ref,
    image_ref, shift_ref, gram_ref, strain_ref, low_ref, high_ref,
):
    cases, dofs = field_ref.shape
    trace = trace_ref[...]
    weight = pen_ref[...] * match_pen_ref[...]
    jump = weight * (own_ref[...] - match_ref[...])
    image_ref[...] = add_jump(
        part_ref[...], jump, one_hot_low(trace & (WIDE - 1), trace.shape[1]), trace >> 8
    )
    moved = dot_nn(stack2(jump), same_ref[...])
    shift_ref[...] = moved[:cases] + moved[cases:]
    spread_blocks(image_ref, low_ref, high_ref)
    strain_rows(cols_ref, stiff_ref, low_ref, high_ref, strain_ref)
    in_low = iota((2 * cases, LANES), 1) < LANES // 2
    strain = jnp.concatenate(
        [
            jnp.where(in_low, strain_ref[2 * j].astype(F32), strain_ref[2 * j + 1].astype(F32)).astype(BF16)
            for j in range(strain_ref.shape[0] // 2)
        ],
        axis=1,
    )
    image = image_ref[...]
    image_rows = stack2(image)
    rows = jnp.concatenate([stack2(field_ref[...]), image_rows], axis=0)
    every = dot_nt(rows, image_rows)
    every = every[:, :cases] + every[:, cases:]
    cross = every[:cases] + every[cases:2 * cases]
    square = every[2 * cases:3 * cases] + every[3 * cases:]
    start = dot_nt(rows[:2 * cases], rows[:2 * cases])
    start = start[:, :cases] + start[:, cases:]
    start = start[:cases] + start[cases:]
    last = dot_nt(image_rows, stack2(image * mass_ref[...])) + dot_nt(strain, strain)
    last = last[:, :cases] + last[:, cases:]
    last = last[:cases] + last[cases:]
    gram_ref[...] = jnp.concatenate([cross, start, square, last], axis=1)


def gram_trace(gram_ref, own_ref, match_ref, shift_ref, pen_ref, match_pen_ref, out_ref, jump_ref):
    cases = gram_ref.shape[0]
    apart = (own_ref[...] - match_ref[...]) + shift_ref[...]
    jump = (pen_ref[...] * match_pen_ref[...]) * apart
    jump_ref[...] = jump
    more = dot_nt(stack2(0.5 * apart), stack2(jump))
    more = more[:, :cases] + more[:, cases:]
    more = more[:cases] + more[cases:]
    zeros = jnp.zeros((cases, 3 * cases), F32)
    out_ref[...] = gram_ref[...] + jnp.concatenate([zeros, more], axis=1)


def second_image(
    cols_ref, field_ref, image_ref, mass_ref, stiff_ref, strain_ref, jump_ref, trace_ref, out_ref, *sums
):
    transposed_sums(cols_ref, stiff_ref, strain_ref, sums)
    trace = trace_ref[...]
    one_hot = one_hot_low(trace & (WIDE - 1), trace.shape[1])
    folded = jnp.concatenate(
        [folded_tile(sums, j) for j in range(image_ref.shape[1] // LANES)], axis=1
    )
    image = image_ref[...]
    rows = 2 * image.shape[0]
    second = add_jump(image * mass_ref[...] + folded, jump_ref[...], one_hot, trace >> 8)
    for i, part in enumerate((field_ref[...], image, second)):
        out_ref[i * rows:(i + 1) * rows, :] = stack2(part)
    out_ref[3 * rows:, :] = jnp.zeros((out_ref.shape[0] - 3 * rows, out_ref.shape[1]), BF16)


def eliminate(matrix, size, group=8):
    rows = iota(matrix.shape, 0)
    for first in range(0, size, group):
        columns = [
            jnp.broadcast_to(matrix[:, p:p + 1], matrix.shape) for p in range(first, first + group)
        ]
        for q in range(group):
            p = first + q
            column = columns[q]
            inverse = 1.0 / column[p:p + 1]
            row = matrix[p:p + 1] * inverse
            here = rows == p
            matrix = jnp.where(here, row, matrix - column * row)
            for r in range(q + 1, group):
                entry = column[first + r:first + r + 1] * inverse
                columns[r] = jnp.where(here, entry, columns[r] - column * entry)
    return matrix


def small_dot(a, b):
    return jnp.dot(a, b, precision=lax.Precision.HIGHEST, preferred_element_type=F32)


def finish(*refs):
    *gram_refs, field_ref, rows_ref, solution_ref, residual_ref = refs
    cases = field_ref.shape[0]
    gram = sum_of([ref[...] for ref in gram_refs])
    square = gram[:, 2 * cases:3 * cases]
    solved = eliminate(gram, cases)
    zeros = jnp.zeros((cases, 2 * cases), F32)
    given = jnp.concatenate([gram[:, 3 * cases:], gram[:, :cases]], axis=1)
    both = jnp.concatenate([solved[:, 2 * cases:3 * cases], solved[:, cases:2 * cases]], axis=1)
    second_part = eliminate(
        jnp.concatenate([given - small_dot(square, both), zeros], axis=1), cases
    )[:, cases:2 * cases]
    first_part = both[:, cases:] - small_dot(both[:, :cases], second_part)
    zero = jnp.zeros((cases, cases), F32)
    blocks = [[first_part, zero], [second_part, -first_part], [zero, -second_part], [zero, zero]]
    weights = [jnp.concatenate(block + [zero, zero], axis=1) for block in blocks]
    weights = jnp.concatenate([weights[i // 2] for i in range(8)], axis=0)
    weights = jnp.concatenate([weights[:LANES].T, weights[LANES:].T], axis=1)[:2 * cases]
    out = dot_nn(stack2(weights), rows_ref[...])
    out = out[:2 * cases] + out[2 * cases:]
    solution_ref[...] = out[:cases]
    residual_ref[...] = field_ref[...] + out[cases:]


def sum_of(terms):
    while len(terms) > 1:
        terms = [sum(terms[i:i + 2][1:], terms[i]) for i in range(0, len(terms), 2)]
    return terms[0]


def paired(array, axis, by):
    return lax.ppermute(array, axis, [(i, i ^ by) for i in range(lax.axis_size(axis))])


def from_all(array, axis, stride, radix):
    return [array] + [paired(array, axis, by * stride) for by in range(1, radix)]


def digits(count):
    stages, stride = [], 1
    while stride < count:
        left = count // stride
        radix = 2 if stride == 1 and left % 2 == 0 else 4 if left % 4 == 0 else left
        stages.append((stride, radix))
        stride *= radix
    return stages


def run(body, outs, args, scratch=(), scalars=0, cost=None, far=0):
    whole = pl.BlockSpec(memory_space=pltpu.VMEM)
    args = [
        pltpu.with_memory_space_constraint(arg, pltpu.HBM) if scalars <= i < scalars + far else arg
        for i, arg in enumerate(args)
    ]
    return pl.pallas_call(
        body,
        out_shape=outs,
        in_specs=[pl.BlockSpec(memory_space=pltpu.SMEM)] * scalars
        + [pl.BlockSpec(memory_space=pltpu.HBM)] * far
        + [whole] * (len(args) - scalars - far),
        out_specs=jax.tree.map(lambda _: whole, outs),
        scratch_shapes=list(scratch),
        compiler_params=pltpu.CompilerParams(vmem_limit_bytes=VMEM_BYTES),
        cost_estimate=cost,
    )(*args)


def shards(
    load_cases,
    mass_diag,
    stiffness,
    block_cols,
    trace_dofs,
    penalty,
    cell_partials,
    cell_owner,
    cell_dof,
):
    cases, dofs = load_cases.shape
    count, blk, width = stiffness.shape
    cells = cell_partials.shape[1]
    slots = trace_dofs.shape[0]
    patches = lax.axis_size("patch")
    cap = 4 * cells // patches
    rows = cases + 8
    far_rows = cases + -(-(1 + 2 * (slots // cap)) // 8) * 8
    shape = jax.ShapeDtypeStruct
    field_shape = shape((cases, dofs), F32)
    slot_shape = shape((cases, slots), F32)
    mass = mass_diag.reshape(1, dofs)
    trace = trace_dofs.reshape(1, slots)
    pen = penalty.reshape(1, slots)
    cols = block_cols.T

    half = patches // 2
    packets = run(
        pack_cells,
        [shape((far_rows if by == half else rows, cap), F32) for by in range(patches)],
        (cell_partials, cell_owner.reshape(1, cells), cell_dof.reshape(1, cells), pen, trace),
        scratch=[
            pltpu.VMEM((cases, cells), F32),
            pltpu.VMEM((1, cells), jnp.int32),
            pltpu.VMEM((1, cells), jnp.int32),
            pltpu.VMEM((1, slots), F32),
            pltpu.VMEM((1, slots), jnp.int32),
            pltpu.SemaphoreType.DMA((5,)),
        ],
        far=5,
    )
    received = [packets[0]] + [
        paired(packets[by], "patch", by) for by in [*range(half, patches), *range(1, half)]
    ]
    stiff = run(
        split_stiffness,
        shape((count, 2 * blk, width), BF16),
        (stiffness,),
        cost=pl.CostEstimate(flops=4 * stiffness.size, bytes_accessed=8 * stiffness.size, transcendentals=0),
    )

    received, stiff, cols, mass, load_cases, trace = lax.optimization_barrier(
        (received, stiff, cols, mass, load_cases, trace)
    )

    spread = [pltpu.VMEM((dofs // blk, 2 * cases, LANES), BF16)] * 2
    strain_scratch = pltpu.VMEM((count, 2 * cases, LANES), BF16)
    sums = [pltpu.VMEM((dofs // blk, cases, LANES), F32)] * 2

    row_shape = shape((1, slots), F32)
    field, own, match_pen, match_trace = run(
        assemble, (field_shape, slot_shape, row_shape, row_shape), (load_cases, trace, *received)
    )
    match = paired(own, "patch", half)
    part, part_own = run(
        operator_body,
        (field_shape, slot_shape),
        (cols, field, mass, trace, stiff),
        scratch=[*spread, strain_scratch, *sums],
        scalars=1,
    )
    part_match = paired(part_own, "patch", half)
    same = run(coincidence, shape((slots, slots), BF16), (trace, match_trace))
    image, shift, gram, strain = run(
        first_image,
        (
            field_shape,
            slot_shape,
            shape((cases, 4 * cases), F32),
            shape((count, 2 * cases, LANES), BF16),
        ),
        (cols, field, part, own, match, pen, match_pen, trace, mass, same, stiff),
        scratch=spread,
        scalars=1,
    )
    gram, jump = run(
        gram_trace,
        (shape((cases, 4 * cases), F32), slot_shape),
        (gram, part_own, part_match, shift, pen, match_pen),
    )
    gram = sum_of(from_all(gram, "comp", 1, lax.axis_size("comp")))
    *early, last = digits(patches)
    for stride, radix in early:
        gram = sum_of(from_all(gram, "patch", stride, radix))
    grams = from_all(gram, "patch", *last)
    stacked = run(
        second_image,
        shape((-(-6 * cases // LANES) * LANES, dofs), BF16),
        (cols, field, image, mass, stiff, strain, jump, trace),
        scratch=sums,
        scalars=1,
    )
    return run(finish, (field_shape, field_shape), (*grams, field, stacked))


def solution(mesh):
    return jax.shard_map(
        shards,
        mesh=mesh,
        in_specs=(
            P(None, ("comp", "patch")),
            P(("comp", "patch")),
            P(("comp", "patch"), None, None),
            P(("comp", "patch"), None),
            P(("comp", "patch")),
            P(("comp", "patch")),
            P(None, ("comp", "patch")),
            P(("comp", "patch"), None),
            P(("comp", "patch")),
        ),
        out_specs=(P(None, ("comp", "patch")), P(None, ("comp", "patch"))),
        check_vma=False,
    )
```

```python
import jax
import jax.numpy as jnp
from jax import lax
from jax.experimental import pallas as pl
from jax.experimental.pallas import tpu as pltpu
from jax.sharding import PartitionSpec as P

F32 = jnp.float32
BF16 = jnp.bfloat16
WIDE = 256
LANES = 128
VMEM_BYTES = 32 * 1024 * 1024


def split2(x):
    high = x.astype(BF16)
    low = (x - high.astype(F32)).astype(BF16)
    return high, low


def stack2(x):
    return jnp.concatenate(split2(x), axis=0)


def dot_nn(a, b):
    return lax.dot_general(a, b, (((1,), (0,)), ((), ())), preferred_element_type=F32)


def dot_nt(a, b):
    return lax.dot_general(a, b, (((1,), (1,)), ((), ())), preferred_element_type=F32)


def iota(shape, axis):
    return lax.broadcasted_iota(jnp.int32, shape, axis)


def one_hot_low(low, width):
    return (iota((WIDE, width), 0) == low).astype(F32).astype(BF16)


def masked_groups(stacked, group, count):
    parts = []
    for g in range(count):
        mask = (group == g).astype(F32).astype(BF16)
        parts.append(stacked * jnp.broadcast_to(mask, stacked.shape))
    return jnp.concatenate(parts, axis=0)


def gather_slots(field, one_hot, group, groups):
    cases = field.shape[0]
    rows = jnp.concatenate(
        [stack2(field[:, g * WIDE:(g + 1) * WIDE]) for g in range(groups)], axis=0
    )
    found = dot_nn(rows, one_hot)
    total = jnp.zeros((cases, group.shape[1]), F32)
    for g in range(groups):
        base = g * 2 * cases
        both = found[base:base + cases] + found[base + cases:base + 2 * cases]
        total = jnp.where(group == g, both, total)
    return total


def fetch(sources, targets, sems):
    copies = [
        pltpu.make_async_copy(source, target, sems.at[i])
        for i, (source, target) in enumerate(zip(sources, targets))
    ]
    for copy in copies:
        copy.start()
    for copy in copies:
        copy.wait()


def pack_cells(*refs):
    sources, out_refs, targets, sems = refs[:5], refs[5:-6], refs[-6:-1], refs[-1]
    fetch(sources, targets, sems)
    partials_ref, owner_ref, dof_ref, pen_ref, trace_ref = targets
    patches = len(out_refs)
    rows, cap = out_refs[0].shape
    cases, cells = partials_ref.shape
    me = lax.axis_index("patch")
    shift = owner_ref[...] - me
    shift = jnp.where(shift < 0, shift + patches, shift)
    mine = (iota((patches, cells), 0) == shift).astype(F32)
    before = (iota((cells, cells), 0) < iota((cells, cells), 1)).astype(F32).astype(BF16)
    counts = dot_nn(mine.astype(BF16), before)
    rank = jnp.sum(mine * counts, axis=0, keepdims=True).astype(jnp.int32)
    extra = jnp.where(iota((rows - cases, cells), 0) == 0, dof_ref[...] + 1, 0).astype(F32)
    body = stack2(jnp.concatenate([partials_ref[...], extra], axis=0))
    for by, out_ref in enumerate(out_refs):
        key = jnp.where(shift == by, rank, -1)
        pick = (iota((cap, cells), 0) == key).astype(F32).astype(BF16)
        packed = dot_nt(body, pick)
        out_ref[:rows, :] = packed[:rows] + packed[rows:]
        if by == patches // 2:
            more = pen_ref.shape[1] // cap
            for i in range(more):
                at = cases + 1 + i
                out_ref[at:at + 1, :] = pen_ref[:, i * cap:(i + 1) * cap]
                out_ref[at + more:at + more + 1, :] = trace_ref[:, i * cap:(i + 1) * cap].astype(F32)


def split_stiffness(stiff_ref, out_ref):
    blk = stiff_ref.shape[1]
    high, low = split2(stiff_ref[...])
    out_ref[:, :blk, :] = high
    out_ref[:, blk:, :] = low


def assemble(load_ref, trace_ref, *refs):
    *recv_refs, field_ref, own_ref, pen_ref, match_trace_ref = refs
    patches = len(recv_refs)
    cases, dofs = load_ref.shape
    groups = dofs // WIDE
    rows, cap = recv_refs[0].shape
    cells = jnp.concatenate([ref[:rows, :] for ref in recv_refs], axis=1)
    far_ref = recv_refs[patches // 2]
    more = pen_ref.shape[1] // cap
    for i in range(more):
        at = cases + 1 + i
        pen_ref[:, i * cap:(i + 1) * cap] = far_ref[at:at + 1, :]
        match_trace_ref[:, i * cap:(i + 1) * cap] = far_ref[at + more:at + more + 1, :]
    slots = cells.shape[1]
    dof = cells[cases:cases + 1].astype(jnp.int32) - 1
    rows = masked_groups(stack2(cells[:cases]), dof >> 8, groups)
    sums = dot_nt(rows, one_hot_low(jnp.where(dof < 0, -1, dof & (WIDE - 1)), slots))
    pieces = []
    for g in range(groups):
        base = g * 2 * cases
        pieces.append(
            load_ref[:, g * WIDE:(g + 1) * WIDE]
            + (sums[base:base + cases] + sums[base + cases:base + 2 * cases])
        )
    field = jnp.concatenate(pieces, axis=1)
    field_ref[...] = field
    trace = trace_ref[...]
    own_ref[...] = gather_slots(
        field, one_hot_low(trace & (WIDE - 1), trace.shape[1]), trace >> 8, groups
    )


def spread_blocks(field_ref, low_ref, high_ref):
    cases, dofs = field_ref.shape
    in_low = iota((cases, LANES), 1) < LANES // 2
    for j in range(dofs // LANES):
        tile = field_ref[:, j * LANES:(j + 1) * LANES]
        turned = pltpu.roll(tile, LANES // 2, 1)
        low_ref[2 * j] = stack2(jnp.where(in_low, tile, 0.0))
        high_ref[2 * j + 1] = stack2(jnp.where(in_low, 0.0, tile))
        low_ref[2 * j + 1] = stack2(jnp.where(in_low, turned, 0.0))
        high_ref[2 * j] = stack2(jnp.where(in_low, 0.0, turned))


def strain_rows(cols_ref, stiff_ref, low_ref, high_ref, strain_ref):
    count = stiff_ref.shape[0]
    cases = strain_ref.shape[1] // 2
    for n in range(count):
        c = [cols_ref[k, n] for k in range(4)]
        near = jnp.concatenate(
            [low_ref[c[0]] + high_ref[c[1]], low_ref[c[2]] + high_ref[c[3]]], axis=1
        )
        both = dot_nt(near, stiff_ref[n])
        both = both[:cases] + both[cases:]
        strain_ref[n] = stack2(both + pltpu.roll(both, LANES // 2, 1))


def transposed_sums(cols_ref, stiff_ref, strain_ref, sums):
    count = stiff_ref.shape[0]
    cases = strain_ref.shape[1] // 2
    for ref in sums:
        ref[...] = jnp.zeros_like(ref)
    for n in range(count):
        c = [cols_ref[k, n] for k in range(4)]
        both = dot_nn(strain_ref[n], stiff_ref[n])
        both = both[:cases] + both[cases:]
        left, right = both[:, :LANES], both[:, LANES:]
        sums[0][c[0]] += left
        sums[1][c[1]] += left
        sums[0][c[2]] += right
        sums[1][c[3]] += right


def folded_tile(sums, j):
    cases = sums[0].shape[1]
    in_low = iota((cases, LANES), 1) < LANES // 2
    even, odd = 2 * j, 2 * j + 1
    straight = jnp.where(in_low, sums[0][even], sums[1][odd])
    crossed = jnp.where(in_low, sums[0][odd], sums[1][even])
    return straight + pltpu.roll(crossed, LANES // 2, 1)


def operator_body(
    cols_ref, field_ref, mass_ref, trace_ref, stiff_ref, out_ref, own_ref, low_ref, high_ref, strain_ref, *sums
):
    spread_blocks(field_ref, low_ref, high_ref)
    strain_rows(cols_ref, stiff_ref, low_ref, high_ref, strain_ref)
    transposed_sums(cols_ref, stiff_ref, strain_ref, sums)
    dofs = field_ref.shape[1]
    for j in range(dofs // LANES):
        at = slice(j * LANES, (j + 1) * LANES)
        out_ref[:, at] = field_ref[:, at] * mass_ref[:, at] + folded_tile(sums, j)
    trace = trace_ref[...]
    own_ref[...] = gather_slots(
        out_ref[...], one_hot_low(trace & (WIDE - 1), trace.shape[1]), trace >> 8, dofs // WIDE
    )


def coincidence(trace_ref, match_trace_ref, out_ref):
    slots = trace_ref.shape[1]
    rows = [trace_ref[...].astype(F32), match_trace_ref[...]]
    for i in range(slots // LANES):
        at = slice(i * LANES, (i + 1) * LANES)
        total = jnp.zeros((LANES, slots), F32)
        for row in rows:
            column = jnp.broadcast_to(row[:, at], (LANES, LANES)).T
            total += (jnp.broadcast_to(column[:, :1], (LANES, slots)) == row).astype(F32)
        out_ref[at, :] = total.astype(BF16)


def add_jump(base, jump, one_hot, group):
    cases, dofs = base.shape
    groups = dofs // WIDE
    sums = dot_nt(masked_groups(stack2(jump), group, groups), one_hot)
    pieces = []
    for g in range(groups):
        row = g * 2 * cases
        pieces.append(
            base[:, g * WIDE:(g + 1) * WIDE]
            + (sums[row:row + cases] + sums[row + cases:row + 2 * cases])
        )
    return jnp.concatenate(pieces, axis=1)


def first_image(
    cols_ref, field_ref, part_ref, own_ref, match_ref, pen_ref, match_pen_ref, trace_ref, mass_ref, same_ref, stiff_ref,
    image_ref, shift_ref, gram_ref, strain_ref, low_ref, high_ref,
):
    cases, dofs = field_ref.shape
    trace = trace_ref[...]
    weight = pen_ref[...] * match_pen_ref[...]
    jump = weight * (own_ref[...] - match_ref[...])
    image_ref[...] = add_jump(
        part_ref[...], jump, one_hot_low(trace & (WIDE - 1), trace.shape[1]), trace >> 8
    )
    moved = dot_nn(stack2(jump), same_ref[...])
    shift_ref[...] = moved[:cases] + moved[cases:]
    spread_blocks(image_ref, low_ref, high_ref)
    strain_rows(cols_ref, stiff_ref, low_ref, high_ref, strain_ref)
    in_low = iota((2 * cases, LANES), 1) < LANES // 2
    strain = jnp.concatenate(
        [
            jnp.where(in_low, strain_ref[2 * j].astype(F32), strain_ref[2 * j + 1].astype(F32)).astype(BF16)
            for j in range(strain_ref.shape[0] // 2)
        ],
        axis=1,
    )
    image = image_ref[...]
    image_rows = stack2(image)
    rows = jnp.concatenate([stack2(field_ref[...]), image_rows], axis=0)
    every = dot_nt(rows, image_rows)
    every = every[:, :cases] + every[:, cases:]
    cross = every[:cases] + every[cases:2 * cases]
    square = every[2 * cases:3 * cases] + every[3 * cases:]
    start = dot_nt(rows[:2 * cases], rows[:2 * cases])
    start = start[:, :cases] + start[:, cases:]
    start = start[:cases] + start[cases:]
    last = dot_nt(image_rows, stack2(image * mass_ref[...])) + dot_nt(strain, strain)
    last = last[:, :cases] + last[:, cases:]
    last = last[:cases] + last[cases:]
    gram_ref[...] = jnp.concatenate([cross, start, square, last], axis=1)


def gram_trace(gram_ref, own_ref, match_ref, shift_ref, pen_ref, match_pen_ref, out_ref, jump_ref):
    cases = gram_ref.shape[0]
    apart = (own_ref[...] - match_ref[...]) + shift_ref[...]
    jump = (pen_ref[...] * match_pen_ref[...]) * apart
    jump_ref[...] = jump
    more = dot_nt(stack2(0.5 * apart), stack2(jump))
    more = more[:, :cases] + more[:, cases:]
    more = more[:cases] + more[cases:]
    zeros = jnp.zeros((cases, 3 * cases), F32)
    out_ref[...] = gram_ref[...] + jnp.concatenate([zeros, more], axis=1)


def second_image(
    cols_ref, field_ref, image_ref, mass_ref, stiff_ref, strain_ref, jump_ref, trace_ref, out_ref, *sums
):
    transposed_sums(cols_ref, stiff_ref, strain_ref, sums)
    trace = trace_ref[...]
    one_hot = one_hot_low(trace & (WIDE - 1), trace.shape[1])
    folded = jnp.concatenate(
        [folded_tile(sums, j) for j in range(image_ref.shape[1] // LANES)], axis=1
    )
    image = image_ref[...]
    rows = 2 * image.shape[0]
    second = add_jump(image * mass_ref[...] + folded, jump_ref[...], one_hot, trace >> 8)
    for i, part in enumerate((field_ref[...], image, second)):
        out_ref[i * rows:(i + 1) * rows, :] = stack2(part)
    out_ref[3 * rows:, :] = jnp.zeros((out_ref.shape[0] - 3 * rows, out_ref.shape[1]), BF16)


def eliminate(matrix, size, group=8):
    rows = iota(matrix.shape, 0)
    for first in range(0, size, group):
        columns = [
            jnp.broadcast_to(matrix[:, p:p + 1], matrix.shape) for p in range(first, first + group)
        ]
        for q in range(group):
            p = first + q
            column = columns[q]
            inverse = 1.0 / column[p:p + 1]
            row = matrix[p:p + 1] * inverse
            here = rows == p
            matrix = jnp.where(here, row, matrix - column * row)
            for r in range(q + 1, group):
                entry = column[first + r:first + r + 1] * inverse
                columns[r] = jnp.where(here, entry, columns[r] - column * entry)
    return matrix


def small_dot(a, b):
    return jnp.dot(a, b, precision=lax.Precision.HIGHEST, preferred_element_type=F32)


def finish(*refs):
    *gram_refs, field_ref, rows_ref, solution_ref, residual_ref = refs
    cases = field_ref.shape[0]
    gram = sum_of([ref[...] for ref in gram_refs])
    square = gram[:, 2 * cases:3 * cases]
    solved = eliminate(gram, cases)
    zeros = jnp.zeros((cases, 2 * cases), F32)
    given = jnp.concatenate([gram[:, 3 * cases:], gram[:, :cases]], axis=1)
    both = jnp.concatenate([solved[:, 2 * cases:3 * cases], solved[:, cases:2 * cases]], axis=1)
    second_part = eliminate(
        jnp.concatenate([given - small_dot(square, both), zeros], axis=1), cases
    )[:, cases:2 * cases]
    first_part = both[:, cases:] - small_dot(both[:, :cases], second_part)
    zero = jnp.zeros((cases, cases), F32)
    blocks = [[first_part, zero], [second_part, -first_part], [zero, -second_part], [zero, zero]]
    weights = [jnp.concatenate(block + [zero, zero], axis=1) for block in blocks]
    weights = jnp.concatenate([weights[i // 2] for i in range(8)], axis=0)
    weights = jnp.concatenate([weights[:LANES].T, weights[LANES:].T], axis=1)[:2 * cases]
    out = dot_nn(stack2(weights), rows_ref[...])
    out = out[:2 * cases] + out[2 * cases:]
    solution_ref[...] = out[:cases]
    residual_ref[...] = field_ref[...] + out[cases:]


def sum_of(terms):
    while len(terms) > 1:
        terms = [sum(terms[i:i + 2][1:], terms[i]) for i in range(0, len(terms), 2)]
    return terms[0]


def from_all(array, axis, stride=1, radix=None):
    count = lax.axis_size(axis)
    radix = radix or count
    span = stride * radix

    def target(i, by):
        digit = i // stride % radix
        return i // span * span + (digit + by) % radix * stride + i % stride

    return [array] + [
        lax.ppermute(array, axis, [(i, target(i, by)) for i in range(count)])
        for by in range(1, radix)
    ]


def digits(count):
    stages, stride = [], 1
    while stride < count:
        left = count // stride
        radix = 2 if stride == 1 and left % 2 == 0 else 4 if left % 4 == 0 else left
        stages.append((stride, radix))
        stride *= radix
    return stages


def run(body, outs, args, scratch=(), scalars=0, cost=None, far=0):
    whole = pl.BlockSpec(memory_space=pltpu.VMEM)
    args = [
        pltpu.with_memory_space_constraint(arg, pltpu.HBM) if scalars <= i < scalars + far else arg
        for i, arg in enumerate(args)
    ]
    return pl.pallas_call(
        body,
        out_shape=outs,
        in_specs=[pl.BlockSpec(memory_space=pltpu.SMEM)] * scalars
        + [pl.BlockSpec(memory_space=pltpu.HBM)] * far
        + [whole] * (len(args) - scalars - far),
        out_specs=jax.tree.map(lambda _: whole, outs),
        scratch_shapes=list(scratch),
        compiler_params=pltpu.CompilerParams(vmem_limit_bytes=VMEM_BYTES),
        cost_estimate=cost,
    )(*args)


def shards(
    load_cases,
    mass_diag,
    stiffness,
    block_cols,
    trace_dofs,
    penalty,
    cell_partials,
    cell_owner,
    cell_dof,
):
    cases, dofs = load_cases.shape
    count, blk, width = stiffness.shape
    cells = cell_partials.shape[1]
    slots = trace_dofs.shape[0]
    patches = lax.axis_size("patch")
    cap = 4 * cells // patches
    rows = cases + 8
    far_rows = cases + -(-(1 + 2 * (slots // cap)) // 8) * 8
    shape = jax.ShapeDtypeStruct
    field_shape = shape((cases, dofs), F32)
    slot_shape = shape((cases, slots), F32)
    mass = mass_diag.reshape(1, dofs)
    trace = trace_dofs.reshape(1, slots)
    pen = penalty.reshape(1, slots)
    cols = block_cols.T

    half = patches // 2
    pairs = [(i, (i + half) % patches) for i in range(patches)]
    packets = run(
        pack_cells,
        [shape((far_rows if by == half else rows, cap), F32) for by in range(patches)],
        (cell_partials, cell_owner.reshape(1, cells), cell_dof.reshape(1, cells), pen, trace),
        scratch=[
            pltpu.VMEM((cases, cells), F32),
            pltpu.VMEM((1, cells), jnp.int32),
            pltpu.VMEM((1, cells), jnp.int32),
            pltpu.VMEM((1, slots), F32),
            pltpu.VMEM((1, slots), jnp.int32),
            pltpu.SemaphoreType.DMA((5,)),
        ],
        far=5,
    )
    received = [packets[0]] + [
        lax.ppermute(packets[by], "patch", [(i, (i + by) % patches) for i in range(patches)])
        for by in range(1, patches)
    ]
    stiff = run(
        split_stiffness,
        shape((count, 2 * blk, width), BF16),
        (stiffness,),
        cost=pl.CostEstimate(flops=4 * stiffness.size, bytes_accessed=8 * stiffness.size, transcendentals=0),
    )

    received, stiff, cols, mass, load_cases, trace = lax.optimization_barrier(
        (received, stiff, cols, mass, load_cases, trace)
    )

    spread = [pltpu.VMEM((dofs // blk, 2 * cases, LANES), BF16)] * 2
    strain_scratch = pltpu.VMEM((count, 2 * cases, LANES), BF16)
    sums = [pltpu.VMEM((dofs // blk, cases, LANES), F32)] * 2

    row_shape = shape((1, slots), F32)
    field, own, match_pen, match_trace = run(
        assemble, (field_shape, slot_shape, row_shape, row_shape), (load_cases, trace, *received)
    )
    match = lax.ppermute(own, "patch", pairs)
    part, part_own = run(
        operator_body,
        (field_shape, slot_shape),
        (cols, field, mass, trace, stiff),
        scratch=[*spread, strain_scratch, *sums],
        scalars=1,
    )
    part_match = lax.ppermute(part_own, "patch", pairs)
    same = run(coincidence, shape((slots, slots), BF16), (trace, match_trace))
    image, shift, gram, strain = run(
        first_image,
        (
            field_shape,
            slot_shape,
            shape((cases, 4 * cases), F32),
            shape((count, 2 * cases, LANES), BF16),
        ),
        (cols, field, part, own, match, pen, match_pen, trace, mass, same, stiff),
        scratch=spread,
        scalars=1,
    )
    gram, jump = run(
        gram_trace,
        (shape((cases, 4 * cases), F32), slot_shape),
        (gram, part_own, part_match, shift, pen, match_pen),
    )
    everyone = ("comp", "patch")
    count_all = lax.axis_size("comp") * patches
    share = -(-cases // count_all)
    padded = jnp.pad(gram, ((0, share * count_all - cases), (0, 0))) if share * count_all > cases else gram
    parts = lax.all_to_all(padded.reshape(count_all, share, 4 * cases), everyone, 0, 0)
    total = jnp.broadcast_to(jnp.sum(parts, axis=0)[None], parts.shape)
    whole = lax.all_to_all(total, everyone, 0, 0).reshape(count_all * share, 4 * cases)[:cases]
    stacked = run(
        second_image,
        shape((-(-6 * cases // LANES) * LANES, dofs), BF16),
        (cols, field, image, mass, stiff, strain, jump, trace),
        scratch=sums,
        scalars=1,
    )
    return run(finish, (field_shape, field_shape), (whole, field, stacked))


def solution(mesh):
    return jax.shard_map(
        shards,
        mesh=mesh,
        in_specs=(
            P(None, ("comp", "patch")),
            P(("comp", "patch")),
            P(("comp", "patch"), None, None),
            P(("comp", "patch"), None),
            P(("comp", "patch")),
            P(("comp", "patch")),
            P(None, ("comp", "patch")),
            P(("comp", "patch"), None),
            P(("comp", "patch")),
        ),
        out_specs=(P(None, ("comp", "patch")), P(None, ("comp", "patch"))),
        check_vma=False,
    )
```

```python
import jax
import jax.numpy as jnp
from jax import lax
from jax.experimental import pallas as pl
from jax.experimental.pallas import tpu as pltpu
from jax.sharding import PartitionSpec as P

F32 = jnp.float32
BF16 = jnp.bfloat16
WIDE = 256
LANES = 128
VMEM_BYTES = 32 * 1024 * 1024


def split2(x):
    high = x.astype(BF16)
    low = (x - high.astype(F32)).astype(BF16)
    return high, low


def stack2(x):
    return jnp.concatenate(split2(x), axis=0)


def dot_nn(a, b):
    return lax.dot_general(a, b, (((1,), (0,)), ((), ())), preferred_element_type=F32)


def dot_nt(a, b):
    return lax.dot_general(a, b, (((1,), (1,)), ((), ())), preferred_element_type=F32)


def iota(shape, axis):
    return lax.broadcasted_iota(jnp.int32, shape, axis)


def one_hot_low(low, width):
    return (iota((WIDE, width), 0) == low).astype(F32).astype(BF16)


def masked_groups(stacked, group, count):
    parts = []
    for g in range(count):
        mask = (group == g).astype(F32).astype(BF16)
        parts.append(stacked * jnp.broadcast_to(mask, stacked.shape))
    return jnp.concatenate(parts, axis=0)


def gather_slots(field, one_hot, group, groups):
    cases = field.shape[0]
    rows = jnp.concatenate(
        [stack2(field[:, g * WIDE:(g + 1) * WIDE]) for g in range(groups)], axis=0
    )
    found = dot_nn(rows, one_hot)
    total = jnp.zeros((cases, group.shape[1]), F32)
    for g in range(groups):
        base = g * 2 * cases
        both = found[base:base + cases] + found[base + cases:base + 2 * cases]
        total = jnp.where(group == g, both, total)
    return total


def fetch(sources, targets, sems):
    copies = [
        pltpu.make_async_copy(source, target, sems.at[i])
        for i, (source, target) in enumerate(zip(sources, targets))
    ]
    for copy in copies:
        copy.start()
    for copy in copies:
        copy.wait()


def pack_cells(*refs):
    sources, stiff_ref, out_refs, split_ref = refs[:5], refs[5], refs[6:-9], refs[-9]
    targets, sems, wide_ref, wide_sem = refs[-8:-3], refs[-3], refs[-2], refs[-1]
    fetch(sources, targets, sems)
    partials_ref, owner_ref, dof_ref, pen_ref, trace_ref = targets
    patches = len(out_refs)
    rows, cap = out_refs[0].shape
    cases, cells = partials_ref.shape
    me = lax.axis_index("patch")
    shift = owner_ref[...] - me
    shift = jnp.where(shift < 0, shift + patches, shift)
    mine = (iota((patches, cells), 0) == shift).astype(F32)
    before = (iota((cells, cells), 0) < iota((cells, cells), 1)).astype(F32).astype(BF16)
    counts = dot_nn(mine.astype(BF16), before)
    rank = jnp.sum(mine * counts, axis=0, keepdims=True).astype(jnp.int32)
    extra = jnp.where(iota((rows - cases, cells), 0) == 0, dof_ref[...] + 1, 0).astype(F32)
    body = stack2(jnp.concatenate([partials_ref[...], extra], axis=0))
    for by, out_ref in enumerate(out_refs):
        key = jnp.where(shift == by, rank, -1)
        pick = (iota((cap, cells), 0) == key).astype(F32).astype(BF16)
        packed = dot_nt(body, pick)
        out_ref[:rows, :] = packed[:rows] + packed[rows:]
        if by == patches // 2:
            more = pen_ref.shape[1] // cap
            for i in range(more):
                at = cases + 1 + i
                out_ref[at:at + 1, :] = pen_ref[:, i * cap:(i + 1) * cap]
                out_ref[at + more:at + more + 1, :] = trace_ref[:, i * cap:(i + 1) * cap].astype(F32)

    @pl.when(second_core())
    def _():
        split_stiffness(stiff_ref, split_ref, wide_ref, wide_sem)


def second_core():
    return lax.axis_index("comp") % 2 == 1


def split_stiffness(stiff_ref, out_ref, wide_ref, sem):
    blk = stiff_ref.shape[1]
    copy = pltpu.make_async_copy(stiff_ref, wide_ref, sem)
    copy.start()
    copy.wait()
    high, low = split2(wide_ref[...])
    out_ref[:, :blk, :] = high
    out_ref[:, blk:, :] = low


def split_rest(stiff_ref, given_ref, out_ref, wide_ref, sem):
    @pl.when(second_core())
    def _():
        out_ref[...] = given_ref[...]

    @pl.when(jnp.logical_not(second_core()))
    def _():
        split_stiffness(stiff_ref, out_ref, wide_ref, sem)


def assemble(load_ref, trace_ref, *refs):
    *recv_refs, field_ref, own_ref, pen_ref, match_trace_ref = refs
    patches = len(recv_refs)
    cases, dofs = load_ref.shape
    groups = dofs // WIDE
    rows, cap = recv_refs[0].shape
    cells = jnp.concatenate([ref[:rows, :] for ref in recv_refs], axis=1)
    far_ref = recv_refs[patches // 2]
    more = pen_ref.shape[1] // cap
    for i in range(more):
        at = cases + 1 + i
        pen_ref[:, i * cap:(i + 1) * cap] = far_ref[at:at + 1, :]
        match_trace_ref[:, i * cap:(i + 1) * cap] = far_ref[at + more:at + more + 1, :]
    slots = cells.shape[1]
    dof = cells[cases:cases + 1].astype(jnp.int32) - 1
    rows = masked_groups(stack2(cells[:cases]), dof >> 8, groups)
    sums = dot_nt(rows, one_hot_low(jnp.where(dof < 0, -1, dof & (WIDE - 1)), slots))
    pieces = []
    for g in range(groups):
        base = g * 2 * cases
        pieces.append(
            load_ref[:, g * WIDE:(g + 1) * WIDE]
            + (sums[base:base + cases] + sums[base + cases:base + 2 * cases])
        )
    field = jnp.concatenate(pieces, axis=1)
    field_ref[...] = field
    trace = trace_ref[...]
    own_ref[...] = gather_slots(
        field, one_hot_low(trace & (WIDE - 1), trace.shape[1]), trace >> 8, groups
    )


def spread_blocks(field_ref, low_ref, high_ref):
    cases, dofs = field_ref.shape
    in_low = iota((cases, LANES), 1) < LANES // 2
    for j in range(dofs // LANES):
        tile = field_ref[:, j * LANES:(j + 1) * LANES]
        turned = pltpu.roll(tile, LANES // 2, 1)
        low_ref[2 * j] = stack2(jnp.where(in_low, tile, 0.0))
        high_ref[2 * j + 1] = stack2(jnp.where(in_low, 0.0, tile))
        low_ref[2 * j + 1] = stack2(jnp.where(in_low, turned, 0.0))
        high_ref[2 * j] = stack2(jnp.where(in_low, 0.0, turned))


def strain_rows(cols_ref, stiff_ref, low_ref, high_ref, strain_ref):
    count = stiff_ref.shape[0]
    cases = strain_ref.shape[1] // 2
    for n in range(count):
        c = [cols_ref[k, n] for k in range(4)]
        near = jnp.concatenate(
            [low_ref[c[0]] + high_ref[c[1]], low_ref[c[2]] + high_ref[c[3]]], axis=1
        )
        both = dot_nt(near, stiff_ref[n])
        both = both[:cases] + both[cases:]
        strain_ref[n] = stack2(both + pltpu.roll(both, LANES // 2, 1))


def transposed_sums(cols_ref, stiff_ref, strain_ref, sums):
    count = stiff_ref.shape[0]
    cases = strain_ref.shape[1] // 2
    for ref in sums:
        ref[...] = jnp.zeros_like(ref)
    for n in range(count):
        c = [cols_ref[k, n] for k in range(4)]
        both = dot_nn(strain_ref[n], stiff_ref[n])
        both = both[:cases] + both[cases:]
        left, right = both[:, :LANES], both[:, LANES:]
        sums[0][c[0]] += left
        sums[1][c[1]] += left
        sums[0][c[2]] += right
        sums[1][c[3]] += right


def folded_tile(sums, j):
    cases = sums[0].shape[1]
    in_low = iota((cases, LANES), 1) < LANES // 2
    even, odd = 2 * j, 2 * j + 1
    straight = jnp.where(in_low, sums[0][even], sums[1][odd])
    crossed = jnp.where(in_low, sums[0][odd], sums[1][even])
    return straight + pltpu.roll(crossed, LANES // 2, 1)


def operator_body(
    cols_ref, field_ref, mass_ref, trace_ref, stiff_ref, out_ref, own_ref, low_ref, high_ref, strain_ref, *sums
):
    spread_blocks(field_ref, low_ref, high_ref)
    strain_rows(cols_ref, stiff_ref, low_ref, high_ref, strain_ref)
    transposed_sums(cols_ref, stiff_ref, strain_ref, sums)
    dofs = field_ref.shape[1]
    for j in range(dofs // LANES):
        at = slice(j * LANES, (j + 1) * LANES)
        out_ref[:, at] = field_ref[:, at] * mass_ref[:, at] + folded_tile(sums, j)
    trace = trace_ref[...]
    own_ref[...] = gather_slots(
        out_ref[...], one_hot_low(trace & (WIDE - 1), trace.shape[1]), trace >> 8, dofs // WIDE
    )


def coincidence(trace_ref, match_trace_ref, out_ref):
    slots = trace_ref.shape[1]
    rows = [trace_ref[...].astype(F32), match_trace_ref[...]]
    for i in range(slots // LANES):
        at = slice(i * LANES, (i + 1) * LANES)
        total = jnp.zeros((LANES, slots), F32)
        for row in rows:
            column = jnp.broadcast_to(row[:, at], (LANES, LANES)).T
            total += (jnp.broadcast_to(column[:, :1], (LANES, slots)) == row).astype(F32)
        out_ref[at, :] = total.astype(BF16)


def add_jump(base, jump, one_hot, group):
    cases, dofs = base.shape
    groups = dofs // WIDE
    sums = dot_nt(masked_groups(stack2(jump), group, groups), one_hot)
    pieces = []
    for g in range(groups):
        row = g * 2 * cases
        pieces.append(
            base[:, g * WIDE:(g + 1) * WIDE]
            + (sums[row:row + cases] + sums[row + cases:row + 2 * cases])
        )
    return jnp.concatenate(pieces, axis=1)


def first_image(
    cols_ref, field_ref, part_ref, own_ref, match_ref, pen_ref, match_pen_ref, trace_ref, mass_ref, same_ref, stiff_ref,
    image_ref, shift_ref, gram_ref, strain_ref, low_ref, high_ref,
):
    cases, dofs = field_ref.shape
    trace = trace_ref[...]
    weight = pen_ref[...] * match_pen_ref[...]
    jump = weight * (own_ref[...] - match_ref[...])
    image_ref[...] = add_jump(
        part_ref[...], jump, one_hot_low(trace & (WIDE - 1), trace.shape[1]), trace >> 8
    )
    moved = dot_nn(stack2(jump), same_ref[...])
    shift_ref[...] = moved[:cases] + moved[cases:]
    spread_blocks(image_ref, low_ref, high_ref)
    strain_rows(cols_ref, stiff_ref, low_ref, high_ref, strain_ref)
    in_low = iota((2 * cases, LANES), 1) < LANES // 2
    strain = jnp.concatenate(
        [
            jnp.where(in_low, strain_ref[2 * j].astype(F32), strain_ref[2 * j + 1].astype(F32)).astype(BF16)
            for j in range(strain_ref.shape[0] // 2)
        ],
        axis=1,
    )
    image = image_ref[...]
    image_rows = stack2(image)
    rows = jnp.concatenate([stack2(field_ref[...]), image_rows], axis=0)
    every = dot_nt(rows, image_rows)
    every = every[:, :cases] + every[:, cases:]
    cross = every[:cases] + every[cases:2 * cases]
    square = every[2 * cases:3 * cases] + every[3 * cases:]
    start = dot_nt(rows[:2 * cases], rows[:2 * cases])
    start = start[:, :cases] + start[:, cases:]
    start = start[:cases] + start[cases:]
    last = dot_nt(image_rows, stack2(image * mass_ref[...])) + dot_nt(strain, strain)
    last = last[:, :cases] + last[:, cases:]
    last = last[:cases] + last[cases:]
    gram_ref[...] = jnp.concatenate([cross, start, square, last], axis=1)


def gram_trace(gram_ref, own_ref, match_ref, shift_ref, pen_ref, match_pen_ref, out_ref, jump_ref):
    cases = gram_ref.shape[0]
    apart = (own_ref[...] - match_ref[...]) + shift_ref[...]
    jump = (pen_ref[...] * match_pen_ref[...]) * apart
    jump_ref[...] = jump
    more = dot_nt(stack2(0.5 * apart), stack2(jump))
    more = more[:, :cases] + more[:, cases:]
    more = more[:cases] + more[cases:]
    zeros = jnp.zeros((cases, 3 * cases), F32)
    out_ref[...] = gram_ref[...] + jnp.concatenate([zeros, more], axis=1)


def second_image(
    cols_ref, field_ref, image_ref, mass_ref, stiff_ref, strain_ref, jump_ref, trace_ref, out_ref, *sums
):
    transposed_sums(cols_ref, stiff_ref, strain_ref, sums)
    trace = trace_ref[...]
    one_hot = one_hot_low(trace & (WIDE - 1), trace.shape[1])
    folded = jnp.concatenate(
        [folded_tile(sums, j) for j in range(image_ref.shape[1] // LANES)], axis=1
    )
    image = image_ref[...]
    rows = 2 * image.shape[0]
    second = add_jump(image * mass_ref[...] + folded, jump_ref[...], one_hot, trace >> 8)
    for i, part in enumerate((field_ref[...], image, second)):
        out_ref[i * rows:(i + 1) * rows, :] = stack2(part)
    out_ref[3 * rows:, :] = jnp.zeros((out_ref.shape[0] - 3 * rows, out_ref.shape[1]), BF16)


def eliminate(matrix, size, group=8):
    rows = iota(matrix.shape, 0)
    for first in range(0, size, group):
        columns = [
            jnp.broadcast_to(matrix[:, p:p + 1], matrix.shape) for p in range(first, first + group)
        ]
        for q in range(group):
            p = first + q
            column = columns[q]
            inverse = 1.0 / column[p:p + 1]
            row = matrix[p:p + 1] * inverse
            here = rows == p
            matrix = jnp.where(here, row, matrix - column * row)
            for r in range(q + 1, group):
                entry = column[first + r:first + r + 1] * inverse
                columns[r] = jnp.where(here, entry, columns[r] - column * entry)
    return matrix


def small_dot(a, b):
    return jnp.dot(a, b, precision=lax.Precision.HIGHEST, preferred_element_type=F32)


def finish(*refs):
    *gram_refs, field_ref, rows_ref, solution_ref, residual_ref = refs
    cases = field_ref.shape[0]
    gram = sum_of([ref[...] for ref in gram_refs])
    square = gram[:, 2 * cases:3 * cases]
    solved = eliminate(gram, cases)
    zeros = jnp.zeros((cases, 2 * cases), F32)
    given = jnp.concatenate([gram[:, 3 * cases:], gram[:, :cases]], axis=1)
    both = jnp.concatenate([solved[:, 2 * cases:3 * cases], solved[:, cases:2 * cases]], axis=1)
    second_part = eliminate(
        jnp.concatenate([given - small_dot(square, both), zeros], axis=1), cases
    )[:, cases:2 * cases]
    first_part = both[:, cases:] - small_dot(both[:, :cases], second_part)
    zero = jnp.zeros((cases, cases), F32)
    blocks = [[first_part, zero], [second_part, -first_part], [zero, -second_part], [zero, zero]]
    weights = [jnp.concatenate(block + [zero, zero], axis=1) for block in blocks]
    weights = jnp.concatenate([weights[i // 2] for i in range(8)], axis=0)
    weights = jnp.concatenate([weights[:LANES].T, weights[LANES:].T], axis=1)[:2 * cases]
    out = dot_nn(stack2(weights), rows_ref[...])
    out = out[:2 * cases] + out[2 * cases:]
    solution_ref[...] = out[:cases]
    residual_ref[...] = field_ref[...] + out[cases:]


def sum_of(terms):
    while len(terms) > 1:
        terms = [sum(terms[i:i + 2][1:], terms[i]) for i in range(0, len(terms), 2)]
    return terms[0]


def from_all(array, axis, stride=1, radix=None):
    count = lax.axis_size(axis)
    radix = radix or count
    span = stride * radix

    def target(i, by):
        digit = i // stride % radix
        return i // span * span + (digit + by) % radix * stride + i % stride

    return [array] + [
        lax.ppermute(array, axis, [(i, target(i, by)) for i in range(count)])
        for by in range(1, radix)
    ]


def digits(count):
    stages, stride = [], 1
    while stride < count:
        left = count // stride
        radix = 2 if stride == 1 and left % 2 == 0 else 4 if left % 4 == 0 else left
        stages.append((stride, radix))
        stride *= radix
    return stages


def run(body, outs, args, scratch=(), scalars=0, cost=None, far=0):
    whole = pl.BlockSpec(memory_space=pltpu.VMEM)
    args = [
        pltpu.with_memory_space_constraint(arg, pltpu.HBM) if scalars <= i < scalars + far else arg
        for i, arg in enumerate(args)
    ]
    return pl.pallas_call(
        body,
        out_shape=outs,
        in_specs=[pl.BlockSpec(memory_space=pltpu.SMEM)] * scalars
        + [pl.BlockSpec(memory_space=pltpu.HBM)] * far
        + [whole] * (len(args) - scalars - far),
        out_specs=jax.tree.map(lambda _: whole, outs),
        scratch_shapes=list(scratch),
        compiler_params=pltpu.CompilerParams(vmem_limit_bytes=VMEM_BYTES),
        cost_estimate=cost,
    )(*args)


def shards(
    load_cases,
    mass_diag,
    stiffness,
    block_cols,
    trace_dofs,
    penalty,
    cell_partials,
    cell_owner,
    cell_dof,
):
    cases, dofs = load_cases.shape
    count, blk, width = stiffness.shape
    cells = cell_partials.shape[1]
    slots = trace_dofs.shape[0]
    patches = lax.axis_size("patch")
    cap = 4 * cells // patches
    rows = cases + 8
    far_rows = cases + -(-(1 + 2 * (slots // cap)) // 8) * 8
    shape = jax.ShapeDtypeStruct
    field_shape = shape((cases, dofs), F32)
    slot_shape = shape((cases, slots), F32)
    mass = mass_diag.reshape(1, dofs)
    trace = trace_dofs.reshape(1, slots)
    pen = penalty.reshape(1, slots)
    cols = block_cols.T

    half = patches // 2
    split_shape = shape((count, 2 * blk, width), BF16)
    wide = [pltpu.VMEM(stiffness.shape, F32), pltpu.SemaphoreType.DMA]
    pairs = [(i, (i + half) % patches) for i in range(patches)]
    *packets, stiff = run(
        pack_cells,
        [
            *[shape((far_rows if by == half else rows, cap), F32) for by in range(patches)],
            split_shape,
        ],
        (cell_partials, cell_owner.reshape(1, cells), cell_dof.reshape(1, cells), pen, trace, stiffness),
        scratch=[
            pltpu.VMEM((cases, cells), F32),
            pltpu.VMEM((1, cells), jnp.int32),
            pltpu.VMEM((1, cells), jnp.int32),
            pltpu.VMEM((1, slots), F32),
            pltpu.VMEM((1, slots), jnp.int32),
            pltpu.SemaphoreType.DMA((5,)),
            *wide,
        ],
        far=6,
    )
    received = [packets[0]] + [
        lax.ppermute(packets[by], "patch", [(i, (i + by) % patches) for i in range(patches)])
        for by in range(1, patches)
    ]
    stiff = run(
        split_rest,
        split_shape,
        (stiffness, stiff),
        scratch=wide,
        cost=pl.CostEstimate(flops=4 * stiffness.size, bytes_accessed=8 * stiffness.size, transcendentals=0),
        far=1,
    )
    received, stiff, cols, mass, load_cases, trace = lax.optimization_barrier(
        (received, stiff, cols, mass, load_cases, trace)
    )

    spread = [pltpu.VMEM((dofs // blk, 2 * cases, LANES), BF16)] * 2
    strain_scratch = pltpu.VMEM((count, 2 * cases, LANES), BF16)
    sums = [pltpu.VMEM((dofs // blk, cases, LANES), F32)] * 2

    row_shape = shape((1, slots), F32)
    field, own, match_pen, match_trace = run(
        assemble, (field_shape, slot_shape, row_shape, row_shape), (load_cases, trace, *received)
    )
    match = lax.ppermute(own, "patch", pairs)
    part, part_own = run(
        operator_body,
        (field_shape, slot_shape),
        (cols, field, mass, trace, stiff),
        scratch=[*spread, strain_scratch, *sums],
        scalars=1,
    )
    part_match = lax.ppermute(part_own, "patch", pairs)
    same = run(coincidence, shape((slots, slots), BF16), (trace, match_trace))
    image, shift, gram, strain = run(
        first_image,
        (
            field_shape,
            slot_shape,
            shape((cases, 4 * cases), F32),
            shape((count, 2 * cases, LANES), BF16),
        ),
        (cols, field, part, own, match, pen, match_pen, trace, mass, same, stiff),
        scratch=spread,
        scalars=1,
    )
    gram, jump = run(
        gram_trace,
        (shape((cases, 4 * cases), F32), slot_shape),
        (gram, part_own, part_match, shift, pen, match_pen),
    )
    gram = sum_of(from_all(gram, "comp"))
    *early, last = digits(patches)
    for stride, radix in early:
        gram = sum_of(from_all(gram, "patch", stride, radix))
    grams = from_all(gram, "patch", *last)
    stacked = run(
        second_image,
        shape((-(-6 * cases // LANES) * LANES, dofs), BF16),
        (cols, field, image, mass, stiff, strain, jump, trace),
        scratch=sums,
        scalars=1,
    )
    return run(finish, (field_shape, field_shape), (*grams, field, stacked))


def solution(mesh):
    return jax.shard_map(
        shards,
        mesh=mesh,
        in_specs=(
            P(None, ("comp", "patch")),
            P(("comp", "patch")),
            P(("comp", "patch"), None, None),
            P(("comp", "patch"), None),
            P(("comp", "patch")),
            P(("comp", "patch")),
            P(None, ("comp", "patch")),
            P(("comp", "patch"), None),
            P(("comp", "patch")),
        ),
        out_specs=(P(None, ("comp", "patch")), P(None, ("comp", "patch"))),
        check_vma=False,
    )
```

```python
import jax
import jax.numpy as jnp
from jax import lax
from jax.experimental import pallas as pl
from jax.experimental.pallas import tpu as pltpu
from jax.sharding import PartitionSpec as P

F32 = jnp.float32
BF16 = jnp.bfloat16
WIDE = 256
LANES = 128
VMEM_BYTES = 32 * 1024 * 1024


def split2(x):
    high = x.astype(BF16)
    low = (x - high.astype(F32)).astype(BF16)
    return high, low


def stack2(x):
    return jnp.concatenate(split2(x), axis=0)


def dot_nn(a, b):
    return lax.dot_general(a, b, (((1,), (0,)), ((), ())), preferred_element_type=F32)


def dot_nt(a, b):
    return lax.dot_general(a, b, (((1,), (1,)), ((), ())), preferred_element_type=F32)


def iota(shape, axis):
    return lax.broadcasted_iota(jnp.int32, shape, axis)


def one_hot_low(low, width):
    return (iota((WIDE, width), 0) == low).astype(F32).astype(BF16)


def masked_groups(stacked, group, count):
    parts = []
    for g in range(count):
        mask = (group == g).astype(F32).astype(BF16)
        parts.append(stacked * jnp.broadcast_to(mask, stacked.shape))
    return jnp.concatenate(parts, axis=0)


def gather_slots(field, one_hot, group, groups):
    cases = field.shape[0]
    rows = jnp.concatenate(
        [stack2(field[:, g * WIDE:(g + 1) * WIDE]) for g in range(groups)], axis=0
    )
    found = dot_nn(rows, one_hot)
    total = jnp.zeros((cases, group.shape[1]), F32)
    for g in range(groups):
        base = g * 2 * cases
        both = found[base:base + cases] + found[base + cases:base + 2 * cases]
        total = jnp.where(group == g, both, total)
    return total


def fetch(sources, targets, sems):
    copies = [
        pltpu.make_async_copy(source, target, sems.at[i])
        for i, (source, target) in enumerate(zip(sources, targets))
    ]
    for copy in copies:
        copy.start()
    for copy in copies:
        copy.wait()


def pack_cells(*refs):
    sources, out_refs, targets, sems = refs[:5], refs[5:-6], refs[-6:-1], refs[-1]
    fetch(sources, targets, sems)
    partials_ref, owner_ref, dof_ref, pen_ref, trace_ref = targets
    patches = len(out_refs)
    rows, cap = out_refs[0].shape
    cases, cells = partials_ref.shape
    me = lax.axis_index("patch")
    shift = owner_ref[...] - me
    shift = jnp.where(shift < 0, shift + patches, shift)
    mine = (iota((patches, cells), 0) == shift).astype(F32)
    before = (iota((cells, cells), 0) < iota((cells, cells), 1)).astype(F32).astype(BF16)
    counts = dot_nn(mine.astype(BF16), before)
    rank = jnp.sum(mine * counts, axis=0, keepdims=True).astype(jnp.int32)
    extra = jnp.where(iota((rows - cases, cells), 0) == 0, dof_ref[...] + 1, 0).astype(F32)
    body = stack2(jnp.concatenate([partials_ref[...], extra], axis=0))
    for by, out_ref in enumerate(out_refs):
        key = jnp.where(shift == by, rank, -1)
        pick = (iota((cap, cells), 0) == key).astype(F32).astype(BF16)
        packed = dot_nt(body, pick)
        out_ref[:rows, :] = packed[:rows] + packed[rows:]
        if by == patches // 2:
            more = pen_ref.shape[1] // cap
            for i in range(more):
                at = cases + 1 + i
                out_ref[at:at + 1, :] = pen_ref[:, i * cap:(i + 1) * cap]
                out_ref[at + more:at + more + 1, :] = trace_ref[:, i * cap:(i + 1) * cap].astype(F32)


def split_stiffness(stiff_ref, out_ref):
    blk = stiff_ref.shape[1]
    high, low = split2(stiff_ref[...])
    out_ref[:, :blk, :] = high
    out_ref[:, blk:, :] = low


def assemble(load_ref, trace_ref, *refs):
    *recv_refs, field_ref, own_ref, pen_ref, match_trace_ref = refs
    patches = len(recv_refs)
    cases, dofs = load_ref.shape
    groups = dofs // WIDE
    rows, cap = recv_refs[0].shape
    cells = jnp.concatenate([ref[:rows, :] for ref in recv_refs], axis=1)
    far_ref = recv_refs[patches // 2]
    more = pen_ref.shape[1] // cap
    for i in range(more):
        at = cases + 1 + i
        pen_ref[:, i * cap:(i + 1) * cap] = far_ref[at:at + 1, :]
        match_trace_ref[:, i * cap:(i + 1) * cap] = far_ref[at + more:at + more + 1, :]
    slots = cells.shape[1]
    dof = cells[cases:cases + 1].astype(jnp.int32) - 1
    rows = masked_groups(stack2(cells[:cases]), dof >> 8, groups)
    sums = dot_nt(rows, one_hot_low(jnp.where(dof < 0, -1, dof & (WIDE - 1)), slots))
    pieces = []
    for g in range(groups):
        base = g * 2 * cases
        pieces.append(
            load_ref[:, g * WIDE:(g + 1) * WIDE]
            + (sums[base:base + cases] + sums[base + cases:base + 2 * cases])
        )
    field = jnp.concatenate(pieces, axis=1)
    field_ref[...] = field
    trace = trace_ref[...]
    own_ref[...] = gather_slots(
        field, one_hot_low(trace & (WIDE - 1), trace.shape[1]), trace >> 8, groups
    )


def spread_blocks(field_ref, low_ref, high_ref):
    cases, dofs = field_ref.shape
    in_low = iota((cases, LANES), 1) < LANES // 2
    for j in range(dofs // LANES):
        tile = field_ref[:, j * LANES:(j + 1) * LANES]
        turned = pltpu.roll(tile, LANES // 2, 1)
        low_ref[2 * j] = stack2(jnp.where(in_low, tile, 0.0))
        high_ref[2 * j + 1] = stack2(jnp.where(in_low, 0.0, tile))
        low_ref[2 * j + 1] = stack2(jnp.where(in_low, turned, 0.0))
        high_ref[2 * j] = stack2(jnp.where(in_low, 0.0, turned))


def strain_rows(cols_ref, stiff_ref, low_ref, high_ref, strain_ref, flat_ref=None):
    count = stiff_ref.shape[0]
    cases = strain_ref.shape[1] // 2
    for n in range(count):
        c = [cols_ref[k, n] for k in range(4)]
        near = jnp.concatenate(
            [low_ref[c[0]] + high_ref[c[1]], low_ref[c[2]] + high_ref[c[3]]], axis=1
        )
        both = dot_nt(near, stiff_ref[n])
        both = both[:cases] + both[cases:]
        rows = stack2(both + pltpu.roll(both, LANES // 2, 1))
        strain_ref[n] = rows
        if flat_ref is not None:
            half = LANES // 2
            flat_ref[:, n * half:(n + 1) * half] = rows[:, n % 2 * half:(n % 2 + 1) * half]


def transposed_sums(cols_ref, stiff_ref, strain_ref, sums):
    count = stiff_ref.shape[0]
    cases = strain_ref.shape[1] // 2
    for ref in sums:
        ref[...] = jnp.zeros_like(ref)
    for n in range(count):
        c = [cols_ref[k, n] for k in range(4)]
        both = dot_nn(strain_ref[n], stiff_ref[n])
        both = both[:cases] + both[cases:]
        left, right = both[:, :LANES], both[:, LANES:]
        sums[0][c[0]] += left
        sums[1][c[1]] += left
        sums[0][c[2]] += right
        sums[1][c[3]] += right


def folded_tile(sums, j):
    cases = sums[0].shape[1]
    in_low = iota((cases, LANES), 1) < LANES // 2
    even, odd = 2 * j, 2 * j + 1
    straight = jnp.where(in_low, sums[0][even], sums[1][odd])
    crossed = jnp.where(in_low, sums[0][odd], sums[1][even])
    return straight + pltpu.roll(crossed, LANES // 2, 1)


def operator_body(
    cols_ref, field_ref, mass_ref, trace_ref, stiff_ref, out_ref, own_ref, low_ref, high_ref, strain_ref, *sums
):
    spread_blocks(field_ref, low_ref, high_ref)
    strain_rows(cols_ref, stiff_ref, low_ref, high_ref, strain_ref)
    transposed_sums(cols_ref, stiff_ref, strain_ref, sums)
    dofs = field_ref.shape[1]
    for j in range(dofs // LANES):
        at = slice(j * LANES, (j + 1) * LANES)
        out_ref[:, at] = field_ref[:, at] * mass_ref[:, at] + folded_tile(sums, j)
    trace = trace_ref[...]
    own_ref[...] = gather_slots(
        out_ref[...], one_hot_low(trace & (WIDE - 1), trace.shape[1]), trace >> 8, dofs // WIDE
    )


def fold2(product):
    rows, columns = product.shape[0] // 2, product.shape[1] // 2
    product = product[:rows] + product[rows:]
    return product[:, :columns] + product[:, columns:]


def coincidence(trace_ref, match_trace_ref, field_ref, out_ref, start_ref):
    split = stack2(field_ref[...])
    start_ref[...] = fold2(dot_nt(split, split))
    slots = trace_ref.shape[1]
    rows = [trace_ref[...].astype(F32), match_trace_ref[...]]
    for i in range(slots // LANES):
        at = slice(i * LANES, (i + 1) * LANES)
        total = jnp.zeros((LANES, slots), F32)
        for row in rows:
            column = jnp.broadcast_to(row[:, at], (LANES, LANES)).T
            total += (jnp.broadcast_to(column[:, :1], (LANES, slots)) == row).astype(F32)
        out_ref[at, :] = total.astype(BF16)


def add_jump(base, jump, one_hot, group):
    cases, dofs = base.shape
    groups = dofs // WIDE
    sums = dot_nt(masked_groups(stack2(jump), group, groups), one_hot)
    pieces = []
    for g in range(groups):
        row = g * 2 * cases
        pieces.append(
            base[:, g * WIDE:(g + 1) * WIDE]
            + (sums[row:row + cases] + sums[row + cases:row + 2 * cases])
        )
    return jnp.concatenate(pieces, axis=1)


def first_image(
    cols_ref, field_ref, part_ref, own_ref, match_ref, pen_ref, match_pen_ref, trace_ref, mass_ref, same_ref, start_ref,
    stiff_ref, image_ref, shift_ref, gram_ref, strain_ref, low_ref, high_ref, flat_ref,
):
    cases, dofs = field_ref.shape
    trace = trace_ref[...]
    weight = pen_ref[...] * match_pen_ref[...]
    jump = weight * (own_ref[...] - match_ref[...])
    image_ref[...] = add_jump(
        part_ref[...], jump, one_hot_low(trace & (WIDE - 1), trace.shape[1]), trace >> 8
    )
    moved = dot_nn(stack2(jump), same_ref[...])
    shift_ref[...] = moved[:cases] + moved[cases:]
    spread_blocks(image_ref, low_ref, high_ref)
    strain_rows(cols_ref, stiff_ref, low_ref, high_ref, strain_ref, flat_ref)
    image = image_ref[...]
    image_rows = stack2(image)
    against = jnp.concatenate([stack2(field_ref[...]), image_rows, stack2(image * mass_ref[...])], axis=0)
    every = dot_nt(image_rows, against)
    cross, square, last = (fold2(every[:, i * 2 * cases:(i + 1) * 2 * cases]) for i in range(3))
    last = last + fold2(dot_nt(flat_ref[...], flat_ref[...]))
    gram_ref[...] = jnp.concatenate([cross, start_ref[...], square, last], axis=1)


def gram_trace(gram_ref, own_ref, match_ref, shift_ref, pen_ref, match_pen_ref, out_ref, jump_ref):
    cases = gram_ref.shape[0]
    apart = (own_ref[...] - match_ref[...]) + shift_ref[...]
    jump = (pen_ref[...] * match_pen_ref[...]) * apart
    jump_ref[...] = jump
    more = fold2(dot_nt(stack2(0.5 * apart), stack2(jump)))
    zeros = jnp.zeros((cases, 3 * cases), F32)
    out_ref[...] = gram_ref[...] + jnp.concatenate([zeros, more], axis=1)


def second_image(
    cols_ref, field_ref, image_ref, mass_ref, stiff_ref, strain_ref, jump_ref, trace_ref, out_ref, *sums
):
    transposed_sums(cols_ref, stiff_ref, strain_ref, sums)
    trace = trace_ref[...]
    one_hot = one_hot_low(trace & (WIDE - 1), trace.shape[1])
    folded = jnp.concatenate(
        [folded_tile(sums, j) for j in range(image_ref.shape[1] // LANES)], axis=1
    )
    image = image_ref[...]
    rows = 2 * image.shape[0]
    second = add_jump(image * mass_ref[...] + folded, jump_ref[...], one_hot, trace >> 8)
    for i, part in enumerate((field_ref[...], image, second)):
        out_ref[i * rows:(i + 1) * rows, :] = stack2(part)
    out_ref[3 * rows:, :] = jnp.zeros((out_ref.shape[0] - 3 * rows, out_ref.shape[1]), BF16)


def eliminate(matrix, size, group=8):
    rows = iota(matrix.shape, 0)
    for first in range(0, size, group):
        columns = [
            jnp.broadcast_to(matrix[:, p:p + 1], matrix.shape) for p in range(first, first + group)
        ]
        for q in range(group):
            p = first + q
            column = columns[q]
            inverse = 1.0 / column[p:p + 1]
            row = matrix[p:p + 1] * inverse
            here = rows == p
            matrix = jnp.where(here, row, matrix - column * row)
            for r in range(q + 1, group):
                entry = column[first + r:first + r + 1] * inverse
                columns[r] = jnp.where(here, entry, columns[r] - column * entry)
    return matrix


def small_dot(a, b):
    return jnp.dot(a, b, precision=lax.Precision.HIGHEST, preferred_element_type=F32)


def finish(*refs):
    *gram_refs, field_ref, rows_ref, solution_ref, residual_ref, held_ref, sems = refs
    cases = field_ref.shape[0]
    gram = sum_of([ref[...] for ref in gram_refs])
    square = gram[:, 2 * cases:3 * cases]
    solved = eliminate(gram, cases)
    zeros = jnp.zeros((cases, 2 * cases), F32)
    given = jnp.concatenate([gram[:, 3 * cases:], gram[:, :cases]], axis=1)
    both = jnp.concatenate([solved[:, 2 * cases:3 * cases], solved[:, cases:2 * cases]], axis=1)
    second_part = eliminate(
        jnp.concatenate([given - small_dot(square, both), zeros], axis=1), cases
    )[:, cases:2 * cases]
    first_part = both[:, cases:] - small_dot(both[:, :cases], second_part)
    zero = jnp.zeros((cases, cases), F32)
    blocks = [[first_part, zero], [second_part, -first_part], [zero, -second_part], [zero, zero]]
    weights = [jnp.concatenate(block + [zero, zero], axis=1) for block in blocks]
    weights = jnp.concatenate([weights[i // 2] for i in range(8)], axis=0)
    weights = jnp.concatenate([weights[:LANES].T, weights[LANES:].T], axis=1)[:2 * cases]
    coefs = stack2(weights)
    piece = field_ref.shape[1] // sems.shape[1]
    copies = []
    for i in range(sems.shape[1]):
        at = slice(i * piece, (i + 1) * piece)
        out = dot_nn(coefs, rows_ref[:, at])
        out = out[:2 * cases] + out[2 * cases:]
        held_ref[0, :, at] = out[:cases]
        held_ref[1, :, at] = field_ref[:, at] + out[cases:]
        for j, target in enumerate((solution_ref, residual_ref)):
            copies.append(pltpu.make_async_copy(held_ref.at[j, :, at], target.at[:, at], sems.at[j, i]))
            copies[-1].start()
    for copy in copies:
        copy.wait()


def sum_of(terms):
    while len(terms) > 1:
        terms = [sum(terms[i:i + 2][1:], terms[i]) for i in range(0, len(terms), 2)]
    return terms[0]


def from_all(array, axis, stride=1, radix=None):
    count = lax.axis_size(axis)
    radix = radix or count
    span = stride * radix

    def target(i, by):
        digit = i // stride % radix
        return i // span * span + (digit + by) % radix * stride + i % stride

    return [array] + [
        lax.ppermute(array, axis, [(i, target(i, by)) for i in range(count)])
        for by in range(1, radix)
    ]


def digits(count):
    stages, stride = [], 1
    while stride < count:
        left = count // stride
        radix = 2 if stride == 1 and left % 2 == 0 else 4 if left % 4 == 0 else left
        stages.append((stride, radix))
        stride *= radix
    return stages


def run(body, outs, args, scratch=(), scalars=0, cost=None, far=0, out_space=pltpu.VMEM):
    whole = pl.BlockSpec(memory_space=pltpu.VMEM)
    args = [
        pltpu.with_memory_space_constraint(arg, pltpu.HBM) if scalars <= i < scalars + far else arg
        for i, arg in enumerate(args)
    ]
    return pl.pallas_call(
        body,
        out_shape=outs,
        in_specs=[pl.BlockSpec(memory_space=pltpu.SMEM)] * scalars
        + [pl.BlockSpec(memory_space=pltpu.HBM)] * far
        + [whole] * (len(args) - scalars - far),
        out_specs=jax.tree.map(lambda _: pl.BlockSpec(memory_space=out_space), outs),
        scratch_shapes=list(scratch),
        compiler_params=pltpu.CompilerParams(vmem_limit_bytes=VMEM_BYTES),
        cost_estimate=cost,
    )(*args)


def shards(
    load_cases,
    mass_diag,
    stiffness,
    block_cols,
    trace_dofs,
    penalty,
    cell_partials,
    cell_owner,
    cell_dof,
):
    cases, dofs = load_cases.shape
    count, blk, width = stiffness.shape
    cells = cell_partials.shape[1]
    slots = trace_dofs.shape[0]
    patches = lax.axis_size("patch")
    cap = 4 * cells // patches
    rows = cases + 8
    far_rows = cases + -(-(1 + 2 * (slots // cap)) // 8) * 8
    shape = jax.ShapeDtypeStruct
    field_shape = shape((cases, dofs), F32)
    slot_shape = shape((cases, slots), F32)
    mass = mass_diag.reshape(1, dofs)
    trace = trace_dofs.reshape(1, slots)
    pen = penalty.reshape(1, slots)
    cols = block_cols.T

    half = patches // 2
    pairs = [(i, (i + half) % patches) for i in range(patches)]
    packets = run(
        pack_cells,
        [shape((far_rows if by == half else rows, cap), F32) for by in range(patches)],
        (cell_partials, cell_owner.reshape(1, cells), cell_dof.reshape(1, cells), pen, trace),
        scratch=[
            pltpu.VMEM((cases, cells), F32),
            pltpu.VMEM((1, cells), jnp.int32),
            pltpu.VMEM((1, cells), jnp.int32),
            pltpu.VMEM((1, slots), F32),
            pltpu.VMEM((1, slots), jnp.int32),
            pltpu.SemaphoreType.DMA((5,)),
        ],
        far=5,
    )
    received = [packets[0]] + [
        lax.ppermute(packets[by], "patch", [(i, (i + by) % patches) for i in range(patches)])
        for by in range(1, patches)
    ]
    stiff = run(
        split_stiffness,
        shape((count, 2 * blk, width), BF16),
        (stiffness,),
        cost=pl.CostEstimate(flops=4 * stiffness.size, bytes_accessed=8 * stiffness.size, transcendentals=0),
    )

    received, stiff, cols, mass, load_cases, trace = lax.optimization_barrier(
        (received, stiff, cols, mass, load_cases, trace)
    )

    spread = [pltpu.VMEM((dofs // blk, 2 * cases, LANES), BF16)] * 2
    strain_scratch = pltpu.VMEM((count, 2 * cases, LANES), BF16)
    sums = [pltpu.VMEM((dofs // blk, cases, LANES), F32)] * 2

    row_shape = shape((1, slots), F32)
    field, own, match_pen, match_trace = run(
        assemble, (field_shape, slot_shape, row_shape, row_shape), (load_cases, trace, *received)
    )
    match = lax.ppermute(own, "patch", pairs)
    part, part_own = run(
        operator_body,
        (field_shape, slot_shape),
        (cols, field, mass, trace, stiff),
        scratch=[*spread, strain_scratch, *sums],
        scalars=1,
    )
    part_match = lax.ppermute(part_own, "patch", pairs)
    same, start = run(
        coincidence,
        (shape((slots, slots), BF16), shape((cases, cases), F32)),
        (trace, match_trace, field),
    )
    image, shift, gram, strain = run(
        first_image,
        (
            field_shape,
            slot_shape,
            shape((cases, 4 * cases), F32),
            shape((count, 2 * cases, LANES), BF16),
        ),
        (cols, field, part, own, match, pen, match_pen, trace, mass, same, start, stiff),
        scratch=[*spread, pltpu.VMEM((2 * cases, dofs), BF16)],
        scalars=1,
    )
    gram, jump = run(
        gram_trace,
        (shape((cases, 4 * cases), F32), slot_shape),
        (gram, part_own, part_match, shift, pen, match_pen),
    )
    gram = sum_of(from_all(gram, "comp"))
    *early, last = digits(patches)
    for stride, radix in early:
        gram = sum_of(from_all(gram, "patch", stride, radix))
    grams = from_all(gram, "patch", *last)
    stacked = run(
        second_image,
        shape((-(-6 * cases // LANES) * LANES, dofs), BF16),
        (cols, field, image, mass, stiff, strain, jump, trace),
        scratch=sums,
        scalars=1,
    )
    return run(
        finish,
        (field_shape, field_shape),
        (*grams, field, stacked),
        scratch=[pltpu.VMEM((2, cases, dofs), F32), pltpu.SemaphoreType.DMA((2, 4))],
        out_space=pltpu.HBM,
    )


def solution(mesh):
    return jax.shard_map(
        shards,
        mesh=mesh,
        in_specs=(
            P(None, ("comp", "patch")),
            P(("comp", "patch")),
            P(("comp", "patch"), None, None),
            P(("comp", "patch"), None),
            P(("comp", "patch")),
            P(("comp", "patch")),
            P(None, ("comp", "patch")),
            P(("comp", "patch"), None),
            P(("comp", "patch")),
        ),
        out_specs=(P(None, ("comp", "patch")), P(None, ("comp", "patch"))),
        check_vma=False,
    )
```

```python
import jax
import jax.numpy as jnp
from jax import lax
from jax.experimental import pallas as pl
from jax.experimental.pallas import tpu as pltpu
from jax.sharding import PartitionSpec as P

F32 = jnp.float32
BF16 = jnp.bfloat16
WIDE = 256
LANES = 128
VMEM_BYTES = 32 * 1024 * 1024


def split2(x):
    high = x.astype(BF16)
    low = (x - high.astype(F32)).astype(BF16)
    return high, low


def stack2(x):
    return jnp.concatenate(split2(x), axis=0)


def dot_nn(a, b):
    return lax.dot_general(a, b, (((1,), (0,)), ((), ())), preferred_element_type=F32)


def dot_nt(a, b):
    return lax.dot_general(a, b, (((1,), (1,)), ((), ())), preferred_element_type=F32)


def iota(shape, axis):
    return lax.broadcasted_iota(jnp.int32, shape, axis)


def one_hot_low(low, width):
    return (iota((WIDE, width), 0) == low).astype(F32).astype(BF16)


def masked_groups(stacked, group, count):
    parts = []
    for g in range(count):
        mask = (group == g).astype(F32).astype(BF16)
        parts.append(stacked * jnp.broadcast_to(mask, stacked.shape))
    return jnp.concatenate(parts, axis=0)


def gather_slots(field, one_hot, group, groups):
    cases = field.shape[0]
    rows = jnp.concatenate(
        [stack2(field[:, g * WIDE:(g + 1) * WIDE]) for g in range(groups)], axis=0
    )
    found = dot_nn(rows, one_hot)
    total = jnp.zeros((cases, group.shape[1]), F32)
    for g in range(groups):
        base = g * 2 * cases
        both = found[base:base + cases] + found[base + cases:base + 2 * cases]
        total = jnp.where(group == g, both, total)
    return total


def pack_cells(*refs):
    sources, out_refs, targets, sems = refs[:5], refs[5:-6], refs[-6:-1], refs[-1]
    copies = [
        pltpu.make_async_copy(source, target, sems.at[i])
        for i, (source, target) in enumerate(zip(sources, targets))
    ]
    for copy in copies:
        copy.start()
    partials_ref, owner_ref, dof_ref, pen_ref, trace_ref = targets
    patches = len(out_refs)
    rows, cap = out_refs[0].shape
    cases, cells = partials_ref.shape
    me = lax.axis_index("patch")
    before = (iota((cells, cells), 0) < iota((cells, cells), 1)).astype(F32).astype(BF16)
    for copy in copies[1:]:
        copy.wait()
    shift = owner_ref[...] - me
    shift = jnp.where(shift < 0, shift + patches, shift)
    mine = (iota((patches, cells), 0) == shift).astype(F32)
    counts = dot_nn(mine.astype(BF16), before)
    rank = jnp.sum(mine * counts, axis=0, keepdims=True).astype(jnp.int32)
    extra = jnp.where(iota((rows - cases, cells), 0) == 0, dof_ref[...] + 1, 0).astype(F32)
    copies[0].wait()
    body = stack2(jnp.concatenate([partials_ref[...], extra], axis=0))
    for by, out_ref in enumerate(out_refs):
        key = jnp.where(shift == by, rank, -1)
        pick = (iota((cap, cells), 0) == key).astype(F32).astype(BF16)
        packed = dot_nt(body, pick)
        out_ref[:rows, :] = packed[:rows] + packed[rows:]
        if by == patches // 2:
            more = pen_ref.shape[1] // cap
            for i in range(more):
                at = cases + 1 + i
                out_ref[at:at + 1, :] = pen_ref[:, i * cap:(i + 1) * cap]
                out_ref[at + more:at + more + 1, :] = trace_ref[:, i * cap:(i + 1) * cap].astype(F32)


def add_cells(base, packet_refs):
    cases, dofs = base.shape
    groups = dofs // WIDE
    cells = jnp.concatenate([ref[:cases + 8, :] for ref in packet_refs], axis=1)
    slots = cells.shape[1]
    dof = cells[cases:cases + 1].astype(jnp.int32) - 1
    low = jnp.where(dof < 0, -1, dof & (WIDE - 1))
    return add_rows(base, cells[:cases], one_hot_low(low, slots), dof >> 8)


def early_cells(stiff_ref, load_ref, *refs):
    *packet_refs, field_ref, split_ref, load_copy_ref, wide_ref, sems = refs
    load_copy = pltpu.make_async_copy(load_ref, load_copy_ref, sems.at[0])
    load_copy.start()
    copy = pltpu.make_async_copy(stiff_ref, wide_ref, sems.at[1])
    copy.start()
    load_copy.wait()
    field_ref[...] = add_cells(load_copy_ref[...], packet_refs)
    copy.wait()
    blk = stiff_ref.shape[1]
    high, low = split2(wide_ref[...])
    split_ref[:, :blk, :] = high
    split_ref[:, blk:, :] = low


def assemble(base_ref, trace_ref, far_ref, *refs):
    *packet_refs, field_ref, own_ref, pen_ref, match_trace_ref = refs
    cases, dofs = base_ref.shape
    cap = far_ref.shape[1]
    more = pen_ref.shape[1] // cap
    for i in range(more):
        at = cases + 1 + i
        pen_ref[:, i * cap:(i + 1) * cap] = far_ref[at:at + 1, :]
        match_trace_ref[:, i * cap:(i + 1) * cap] = far_ref[at + more:at + more + 1, :]
    field = add_cells(base_ref[...], packet_refs)
    field_ref[...] = field
    trace = trace_ref[...]
    own_ref[...] = gather_slots(
        field, one_hot_low(trace & (WIDE - 1), trace.shape[1]), trace >> 8, dofs // WIDE
    )


def spread_blocks(field_ref, low_ref, high_ref):
    cases, dofs = field_ref.shape
    in_low = iota((cases, LANES), 1) < LANES // 2
    for j in range(dofs // LANES):
        tile = field_ref[:, j * LANES:(j + 1) * LANES]
        turned = pltpu.roll(tile, LANES // 2, 1)
        low_ref[2 * j] = stack2(jnp.where(in_low, tile, 0.0))
        high_ref[2 * j + 1] = stack2(jnp.where(in_low, 0.0, tile))
        low_ref[2 * j + 1] = stack2(jnp.where(in_low, turned, 0.0))
        high_ref[2 * j] = stack2(jnp.where(in_low, 0.0, turned))


def strain_rows(cols_ref, stiff_ref, low_ref, high_ref, strain_ref):
    count = stiff_ref.shape[0]
    cases = strain_ref.shape[1] // 2
    for n in range(count):
        c = [cols_ref[k, n] for k in range(4)]
        near = jnp.concatenate(
            [low_ref[c[0]] + high_ref[c[1]], low_ref[c[2]] + high_ref[c[3]]], axis=1
        )
        both = dot_nt(near, stiff_ref[n])
        both = both[:cases] + both[cases:]
        strain_ref[n] = stack2(both + pltpu.roll(both, LANES // 2, 1))


def transposed_sums(cols_ref, stiff_ref, strain_ref, sums):
    count = stiff_ref.shape[0]
    cases = strain_ref.shape[1] // 2
    for ref in sums:
        ref[...] = jnp.zeros_like(ref)
    for n in range(count):
        c = [cols_ref[k, n] for k in range(4)]
        both = dot_nn(strain_ref[n], stiff_ref[n])
        both = both[:cases] + both[cases:]
        left, right = both[:, :LANES], both[:, LANES:]
        sums[0][c[0]] += left
        sums[1][c[1]] += left
        sums[0][c[2]] += right
        sums[1][c[3]] += right


def folded_tile(sums, j):
    cases = sums[0].shape[1]
    in_low = iota((cases, LANES), 1) < LANES // 2
    even, odd = 2 * j, 2 * j + 1
    straight = jnp.where(in_low, sums[0][even], sums[1][odd])
    crossed = jnp.where(in_low, sums[0][odd], sums[1][even])
    return straight + pltpu.roll(crossed, LANES // 2, 1)


def operator_body(
    cols_ref, field_ref, mass_ref, trace_ref, stiff_ref, out_ref, own_ref, low_ref, high_ref, strain_ref, *sums
):
    spread_blocks(field_ref, low_ref, high_ref)
    strain_rows(cols_ref, stiff_ref, low_ref, high_ref, strain_ref)
    transposed_sums(cols_ref, stiff_ref, strain_ref, sums)
    dofs = field_ref.shape[1]
    for j in range(dofs // LANES):
        at = slice(j * LANES, (j + 1) * LANES)
        out_ref[:, at] = field_ref[:, at] * mass_ref[:, at] + folded_tile(sums, j)
    trace = trace_ref[...]
    own_ref[...] = gather_slots(
        out_ref[...], one_hot_low(trace & (WIDE - 1), trace.shape[1]), trace >> 8, dofs // WIDE
    )


def coincidence(trace_ref, match_trace_ref, out_ref):
    slots = trace_ref.shape[1]
    rows = [trace_ref[...].astype(F32), match_trace_ref[...]]
    for i in range(slots // LANES):
        at = slice(i * LANES, (i + 1) * LANES)
        total = jnp.zeros((LANES, slots), F32)
        for row in rows:
            column = jnp.broadcast_to(row[:, at], (LANES, LANES)).T
            total += (jnp.broadcast_to(column[:, :1], (LANES, slots)) == row).astype(F32)
        out_ref[at, :] = total.astype(BF16)


def add_rows(base, rows, one_hot, group):
    cases, dofs = base.shape
    groups = dofs // WIDE
    sums = dot_nt(masked_groups(stack2(rows), group, groups), one_hot)
    pieces = []
    for g in range(groups):
        row = g * 2 * cases
        pieces.append(
            base[:, g * WIDE:(g + 1) * WIDE]
            + (sums[row:row + cases] + sums[row + cases:row + 2 * cases])
        )
    return jnp.concatenate(pieces, axis=1)


def first_image(
    cols_ref, field_ref, part_ref, own_ref, match_ref, pen_ref, match_pen_ref, trace_ref, mass_ref, same_ref, stiff_ref,
    image_ref, shift_ref, gram_ref, strain_ref, low_ref, high_ref,
):
    cases, dofs = field_ref.shape
    trace = trace_ref[...]
    weight = pen_ref[...] * match_pen_ref[...]
    jump = weight * (own_ref[...] - match_ref[...])
    image_ref[...] = add_rows(
        part_ref[...], jump, one_hot_low(trace & (WIDE - 1), trace.shape[1]), trace >> 8
    )
    moved = dot_nn(stack2(jump), same_ref[...])
    shift_ref[...] = moved[:cases] + moved[cases:]
    spread_blocks(image_ref, low_ref, high_ref)
    strain_rows(cols_ref, stiff_ref, low_ref, high_ref, strain_ref)
    in_low = iota((2 * cases, LANES), 1) < LANES // 2
    strain = jnp.concatenate(
        [
            jnp.where(in_low, strain_ref[2 * j].astype(F32), strain_ref[2 * j + 1].astype(F32)).astype(BF16)
            for j in range(strain_ref.shape[0] // 2)
        ],
        axis=1,
    )
    image = image_ref[...]
    image_rows = stack2(image)
    rows = jnp.concatenate([stack2(field_ref[...]), image_rows], axis=0)
    every = dot_nt(rows, image_rows)
    every = every[:, :cases] + every[:, cases:]
    cross = every[:cases] + every[cases:2 * cases]
    square = every[2 * cases:3 * cases] + every[3 * cases:]
    start = dot_nt(rows[:2 * cases], rows[:2 * cases])
    start = start[:, :cases] + start[:, cases:]
    start = start[:cases] + start[cases:]
    last = dot_nt(image_rows, stack2(image * mass_ref[...])) + dot_nt(strain, strain)
    last = last[:, :cases] + last[:, cases:]
    last = last[:cases] + last[cases:]
    gram_ref[...] = jnp.concatenate([cross, start, square, last], axis=1)


def gram_trace(gram_ref, own_ref, match_ref, shift_ref, pen_ref, match_pen_ref, out_ref, jump_ref):
    cases = gram_ref.shape[0]
    apart = (own_ref[...] - match_ref[...]) + shift_ref[...]
    jump = (pen_ref[...] * match_pen_ref[...]) * apart
    jump_ref[...] = jump
    more = dot_nt(stack2(0.5 * apart), stack2(jump))
    more = more[:, :cases] + more[:, cases:]
    more = more[:cases] + more[cases:]
    zeros = jnp.zeros((cases, 3 * cases), F32)
    out_ref[...] = gram_ref[...] + jnp.concatenate([zeros, more], axis=1)


def second_image(
    cols_ref, field_ref, image_ref, mass_ref, stiff_ref, strain_ref, jump_ref, trace_ref, out_ref, *sums
):
    transposed_sums(cols_ref, stiff_ref, strain_ref, sums)
    trace = trace_ref[...]
    one_hot = one_hot_low(trace & (WIDE - 1), trace.shape[1])
    folded = jnp.concatenate(
        [folded_tile(sums, j) for j in range(image_ref.shape[1] // LANES)], axis=1
    )
    image = image_ref[...]
    rows = 2 * image.shape[0]
    second = add_rows(image * mass_ref[...] + folded, jump_ref[...], one_hot, trace >> 8)
    for i, part in enumerate((field_ref[...], image, second)):
        out_ref[i * rows:(i + 1) * rows, :] = stack2(part)
    out_ref[3 * rows:, :] = jnp.zeros((out_ref.shape[0] - 3 * rows, out_ref.shape[1]), BF16)


def eliminate(matrix, size, group=8):
    rows = iota(matrix.shape, 0)
    for first in range(0, size, group):
        columns = [
            jnp.broadcast_to(matrix[:, p:p + 1], matrix.shape) for p in range(first, first + group)
        ]
        for q in range(group):
            p = first + q
            column = columns[q]
            inverse = 1.0 / column[p:p + 1]
            row = matrix[p:p + 1] * inverse
            here = rows == p
            matrix = jnp.where(here, row, matrix - column * row)
            for r in range(q + 1, group):
                entry = column[first + r:first + r + 1] * inverse
                columns[r] = jnp.where(here, entry, columns[r] - column * entry)
    return matrix


def small_dot(a, b):
    return jnp.dot(a, b, precision=lax.Precision.HIGHEST, preferred_element_type=F32)


def finish(*refs):
    *gram_refs, field_ref, rows_ref, solution_ref, residual_ref = refs
    cases = field_ref.shape[0]
    gram = sum_of([ref[...] for ref in gram_refs])
    square = gram[:, 2 * cases:3 * cases]
    solved = eliminate(gram, cases)
    zeros = jnp.zeros((cases, 2 * cases), F32)
    given = jnp.concatenate([gram[:, 3 * cases:], gram[:, :cases]], axis=1)
    both = jnp.concatenate([solved[:, 2 * cases:3 * cases], solved[:, cases:2 * cases]], axis=1)
    second_part = eliminate(
        jnp.concatenate([given - small_dot(square, both), zeros], axis=1), cases
    )[:, cases:2 * cases]
    first_part = both[:, cases:] - small_dot(both[:, :cases], second_part)
    zero = jnp.zeros((cases, cases), F32)
    blocks = [[first_part, zero], [second_part, -first_part], [zero, -second_part], [zero, zero]]
    weights = [jnp.concatenate(block + [zero, zero], axis=1) for block in blocks]
    weights = jnp.concatenate([weights[i // 2] for i in range(8)], axis=0)
    weights = jnp.concatenate([weights[:LANES].T, weights[LANES:].T], axis=1)[:2 * cases]
    out = dot_nn(stack2(weights), rows_ref[...])
    out = out[:2 * cases] + out[2 * cases:]
    solution_ref[...] = out[:cases]
    residual_ref[...] = field_ref[...] + out[cases:]


def sum_of(terms):
    while len(terms) > 1:
        terms = [sum(terms[i:i + 2][1:], terms[i]) for i in range(0, len(terms), 2)]
    return terms[0]


def from_all(array, axis, stride=1, radix=None):
    count = lax.axis_size(axis)
    radix = radix or count
    span = stride * radix

    def target(i, by):
        digit = i // stride % radix
        return i // span * span + (digit + by) % radix * stride + i % stride

    return [array] + [
        lax.ppermute(array, axis, [(i, target(i, by)) for i in range(count)])
        for by in range(1, radix)
    ]


def digits(count):
    stages, stride = [], 1
    while stride < count:
        left = count // stride
        radix = 2 if stride == 1 and left % 2 == 0 else 4 if left % 4 == 0 else left
        stages.append((stride, radix))
        stride *= radix
    return stages


def run(body, outs, args, scratch=(), scalars=0, cost=None, far=0):
    whole = pl.BlockSpec(memory_space=pltpu.VMEM)
    args = [
        pltpu.with_memory_space_constraint(arg, pltpu.HBM) if scalars <= i < scalars + far else arg
        for i, arg in enumerate(args)
    ]
    return pl.pallas_call(
        body,
        out_shape=outs,
        in_specs=[pl.BlockSpec(memory_space=pltpu.SMEM)] * scalars
        + [pl.BlockSpec(memory_space=pltpu.HBM)] * far
        + [whole] * (len(args) - scalars - far),
        out_specs=jax.tree.map(lambda _: whole, outs),
        scratch_shapes=list(scratch),
        compiler_params=pltpu.CompilerParams(vmem_limit_bytes=VMEM_BYTES),
        cost_estimate=cost,
    )(*args)


def shards(
    load_cases,
    mass_diag,
    stiffness,
    block_cols,
    trace_dofs,
    penalty,
    cell_partials,
    cell_owner,
    cell_dof,
):
    cases, dofs = load_cases.shape
    count, blk, width = stiffness.shape
    cells = cell_partials.shape[1]
    slots = trace_dofs.shape[0]
    patches = lax.axis_size("patch")
    cap = 4 * cells // patches
    rows = cases + 8
    far_rows = cases + -(-(1 + 2 * (slots // cap)) // 8) * 8
    shape = jax.ShapeDtypeStruct
    field_shape = shape((cases, dofs), F32)
    slot_shape = shape((cases, slots), F32)
    mass = mass_diag.reshape(1, dofs)
    trace = trace_dofs.reshape(1, slots)
    pen = penalty.reshape(1, slots)
    cols = block_cols.T

    half = patches // 2
    pairs = [(i, (i + half) % patches) for i in range(patches)]
    packets = run(
        pack_cells,
        [shape((far_rows if by == half else rows, cap), F32) for by in range(patches)],
        (cell_partials, cell_owner.reshape(1, cells), cell_dof.reshape(1, cells), pen, trace),
        scratch=[
            pltpu.VMEM((cases, cells), F32),
            pltpu.VMEM((1, cells), jnp.int32),
            pltpu.VMEM((1, cells), jnp.int32),
            pltpu.VMEM((1, slots), F32),
            pltpu.VMEM((1, slots), jnp.int32),
            pltpu.SemaphoreType.DMA((5,)),
        ],
        far=5,
    )
    order = [0, 1, 2, half, *(by for by in range(3, patches) if by != half)]
    received = [packets[0]] + [
        lax.ppermute(packets[by], "patch", [(i, (i + by) % patches) for i in range(patches)])
        for by in order[1:]
    ]
    far, first = received[3], 5 * patches // 8
    base, stiff = run(
        early_cells,
        (field_shape, shape((count, 2 * blk, width), BF16)),
        (stiffness, load_cases, *received[:first]),
        scratch=[
            pltpu.VMEM((cases, dofs), F32),
            pltpu.VMEM(stiffness.shape, F32),
            pltpu.SemaphoreType.DMA((2,)),
        ],
        cost=pl.CostEstimate(flops=8 * stiffness.size, bytes_accessed=8 * stiffness.size, transcendentals=0),
        far=2,
    )
    late, base, stiff, cols, mass, trace = lax.optimization_barrier(
        (received[first:], base, stiff, cols, mass, trace)
    )

    spread = [pltpu.VMEM((dofs // blk, 2 * cases, LANES), BF16)] * 2
    strain_scratch = pltpu.VMEM((count, 2 * cases, LANES), BF16)
    sums = [pltpu.VMEM((dofs // blk, cases, LANES), F32)] * 2

    row_shape = shape((1, slots), F32)
    field, own, match_pen, match_trace = run(
        assemble, (field_shape, slot_shape, row_shape, row_shape), (base, trace, far, *late)
    )
    match = lax.ppermute(own, "patch", pairs)
    part, part_own = run(
        operator_body,
        (field_shape, slot_shape),
        (cols, field, mass, trace, stiff),
        scratch=[*spread, strain_scratch, *sums],
        scalars=1,
    )
    part_match = lax.ppermute(part_own, "patch", pairs)
    same = run(coincidence, shape((slots, slots), BF16), (trace, match_trace))
    image, shift, gram, strain = run(
        first_image,
        (
            field_shape,
            slot_shape,
            shape((cases, 4 * cases), F32),
            shape((count, 2 * cases, LANES), BF16),
        ),
        (cols, field, part, own, match, pen, match_pen, trace, mass, same, stiff),
        scratch=spread,
        scalars=1,
    )
    gram, jump = run(
        gram_trace,
        (shape((cases, 4 * cases), F32), slot_shape),
        (gram, part_own, part_match, shift, pen, match_pen),
    )
    gram = sum_of(from_all(gram, "comp"))
    *early, last = digits(patches)
    for stride, radix in early:
        gram = sum_of(from_all(gram, "patch", stride, radix))
    grams = from_all(gram, "patch", *last)
    stacked = run(
        second_image,
        shape((-(-6 * cases // LANES) * LANES, dofs), BF16),
        (cols, field, image, mass, stiff, strain, jump, trace),
        scratch=sums,
        scalars=1,
    )
    return run(finish, (field_shape, field_shape), (*grams, field, stacked))


def solution(mesh):
    return jax.shard_map(
        shards,
        mesh=mesh,
        in_specs=(
            P(None, ("comp", "patch")),
            P(("comp", "patch")),
            P(("comp", "patch"), None, None),
            P(("comp", "patch"), None),
            P(("comp", "patch")),
            P(("comp", "patch")),
            P(None, ("comp", "patch")),
            P(("comp", "patch"), None),
            P(("comp", "patch")),
        ),
        out_specs=(P(None, ("comp", "patch")), P(None, ("comp", "patch"))),
        check_vma=False,
    )
```

```python
import jax
import jax.numpy as jnp
from jax import lax
from jax.experimental import pallas as pl
from jax.experimental.pallas import tpu as pltpu
from jax.sharding import PartitionSpec as P

F32 = jnp.float32
BF16 = jnp.bfloat16
WIDE = 256
LANES = 128
VMEM_BYTES = 32 * 1024 * 1024


def split2(x):
    high = x.astype(BF16)
    low = (x - high.astype(F32)).astype(BF16)
    return high, low


def stack2(x):
    return jnp.concatenate(split2(x), axis=0)


def dot_nn(a, b):
    return lax.dot_general(a, b, (((1,), (0,)), ((), ())), preferred_element_type=F32)


def dot_nt(a, b):
    return lax.dot_general(a, b, (((1,), (1,)), ((), ())), preferred_element_type=F32)


def iota(shape, axis):
    return lax.broadcasted_iota(jnp.int32, shape, axis)


def one_hot_low(low, width):
    return (iota((WIDE, width), 0) == low).astype(F32).astype(BF16)


def masked_groups(stacked, group, count):
    parts = []
    for g in range(count):
        mask = (group == g).astype(F32).astype(BF16)
        parts.append(stacked * jnp.broadcast_to(mask, stacked.shape))
    return jnp.concatenate(parts, axis=0)


def gather_slots(field, one_hot, group, groups):
    cases = field.shape[0]
    rows = jnp.concatenate(
        [stack2(field[:, g * WIDE:(g + 1) * WIDE]) for g in range(groups)], axis=0
    )
    found = dot_nn(rows, one_hot)
    total = jnp.zeros((cases, group.shape[1]), F32)
    for g in range(groups):
        base = g * 2 * cases
        both = found[base:base + cases] + found[base + cases:base + 2 * cases]
        total = jnp.where(group == g, both, total)
    return total


def pack_cells(*refs):
    sources, out_refs, targets, sems = refs[:5], refs[5:-6], refs[-6:-1], refs[-1]
    copies = [
        pltpu.make_async_copy(source, target, sems.at[i])
        for i, (source, target) in enumerate(zip(sources, targets))
    ]
    for copy in copies:
        copy.start()
    partials_ref, owner_ref, dof_ref, pen_ref, trace_ref = targets
    patches = len(out_refs)
    rows, cap = out_refs[0].shape
    cases, cells = partials_ref.shape
    me = lax.axis_index("patch")
    before = (iota((cells, cells), 0) < iota((cells, cells), 1)).astype(F32).astype(BF16)
    for copy in copies[1:]:
        copy.wait()
    shift = owner_ref[...] - me
    shift = jnp.where(shift < 0, shift + patches, shift)
    mine = (iota((patches, cells), 0) == shift).astype(F32)
    counts = dot_nn(mine.astype(BF16), before)
    rank = jnp.sum(mine * counts, axis=0, keepdims=True).astype(jnp.int32)
    extra = jnp.where(iota((rows - cases, cells), 0) == 0, dof_ref[...] + 1, 0).astype(F32)
    copies[0].wait()
    body = stack2(jnp.concatenate([partials_ref[...], extra], axis=0))
    for by, out_ref in enumerate(out_refs):
        key = jnp.where(shift == by, rank, -1)
        pick = (iota((cap, cells), 0) == key).astype(F32).astype(BF16)
        packed = dot_nt(body, pick)
        out_ref[:rows, :] = packed[:rows] + packed[rows:]
        if by == patches // 2:
            more = pen_ref.shape[1] // cap
            for i in range(more):
                at = cases + 1 + i
                out_ref[at:at + 1, :] = pen_ref[:, i * cap:(i + 1) * cap]
                out_ref[at + more:at + more + 1, :] = trace_ref[:, i * cap:(i + 1) * cap].astype(F32)


def add_cells(base, packet_refs):
    cases, dofs = base.shape
    groups = dofs // WIDE
    cells = jnp.concatenate([ref[:cases + 8, :] for ref in packet_refs], axis=1)
    slots = cells.shape[1]
    dof = cells[cases:cases + 1].astype(jnp.int32) - 1
    low = jnp.where(dof < 0, -1, dof & (WIDE - 1))
    return add_rows(base, cells[:cases], one_hot_low(low, slots), dof >> 8)


def early_cells(stiff_ref, load_ref, *refs):
    *packet_refs, field_ref, split_ref, load_copy_ref, wide_ref, sems = refs
    load_copy = pltpu.make_async_copy(load_ref, load_copy_ref, sems.at[0])
    load_copy.start()
    copy = pltpu.make_async_copy(stiff_ref, wide_ref, sems.at[1])
    copy.start()
    load_copy.wait()
    field_ref[...] = add_cells(load_copy_ref[...], packet_refs)
    copy.wait()
    blk = stiff_ref.shape[1]
    high, low = split2(wide_ref[...])
    split_ref[:, :blk, :] = high
    split_ref[:, blk:, :] = low


def assemble(base_ref, trace_ref, far_ref, *refs):
    *packet_refs, field_ref, own_ref, pen_ref, match_trace_ref = refs
    cases, dofs = base_ref.shape
    cap = far_ref.shape[1]
    more = pen_ref.shape[1] // cap
    for i in range(more):
        at = cases + 1 + i
        pen_ref[:, i * cap:(i + 1) * cap] = far_ref[at:at + 1, :]
        match_trace_ref[:, i * cap:(i + 1) * cap] = far_ref[at + more:at + more + 1, :]
    field = add_cells(base_ref[...], packet_refs)
    field_ref[...] = field
    trace = trace_ref[...]
    own_ref[...] = gather_slots(
        field, one_hot_low(trace & (WIDE - 1), trace.shape[1]), trace >> 8, dofs // WIDE
    )


def spread_blocks(field_ref, low_ref, high_ref):
    cases, dofs = field_ref.shape
    in_low = iota((cases, LANES), 1) < LANES // 2
    for j in range(dofs // LANES):
        tile = field_ref[:, j * LANES:(j + 1) * LANES]
        turned = pltpu.roll(tile, LANES // 2, 1)
        low_ref[2 * j] = stack2(jnp.where(in_low, tile, 0.0))
        high_ref[2 * j + 1] = stack2(jnp.where(in_low, 0.0, tile))
        low_ref[2 * j + 1] = stack2(jnp.where(in_low, turned, 0.0))
        high_ref[2 * j] = stack2(jnp.where(in_low, 0.0, turned))


def strain_rows(cols_ref, stiff_ref, low_ref, high_ref, strain_ref):
    count = stiff_ref.shape[0]
    cases = strain_ref.shape[1] // 2
    for n in range(count):
        c = [cols_ref[k, n] for k in range(4)]
        near = jnp.concatenate(
            [low_ref[c[0]] + high_ref[c[1]], low_ref[c[2]] + high_ref[c[3]]], axis=1
        )
        both = dot_nt(near, stiff_ref[n])
        both = both[:cases] + both[cases:]
        strain_ref[n] = stack2(both + pltpu.roll(both, LANES // 2, 1))


def transposed_sums(cols_ref, stiff_ref, strain_ref, sums):
    count = stiff_ref.shape[0]
    cases = strain_ref.shape[1] // 2
    for ref in sums:
        ref[...] = jnp.zeros_like(ref)
    for n in range(count):
        c = [cols_ref[k, n] for k in range(4)]
        both = dot_nn(strain_ref[n], stiff_ref[n])
        both = both[:cases] + both[cases:]
        left, right = both[:, :LANES], both[:, LANES:]
        sums[0][c[0]] += left
        sums[1][c[1]] += left
        sums[0][c[2]] += right
        sums[1][c[3]] += right


def folded_tile(sums, j):
    cases = sums[0].shape[1]
    in_low = iota((cases, LANES), 1) < LANES // 2
    even, odd = 2 * j, 2 * j + 1
    straight = jnp.where(in_low, sums[0][even], sums[1][odd])
    crossed = jnp.where(in_low, sums[0][odd], sums[1][even])
    return straight + pltpu.roll(crossed, LANES // 2, 1)


def operator_body(
    cols_ref, field_ref, mass_ref, trace_ref, stiff_ref, out_ref, own_ref, low_ref, high_ref, strain_ref, *sums
):
    spread_blocks(field_ref, low_ref, high_ref)
    strain_rows(cols_ref, stiff_ref, low_ref, high_ref, strain_ref)
    transposed_sums(cols_ref, stiff_ref, strain_ref, sums)
    dofs = field_ref.shape[1]
    for j in range(dofs // LANES):
        at = slice(j * LANES, (j + 1) * LANES)
        out_ref[:, at] = field_ref[:, at] * mass_ref[:, at] + folded_tile(sums, j)
    trace = trace_ref[...]
    own_ref[...] = gather_slots(
        out_ref[...], one_hot_low(trace & (WIDE - 1), trace.shape[1]), trace >> 8, dofs // WIDE
    )


def coincidence(trace_ref, match_trace_ref, out_ref):
    slots = trace_ref.shape[1]
    rows = [trace_ref[...].astype(F32), match_trace_ref[...]]
    for i in range(slots // LANES):
        at = slice(i * LANES, (i + 1) * LANES)
        total = jnp.zeros((LANES, slots), F32)
        for row in rows:
            column = jnp.broadcast_to(row[:, at], (LANES, LANES)).T
            total += (jnp.broadcast_to(column[:, :1], (LANES, slots)) == row).astype(F32)
        out_ref[at, :] = total.astype(BF16)


def add_rows(base, rows, one_hot, group):
    cases, dofs = base.shape
    groups = dofs // WIDE
    sums = dot_nt(masked_groups(stack2(rows), group, groups), one_hot)
    pieces = []
    for g in range(groups):
        row = g * 2 * cases
        pieces.append(
            base[:, g * WIDE:(g + 1) * WIDE]
            + (sums[row:row + cases] + sums[row + cases:row + 2 * cases])
        )
    return jnp.concatenate(pieces, axis=1)


def first_image(
    cols_ref, field_ref, part_ref, own_ref, match_ref, pen_ref, match_pen_ref, trace_ref, mass_ref, same_ref, stiff_ref,
    image_ref, shift_ref, gram_ref, strain_ref, low_ref, high_ref,
):
    cases, dofs = field_ref.shape
    trace = trace_ref[...]
    weight = pen_ref[...] * match_pen_ref[...]
    jump = weight * (own_ref[...] - match_ref[...])
    image_ref[...] = add_rows(
        part_ref[...], jump, one_hot_low(trace & (WIDE - 1), trace.shape[1]), trace >> 8
    )
    moved = dot_nn(stack2(jump), same_ref[...])
    shift_ref[...] = moved[:cases] + moved[cases:]
    spread_blocks(image_ref, low_ref, high_ref)
    strain_rows(cols_ref, stiff_ref, low_ref, high_ref, strain_ref)
    in_low = iota((2 * cases, LANES), 1) < LANES // 2
    strain = jnp.concatenate(
        [
            jnp.where(in_low, strain_ref[2 * j].astype(F32), strain_ref[2 * j + 1].astype(F32)).astype(BF16)
            for j in range(strain_ref.shape[0] // 2)
        ],
        axis=1,
    )
    image = image_ref[...]
    image_rows = stack2(image)
    rows = jnp.concatenate([stack2(field_ref[...]), image_rows], axis=0)
    every = dot_nt(rows, image_rows)
    every = every[:, :cases] + every[:, cases:]
    cross = every[:cases] + every[cases:2 * cases]
    square = every[2 * cases:3 * cases] + every[3 * cases:]
    start = dot_nt(rows[:2 * cases], rows[:2 * cases])
    start = start[:, :cases] + start[:, cases:]
    start = start[:cases] + start[cases:]
    last = dot_nt(image_rows, stack2(image * mass_ref[...])) + dot_nt(strain, strain)
    last = last[:, :cases] + last[:, cases:]
    last = last[:cases] + last[cases:]
    gram_ref[...] = jnp.concatenate([cross, start, square, last], axis=1)


def gram_trace(gram_ref, own_ref, match_ref, shift_ref, pen_ref, match_pen_ref, out_ref, jump_ref):
    cases = gram_ref.shape[0]
    apart = (own_ref[...] - match_ref[...]) + shift_ref[...]
    jump = (pen_ref[...] * match_pen_ref[...]) * apart
    jump_ref[...] = jump
    more = dot_nt(stack2(0.5 * apart), stack2(jump))
    more = more[:, :cases] + more[:, cases:]
    more = more[:cases] + more[cases:]
    zeros = jnp.zeros((cases, 3 * cases), F32)
    out_ref[...] = gram_ref[...] + jnp.concatenate([zeros, more], axis=1)


def second_image(
    cols_ref, field_ref, image_ref, mass_ref, stiff_ref, strain_ref, jump_ref, trace_ref, out_ref, *sums
):
    transposed_sums(cols_ref, stiff_ref, strain_ref, sums)
    trace = trace_ref[...]
    one_hot = one_hot_low(trace & (WIDE - 1), trace.shape[1])
    folded = jnp.concatenate(
        [folded_tile(sums, j) for j in range(image_ref.shape[1] // LANES)], axis=1
    )
    image = image_ref[...]
    rows = 2 * image.shape[0]
    second = add_rows(image * mass_ref[...] + folded, jump_ref[...], one_hot, trace >> 8)
    for i, part in enumerate((field_ref[...], image, second)):
        out_ref[i * rows:(i + 1) * rows, :] = stack2(part)
    out_ref[3 * rows:, :] = jnp.zeros((out_ref.shape[0] - 3 * rows, out_ref.shape[1]), BF16)


def eliminate(matrix, size, group=8):
    rows = iota(matrix.shape, 0)
    for first in range(0, size, group):
        columns = [
            jnp.broadcast_to(matrix[:, p:p + 1], matrix.shape) for p in range(first, first + group)
        ]
        for q in range(group):
            p = first + q
            column = columns[q]
            inverse = 1.0 / column[p:p + 1]
            row = matrix[p:p + 1] * inverse
            here = rows == p
            matrix = jnp.where(here, row, matrix - column * row)
            for r in range(q + 1, group):
                entry = column[first + r:first + r + 1] * inverse
                columns[r] = jnp.where(here, entry, columns[r] - column * entry)
    return matrix


def small_dot(a, b):
    return jnp.dot(a, b, precision=lax.Precision.HIGHEST, preferred_element_type=F32)


def finish(*refs):
    *gram_refs, field_ref, rows_ref, solution_ref, residual_ref = refs
    cases = field_ref.shape[0]
    gram = sum_of([ref[...] for ref in gram_refs])
    square = gram[:, 2 * cases:3 * cases]
    solved = eliminate(gram, cases)
    zeros = jnp.zeros((cases, 2 * cases), F32)
    given = jnp.concatenate([gram[:, 3 * cases:], gram[:, :cases]], axis=1)
    both = jnp.concatenate([solved[:, 2 * cases:3 * cases], solved[:, cases:2 * cases]], axis=1)
    second_part = eliminate(
        jnp.concatenate([given - small_dot(square, both), zeros], axis=1), cases
    )[:, cases:2 * cases]
    first_part = both[:, cases:] - small_dot(both[:, :cases], second_part)
    zero = jnp.zeros((cases, cases), F32)
    blocks = [[first_part, zero], [second_part, -first_part], [zero, -second_part], [zero, zero]]
    weights = [jnp.concatenate(block + [zero, zero], axis=1) for block in blocks]
    weights = jnp.concatenate([weights[i // 2] for i in range(8)], axis=0)
    weights = jnp.concatenate([weights[:LANES].T, weights[LANES:].T], axis=1)[:2 * cases]
    out = dot_nn(stack2(weights), rows_ref[...])
    out = out[:2 * cases] + out[2 * cases:]
    solution_ref[...] = out[:cases]
    residual_ref[...] = field_ref[...] + out[cases:]


def sum_of(terms):
    while len(terms) > 1:
        terms = [sum(terms[i:i + 2][1:], terms[i]) for i in range(0, len(terms), 2)]
    return terms[0]


def from_all(array, axis, stride=1, radix=None):
    count = lax.axis_size(axis)
    radix = radix or count
    span = stride * radix

    def target(i, by):
        digit = i // stride % radix
        return i // span * span + (digit + by) % radix * stride + i % stride

    return [array] + [
        lax.ppermute(array, axis, [(i, target(i, by)) for i in range(count)])
        for by in range(1, radix)
    ]


def digits(count):
    stages, stride = [], 1
    while stride < count:
        left = count // stride
        radix = 2 if stride == 1 and left % 2 == 0 else 4 if left % 4 == 0 else left
        stages.append((stride, radix))
        stride *= radix
    return stages


def run(body, outs, args, scratch=(), scalars=0, cost=None, far=0):
    whole = pl.BlockSpec(memory_space=pltpu.VMEM)
    args = [
        pltpu.with_memory_space_constraint(arg, pltpu.HBM) if scalars <= i < scalars + far else arg
        for i, arg in enumerate(args)
    ]
    return pl.pallas_call(
        body,
        out_shape=outs,
        in_specs=[pl.BlockSpec(memory_space=pltpu.SMEM)] * scalars
        + [pl.BlockSpec(memory_space=pltpu.HBM)] * far
        + [whole] * (len(args) - scalars - far),
        out_specs=jax.tree.map(lambda _: whole, outs),
        scratch_shapes=list(scratch),
        compiler_params=pltpu.CompilerParams(vmem_limit_bytes=VMEM_BYTES),
        cost_estimate=cost,
    )(*args)


def shards(
    load_cases,
    mass_diag,
    stiffness,
    block_cols,
    trace_dofs,
    penalty,
    cell_partials,
    cell_owner,
    cell_dof,
):
    cases, dofs = load_cases.shape
    count, blk, width = stiffness.shape
    cells = cell_partials.shape[1]
    slots = trace_dofs.shape[0]
    patches = lax.axis_size("patch")
    cap = 4 * cells // patches
    rows = cases + 8
    far_rows = cases + -(-(1 + 2 * (slots // cap)) // 8) * 8
    shape = jax.ShapeDtypeStruct
    field_shape = shape((cases, dofs), F32)
    slot_shape = shape((cases, slots), F32)
    mass = mass_diag.reshape(1, dofs)
    trace = trace_dofs.reshape(1, slots)
    pen = penalty.reshape(1, slots)
    cols = block_cols.T

    half = patches // 2
    pairs = [(i, (i + half) % patches) for i in range(patches)]
    packets = run(
        pack_cells,
        [shape((far_rows if by == half else rows, cap), F32) for by in range(patches)],
        (cell_partials, cell_owner.reshape(1, cells), cell_dof.reshape(1, cells), pen, trace),
        scratch=[
            pltpu.VMEM((cases, cells), F32),
            pltpu.VMEM((1, cells), jnp.int32),
            pltpu.VMEM((1, cells), jnp.int32),
            pltpu.VMEM((1, slots), F32),
            pltpu.VMEM((1, slots), jnp.int32),
            pltpu.SemaphoreType.DMA((5,)),
        ],
        far=5,
    )
    order = [0, 1, 2, half, *(by for by in range(3, patches) if by != half)]
    received = [packets[0]] + [
        lax.ppermute(packets[by], "patch", [(i, (i + by) % patches) for i in range(patches)])
        for by in order[1:]
    ]
    far, first = received[3], 5 * patches // 8
    base, stiff = run(
        early_cells,
        (field_shape, shape((count, 2 * blk, width), BF16)),
        (stiffness, load_cases, *received[:first]),
        scratch=[
            pltpu.VMEM((cases, dofs), F32),
            pltpu.VMEM(stiffness.shape, F32),
            pltpu.SemaphoreType.DMA((2,)),
        ],
        cost=pl.CostEstimate(flops=8 * stiffness.size, bytes_accessed=8 * stiffness.size, transcendentals=0),
        far=2,
    )
    late, base, stiff, cols, mass, trace = lax.optimization_barrier(
        (received[first:], base, stiff, cols, mass, trace)
    )

    spread = [pltpu.VMEM((dofs // blk, 2 * cases, LANES), BF16)] * 2
    strain_scratch = pltpu.VMEM((count, 2 * cases, LANES), BF16)
    sums = [pltpu.VMEM((dofs // blk, cases, LANES), F32)] * 2

    row_shape = shape((1, slots), F32)
    field, own, match_pen, match_trace = run(
        assemble, (field_shape, slot_shape, row_shape, row_shape), (base, trace, far, *late)
    )
    match = lax.ppermute(own, "patch", pairs)
    part, part_own = run(
        operator_body,
        (field_shape, slot_shape),
        (cols, field, mass, trace, stiff),
        scratch=[*spread, strain_scratch, *sums],
        scalars=1,
    )
    same = run(coincidence, shape((slots, slots), BF16), (trace, match_trace))
    part_own, same = lax.optimization_barrier((part_own, same))
    part_match = lax.ppermute(part_own, "patch", pairs)
    image, shift, gram, strain = run(
        first_image,
        (
            field_shape,
            slot_shape,
            shape((cases, 4 * cases), F32),
            shape((count, 2 * cases, LANES), BF16),
        ),
        (cols, field, part, own, match, pen, match_pen, trace, mass, same, stiff),
        scratch=spread,
        scalars=1,
    )
    gram, jump = run(
        gram_trace,
        (shape((cases, 4 * cases), F32), slot_shape),
        (gram, part_own, part_match, shift, pen, match_pen),
    )
    gram = sum_of(from_all(gram, "comp"))
    *early, last = digits(patches)
    for stride, radix in early:
        gram = sum_of(from_all(gram, "patch", stride, radix))
    grams = from_all(gram, "patch", *last)
    stacked = run(
        second_image,
        shape((-(-6 * cases // LANES) * LANES, dofs), BF16),
        (cols, field, image, mass, stiff, strain, jump, trace),
        scratch=sums,
        scalars=1,
    )
    return run(finish, (field_shape, field_shape), (*grams, field, stacked))


def solution(mesh):
    return jax.shard_map(
        shards,
        mesh=mesh,
        in_specs=(
            P(None, ("comp", "patch")),
            P(("comp", "patch")),
            P(("comp", "patch"), None, None),
            P(("comp", "patch"), None),
            P(("comp", "patch")),
            P(("comp", "patch")),
            P(None, ("comp", "patch")),
            P(("comp", "patch"), None),
            P(("comp", "patch")),
        ),
        out_specs=(P(None, ("comp", "patch")), P(None, ("comp", "patch"))),
        check_vma=False,
    )
```

```python
import jax
import jax.numpy as jnp
from jax import lax
from jax.experimental import pallas as pl
from jax.experimental.pallas import tpu as pltpu
from jax.sharding import PartitionSpec as P

F32 = jnp.float32
BF16 = jnp.bfloat16
WIDE = 256
LANES = 128
VMEM_BYTES = 32 * 1024 * 1024


def split2(x):
    high = x.astype(BF16)
    low = (x - high.astype(F32)).astype(BF16)
    return high, low


def stack2(x):
    return jnp.concatenate(split2(x), axis=0)


def dot_nn(a, b):
    return lax.dot_general(a, b, (((1,), (0,)), ((), ())), preferred_element_type=F32)


def dot_nt(a, b):
    return lax.dot_general(a, b, (((1,), (1,)), ((), ())), preferred_element_type=F32)


def iota(shape, axis):
    return lax.broadcasted_iota(jnp.int32, shape, axis)


def one_hot_low(low, width):
    return (iota((WIDE, width), 0) == low).astype(F32).astype(BF16)


def masked_groups(stacked, group, count):
    parts = []
    for g in range(count):
        mask = (group == g).astype(F32).astype(BF16)
        parts.append(stacked * jnp.broadcast_to(mask, stacked.shape))
    return jnp.concatenate(parts, axis=0)


def gather_slots(field, one_hot, group, groups):
    cases = field.shape[0]
    rows = jnp.concatenate(
        [stack2(field[:, g * WIDE:(g + 1) * WIDE]) for g in range(groups)], axis=0
    )
    found = dot_nn(rows, one_hot)
    total = jnp.zeros((cases, group.shape[1]), F32)
    for g in range(groups):
        base = g * 2 * cases
        both = found[base:base + cases] + found[base + cases:base + 2 * cases]
        total = jnp.where(group == g, both, total)
    return total


def pack_cells(*refs):
    sources, out_refs, targets, sems = refs[:5], refs[5:-6], refs[-6:-1], refs[-1]
    copies = [
        pltpu.make_async_copy(source, target, sems.at[i])
        for i, (source, target) in enumerate(zip(sources, targets))
    ]
    for copy in copies:
        copy.start()
    partials_ref, owner_ref, dof_ref, pen_ref, trace_ref = targets
    patches = len(out_refs)
    rows, cap = out_refs[0].shape
    cases, cells = partials_ref.shape
    me = lax.axis_index("patch")
    before = (iota((cells, cells), 0) < iota((cells, cells), 1)).astype(F32).astype(BF16)
    for copy in copies[1:]:
        copy.wait()
    shift = owner_ref[...] - me
    shift = jnp.where(shift < 0, shift + patches, shift)
    mine = (iota((patches, cells), 0) == shift).astype(F32)
    counts = dot_nn(mine.astype(BF16), before)
    rank = jnp.sum(mine * counts, axis=0, keepdims=True).astype(jnp.int32)
    extra = jnp.where(iota((rows - cases, cells), 0) == 0, dof_ref[...] + 1, 0).astype(F32)
    copies[0].wait()
    body = stack2(jnp.concatenate([partials_ref[...], extra], axis=0))
    for by, out_ref in enumerate(out_refs):
        key = jnp.where(shift == by, rank, -1)
        pick = (iota((cap, cells), 0) == key).astype(F32).astype(BF16)
        packed = dot_nt(body, pick)
        out_ref[:rows, :] = packed[:rows] + packed[rows:]
        if by == patches // 2:
            more = pen_ref.shape[1] // cap
            for i in range(more):
                at = cases + 1 + i
                out_ref[at:at + 1, :] = pen_ref[:, i * cap:(i + 1) * cap]
                out_ref[at + more:at + more + 1, :] = trace_ref[:, i * cap:(i + 1) * cap].astype(F32)


def add_cells(base, packet_refs):
    cases, dofs = base.shape
    groups = dofs // WIDE
    cells = jnp.concatenate([ref[:cases + 8, :] for ref in packet_refs], axis=1)
    slots = cells.shape[1]
    dof = cells[cases:cases + 1].astype(jnp.int32) - 1
    low = jnp.where(dof < 0, -1, dof & (WIDE - 1))
    return add_rows(base, cells[:cases], one_hot_low(low, slots), dof >> 8)


def early_cells(stiff_ref, load_ref, *refs):
    *packet_refs, field_ref, split_ref, load_copy_ref, wide_ref, sems = refs
    load_copy = pltpu.make_async_copy(load_ref, load_copy_ref, sems.at[0])
    load_copy.start()
    copy = pltpu.make_async_copy(stiff_ref, wide_ref, sems.at[1])
    copy.start()
    load_copy.wait()
    field_ref[...] = add_cells(load_copy_ref[...], packet_refs)
    copy.wait()
    blk = stiff_ref.shape[1]
    high, low = split2(wide_ref[...])
    split_ref[:, :blk, :] = high
    split_ref[:, blk:, :] = low


def assemble(base_ref, trace_ref, far_ref, *refs):
    *packet_refs, field_ref, own_ref, pen_ref, match_trace_ref = refs
    cases, dofs = base_ref.shape
    cap = far_ref.shape[1]
    more = pen_ref.shape[1] // cap
    for i in range(more):
        at = cases + 1 + i
        pen_ref[:, i * cap:(i + 1) * cap] = far_ref[at:at + 1, :]
        match_trace_ref[:, i * cap:(i + 1) * cap] = far_ref[at + more:at + more + 1, :]
    field = add_cells(base_ref[...], packet_refs)
    field_ref[...] = field
    trace = trace_ref[...]
    own_ref[...] = gather_slots(
        field, one_hot_low(trace & (WIDE - 1), trace.shape[1]), trace >> 8, dofs // WIDE
    )


def spread_blocks(field_ref, low_ref, high_ref):
    cases, dofs = field_ref.shape
    in_low = iota((cases, LANES), 1) < LANES // 2
    for j in range(dofs // LANES):
        tile = field_ref[:, j * LANES:(j + 1) * LANES]
        turned = pltpu.roll(tile, LANES // 2, 1)
        low_ref[2 * j] = stack2(jnp.where(in_low, tile, 0.0))
        high_ref[2 * j + 1] = stack2(jnp.where(in_low, 0.0, tile))
        low_ref[2 * j + 1] = stack2(jnp.where(in_low, turned, 0.0))
        high_ref[2 * j] = stack2(jnp.where(in_low, 0.0, turned))


def strain_rows(cols_ref, stiff_ref, low_ref, high_ref, strain_ref):
    count = stiff_ref.shape[0]
    cases = strain_ref.shape[1] // 2
    for n in range(count):
        c = [cols_ref[k, n] for k in range(4)]
        near = jnp.concatenate(
            [low_ref[c[0]] + high_ref[c[1]], low_ref[c[2]] + high_ref[c[3]]], axis=1
        )
        both = dot_nt(near, stiff_ref[n])
        both = both[:cases] + both[cases:]
        strain_ref[n] = stack2(both + pltpu.roll(both, LANES // 2, 1))


def transposed_sums(cols_ref, stiff_ref, strain_ref, sums):
    count = stiff_ref.shape[0]
    cases = strain_ref.shape[1] // 2
    for ref in sums:
        ref[...] = jnp.zeros_like(ref)
    for n in range(count):
        c = [cols_ref[k, n] for k in range(4)]
        both = dot_nn(strain_ref[n], stiff_ref[n])
        both = both[:cases] + both[cases:]
        left, right = both[:, :LANES], both[:, LANES:]
        sums[0][c[0]] += left
        sums[1][c[1]] += left
        sums[0][c[2]] += right
        sums[1][c[3]] += right


def folded_tile(sums, j):
    cases = sums[0].shape[1]
    in_low = iota((cases, LANES), 1) < LANES // 2
    even, odd = 2 * j, 2 * j + 1
    straight = jnp.where(in_low, sums[0][even], sums[1][odd])
    crossed = jnp.where(in_low, sums[0][odd], sums[1][even])
    return straight + pltpu.roll(crossed, LANES // 2, 1)


def operator_body(
    cols_ref, field_ref, mass_ref, trace_ref, stiff_ref, out_ref, own_ref, low_ref, high_ref, strain_ref, *sums
):
    spread_blocks(field_ref, low_ref, high_ref)
    strain_rows(cols_ref, stiff_ref, low_ref, high_ref, strain_ref)
    transposed_sums(cols_ref, stiff_ref, strain_ref, sums)
    dofs = field_ref.shape[1]
    for j in range(dofs // LANES):
        at = slice(j * LANES, (j + 1) * LANES)
        out_ref[:, at] = field_ref[:, at] * mass_ref[:, at] + folded_tile(sums, j)
    trace = trace_ref[...]
    own_ref[...] = gather_slots(
        out_ref[...], one_hot_low(trace & (WIDE - 1), trace.shape[1]), trace >> 8, dofs // WIDE
    )


def coincidence(trace_ref, match_trace_ref, out_ref):
    slots = trace_ref.shape[1]
    rows = [trace_ref[...].astype(F32), match_trace_ref[...]]
    for i in range(slots // LANES):
        at = slice(i * LANES, (i + 1) * LANES)
        total = jnp.zeros((LANES, slots), F32)
        for row in rows:
            column = jnp.broadcast_to(row[:, at], (LANES, LANES)).T
            total += (jnp.broadcast_to(column[:, :1], (LANES, slots)) == row).astype(F32)
        out_ref[at, :] = total.astype(BF16)


def add_rows(base, rows, one_hot, group):
    cases, dofs = base.shape
    groups = dofs // WIDE
    sums = dot_nt(masked_groups(stack2(rows), group, groups), one_hot)
    pieces = []
    for g in range(groups):
        row = g * 2 * cases
        pieces.append(
            base[:, g * WIDE:(g + 1) * WIDE]
            + (sums[row:row + cases] + sums[row + cases:row + 2 * cases])
        )
    return jnp.concatenate(pieces, axis=1)


def first_image(
    cols_ref, field_ref, part_ref, own_ref, match_ref, pen_ref, match_pen_ref, trace_ref, mass_ref, same_ref, stiff_ref,
    image_ref, shift_ref, gram_ref, strain_ref, low_ref, high_ref,
):
    cases, dofs = field_ref.shape
    trace = trace_ref[...]
    weight = pen_ref[...] * match_pen_ref[...]
    jump = weight * (own_ref[...] - match_ref[...])
    image_ref[...] = add_rows(
        part_ref[...], jump, one_hot_low(trace & (WIDE - 1), trace.shape[1]), trace >> 8
    )
    moved = dot_nn(stack2(jump), same_ref[...])
    shift_ref[...] = moved[:cases] + moved[cases:]
    spread_blocks(image_ref, low_ref, high_ref)
    strain_rows(cols_ref, stiff_ref, low_ref, high_ref, strain_ref)
    in_low = iota((2 * cases, LANES), 1) < LANES // 2
    strain = jnp.concatenate(
        [
            jnp.where(in_low, strain_ref[2 * j].astype(F32), strain_ref[2 * j + 1].astype(F32)).astype(BF16)
            for j in range(strain_ref.shape[0] // 2)
        ],
        axis=1,
    )
    image = image_ref[...]
    image_rows = stack2(image)
    rows = jnp.concatenate([stack2(field_ref[...]), image_rows], axis=0)
    every = dot_nt(rows, image_rows)
    every = every[:, :cases] + every[:, cases:]
    cross = every[:cases] + every[cases:2 * cases]
    square = every[2 * cases:3 * cases] + every[3 * cases:]
    start = dot_nt(rows[:2 * cases], rows[:2 * cases])
    start = start[:, :cases] + start[:, cases:]
    start = start[:cases] + start[cases:]
    last = dot_nt(image_rows, stack2(image * mass_ref[...])) + dot_nt(strain, strain)
    last = last[:, :cases] + last[:, cases:]
    last = last[:cases] + last[cases:]
    gram_ref[...] = jnp.concatenate([cross, start, square, last], axis=1)


def gram_trace(gram_ref, match_gram_ref, own_ref, match_ref, shift_ref, pen_ref, match_pen_ref, out_ref, jump_ref):
    cases = gram_ref.shape[0]
    apart = (own_ref[...] - match_ref[...]) + shift_ref[...]
    jump = (pen_ref[...] * match_pen_ref[...]) * apart
    jump_ref[...] = jump
    more = dot_nt(stack2(apart), stack2(jump))
    more = more[:, :cases] + more[:, cases:]
    more = more[:cases] + more[cases:]
    zeros = jnp.zeros((cases, 3 * cases), F32)
    out_ref[...] = (gram_ref[...] + match_gram_ref[...]) + jnp.concatenate([zeros, more], axis=1)


def second_image(
    cols_ref, field_ref, image_ref, mass_ref, stiff_ref, strain_ref, jump_ref, trace_ref, out_ref, *sums
):
    transposed_sums(cols_ref, stiff_ref, strain_ref, sums)
    trace = trace_ref[...]
    one_hot = one_hot_low(trace & (WIDE - 1), trace.shape[1])
    folded = jnp.concatenate(
        [folded_tile(sums, j) for j in range(image_ref.shape[1] // LANES)], axis=1
    )
    image = image_ref[...]
    rows = 2 * image.shape[0]
    second = add_rows(image * mass_ref[...] + folded, jump_ref[...], one_hot, trace >> 8)
    for i, part in enumerate((field_ref[...], image, second)):
        out_ref[i * rows:(i + 1) * rows, :] = stack2(part)
    out_ref[3 * rows:, :] = jnp.zeros((out_ref.shape[0] - 3 * rows, out_ref.shape[1]), BF16)


def eliminate(matrix, size, group=8):
    rows = iota(matrix.shape, 0)
    for first in range(0, size, group):
        columns = [
            jnp.broadcast_to(matrix[:, p:p + 1], matrix.shape) for p in range(first, first + group)
        ]
        for q in range(group):
            p = first + q
            column = columns[q]
            inverse = 1.0 / column[p:p + 1]
            row = matrix[p:p + 1] * inverse
            here = rows == p
            matrix = jnp.where(here, row, matrix - column * row)
            for r in range(q + 1, group):
                entry = column[first + r:first + r + 1] * inverse
                columns[r] = jnp.where(here, entry, columns[r] - column * entry)
    return matrix


def small_dot(a, b):
    return jnp.dot(a, b, precision=lax.Precision.HIGHEST, preferred_element_type=F32)


def finish(*refs):
    *gram_refs, field_ref, rows_ref, solution_ref, residual_ref = refs
    cases = field_ref.shape[0]
    gram = sum_of([ref[...] for ref in gram_refs])
    square = gram[:, 2 * cases:3 * cases]
    solved = eliminate(gram, cases)
    zeros = jnp.zeros((cases, 2 * cases), F32)
    given = jnp.concatenate([gram[:, 3 * cases:], gram[:, :cases]], axis=1)
    both = jnp.concatenate([solved[:, 2 * cases:3 * cases], solved[:, cases:2 * cases]], axis=1)
    second_part = eliminate(
        jnp.concatenate([given - small_dot(square, both), zeros], axis=1), cases
    )[:, cases:2 * cases]
    first_part = both[:, cases:] - small_dot(both[:, :cases], second_part)
    zero = jnp.zeros((cases, cases), F32)
    blocks = [[first_part, zero], [second_part, -first_part], [zero, -second_part], [zero, zero]]
    weights = [jnp.concatenate(block + [zero, zero], axis=1) for block in blocks]
    weights = jnp.concatenate([weights[i // 2] for i in range(8)], axis=0)
    weights = jnp.concatenate([weights[:LANES].T, weights[LANES:].T], axis=1)[:2 * cases]
    out = dot_nn(stack2(weights), rows_ref[...])
    out = out[:2 * cases] + out[2 * cases:]
    solution_ref[...] = out[:cases]
    residual_ref[...] = field_ref[...] + out[cases:]


def sum_of(terms):
    while len(terms) > 1:
        terms = [sum(terms[i:i + 2][1:], terms[i]) for i in range(0, len(terms), 2)]
    return terms[0]


def from_all(array, axis, stride=1, radix=None):
    count = lax.axis_size(axis)
    radix = radix or count
    span = stride * radix

    def target(i, by):
        digit = i // stride % radix
        return i // span * span + (digit + by) % radix * stride + i % stride

    return [array] + [
        lax.ppermute(array, axis, [(i, target(i, by)) for i in range(count)])
        for by in range(1, radix)
    ]


def digits(count):
    stages, stride = [], 1
    while stride < count:
        left = count // stride
        radix = 4 if left % 4 == 0 else left
        stages.append((stride, radix))
        stride *= radix
    return stages


def run(body, outs, args, scratch=(), scalars=0, cost=None, far=0):
    whole = pl.BlockSpec(memory_space=pltpu.VMEM)
    args = [
        pltpu.with_memory_space_constraint(arg, pltpu.HBM) if scalars <= i < scalars + far else arg
        for i, arg in enumerate(args)
    ]
    return pl.pallas_call(
        body,
        out_shape=outs,
        in_specs=[pl.BlockSpec(memory_space=pltpu.SMEM)] * scalars
        + [pl.BlockSpec(memory_space=pltpu.HBM)] * far
        + [whole] * (len(args) - scalars - far),
        out_specs=jax.tree.map(lambda _: whole, outs),
        scratch_shapes=list(scratch),
        compiler_params=pltpu.CompilerParams(vmem_limit_bytes=VMEM_BYTES),
        cost_estimate=cost,
    )(*args)


def shards(
    load_cases,
    mass_diag,
    stiffness,
    block_cols,
    trace_dofs,
    penalty,
    cell_partials,
    cell_owner,
    cell_dof,
):
    cases, dofs = load_cases.shape
    count, blk, width = stiffness.shape
    cells = cell_partials.shape[1]
    slots = trace_dofs.shape[0]
    patches = lax.axis_size("patch")
    cap = 4 * cells // patches
    rows = cases + 8
    far_rows = cases + -(-(1 + 2 * (slots // cap)) // 8) * 8
    shape = jax.ShapeDtypeStruct
    field_shape = shape((cases, dofs), F32)
    slot_shape = shape((cases, slots), F32)
    mass = mass_diag.reshape(1, dofs)
    trace = trace_dofs.reshape(1, slots)
    pen = penalty.reshape(1, slots)
    cols = block_cols.T

    half = patches // 2
    pairs = [(i, (i + half) % patches) for i in range(patches)]
    packets = run(
        pack_cells,
        [shape((far_rows if by == half else rows, cap), F32) for by in range(patches)],
        (cell_partials, cell_owner.reshape(1, cells), cell_dof.reshape(1, cells), pen, trace),
        scratch=[
            pltpu.VMEM((cases, cells), F32),
            pltpu.VMEM((1, cells), jnp.int32),
            pltpu.VMEM((1, cells), jnp.int32),
            pltpu.VMEM((1, slots), F32),
            pltpu.VMEM((1, slots), jnp.int32),
            pltpu.SemaphoreType.DMA((5,)),
        ],
        far=5,
    )
    order = [0, 1, 2, half, *(by for by in range(3, patches) if by != half)]
    received = [packets[0]] + [
        lax.ppermute(packets[by], "patch", [(i, (i + by) % patches) for i in range(patches)])
        for by in order[1:]
    ]
    far, first = received[3], 5 * patches // 8
    base, stiff = run(
        early_cells,
        (field_shape, shape((count, 2 * blk, width), BF16)),
        (stiffness, load_cases, *received[:first]),
        scratch=[
            pltpu.VMEM((cases, dofs), F32),
            pltpu.VMEM(stiffness.shape, F32),
            pltpu.SemaphoreType.DMA((2,)),
        ],
        cost=pl.CostEstimate(flops=8 * stiffness.size, bytes_accessed=8 * stiffness.size, transcendentals=0),
        far=2,
    )
    late, base, stiff, cols, mass, trace = lax.optimization_barrier(
        (received[first:], base, stiff, cols, mass, trace)
    )

    spread = [pltpu.VMEM((dofs // blk, 2 * cases, LANES), BF16)] * 2
    strain_scratch = pltpu.VMEM((count, 2 * cases, LANES), BF16)
    sums = [pltpu.VMEM((dofs // blk, cases, LANES), F32)] * 2

    row_shape = shape((1, slots), F32)
    field, own, match_pen, match_trace = run(
        assemble, (field_shape, slot_shape, row_shape, row_shape), (base, trace, far, *late)
    )
    match = lax.ppermute(own, "patch", pairs)
    part, part_own = run(
        operator_body,
        (field_shape, slot_shape),
        (cols, field, mass, trace, stiff),
        scratch=[*spread, strain_scratch, *sums],
        scalars=1,
    )
    same = run(coincidence, shape((slots, slots), BF16), (trace, match_trace))
    part_own, same = lax.optimization_barrier((part_own, same))
    part_match = lax.ppermute(part_own, "patch", pairs)
    image, shift, gram, strain = run(
        first_image,
        (
            field_shape,
            slot_shape,
            shape((cases, 4 * cases), F32),
            shape((count, 2 * cases, LANES), BF16),
        ),
        (cols, field, part, own, match, pen, match_pen, trace, mass, same, stiff),
        scratch=spread,
        scalars=1,
    )
    match_gram = lax.ppermute(gram, "patch", pairs)
    gram, jump = run(
        gram_trace,
        (shape((cases, 4 * cases), F32), slot_shape),
        (gram, match_gram, part_own, part_match, shift, pen, match_pen),
    )
    gram = sum_of(from_all(gram, "comp"))
    *early, last = digits(half)
    for stride, radix in early:
        gram = sum_of(from_all(gram, "patch", stride, radix))
    grams = from_all(gram, "patch", *last)
    stacked = run(
        second_image,
        shape((-(-6 * cases // LANES) * LANES, dofs), BF16),
        (cols, field, image, mass, stiff, strain, jump, trace),
        scratch=sums,
        scalars=1,
    )
    return run(finish, (field_shape, field_shape), (*grams, field, stacked))


def solution(mesh):
    return jax.shard_map(
        shards,
        mesh=mesh,
        in_specs=(
            P(None, ("comp", "patch")),
            P(("comp", "patch")),
            P(("comp", "patch"), None, None),
            P(("comp", "patch"), None),
            P(("comp", "patch")),
            P(("comp", "patch")),
            P(None, ("comp", "patch")),
            P(("comp", "patch"), None),
            P(("comp", "patch")),
        ),
        out_specs=(P(None, ("comp", "patch")), P(None, ("comp", "patch"))),
        check_vma=False,
    )
```

```python
import jax
import jax.numpy as jnp
from jax import lax
from jax.experimental import pallas as pl
from jax.experimental.pallas import tpu as pltpu
from jax.sharding import PartitionSpec as P

F32 = jnp.float32
BF16 = jnp.bfloat16
WIDE = 256
LANES = 128
VMEM_BYTES = 32 * 1024 * 1024


def split2(x):
    high = x.astype(BF16)
    low = (x - high.astype(F32)).astype(BF16)
    return high, low


def stack2(x):
    return jnp.concatenate(split2(x), axis=0)


def dot_nn(a, b):
    return lax.dot_general(a, b, (((1,), (0,)), ((), ())), preferred_element_type=F32)


def dot_nt(a, b):
    return lax.dot_general(a, b, (((1,), (1,)), ((), ())), preferred_element_type=F32)


def iota(shape, axis):
    return lax.broadcasted_iota(jnp.int32, shape, axis)


def one_hot_low(low, width):
    return (iota((WIDE, width), 0) == low).astype(F32).astype(BF16)


def masked_groups(stacked, group, count):
    parts = []
    for g in range(count):
        mask = (group == g).astype(F32).astype(BF16)
        parts.append(stacked * jnp.broadcast_to(mask, stacked.shape))
    return jnp.concatenate(parts, axis=0)


def gather_slots(field, one_hot, group, groups):
    cases = field.shape[0]
    rows = jnp.concatenate(
        [stack2(field[:, g * WIDE:(g + 1) * WIDE]) for g in range(groups)], axis=0
    )
    found = dot_nn(rows, one_hot)
    total = jnp.zeros((cases, group.shape[1]), F32)
    for g in range(groups):
        base = g * 2 * cases
        both = found[base:base + cases] + found[base + cases:base + 2 * cases]
        total = jnp.where(group == g, both, total)
    return total


def pack_cells(*refs):
    sources, out_refs, targets, sems = refs[:5], refs[5:-6], refs[-6:-1], refs[-1]
    copies = [
        pltpu.make_async_copy(source, target, sems.at[i])
        for i, (source, target) in enumerate(zip(sources, targets))
    ]
    for copy in copies:
        copy.start()
    partials_ref, owner_ref, dof_ref, pen_ref, trace_ref = targets
    patches = len(out_refs)
    rows, cap = out_refs[0].shape
    cases, cells = partials_ref.shape
    me = lax.axis_index("patch")
    before = (iota((cells, cells), 0) < iota((cells, cells), 1)).astype(F32).astype(BF16)
    for copy in copies[1:]:
        copy.wait()
    shift = owner_ref[...] - me
    shift = jnp.where(shift < 0, shift + patches, shift)
    mine = (iota((patches, cells), 0) == shift).astype(F32)
    counts = dot_nn(mine.astype(BF16), before)
    rank = jnp.sum(mine * counts, axis=0, keepdims=True).astype(jnp.int32)
    extra = jnp.where(iota((rows - cases, cells), 0) == 0, dof_ref[...] + 1, 0).astype(F32)
    copies[0].wait()
    body = stack2(jnp.concatenate([partials_ref[...], extra], axis=0))
    for by, out_ref in enumerate(out_refs):
        key = jnp.where(shift == by, rank, -1)
        pick = (iota((cap, cells), 0) == key).astype(F32).astype(BF16)
        packed = dot_nt(body, pick)
        out_ref[:rows, :] = packed[:rows] + packed[rows:]
        if by == patches // 2:
            more = pen_ref.shape[1] // cap
            for i in range(more):
                at = cases + 1 + i
                out_ref[at:at + 1, :] = pen_ref[:, i * cap:(i + 1) * cap]
                out_ref[at + more:at + more + 1, :] = trace_ref[:, i * cap:(i + 1) * cap].astype(F32)


def add_cells(base, packet_refs):
    cases, dofs = base.shape
    groups = dofs // WIDE
    cells = jnp.concatenate([ref[:cases + 8, :] for ref in packet_refs], axis=1)
    slots = cells.shape[1]
    dof = cells[cases:cases + 1].astype(jnp.int32) - 1
    low = jnp.where(dof < 0, -1, dof & (WIDE - 1))
    return add_rows(base, cells[:cases], one_hot_low(low, slots), dof >> 8)


def early_cells(stiff_ref, load_ref, *refs):
    *packet_refs, field_ref, split_ref, load_copy_ref, wide_ref, sems = refs
    load_copy = pltpu.make_async_copy(load_ref, load_copy_ref, sems.at[0])
    load_copy.start()
    copy = pltpu.make_async_copy(stiff_ref, wide_ref, sems.at[1])
    copy.start()
    load_copy.wait()
    field_ref[...] = add_cells(load_copy_ref[...], packet_refs)
    copy.wait()
    blk = stiff_ref.shape[1]
    high, low = split2(wide_ref[...])
    split_ref[:, :blk, :] = high
    split_ref[:, blk:, :] = low


def assemble(base_ref, trace_ref, far_ref, *refs):
    *packet_refs, field_ref, own_ref, pen_ref, match_trace_ref = refs
    cases, dofs = base_ref.shape
    cap = far_ref.shape[1]
    more = pen_ref.shape[1] // cap
    for i in range(more):
        at = cases + 1 + i
        pen_ref[:, i * cap:(i + 1) * cap] = far_ref[at:at + 1, :]
        match_trace_ref[:, i * cap:(i + 1) * cap] = far_ref[at + more:at + more + 1, :]
    field = add_cells(base_ref[...], packet_refs)
    field_ref[...] = field
    trace = trace_ref[...]
    own_ref[...] = gather_slots(
        field, one_hot_low(trace & (WIDE - 1), trace.shape[1]), trace >> 8, dofs // WIDE
    )


def spread_blocks(field_ref, low_ref, high_ref):
    cases, dofs = field_ref.shape
    in_low = iota((cases, LANES), 1) < LANES // 2
    for j in range(dofs // LANES):
        tile = field_ref[:, j * LANES:(j + 1) * LANES]
        turned = pltpu.roll(tile, LANES // 2, 1)
        low_ref[2 * j] = stack2(jnp.where(in_low, tile, 0.0))
        high_ref[2 * j + 1] = stack2(jnp.where(in_low, 0.0, tile))
        low_ref[2 * j + 1] = stack2(jnp.where(in_low, turned, 0.0))
        high_ref[2 * j] = stack2(jnp.where(in_low, 0.0, turned))


def strain_rows(cols_ref, stiff_ref, low_ref, high_ref, strain_ref):
    count = stiff_ref.shape[0]
    cases = strain_ref.shape[1] // 2
    for n in range(count):
        c = [cols_ref[k, n] for k in range(4)]
        near = jnp.concatenate(
            [low_ref[c[0]] + high_ref[c[1]], low_ref[c[2]] + high_ref[c[3]]], axis=1
        )
        both = dot_nt(near, stiff_ref[n])
        both = both[:cases] + both[cases:]
        strain_ref[n] = stack2(both + pltpu.roll(both, LANES // 2, 1))


def transposed_sums(cols_ref, stiff_ref, strain_ref, sums):
    count = stiff_ref.shape[0]
    cases = strain_ref.shape[1] // 2
    for ref in sums:
        ref[...] = jnp.zeros_like(ref)
    for n in range(count):
        c = [cols_ref[k, n] for k in range(4)]
        both = dot_nn(strain_ref[n], stiff_ref[n])
        both = both[:cases] + both[cases:]
        left, right = both[:, :LANES], both[:, LANES:]
        sums[0][c[0]] += left
        sums[1][c[1]] += left
        sums[0][c[2]] += right
        sums[1][c[3]] += right


def folded_tile(sums, j):
    cases = sums[0].shape[1]
    in_low = iota((cases, LANES), 1) < LANES // 2
    even, odd = 2 * j, 2 * j + 1
    straight = jnp.where(in_low, sums[0][even], sums[1][odd])
    crossed = jnp.where(in_low, sums[0][odd], sums[1][even])
    return straight + pltpu.roll(crossed, LANES // 2, 1)


def operator_body(
    cols_ref, field_ref, mass_ref, trace_ref, stiff_ref, out_ref, own_ref, low_ref, high_ref, strain_ref, *sums
):
    spread_blocks(field_ref, low_ref, high_ref)
    strain_rows(cols_ref, stiff_ref, low_ref, high_ref, strain_ref)
    transposed_sums(cols_ref, stiff_ref, strain_ref, sums)
    dofs = field_ref.shape[1]
    for j in range(dofs // LANES):
        at = slice(j * LANES, (j + 1) * LANES)
        out_ref[:, at] = field_ref[:, at] * mass_ref[:, at] + folded_tile(sums, j)
    trace = trace_ref[...]
    own_ref[...] = gather_slots(
        out_ref[...], one_hot_low(trace & (WIDE - 1), trace.shape[1]), trace >> 8, dofs // WIDE
    )


def coincidence(trace_ref, match_trace_ref, out_ref):
    slots = trace_ref.shape[1]
    rows = [trace_ref[...].astype(F32), match_trace_ref[...]]
    for i in range(slots // LANES):
        at = slice(i * LANES, (i + 1) * LANES)
        total = jnp.zeros((LANES, slots), F32)
        for row in rows:
            column = jnp.broadcast_to(row[:, at], (LANES, LANES)).T
            total += (jnp.broadcast_to(column[:, :1], (LANES, slots)) == row).astype(F32)
        out_ref[at, :] = total.astype(BF16)


def add_rows(base, rows, one_hot, group):
    cases, dofs = base.shape
    groups = dofs // WIDE
    sums = dot_nt(masked_groups(stack2(rows), group, groups), one_hot)
    pieces = []
    for g in range(groups):
        row = g * 2 * cases
        pieces.append(
            base[:, g * WIDE:(g + 1) * WIDE]
            + (sums[row:row + cases] + sums[row + cases:row + 2 * cases])
        )
    return jnp.concatenate(pieces, axis=1)


def first_image(
    cols_ref, field_ref, part_ref, own_ref, match_ref, pen_ref, match_pen_ref, trace_ref, mass_ref, same_ref, stiff_ref,
    image_ref, shift_ref, gram_ref, strain_ref, low_ref, high_ref,
):
    cases, dofs = field_ref.shape
    trace = trace_ref[...]
    weight = pen_ref[...] * match_pen_ref[...]
    jump = weight * (own_ref[...] - match_ref[...])
    image_ref[...] = add_rows(
        part_ref[...], jump, one_hot_low(trace & (WIDE - 1), trace.shape[1]), trace >> 8
    )
    moved = dot_nn(stack2(jump), same_ref[...])
    shift_ref[...] = moved[:cases] + moved[cases:]
    spread_blocks(image_ref, low_ref, high_ref)
    strain_rows(cols_ref, stiff_ref, low_ref, high_ref, strain_ref)
    in_low = iota((2 * cases, LANES), 1) < LANES // 2
    strain = jnp.concatenate(
        [
            jnp.where(in_low, strain_ref[2 * j].astype(F32), strain_ref[2 * j + 1].astype(F32)).astype(BF16)
            for j in range(strain_ref.shape[0] // 2)
        ],
        axis=1,
    )
    image = image_ref[...]
    image_rows = stack2(image)
    rows = jnp.concatenate([stack2(field_ref[...]), image_rows], axis=0)
    every = dot_nt(rows, image_rows)
    every = every[:, :cases] + every[:, cases:]
    cross = every[:cases] + every[cases:2 * cases]
    square = every[2 * cases:3 * cases] + every[3 * cases:]
    start = dot_nt(rows[:2 * cases], rows[:2 * cases])
    start = start[:, :cases] + start[:, cases:]
    start = start[:cases] + start[cases:]
    last = dot_nt(image_rows, stack2(image * mass_ref[...])) + dot_nt(strain, strain)
    last = last[:, :cases] + last[:, cases:]
    last = last[:cases] + last[cases:]
    gram_ref[...] = jnp.concatenate([cross, start, square, last], axis=1)


def gram_trace(gram_ref, own_ref, match_ref, shift_ref, pen_ref, match_pen_ref, out_ref, jump_ref):
    cases = gram_ref.shape[0]
    apart = (own_ref[...] - match_ref[...]) + shift_ref[...]
    jump = (pen_ref[...] * match_pen_ref[...]) * apart
    jump_ref[...] = jump
    more = dot_nt(stack2(0.5 * apart), stack2(jump))
    more = more[:, :cases] + more[:, cases:]
    more = more[:cases] + more[cases:]
    zeros = jnp.zeros((cases, 3 * cases), F32)
    out_ref[...] = gram_ref[...] + jnp.concatenate([zeros, more], axis=1)


def second_image(
    cols_ref, field_ref, image_ref, mass_ref, stiff_ref, strain_ref, jump_ref, trace_ref, out_ref, *sums
):
    transposed_sums(cols_ref, stiff_ref, strain_ref, sums)
    trace = trace_ref[...]
    one_hot = one_hot_low(trace & (WIDE - 1), trace.shape[1])
    folded = jnp.concatenate(
        [folded_tile(sums, j) for j in range(image_ref.shape[1] // LANES)], axis=1
    )
    image = image_ref[...]
    rows = 2 * image.shape[0]
    second = add_rows(image * mass_ref[...] + folded, jump_ref[...], one_hot, trace >> 8)
    for i, part in enumerate((field_ref[...], image, second)):
        out_ref[i * rows:(i + 1) * rows, :] = stack2(part)
    out_ref[3 * rows:, :] = jnp.zeros((out_ref.shape[0] - 3 * rows, out_ref.shape[1]), BF16)


def eliminate(matrix, size, group=8):
    rows = iota(matrix.shape, 0)
    for first in range(0, size, group):
        columns = [
            jnp.broadcast_to(matrix[:, p:p + 1], matrix.shape) for p in range(first, first + group)
        ]
        for q in range(group):
            p = first + q
            column = columns[q]
            inverse = 1.0 / column[p:p + 1]
            row = matrix[p:p + 1] * inverse
            here = rows == p
            matrix = jnp.where(here, row, matrix - column * row)
            for r in range(q + 1, group):
                entry = column[first + r:first + r + 1] * inverse
                columns[r] = jnp.where(here, entry, columns[r] - column * entry)
    return matrix


def small_dot(a, b):
    return jnp.dot(a, b, precision=lax.Precision.HIGHEST, preferred_element_type=F32)


def finish(*refs):
    *gram_refs, field_ref, rows_ref, solution_ref, residual_ref = refs
    cases = field_ref.shape[0]
    gram = sum_of([ref[...] for ref in gram_refs])
    square = gram[:, 2 * cases:3 * cases]
    solved = eliminate(gram, cases)
    zeros = jnp.zeros((cases, 2 * cases), F32)
    given = jnp.concatenate([gram[:, 3 * cases:], gram[:, :cases]], axis=1)
    both = jnp.concatenate([solved[:, 2 * cases:3 * cases], solved[:, cases:2 * cases]], axis=1)
    second_part = eliminate(
        jnp.concatenate([given - small_dot(square, both), zeros], axis=1), cases
    )[:, cases:2 * cases]
    first_part = both[:, cases:] - small_dot(both[:, :cases], second_part)
    zero = jnp.zeros((cases, cases), F32)
    blocks = [[first_part, zero], [second_part, -first_part], [zero, -second_part], [zero, zero]]
    weights = [jnp.concatenate(block + [zero, zero], axis=1) for block in blocks]
    weights = jnp.concatenate([weights[i // 2] for i in range(8)], axis=0)
    weights = jnp.concatenate([weights[:LANES].T, weights[LANES:].T], axis=1)[:2 * cases]
    out = dot_nn(stack2(weights), rows_ref[...])
    out = out[:2 * cases] + out[2 * cases:]
    solution_ref[...] = out[:cases]
    residual_ref[...] = field_ref[...] + out[cases:]


def sum_of(terms):
    while len(terms) > 1:
        terms = [sum(terms[i:i + 2][1:], terms[i]) for i in range(0, len(terms), 2)]
    return terms[0]


def from_all(array, axis, stride=1, radix=None):
    count = lax.axis_size(axis)
    radix = radix or count
    span = stride * radix

    def target(i, by):
        digit = i // stride % radix
        return i // span * span + (digit + by) % radix * stride + i % stride

    return [array] + [
        lax.ppermute(array, axis, [(i, target(i, by)) for i in range(count)])
        for by in range(1, radix)
    ]


def digits(count):
    stages, stride = [], 1
    while stride < count:
        left = count // stride
        radix = 2 if stride == 1 and left % 2 == 0 else 4 if left % 4 == 0 else left
        stages.append((stride, radix))
        stride *= radix
    return stages


def run(body, outs, args, scratch=(), scalars=0, cost=None, far=0):
    whole = pl.BlockSpec(memory_space=pltpu.VMEM)
    args = [
        pltpu.with_memory_space_constraint(arg, pltpu.HBM) if scalars <= i < scalars + far else arg
        for i, arg in enumerate(args)
    ]
    return pl.pallas_call(
        body,
        out_shape=outs,
        in_specs=[pl.BlockSpec(memory_space=pltpu.SMEM)] * scalars
        + [pl.BlockSpec(memory_space=pltpu.HBM)] * far
        + [whole] * (len(args) - scalars - far),
        out_specs=jax.tree.map(lambda _: whole, outs),
        scratch_shapes=list(scratch),
        compiler_params=pltpu.CompilerParams(vmem_limit_bytes=VMEM_BYTES),
        cost_estimate=cost,
    )(*args)


def shards(
    load_cases,
    mass_diag,
    stiffness,
    block_cols,
    trace_dofs,
    penalty,
    cell_partials,
    cell_owner,
    cell_dof,
):
    cases, dofs = load_cases.shape
    count, blk, width = stiffness.shape
    cells = cell_partials.shape[1]
    slots = trace_dofs.shape[0]
    patches = lax.axis_size("patch")
    cap = 4 * cells // patches
    rows = cases + 8
    far_rows = cases + -(-(1 + 2 * (slots // cap)) // 8) * 8
    shape = jax.ShapeDtypeStruct
    field_shape = shape((cases, dofs), F32)
    slot_shape = shape((cases, slots), F32)
    mass = mass_diag.reshape(1, dofs)
    trace = trace_dofs.reshape(1, slots)
    pen = penalty.reshape(1, slots)
    cols = block_cols.T

    half = patches // 2
    pairs = [(i, (i + half) % patches) for i in range(patches)]
    packets = run(
        pack_cells,
        [shape((far_rows if by == half else rows, cap), F32) for by in range(patches)],
        (cell_partials, cell_owner.reshape(1, cells), cell_dof.reshape(1, cells), pen, trace),
        scratch=[
            pltpu.VMEM((cases, cells), F32),
            pltpu.VMEM((1, cells), jnp.int32),
            pltpu.VMEM((1, cells), jnp.int32),
            pltpu.VMEM((1, slots), F32),
            pltpu.VMEM((1, slots), jnp.int32),
            pltpu.SemaphoreType.DMA((5,)),
        ],
        far=5,
    )
    order = [0, 1, 2, half, *(by for by in range(3, patches) if by != half)]
    received = [packets[0]] + [
        lax.ppermute(packets[by], "patch", [(i, (i + by) % patches) for i in range(patches)])
        for by in order[1:]
    ]
    far, first = received[3], 5 * patches // 8
    base, stiff = run(
        early_cells,
        (field_shape, shape((count, 2 * blk, width), BF16)),
        (stiffness, load_cases, *received[:first]),
        scratch=[
            pltpu.VMEM((cases, dofs), F32),
            pltpu.VMEM(stiffness.shape, F32),
            pltpu.SemaphoreType.DMA((2,)),
        ],
        cost=pl.CostEstimate(flops=8 * stiffness.size, bytes_accessed=8 * stiffness.size, transcendentals=0),
        far=2,
    )
    late, base, stiff, cols, mass, trace = lax.optimization_barrier(
        (received[first:], base, stiff, cols, mass, trace)
    )

    spread = [pltpu.VMEM((dofs // blk, 2 * cases, LANES), BF16)] * 2
    strain_scratch = pltpu.VMEM((count, 2 * cases, LANES), BF16)
    sums = [pltpu.VMEM((dofs // blk, cases, LANES), F32)] * 2

    row_shape = shape((1, slots), F32)
    field, own, match_pen, match_trace = run(
        assemble, (field_shape, slot_shape, row_shape, row_shape), (base, trace, far, *late)
    )
    match = lax.ppermute(own, "patch", pairs)
    part, part_own = run(
        operator_body,
        (field_shape, slot_shape),
        (cols, field, mass, trace, stiff),
        scratch=[*spread, strain_scratch, *sums],
        scalars=1,
    )
    same = run(coincidence, shape((slots, slots), BF16), (trace, match_trace))
    part_own, same = lax.optimization_barrier((part_own, same))
    part_match = lax.ppermute(part_own, "patch", pairs)
    image, shift, gram, strain = run(
        first_image,
        (
            field_shape,
            slot_shape,
            shape((cases, 4 * cases), F32),
            shape((count, 2 * cases, LANES), BF16),
        ),
        (cols, field, part, own, match, pen, match_pen, trace, mass, same, stiff),
        scratch=spread,
        scalars=1,
    )
    gram, jump = run(
        gram_trace,
        (shape((cases, 4 * cases), F32), slot_shape),
        (gram, part_own, part_match, shift, pen, match_pen),
    )
    for stride, radix in reversed(digits(patches)):
        gram = sum_of(from_all(gram, "patch", stride, radix))
    grams = from_all(gram, "comp")
    stacked = run(
        second_image,
        shape((-(-6 * cases // LANES) * LANES, dofs), BF16),
        (cols, field, image, mass, stiff, strain, jump, trace),
        scratch=sums,
        scalars=1,
    )
    return run(finish, (field_shape, field_shape), (*grams, field, stacked))


def solution(mesh):
    return jax.shard_map(
        shards,
        mesh=mesh,
        in_specs=(
            P(None, ("comp", "patch")),
            P(("comp", "patch")),
            P(("comp", "patch"), None, None),
            P(("comp", "patch"), None),
            P(("comp", "patch")),
            P(("comp", "patch")),
            P(None, ("comp", "patch")),
            P(("comp", "patch"), None),
            P(("comp", "patch")),
        ),
        out_specs=(P(None, ("comp", "patch")), P(None, ("comp", "patch"))),
        check_vma=False,
    )
```

```python
import jax
import jax.numpy as jnp
from jax import lax
from jax.experimental import pallas as pl
from jax.experimental.pallas import tpu as pltpu
from jax.sharding import PartitionSpec as P

F32 = jnp.float32
BF16 = jnp.bfloat16
WIDE = 256
LANES = 128
VMEM_BYTES = 32 * 1024 * 1024


def split2(x):
    high = x.astype(BF16)
    low = (x - high.astype(F32)).astype(BF16)
    return high, low


def stack2(x):
    return jnp.concatenate(split2(x), axis=0)


def dot_nn(a, b):
    return lax.dot_general(a, b, (((1,), (0,)), ((), ())), preferred_element_type=F32)


def dot_nt(a, b):
    return lax.dot_general(a, b, (((1,), (1,)), ((), ())), preferred_element_type=F32)


def iota(shape, axis):
    return lax.broadcasted_iota(jnp.int32, shape, axis)


def one_hot_low(low, width):
    return (iota((WIDE, width), 0) == low).astype(F32).astype(BF16)


def masked_groups(stacked, group, count):
    parts = []
    for g in range(count):
        mask = (group == g).astype(F32).astype(BF16)
        parts.append(stacked * jnp.broadcast_to(mask, stacked.shape))
    return jnp.concatenate(parts, axis=0)


def gather_slots(field, one_hot, group, groups):
    cases = field.shape[0]
    rows = jnp.concatenate(
        [stack2(field[:, g * WIDE:(g + 1) * WIDE]) for g in range(groups)], axis=0
    )
    found = dot_nn(rows, one_hot)
    total = jnp.zeros((cases, group.shape[1]), F32)
    for g in range(groups):
        base = g * 2 * cases
        both = found[base:base + cases] + found[base + cases:base + 2 * cases]
        total = jnp.where(group == g, both, total)
    return total


def pack_cells(*refs):
    sources, out_refs, targets, sems = refs[:5], refs[5:-6], refs[-6:-1], refs[-1]
    copies = [
        pltpu.make_async_copy(source, target, sems.at[i])
        for i, (source, target) in enumerate(zip(sources, targets))
    ]
    for copy in copies:
        copy.start()
    partials_ref, owner_ref, dof_ref, pen_ref, trace_ref = targets
    patches = len(out_refs)
    rows, cap = out_refs[0].shape
    cases, cells = partials_ref.shape
    me = lax.axis_index("patch")
    before = (iota((cells, cells), 0) < iota((cells, cells), 1)).astype(F32).astype(BF16)
    for copy in copies[1:]:
        copy.wait()
    shift = owner_ref[...] - me
    shift = jnp.where(shift < 0, shift + patches, shift)
    mine = (iota((patches, cells), 0) == shift).astype(F32)
    counts = dot_nn(mine.astype(BF16), before)
    rank = jnp.sum(mine * counts, axis=0, keepdims=True).astype(jnp.int32)
    extra = jnp.where(iota((rows - cases, cells), 0) == 0, dof_ref[...] + 1, 0).astype(F32)
    copies[0].wait()
    body = stack2(jnp.concatenate([partials_ref[...], extra], axis=0))
    for by, out_ref in enumerate(out_refs):
        key = jnp.where(shift == by, rank, -1)
        pick = (iota((cap, cells), 0) == key).astype(F32).astype(BF16)
        packed = dot_nt(body, pick)
        out_ref[:rows, :] = packed[:rows] + packed[rows:]
        if by == patches // 2:
            more = pen_ref.shape[1] // cap
            for i in range(more):
                at = cases + 1 + i
                out_ref[at:at + 1, :] = pen_ref[:, i * cap:(i + 1) * cap]
                out_ref[at + more:at + more + 1, :] = trace_ref[:, i * cap:(i + 1) * cap].astype(F32)


def add_cells(base, packet_refs):
    cases, dofs = base.shape
    groups = dofs // WIDE
    cells = jnp.concatenate([ref[:cases + 8, :] for ref in packet_refs], axis=1)
    slots = cells.shape[1]
    dof = cells[cases:cases + 1].astype(jnp.int32) - 1
    low = jnp.where(dof < 0, -1, dof & (WIDE - 1))
    return add_rows(base, cells[:cases], one_hot_low(low, slots), dof >> 8)


def early_cells(stiff_ref, load_ref, *refs):
    *packet_refs, field_ref, split_ref, load_copy_ref, wide_ref, sems = refs
    load_copy = pltpu.make_async_copy(load_ref, load_copy_ref, sems.at[0])
    load_copy.start()
    copy = pltpu.make_async_copy(stiff_ref, wide_ref, sems.at[1])
    copy.start()
    load_copy.wait()
    field_ref[...] = add_cells(load_copy_ref[...], packet_refs)
    copy.wait()
    blk = stiff_ref.shape[1]
    high, low = split2(wide_ref[...])
    split_ref[:, :blk, :] = high
    split_ref[:, blk:, :] = low


def assemble(base_ref, trace_ref, far_ref, *refs):
    *packet_refs, field_ref, own_ref, pen_ref, match_trace_ref = refs
    cases, dofs = base_ref.shape
    cap = far_ref.shape[1]
    more = pen_ref.shape[1] // cap
    for i in range(more):
        at = cases + 1 + i
        pen_ref[:, i * cap:(i + 1) * cap] = far_ref[at:at + 1, :]
        match_trace_ref[:, i * cap:(i + 1) * cap] = far_ref[at + more:at + more + 1, :]
    field = add_cells(base_ref[...], packet_refs)
    field_ref[...] = field
    trace = trace_ref[...]
    own_ref[...] = gather_slots(
        field, one_hot_low(trace & (WIDE - 1), trace.shape[1]), trace >> 8, dofs // WIDE
    )


def spread_blocks(field_ref, low_ref, high_ref):
    cases, dofs = field_ref.shape
    in_low = iota((cases, LANES), 1) < LANES // 2
    for j in range(dofs // LANES):
        tile = field_ref[:, j * LANES:(j + 1) * LANES]
        turned = pltpu.roll(tile, LANES // 2, 1)
        low_ref[2 * j] = stack2(jnp.where(in_low, tile, 0.0))
        high_ref[2 * j + 1] = stack2(jnp.where(in_low, 0.0, tile))
        low_ref[2 * j + 1] = stack2(jnp.where(in_low, turned, 0.0))
        high_ref[2 * j] = stack2(jnp.where(in_low, 0.0, turned))


def strain_rows(cols_ref, stiff_ref, low_ref, high_ref, strain_ref):
    count = stiff_ref.shape[0]
    cases = strain_ref.shape[1] // 2
    for n in range(count):
        c = [cols_ref[k, n] for k in range(4)]
        near = jnp.concatenate(
            [low_ref[c[0]] + high_ref[c[1]], low_ref[c[2]] + high_ref[c[3]]], axis=1
        )
        both = dot_nt(near, stiff_ref[n])
        both = both[:cases] + both[cases:]
        strain_ref[n] = stack2(both + pltpu.roll(both, LANES // 2, 1))


def transposed_sums(cols_ref, stiff_ref, strain_ref, sums):
    count = stiff_ref.shape[0]
    cases = strain_ref.shape[1] // 2
    for ref in sums:
        ref[...] = jnp.zeros_like(ref)
    for n in range(count):
        c = [cols_ref[k, n] for k in range(4)]
        both = dot_nn(strain_ref[n], stiff_ref[n])
        both = both[:cases] + both[cases:]
        left, right = both[:, :LANES], both[:, LANES:]
        sums[0][c[0]] += left
        sums[1][c[1]] += left
        sums[0][c[2]] += right
        sums[1][c[3]] += right


def folded_tile(sums, j):
    cases = sums[0].shape[1]
    in_low = iota((cases, LANES), 1) < LANES // 2
    even, odd = 2 * j, 2 * j + 1
    straight = jnp.where(in_low, sums[0][even], sums[1][odd])
    crossed = jnp.where(in_low, sums[0][odd], sums[1][even])
    return straight + pltpu.roll(crossed, LANES // 2, 1)


def operator_body(
    cols_ref, field_ref, mass_ref, trace_ref, stiff_ref, out_ref, own_ref, low_ref, high_ref, strain_ref, *sums
):
    spread_blocks(field_ref, low_ref, high_ref)
    strain_rows(cols_ref, stiff_ref, low_ref, high_ref, strain_ref)
    transposed_sums(cols_ref, stiff_ref, strain_ref, sums)
    dofs = field_ref.shape[1]
    for j in range(dofs // LANES):
        at = slice(j * LANES, (j + 1) * LANES)
        out_ref[:, at] = field_ref[:, at] * mass_ref[:, at] + folded_tile(sums, j)
    trace = trace_ref[...]
    own_ref[...] = gather_slots(
        out_ref[...], one_hot_low(trace & (WIDE - 1), trace.shape[1]), trace >> 8, dofs // WIDE
    )


def coincidence(trace_ref, match_trace_ref, out_ref):
    slots = trace_ref.shape[1]
    rows = [trace_ref[...].astype(F32), match_trace_ref[...]]
    for i in range(slots // LANES):
        at = slice(i * LANES, (i + 1) * LANES)
        total = jnp.zeros((LANES, slots), F32)
        for row in rows:
            column = jnp.broadcast_to(row[:, at], (LANES, LANES)).T
            total += (jnp.broadcast_to(column[:, :1], (LANES, slots)) == row).astype(F32)
        out_ref[at, :] = total.astype(BF16)


def add_rows(base, rows, one_hot, group):
    cases, dofs = base.shape
    groups = dofs // WIDE
    sums = dot_nt(masked_groups(stack2(rows), group, groups), one_hot)
    pieces = []
    for g in range(groups):
        row = g * 2 * cases
        pieces.append(
            base[:, g * WIDE:(g + 1) * WIDE]
            + (sums[row:row + cases] + sums[row + cases:row + 2 * cases])
        )
    return jnp.concatenate(pieces, axis=1)


def first_image(
    cols_ref, field_ref, part_ref, own_ref, match_ref, pen_ref, match_pen_ref, trace_ref, mass_ref, same_ref, stiff_ref,
    image_ref, shift_ref, gram_ref, strain_ref, low_ref, high_ref,
):
    cases, dofs = field_ref.shape
    trace = trace_ref[...]
    weight = pen_ref[...] * match_pen_ref[...]
    jump = weight * (own_ref[...] - match_ref[...])
    image_ref[...] = add_rows(
        part_ref[...], jump, one_hot_low(trace & (WIDE - 1), trace.shape[1]), trace >> 8
    )
    moved = dot_nn(stack2(jump), same_ref[...])
    shift_ref[...] = moved[:cases] + moved[cases:]
    spread_blocks(image_ref, low_ref, high_ref)
    strain_rows(cols_ref, stiff_ref, low_ref, high_ref, strain_ref)
    in_low = iota((2 * cases, LANES), 1) < LANES // 2
    strain = jnp.concatenate(
        [
            jnp.where(in_low, strain_ref[2 * j].astype(F32), strain_ref[2 * j + 1].astype(F32)).astype(BF16)
            for j in range(strain_ref.shape[0] // 2)
        ],
        axis=1,
    )
    image = image_ref[...]
    image_rows = stack2(image)
    rows = jnp.concatenate([stack2(field_ref[...]), image_rows], axis=0)
    every = dot_nt(rows, image_rows)
    every = every[:, :cases] + every[:, cases:]
    cross = every[:cases] + every[cases:2 * cases]
    square = every[2 * cases:3 * cases] + every[3 * cases:]
    start = dot_nt(rows[:2 * cases], rows[:2 * cases])
    start = start[:, :cases] + start[:, cases:]
    start = start[:cases] + start[cases:]
    last = dot_nt(image_rows, stack2(image * mass_ref[...])) + dot_nt(strain, strain)
    last = last[:, :cases] + last[:, cases:]
    last = last[:cases] + last[cases:]
    gram_ref[...] = jnp.concatenate([cross, start, square, last], axis=1)


def gram_trace(gram_ref, own_ref, match_ref, shift_ref, pen_ref, match_pen_ref, out_ref, jump_ref):
    cases = gram_ref.shape[0]
    apart = (own_ref[...] - match_ref[...]) + shift_ref[...]
    jump = (pen_ref[...] * match_pen_ref[...]) * apart
    jump_ref[...] = jump
    more = dot_nt(stack2(0.5 * apart), stack2(jump))
    more = more[:, :cases] + more[:, cases:]
    more = more[:cases] + more[cases:]
    zeros = jnp.zeros((cases, 3 * cases), F32)
    out_ref[...] = gram_ref[...] + jnp.concatenate([zeros, more], axis=1)


def second_image(
    cols_ref, field_ref, image_ref, mass_ref, stiff_ref, strain_ref, jump_ref, trace_ref, out_ref, *sums
):
    transposed_sums(cols_ref, stiff_ref, strain_ref, sums)
    trace = trace_ref[...]
    one_hot = one_hot_low(trace & (WIDE - 1), trace.shape[1])
    folded = jnp.concatenate(
        [folded_tile(sums, j) for j in range(image_ref.shape[1] // LANES)], axis=1
    )
    image = image_ref[...]
    rows = 2 * image.shape[0]
    second = add_rows(image * mass_ref[...] + folded, jump_ref[...], one_hot, trace >> 8)
    for i, part in enumerate((field_ref[...], image, second)):
        out_ref[i * rows:(i + 1) * rows, :] = stack2(part)
    out_ref[3 * rows:, :] = jnp.zeros((out_ref.shape[0] - 3 * rows, out_ref.shape[1]), BF16)


def eliminate(matrix, size, group=8):
    rows = iota(matrix.shape, 0)
    for first in range(0, size, group):
        columns = [
            jnp.broadcast_to(matrix[:, p:p + 1], matrix.shape) for p in range(first, first + group)
        ]
        for q in range(group):
            p = first + q
            column = columns[q]
            inverse = 1.0 / column[p:p + 1]
            row = matrix[p:p + 1] * inverse
            here = rows == p
            matrix = jnp.where(here, row, matrix - column * row)
            for r in range(q + 1, group):
                entry = column[first + r:first + r + 1] * inverse
                columns[r] = jnp.where(here, entry, columns[r] - column * entry)
    return matrix


def small_dot(a, b):
    return jnp.dot(a, b, precision=lax.Precision.HIGHEST, preferred_element_type=F32)


def finish(*refs):
    *gram_refs, field_ref, rows_ref, solution_ref, residual_ref = refs
    cases = field_ref.shape[0]
    gram = sum_of([ref[...] for ref in gram_refs])
    square = gram[:, 2 * cases:3 * cases]
    solved = eliminate(gram, cases)
    zeros = jnp.zeros((cases, 2 * cases), F32)
    given = jnp.concatenate([gram[:, 3 * cases:], gram[:, :cases]], axis=1)
    both = jnp.concatenate([solved[:, 2 * cases:3 * cases], solved[:, cases:2 * cases]], axis=1)
    second_part = eliminate(
        jnp.concatenate([given - small_dot(square, both), zeros], axis=1), cases
    )[:, cases:2 * cases]
    first_part = both[:, cases:] - small_dot(both[:, :cases], second_part)
    zero = jnp.zeros((cases, cases), F32)
    blocks = [[first_part, zero], [second_part, -first_part], [zero, -second_part], [zero, zero]]
    weights = [jnp.concatenate(block + [zero, zero], axis=1) for block in blocks]
    weights = jnp.concatenate([weights[i // 2] for i in range(8)], axis=0)
    weights = jnp.concatenate([weights[:LANES].T, weights[LANES:].T], axis=1)[:2 * cases]
    out = dot_nn(stack2(weights), rows_ref[...])
    out = out[:2 * cases] + out[2 * cases:]
    solution_ref[...] = out[:cases]
    residual_ref[...] = field_ref[...] + out[cases:]


def sum_of(terms):
    while len(terms) > 1:
        terms = [sum(terms[i:i + 2][1:], terms[i]) for i in range(0, len(terms), 2)]
    return terms[0]


def from_all(array, axis, stride=1, radix=None):
    count = lax.axis_size(axis)
    radix = radix or count
    span = stride * radix

    def target(i, by):
        digit = i // stride % radix
        return i // span * span + (digit + by) % radix * stride + i % stride

    return [array] + [
        lax.ppermute(array, axis, [(i, target(i, by)) for i in range(count)])
        for by in range(1, radix)
    ]


def digits(count):
    stages, stride = [], 1
    while stride < count:
        left = count // stride
        radix = 2 if stride == 1 and left % 2 == 0 else 4 if left % 4 == 0 else left
        stages.append((stride, radix))
        stride *= radix
    return stages


def run(body, outs, args, scratch=(), scalars=0, cost=None, far=0):
    whole = pl.BlockSpec(memory_space=pltpu.VMEM)
    args = [
        pltpu.with_memory_space_constraint(arg, pltpu.HBM) if scalars <= i < scalars + far else arg
        for i, arg in enumerate(args)
    ]
    return pl.pallas_call(
        body,
        out_shape=outs,
        in_specs=[pl.BlockSpec(memory_space=pltpu.SMEM)] * scalars
        + [pl.BlockSpec(memory_space=pltpu.HBM)] * far
        + [whole] * (len(args) - scalars - far),
        out_specs=jax.tree.map(lambda _: whole, outs),
        scratch_shapes=list(scratch),
        compiler_params=pltpu.CompilerParams(vmem_limit_bytes=VMEM_BYTES),
        cost_estimate=cost,
    )(*args)


def shards(
    load_cases,
    mass_diag,
    stiffness,
    block_cols,
    trace_dofs,
    penalty,
    cell_partials,
    cell_owner,
    cell_dof,
):
    cases, dofs = load_cases.shape
    count, blk, width = stiffness.shape
    cells = cell_partials.shape[1]
    slots = trace_dofs.shape[0]
    patches = lax.axis_size("patch")
    cap = 4 * cells // patches
    rows = cases + 8
    far_rows = cases + -(-(1 + 2 * (slots // cap)) // 8) * 8
    shape = jax.ShapeDtypeStruct
    field_shape = shape((cases, dofs), F32)
    slot_shape = shape((cases, slots), F32)
    mass = mass_diag.reshape(1, dofs)
    trace = trace_dofs.reshape(1, slots)
    pen = penalty.reshape(1, slots)
    cols = block_cols.T

    half = patches // 2
    pairs = [(i, (i + half) % patches) for i in range(patches)]
    packets = run(
        pack_cells,
        [shape((far_rows if by == half else rows, cap), F32) for by in range(patches)],
        (cell_partials, cell_owner.reshape(1, cells), cell_dof.reshape(1, cells), pen, trace),
        scratch=[
            pltpu.VMEM((cases, cells), F32),
            pltpu.VMEM((1, cells), jnp.int32),
            pltpu.VMEM((1, cells), jnp.int32),
            pltpu.VMEM((1, slots), F32),
            pltpu.VMEM((1, slots), jnp.int32),
            pltpu.SemaphoreType.DMA((5,)),
        ],
        far=5,
    )
    order = [0, *range(patches - 1, 0, -1)]
    received = [packets[0]] + [
        lax.ppermute(packets[by], "patch", [(i, (i + by) % patches) for i in range(patches)])
        for by in order[1:]
    ]
    far, first = received[order.index(half)], 5 * patches // 8
    base, stiff = run(
        early_cells,
        (field_shape, shape((count, 2 * blk, width), BF16)),
        (stiffness, load_cases, *received[:first]),
        scratch=[
            pltpu.VMEM((cases, dofs), F32),
            pltpu.VMEM(stiffness.shape, F32),
            pltpu.SemaphoreType.DMA((2,)),
        ],
        cost=pl.CostEstimate(flops=8 * stiffness.size, bytes_accessed=8 * stiffness.size, transcendentals=0),
        far=2,
    )
    late, base, stiff, cols, mass, trace = lax.optimization_barrier(
        (received[first:], base, stiff, cols, mass, trace)
    )

    spread = [pltpu.VMEM((dofs // blk, 2 * cases, LANES), BF16)] * 2
    strain_scratch = pltpu.VMEM((count, 2 * cases, LANES), BF16)
    sums = [pltpu.VMEM((dofs // blk, cases, LANES), F32)] * 2

    row_shape = shape((1, slots), F32)
    field, own, match_pen, match_trace = run(
        assemble, (field_shape, slot_shape, row_shape, row_shape), (base, trace, far, *late)
    )
    match = lax.ppermute(own, "patch", pairs)
    part, part_own = run(
        operator_body,
        (field_shape, slot_shape),
        (cols, field, mass, trace, stiff),
        scratch=[*spread, strain_scratch, *sums],
        scalars=1,
    )
    same = run(coincidence, shape((slots, slots), BF16), (trace, match_trace))
    part_own, same = lax.optimization_barrier((part_own, same))
    part_match = lax.ppermute(part_own, "patch", pairs)
    image, shift, gram, strain = run(
        first_image,
        (
            field_shape,
            slot_shape,
            shape((cases, 4 * cases), F32),
            shape((count, 2 * cases, LANES), BF16),
        ),
        (cols, field, part, own, match, pen, match_pen, trace, mass, same, stiff),
        scratch=spread,
        scalars=1,
    )
    gram, jump = run(
        gram_trace,
        (shape((cases, 4 * cases), F32), slot_shape),
        (gram, part_own, part_match, shift, pen, match_pen),
    )
    for stride, radix in reversed(digits(patches)):
        gram = sum_of(from_all(gram, "patch", stride, radix))
    grams = from_all(gram, "comp")
    grams = [grams[0], *grams[2::2], *grams[1::2]]
    stacked = run(
        second_image,
        shape((-(-6 * cases // LANES) * LANES, dofs), BF16),
        (cols, field, image, mass, stiff, strain, jump, trace),
        scratch=sums,
        scalars=1,
    )
    return run(finish, (field_shape, field_shape), (*grams, field, stacked))


def solution(mesh):
    return jax.shard_map(
        shards,
        mesh=mesh,
        in_specs=(
            P(None, ("comp", "patch")),
            P(("comp", "patch")),
            P(("comp", "patch"), None, None),
            P(("comp", "patch"), None),
            P(("comp", "patch")),
            P(("comp", "patch")),
            P(None, ("comp", "patch")),
            P(("comp", "patch"), None),
            P(("comp", "patch")),
        ),
        out_specs=(P(None, ("comp", "patch")), P(None, ("comp", "patch"))),
        check_vma=False,
    )
```

```python
import jax
import jax.numpy as jnp
from jax import lax
from jax.experimental import pallas as pl
from jax.experimental.pallas import tpu as pltpu
from jax.sharding import PartitionSpec as P

F32 = jnp.float32
BF16 = jnp.bfloat16
WIDE = 256
LANES = 128
VMEM_BYTES = 32 * 1024 * 1024


def split2(x):
    high = x.astype(BF16)
    low = (x - high.astype(F32)).astype(BF16)
    return high, low


def stack2(x):
    return jnp.concatenate(split2(x), axis=0)


def dot_nn(a, b):
    return lax.dot_general(a, b, (((1,), (0,)), ((), ())), preferred_element_type=F32)


def dot_nt(a, b):
    return lax.dot_general(a, b, (((1,), (1,)), ((), ())), preferred_element_type=F32)


def iota(shape, axis):
    return lax.broadcasted_iota(jnp.int32, shape, axis)


def one_hot_low(low, width):
    return (iota((WIDE, width), 0) == low).astype(F32).astype(BF16)


def masked_groups(stacked, group, count):
    parts = []
    for g in range(count):
        mask = (group == g).astype(F32).astype(BF16)
        parts.append(stacked * jnp.broadcast_to(mask, stacked.shape))
    return jnp.concatenate(parts, axis=0)


def gather_slots(field, one_hot, group, groups):
    cases = field.shape[0]
    rows = jnp.concatenate(
        [stack2(field[:, g * WIDE:(g + 1) * WIDE]) for g in range(groups)], axis=0
    )
    found = dot_nn(rows, one_hot)
    total = jnp.zeros((cases, group.shape[1]), F32)
    for g in range(groups):
        base = g * 2 * cases
        both = found[base:base + cases] + found[base + cases:base + 2 * cases]
        total = jnp.where(group == g, both, total)
    return total


def pack_cells(*refs):
    sources, out_refs, targets, sems = refs[:5], refs[5:-6], refs[-6:-1], refs[-1]
    copies = [
        pltpu.make_async_copy(source, target, sems.at[i])
        for i, (source, target) in enumerate(zip(sources, targets))
    ]
    for copy in copies:
        copy.start()
    partials_ref, owner_ref, dof_ref, pen_ref, trace_ref = targets
    patches = len(out_refs)
    rows, cap = out_refs[0].shape
    cases, cells = partials_ref.shape
    me = lax.axis_index("patch")
    before = (iota((cells, cells), 0) < iota((cells, cells), 1)).astype(F32).astype(BF16)
    for copy in copies[1:]:
        copy.wait()
    shift = owner_ref[...] - me
    shift = jnp.where(shift < 0, shift + patches, shift)
    mine = (iota((patches, cells), 0) == shift).astype(F32)
    counts = dot_nn(mine.astype(BF16), before)
    rank = jnp.sum(mine * counts, axis=0, keepdims=True).astype(jnp.int32)
    extra = jnp.where(iota((rows - cases, cells), 0) == 0, dof_ref[...] + 1, 0).astype(F32)
    copies[0].wait()
    body = stack2(jnp.concatenate([partials_ref[...], extra], axis=0))
    for by, out_ref in enumerate(out_refs):
        key = jnp.where(shift == by, rank, -1)
        pick = (iota((cap, cells), 0) == key).astype(F32).astype(BF16)
        packed = dot_nt(body, pick)
        out_ref[:rows, :] = packed[:rows] + packed[rows:]
        if by == patches // 2:
            more = pen_ref.shape[1] // cap
            for i in range(more):
                at = cases + 1 + i
                out_ref[at:at + 1, :] = pen_ref[:, i * cap:(i + 1) * cap]
                out_ref[at + more:at + more + 1, :] = trace_ref[:, i * cap:(i + 1) * cap].astype(F32)


def add_cells(base, packet_refs):
    cases, dofs = base.shape
    groups = dofs // WIDE
    cells = jnp.concatenate([ref[:cases + 8, :] for ref in packet_refs], axis=1)
    slots = cells.shape[1]
    dof = cells[cases:cases + 1].astype(jnp.int32) - 1
    low = jnp.where(dof < 0, -1, dof & (WIDE - 1))
    return add_rows(base, cells[:cases], one_hot_low(low, slots), dof >> 8)


def early_cells(stiff_ref, load_ref, *refs):
    *packet_refs, field_ref, split_ref, load_copy_ref, wide_ref, sems = refs
    load_copy = pltpu.make_async_copy(load_ref, load_copy_ref, sems.at[0])
    load_copy.start()
    copy = pltpu.make_async_copy(stiff_ref, wide_ref, sems.at[1])
    copy.start()
    load_copy.wait()
    field_ref[...] = add_cells(load_copy_ref[...], packet_refs)
    copy.wait()
    blk = stiff_ref.shape[1]
    high, low = split2(wide_ref[...])
    split_ref[:, :blk, :] = high
    split_ref[:, blk:, :] = low


def assemble(base_ref, trace_ref, far_ref, *refs):
    *packet_refs, field_ref, own_ref, pen_ref, match_trace_ref = refs
    cases, dofs = base_ref.shape
    cap = far_ref.shape[1]
    more = pen_ref.shape[1] // cap
    for i in range(more):
        at = cases + 1 + i
        pen_ref[:, i * cap:(i + 1) * cap] = far_ref[at:at + 1, :]
        match_trace_ref[:, i * cap:(i + 1) * cap] = far_ref[at + more:at + more + 1, :]
    field = add_cells(base_ref[...], packet_refs)
    field_ref[...] = field
    trace = trace_ref[...]
    own_ref[...] = gather_slots(
        field, one_hot_low(trace & (WIDE - 1), trace.shape[1]), trace >> 8, dofs // WIDE
    )


def spread_blocks(field_ref, low_ref, high_ref):
    cases, dofs = field_ref.shape
    in_low = iota((cases, LANES), 1) < LANES // 2
    for j in range(dofs // LANES):
        tile = field_ref[:, j * LANES:(j + 1) * LANES]
        turned = pltpu.roll(tile, LANES // 2, 1)
        low_ref[2 * j] = stack2(jnp.where(in_low, tile, 0.0))
        high_ref[2 * j + 1] = stack2(jnp.where(in_low, 0.0, tile))
        low_ref[2 * j + 1] = stack2(jnp.where(in_low, turned, 0.0))
        high_ref[2 * j] = stack2(jnp.where(in_low, 0.0, turned))


def strain_rows(cols_ref, stiff_ref, low_ref, high_ref, strain_ref):
    count = stiff_ref.shape[0]
    cases = strain_ref.shape[1] // 2
    for n in range(count):
        c = [cols_ref[k, n] for k in range(4)]
        near = jnp.concatenate(
            [low_ref[c[0]] + high_ref[c[1]], low_ref[c[2]] + high_ref[c[3]]], axis=1
        )
        both = dot_nt(near, stiff_ref[n])
        both = both[:cases] + both[cases:]
        strain_ref[n] = stack2(both + pltpu.roll(both, LANES // 2, 1))


def transposed_sums(cols_ref, stiff_ref, strain_ref, sums):
    count = stiff_ref.shape[0]
    cases = strain_ref.shape[1] // 2
    for ref in sums:
        ref[...] = jnp.zeros_like(ref)
    for n in range(count):
        c = [cols_ref[k, n] for k in range(4)]
        both = dot_nn(strain_ref[n], stiff_ref[n])
        both = both[:cases] + both[cases:]
        left, right = both[:, :LANES], both[:, LANES:]
        sums[0][c[0]] += left
        sums[1][c[1]] += left
        sums[0][c[2]] += right
        sums[1][c[3]] += right


def folded_tile(sums, j):
    cases = sums[0].shape[1]
    in_low = iota((cases, LANES), 1) < LANES // 2
    even, odd = 2 * j, 2 * j + 1
    straight = jnp.where(in_low, sums[0][even], sums[1][odd])
    crossed = jnp.where(in_low, sums[0][odd], sums[1][even])
    return straight + pltpu.roll(crossed, LANES // 2, 1)


def operator_body(
    cols_ref, field_ref, mass_ref, trace_ref, stiff_ref, out_ref, own_ref, low_ref, high_ref, strain_ref, *sums
):
    spread_blocks(field_ref, low_ref, high_ref)
    strain_rows(cols_ref, stiff_ref, low_ref, high_ref, strain_ref)
    transposed_sums(cols_ref, stiff_ref, strain_ref, sums)
    dofs = field_ref.shape[1]
    for j in range(dofs // LANES):
        at = slice(j * LANES, (j + 1) * LANES)
        out_ref[:, at] = field_ref[:, at] * mass_ref[:, at] + folded_tile(sums, j)
    trace = trace_ref[...]
    own_ref[...] = gather_slots(
        out_ref[...], one_hot_low(trace & (WIDE - 1), trace.shape[1]), trace >> 8, dofs // WIDE
    )


def coincidence(trace_ref, match_trace_ref, out_ref):
    slots = trace_ref.shape[1]
    rows = [trace_ref[...].astype(F32), match_trace_ref[...]]
    for i in range(slots // LANES):
        at = slice(i * LANES, (i + 1) * LANES)
        total = jnp.zeros((LANES, slots), F32)
        for row in rows:
            column = jnp.broadcast_to(row[:, at], (LANES, LANES)).T
            total += (jnp.broadcast_to(column[:, :1], (LANES, slots)) == row).astype(F32)
        out_ref[at, :] = total.astype(BF16)


def add_rows(base, rows, one_hot, group):
    cases, dofs = base.shape
    groups = dofs // WIDE
    sums = dot_nt(masked_groups(stack2(rows), group, groups), one_hot)
    pieces = []
    for g in range(groups):
        row = g * 2 * cases
        pieces.append(
            base[:, g * WIDE:(g + 1) * WIDE]
            + (sums[row:row + cases] + sums[row + cases:row + 2 * cases])
        )
    return jnp.concatenate(pieces, axis=1)


def first_image(
    cols_ref, field_ref, part_ref, own_ref, match_ref, pen_ref, match_pen_ref, trace_ref, mass_ref, same_ref, stiff_ref,
    image_ref, shift_ref, gram_ref, strain_ref, low_ref, high_ref,
):
    cases, dofs = field_ref.shape
    trace = trace_ref[...]
    weight = pen_ref[...] * match_pen_ref[...]
    jump = weight * (own_ref[...] - match_ref[...])
    image_ref[...] = add_rows(
        part_ref[...], jump, one_hot_low(trace & (WIDE - 1), trace.shape[1]), trace >> 8
    )
    moved = dot_nn(stack2(jump), same_ref[...])
    shift_ref[...] = moved[:cases] + moved[cases:]
    spread_blocks(image_ref, low_ref, high_ref)
    strain_rows(cols_ref, stiff_ref, low_ref, high_ref, strain_ref)
    in_low = iota((2 * cases, LANES), 1) < LANES // 2
    strain = jnp.concatenate(
        [
            jnp.where(in_low, strain_ref[2 * j].astype(F32), strain_ref[2 * j + 1].astype(F32)).astype(BF16)
            for j in range(strain_ref.shape[0] // 2)
        ],
        axis=1,
    )
    image = image_ref[...]
    image_rows = stack2(image)
    rows = jnp.concatenate([stack2(field_ref[...]), image_rows], axis=0)
    every = dot_nt(rows, image_rows)
    every = every[:, :cases] + every[:, cases:]
    cross = every[:cases] + every[cases:2 * cases]
    square = every[2 * cases:3 * cases] + every[3 * cases:]
    start = dot_nt(rows[:2 * cases], rows[:2 * cases])
    start = start[:, :cases] + start[:, cases:]
    start = start[:cases] + start[cases:]
    last = dot_nt(image_rows, stack2(image * mass_ref[...])) + dot_nt(strain, strain)
    last = last[:, :cases] + last[:, cases:]
    last = last[:cases] + last[cases:]
    gram_ref[...] = jnp.concatenate([cross, start, square, last], axis=1)


def gram_trace(gram_ref, own_ref, match_ref, shift_ref, pen_ref, match_pen_ref, out_ref, jump_ref):
    cases = gram_ref.shape[0]
    apart = (own_ref[...] - match_ref[...]) + shift_ref[...]
    jump = (pen_ref[...] * match_pen_ref[...]) * apart
    jump_ref[...] = jump
    more = dot_nt(stack2(0.5 * apart), stack2(jump))
    more = more[:, :cases] + more[:, cases:]
    more = more[:cases] + more[cases:]
    zeros = jnp.zeros((cases, 3 * cases), F32)
    out_ref[...] = gram_ref[...] + jnp.concatenate([zeros, more], axis=1)


def second_image(
    cols_ref, field_ref, image_ref, mass_ref, stiff_ref, strain_ref, jump_ref, trace_ref, out_ref, *sums
):
    transposed_sums(cols_ref, stiff_ref, strain_ref, sums)
    trace = trace_ref[...]
    one_hot = one_hot_low(trace & (WIDE - 1), trace.shape[1])
    folded = jnp.concatenate(
        [folded_tile(sums, j) for j in range(image_ref.shape[1] // LANES)], axis=1
    )
    image = image_ref[...]
    rows = 2 * image.shape[0]
    second = add_rows(image * mass_ref[...] + folded, jump_ref[...], one_hot, trace >> 8)
    for i, part in enumerate((field_ref[...], image, second)):
        out_ref[i * rows:(i + 1) * rows, :] = stack2(part)
    out_ref[3 * rows:, :] = jnp.zeros((out_ref.shape[0] - 3 * rows, out_ref.shape[1]), BF16)


def eliminate(matrix, size, group=8):
    rows = iota(matrix.shape, 0)
    for first in range(0, size, group):
        columns = [
            jnp.broadcast_to(matrix[:, p:p + 1], matrix.shape) for p in range(first, first + group)
        ]
        for q in range(group):
            p = first + q
            column = columns[q]
            inverse = 1.0 / column[p:p + 1]
            row = matrix[p:p + 1] * inverse
            here = rows == p
            matrix = jnp.where(here, row, matrix - column * row)
            for r in range(q + 1, group):
                entry = column[first + r:first + r + 1] * inverse
                columns[r] = jnp.where(here, entry, columns[r] - column * entry)
    return matrix


def small_dot(a, b):
    return jnp.dot(a, b, precision=lax.Precision.HIGHEST, preferred_element_type=F32)


def finish(*refs):
    *gram_refs, field_ref, rows_ref, solution_ref, residual_ref = refs
    cases = field_ref.shape[0]
    gram = sum_of([ref[...] for ref in gram_refs])
    square = gram[:, 2 * cases:3 * cases]
    solved = eliminate(gram, cases)
    zeros = jnp.zeros((cases, 2 * cases), F32)
    given = jnp.concatenate([gram[:, 3 * cases:], gram[:, :cases]], axis=1)
    both = jnp.concatenate([solved[:, 2 * cases:3 * cases], solved[:, cases:2 * cases]], axis=1)
    second_part = eliminate(
        jnp.concatenate([given - small_dot(square, both), zeros], axis=1), cases
    )[:, cases:2 * cases]
    first_part = both[:, cases:] - small_dot(both[:, :cases], second_part)
    zero = jnp.zeros((cases, cases), F32)
    blocks = [[first_part, zero], [second_part, -first_part], [zero, -second_part], [zero, zero]]
    weights = [jnp.concatenate(block + [zero, zero], axis=1) for block in blocks]
    weights = jnp.concatenate([weights[i // 2] for i in range(8)], axis=0)
    weights = jnp.concatenate([weights[:LANES].T, weights[LANES:].T], axis=1)[:2 * cases]
    out = dot_nn(stack2(weights), rows_ref[...])
    out = out[:2 * cases] + out[2 * cases:]
    solution_ref[...] = out[:cases]
    residual_ref[...] = field_ref[...] + out[cases:]


def sum_of(terms):
    while len(terms) > 1:
        terms = [sum(terms[i:i + 2][1:], terms[i]) for i in range(0, len(terms), 2)]
    return terms[0]


def from_all(array, axis, stride=1, radix=None):
    count = lax.axis_size(axis)
    radix = radix or count
    span = stride * radix

    def target(i, by):
        digit = i // stride % radix
        return i // span * span + (digit + by) % radix * stride + i % stride

    return [array] + [
        lax.ppermute(array, axis, [(i, target(i, by)) for i in range(count)])
        for by in range(1, radix)
    ]


def digits(count):
    stages, stride = [], 1
    while stride < count:
        left = count // stride
        radix = 2 if stride == 1 and left % 2 == 0 else 4 if left % 4 == 0 else left
        stages.append((stride, radix))
        stride *= radix
    return stages


def run(body, outs, args, scratch=(), scalars=0, cost=None, far=0):
    whole = pl.BlockSpec(memory_space=pltpu.VMEM)
    args = [
        pltpu.with_memory_space_constraint(arg, pltpu.HBM) if scalars <= i < scalars + far else arg
        for i, arg in enumerate(args)
    ]
    return pl.pallas_call(
        body,
        out_shape=outs,
        in_specs=[pl.BlockSpec(memory_space=pltpu.SMEM)] * scalars
        + [pl.BlockSpec(memory_space=pltpu.HBM)] * far
        + [whole] * (len(args) - scalars - far),
        out_specs=jax.tree.map(lambda _: whole, outs),
        scratch_shapes=list(scratch),
        compiler_params=pltpu.CompilerParams(vmem_limit_bytes=VMEM_BYTES),
        cost_estimate=cost,
    )(*args)


def shards(
    load_cases,
    mass_diag,
    stiffness,
    block_cols,
    trace_dofs,
    penalty,
    cell_partials,
    cell_owner,
    cell_dof,
):
    cases, dofs = load_cases.shape
    count, blk, width = stiffness.shape
    cells = cell_partials.shape[1]
    slots = trace_dofs.shape[0]
    patches = lax.axis_size("patch")
    cap = 4 * cells // patches
    rows = cases + 8
    far_rows = cases + -(-(1 + 2 * (slots // cap)) // 8) * 8
    shape = jax.ShapeDtypeStruct
    field_shape = shape((cases, dofs), F32)
    slot_shape = shape((cases, slots), F32)
    mass = mass_diag.reshape(1, dofs)
    trace = trace_dofs.reshape(1, slots)
    pen = penalty.reshape(1, slots)
    cols = block_cols.T

    half = patches // 2
    pairs = [(i, (i + half) % patches) for i in range(patches)]
    packets = run(
        pack_cells,
        [shape((far_rows if by == half else rows, cap), F32) for by in range(patches)],
        (cell_partials, cell_owner.reshape(1, cells), cell_dof.reshape(1, cells), pen, trace),
        scratch=[
            pltpu.VMEM((cases, cells), F32),
            pltpu.VMEM((1, cells), jnp.int32),
            pltpu.VMEM((1, cells), jnp.int32),
            pltpu.VMEM((1, slots), F32),
            pltpu.VMEM((1, slots), jnp.int32),
            pltpu.SemaphoreType.DMA((5,)),
        ],
        far=5,
    )
    order = [0, 1, 2, half, *(by for by in range(3, patches) if by != half)]
    received = [packets[0]] + [
        lax.ppermute(packets[by], "patch", [(i, (i + by) % patches) for i in range(patches)])
        for by in order[1:]
    ]
    far, first = received[3], 5 * patches // 8
    base, stiff = run(
        early_cells,
        (field_shape, shape((count, 2 * blk, width), BF16)),
        (stiffness, load_cases, *received[:first]),
        scratch=[
            pltpu.VMEM((cases, dofs), F32),
            pltpu.VMEM(stiffness.shape, F32),
            pltpu.SemaphoreType.DMA((2,)),
        ],
        cost=pl.CostEstimate(flops=8 * stiffness.size, bytes_accessed=8 * stiffness.size, transcendentals=0),
        far=2,
    )
    late, base, stiff, cols, mass, trace = lax.optimization_barrier(
        (received[first:], base, stiff, cols, mass, trace)
    )

    spread = [pltpu.VMEM((dofs // blk, 2 * cases, LANES), BF16)] * 2
    strain_scratch = pltpu.VMEM((count, 2 * cases, LANES), BF16)
    sums = [pltpu.VMEM((dofs // blk, cases, LANES), F32)] * 2

    row_shape = shape((1, slots), F32)
    field, own, match_pen, match_trace = run(
        assemble, (field_shape, slot_shape, row_shape, row_shape), (base, trace, far, *late)
    )
    match = lax.ppermute(own, "patch", pairs)
    part, part_own = run(
        operator_body,
        (field_shape, slot_shape),
        (cols, field, mass, trace, stiff),
        scratch=[*spread, strain_scratch, *sums],
        scalars=1,
    )
    same = run(coincidence, shape((slots, slots), BF16), (trace, match_trace))
    part_own, same = lax.optimization_barrier((part_own, same))
    part_match = lax.ppermute(part_own, "patch", pairs)
    image, shift, gram, strain = run(
        first_image,
        (
            field_shape,
            slot_shape,
            shape((cases, 4 * cases), F32),
            shape((count, 2 * cases, LANES), BF16),
        ),
        (cols, field, part, own, match, pen, match_pen, trace, mass, same, stiff),
        scratch=spread,
        scalars=1,
    )
    gram, jump = run(
        gram_trace,
        (shape((cases, 4 * cases), F32), slot_shape),
        (gram, part_own, part_match, shift, pen, match_pen),
    )
    for stride, radix in reversed(digits(patches)):
        gram = sum_of(from_all(gram, "patch", stride, radix))
    stacked = run(
        second_image,
        shape((-(-6 * cases // LANES) * LANES, dofs), BF16),
        (cols, field, image, mass, stiff, strain, jump, trace),
        scratch=sums,
        scalars=1,
    )
    gram, stacked = lax.optimization_barrier((gram, stacked))
    grams = from_all(gram, "comp")
    grams = [grams[0], *grams[2::2], *grams[1::2]]
    return run(finish, (field_shape, field_shape), (*grams, field, stacked))


def solution(mesh):
    return jax.shard_map(
        shards,
        mesh=mesh,
        in_specs=(
            P(None, ("comp", "patch")),
            P(("comp", "patch")),
            P(("comp", "patch"), None, None),
            P(("comp", "patch"), None),
            P(("comp", "patch")),
            P(("comp", "patch")),
            P(None, ("comp", "patch")),
            P(("comp", "patch"), None),
            P(("comp", "patch")),
        ),
        out_specs=(P(None, ("comp", "patch")), P(None, ("comp", "patch"))),
        check_vma=False,
    )
```

```python
import jax
import jax.numpy as jnp
from jax import lax
from jax.experimental import pallas as pl
from jax.experimental.pallas import tpu as pltpu
from jax.sharding import PartitionSpec as P

F32 = jnp.float32
BF16 = jnp.bfloat16
WIDE = 256
LANES = 128
VMEM_BYTES = 32 * 1024 * 1024


def split2(x):
    high = x.astype(BF16)
    low = (x - high.astype(F32)).astype(BF16)
    return high, low


def stack2(x):
    return jnp.concatenate(split2(x), axis=0)


def dot_nn(a, b):
    return lax.dot_general(a, b, (((1,), (0,)), ((), ())), preferred_element_type=F32)


def dot_nt(a, b):
    return lax.dot_general(a, b, (((1,), (1,)), ((), ())), preferred_element_type=F32)


def iota(shape, axis):
    return lax.broadcasted_iota(jnp.int32, shape, axis)


def one_hot_low(low, width):
    return (iota((WIDE, width), 0) == low).astype(F32).astype(BF16)


def masked_groups(stacked, group, count):
    parts = []
    for g in range(count):
        mask = (group == g).astype(F32).astype(BF16)
        parts.append(stacked * jnp.broadcast_to(mask, stacked.shape))
    return jnp.concatenate(parts, axis=0)


def gather_slots(field, one_hot, group, groups):
    cases = field.shape[0]
    rows = jnp.concatenate(
        [stack2(field[:, g * WIDE:(g + 1) * WIDE]) for g in range(groups)], axis=0
    )
    found = dot_nn(rows, one_hot)
    total = jnp.zeros((cases, group.shape[1]), F32)
    for g in range(groups):
        base = g * 2 * cases
        both = found[base:base + cases] + found[base + cases:base + 2 * cases]
        total = jnp.where(group == g, both, total)
    return total


def pack_cells(*refs):
    sources, out_refs, targets, sems = refs[:5], refs[5:-6], refs[-6:-1], refs[-1]
    copies = [
        pltpu.make_async_copy(source, target, sems.at[i])
        for i, (source, target) in enumerate(zip(sources, targets))
    ]
    for copy in copies:
        copy.start()
    partials_ref, owner_ref, dof_ref, pen_ref, trace_ref = targets
    patches = len(out_refs)
    rows, cap = out_refs[0].shape
    cases, cells = partials_ref.shape
    me = lax.axis_index("patch")
    before = (iota((cells, cells), 0) < iota((cells, cells), 1)).astype(F32).astype(BF16)
    for copy in copies[1:]:
        copy.wait()
    shift = owner_ref[...] - me
    shift = jnp.where(shift < 0, shift + patches, shift)
    mine = (iota((patches, cells), 0) == shift).astype(F32)
    counts = dot_nn(mine.astype(BF16), before)
    rank = jnp.sum(mine * counts, axis=0, keepdims=True).astype(jnp.int32)
    extra = jnp.where(iota((rows - cases, cells), 0) == 0, dof_ref[...] + 1, 0).astype(F32)
    copies[0].wait()
    body = stack2(jnp.concatenate([partials_ref[...], extra], axis=0))
    for by, out_ref in enumerate(out_refs):
        key = jnp.where(shift == by, rank, -1)
        pick = (iota((cap, cells), 0) == key).astype(F32).astype(BF16)
        packed = dot_nt(body, pick)
        out_ref[:rows, :] = packed[:rows] + packed[rows:]
        if by == patches // 2:
            more = pen_ref.shape[1] // cap
            for i in range(more):
                at = cases + 1 + i
                out_ref[at:at + 1, :] = pen_ref[:, i * cap:(i + 1) * cap]
                out_ref[at + more:at + more + 1, :] = trace_ref[:, i * cap:(i + 1) * cap].astype(F32)


def add_cells(base, packet_refs):
    cases, dofs = base.shape
    groups = dofs // WIDE
    cells = jnp.concatenate([ref[:cases + 8, :] for ref in packet_refs], axis=1)
    slots = cells.shape[1]
    dof = cells[cases:cases + 1].astype(jnp.int32) - 1
    low = jnp.where(dof < 0, -1, dof & (WIDE - 1))
    return add_rows(base, cells[:cases], one_hot_low(low, slots), dof >> 8)


def early_cells(stiff_ref, load_ref, *refs):
    *packet_refs, field_ref, split_ref, load_copy_ref, wide_ref, sems = refs
    load_copy = pltpu.make_async_copy(load_ref, load_copy_ref, sems.at[0])
    load_copy.start()
    copy = pltpu.make_async_copy(stiff_ref, wide_ref, sems.at[1])
    copy.start()
    load_copy.wait()
    field_ref[...] = add_cells(load_copy_ref[...], packet_refs)
    copy.wait()
    blk = stiff_ref.shape[1]
    high, low = split2(wide_ref[...])
    split_ref[:, :blk, :] = high
    split_ref[:, blk:, :] = low


def assemble(base_ref, trace_ref, far_ref, *refs):
    *packet_refs, field_ref, own_ref, pen_ref, match_trace_ref = refs
    cases, dofs = base_ref.shape
    cap = far_ref.shape[1]
    more = pen_ref.shape[1] // cap
    for i in range(more):
        at = cases + 1 + i
        pen_ref[:, i * cap:(i + 1) * cap] = far_ref[at:at + 1, :]
        match_trace_ref[:, i * cap:(i + 1) * cap] = far_ref[at + more:at + more + 1, :]
    field = add_cells(base_ref[...], packet_refs)
    field_ref[...] = field
    trace = trace_ref[...]
    own_ref[...] = gather_slots(
        field, one_hot_low(trace & (WIDE - 1), trace.shape[1]), trace >> 8, dofs // WIDE
    )


def spread_blocks(field_ref, low_ref, high_ref):
    cases, dofs = field_ref.shape
    in_low = iota((cases, LANES), 1) < LANES // 2
    for j in range(dofs // LANES):
        tile = field_ref[:, j * LANES:(j + 1) * LANES]
        turned = pltpu.roll(tile, LANES // 2, 1)
        low_ref[2 * j] = stack2(jnp.where(in_low, tile, 0.0))
        high_ref[2 * j + 1] = stack2(jnp.where(in_low, 0.0, tile))
        low_ref[2 * j + 1] = stack2(jnp.where(in_low, turned, 0.0))
        high_ref[2 * j] = stack2(jnp.where(in_low, 0.0, turned))


def strain_rows(cols_ref, stiff_ref, low_ref, high_ref, strain_ref):
    count = stiff_ref.shape[0]
    cases = strain_ref.shape[1] // 2
    for n in range(count):
        c = [cols_ref[k, n] for k in range(4)]
        near = jnp.concatenate(
            [low_ref[c[0]] + high_ref[c[1]], low_ref[c[2]] + high_ref[c[3]]], axis=1
        )
        both = dot_nt(near, stiff_ref[n])
        both = both[:cases] + both[cases:]
        strain_ref[n] = stack2(both + pltpu.roll(both, LANES // 2, 1))


def transposed_sums(cols_ref, stiff_ref, strain_ref, sums):
    count = stiff_ref.shape[0]
    cases = strain_ref.shape[1] // 2
    for ref in sums:
        ref[...] = jnp.zeros_like(ref)
    for n in range(count):
        c = [cols_ref[k, n] for k in range(4)]
        both = dot_nn(strain_ref[n], stiff_ref[n])
        both = both[:cases] + both[cases:]
        left, right = both[:, :LANES], both[:, LANES:]
        sums[0][c[0]] += left
        sums[1][c[1]] += left
        sums[0][c[2]] += right
        sums[1][c[3]] += right


def folded_tile(sums, j):
    cases = sums[0].shape[1]
    in_low = iota((cases, LANES), 1) < LANES // 2
    even, odd = 2 * j, 2 * j + 1
    straight = jnp.where(in_low, sums[0][even], sums[1][odd])
    crossed = jnp.where(in_low, sums[0][odd], sums[1][even])
    return straight + pltpu.roll(crossed, LANES // 2, 1)


def operator_body(
    cols_ref, field_ref, mass_ref, trace_ref, stiff_ref, out_ref, own_ref, low_ref, high_ref, strain_ref, *sums
):
    spread_blocks(field_ref, low_ref, high_ref)
    strain_rows(cols_ref, stiff_ref, low_ref, high_ref, strain_ref)
    transposed_sums(cols_ref, stiff_ref, strain_ref, sums)
    dofs = field_ref.shape[1]
    for j in range(dofs // LANES):
        at = slice(j * LANES, (j + 1) * LANES)
        out_ref[:, at] = field_ref[:, at] * mass_ref[:, at] + folded_tile(sums, j)
    trace = trace_ref[...]
    own_ref[...] = gather_slots(
        out_ref[...], one_hot_low(trace & (WIDE - 1), trace.shape[1]), trace >> 8, dofs // WIDE
    )


def coincidence(trace_ref, match_trace_ref, out_ref):
    slots = trace_ref.shape[1]
    rows = [trace_ref[...].astype(F32), match_trace_ref[...]]
    for i in range(slots // LANES):
        at = slice(i * LANES, (i + 1) * LANES)
        total = jnp.zeros((LANES, slots), F32)
        for row in rows:
            column = jnp.broadcast_to(row[:, at], (LANES, LANES)).T
            total += (jnp.broadcast_to(column[:, :1], (LANES, slots)) == row).astype(F32)
        out_ref[at, :] = total.astype(BF16)


def add_rows(base, rows, one_hot, group):
    cases, dofs = base.shape
    groups = dofs // WIDE
    sums = dot_nt(masked_groups(stack2(rows), group, groups), one_hot)
    pieces = []
    for g in range(groups):
        row = g * 2 * cases
        pieces.append(
            base[:, g * WIDE:(g + 1) * WIDE]
            + (sums[row:row + cases] + sums[row + cases:row + 2 * cases])
        )
    return jnp.concatenate(pieces, axis=1)


def first_image(
    cols_ref, field_ref, part_ref, own_ref, match_ref, pen_ref, match_pen_ref, trace_ref, mass_ref, same_ref, stiff_ref,
    image_ref, shift_ref, gram_ref, strain_ref, low_ref, high_ref,
):
    cases, dofs = field_ref.shape
    trace = trace_ref[...]
    weight = pen_ref[...] * match_pen_ref[...]
    jump = weight * (own_ref[...] - match_ref[...])
    image_ref[...] = add_rows(
        part_ref[...], jump, one_hot_low(trace & (WIDE - 1), trace.shape[1]), trace >> 8
    )
    moved = dot_nn(stack2(jump), same_ref[...])
    shift_ref[...] = moved[:cases] + moved[cases:]
    spread_blocks(image_ref, low_ref, high_ref)
    strain_rows(cols_ref, stiff_ref, low_ref, high_ref, strain_ref)
    in_low = iota((2 * cases, LANES), 1) < LANES // 2
    strain = jnp.concatenate(
        [
            jnp.where(in_low, strain_ref[2 * j].astype(F32), strain_ref[2 * j + 1].astype(F32)).astype(BF16)
            for j in range(strain_ref.shape[0] // 2)
        ],
        axis=1,
    )
    image = image_ref[...]
    image_rows = stack2(image)
    rows = jnp.concatenate([stack2(field_ref[...]), image_rows], axis=0)
    every = dot_nt(rows, image_rows)
    every = every[:, :cases] + every[:, cases:]
    cross = every[:cases] + every[cases:2 * cases]
    square = every[2 * cases:3 * cases] + every[3 * cases:]
    start = dot_nt(rows[:2 * cases], rows[:2 * cases])
    start = start[:, :cases] + start[:, cases:]
    start = start[:cases] + start[cases:]
    last = dot_nt(image_rows, stack2(image * mass_ref[...])) + dot_nt(strain, strain)
    last = last[:, :cases] + last[:, cases:]
    last = last[:cases] + last[cases:]
    gram_ref[...] = jnp.concatenate([cross, start, square, last], axis=1)


def gram_trace(gram_ref, own_ref, match_ref, shift_ref, pen_ref, match_pen_ref, out_ref, jump_ref):
    cases = gram_ref.shape[0]
    apart = (own_ref[...] - match_ref[...]) + shift_ref[...]
    jump = (pen_ref[...] * match_pen_ref[...]) * apart
    jump_ref[...] = jump
    more = dot_nt(stack2(0.5 * apart), stack2(jump))
    more = more[:, :cases] + more[:, cases:]
    more = more[:cases] + more[cases:]
    zeros = jnp.zeros((cases, 3 * cases), F32)
    out_ref[...] = gram_ref[...] + jnp.concatenate([zeros, more], axis=1)


def second_image(
    cols_ref, field_ref, image_ref, mass_ref, stiff_ref, strain_ref, jump_ref, trace_ref, out_ref, *sums
):
    transposed_sums(cols_ref, stiff_ref, strain_ref, sums)
    trace = trace_ref[...]
    one_hot = one_hot_low(trace & (WIDE - 1), trace.shape[1])
    folded = jnp.concatenate(
        [folded_tile(sums, j) for j in range(image_ref.shape[1] // LANES)], axis=1
    )
    image = image_ref[...]
    rows = 2 * image.shape[0]
    second = add_rows(image * mass_ref[...] + folded, jump_ref[...], one_hot, trace >> 8)
    for i, part in enumerate((field_ref[...], image, second)):
        out_ref[i * rows:(i + 1) * rows, :] = stack2(part)
    out_ref[3 * rows:, :] = jnp.zeros((out_ref.shape[0] - 3 * rows, out_ref.shape[1]), BF16)


def eliminate(matrix, size, group=8):
    rows = iota(matrix.shape, 0)
    for first in range(0, size, group):
        columns = [
            jnp.broadcast_to(matrix[:, p:p + 1], matrix.shape) for p in range(first, first + group)
        ]
        for q in range(group):
            p = first + q
            column = columns[q]
            inverse = pl.reciprocal(column[p:p + 1])
            row = matrix[p:p + 1] * inverse
            here = rows == p
            matrix = jnp.where(here, row, matrix - column * row)
            for r in range(q + 1, group):
                entry = column[first + r:first + r + 1] * inverse
                columns[r] = jnp.where(here, entry, columns[r] - column * entry)
    return matrix


def small_dot(a, b):
    return jnp.dot(a, b, precision=lax.Precision.HIGHEST, preferred_element_type=F32)


def finish(*refs):
    *gram_refs, field_ref, rows_ref, solution_ref, residual_ref = refs
    cases = field_ref.shape[0]
    gram = sum_of([ref[...] for ref in gram_refs])
    square = gram[:, 2 * cases:3 * cases]
    solved = eliminate(gram, cases)
    zeros = jnp.zeros((cases, 2 * cases), F32)
    given = jnp.concatenate([gram[:, 3 * cases:], gram[:, :cases]], axis=1)
    both = jnp.concatenate([solved[:, 2 * cases:3 * cases], solved[:, cases:2 * cases]], axis=1)
    second_part = eliminate(
        jnp.concatenate([given - small_dot(square, both), zeros], axis=1), cases
    )[:, cases:2 * cases]
    first_part = both[:, cases:] - small_dot(both[:, :cases], second_part)
    zero = jnp.zeros((cases, cases), F32)
    blocks = [[first_part, zero], [second_part, -first_part], [zero, -second_part], [zero, zero]]
    weights = [jnp.concatenate(block + [zero, zero], axis=1) for block in blocks]
    weights = jnp.concatenate([weights[i // 2] for i in range(8)], axis=0)
    weights = jnp.concatenate([weights[:LANES].T, weights[LANES:].T], axis=1)[:2 * cases]
    out = dot_nn(stack2(weights), rows_ref[...])
    out = out[:2 * cases] + out[2 * cases:]
    solution_ref[...] = out[:cases]
    residual_ref[...] = field_ref[...] + out[cases:]


def sum_of(terms):
    while len(terms) > 1:
        terms = [sum(terms[i:i + 2][1:], terms[i]) for i in range(0, len(terms), 2)]
    return terms[0]


def from_all(array, axis, stride=1, radix=None):
    count = lax.axis_size(axis)
    radix = radix or count
    span = stride * radix

    def target(i, by):
        digit = i // stride % radix
        return i // span * span + (digit + by) % radix * stride + i % stride

    return [array] + [
        lax.ppermute(array, axis, [(i, target(i, by)) for i in range(count)])
        for by in range(1, radix)
    ]


def digits(count):
    stages, stride = [], 1
    while stride < count:
        left = count // stride
        radix = 2 if stride == 1 and left % 2 == 0 else 4 if left % 4 == 0 else left
        stages.append((stride, radix))
        stride *= radix
    return stages


def run(body, outs, args, scratch=(), scalars=0, cost=None, far=0):
    whole = pl.BlockSpec(memory_space=pltpu.VMEM)
    args = [
        pltpu.with_memory_space_constraint(arg, pltpu.HBM) if scalars <= i < scalars + far else arg
        for i, arg in enumerate(args)
    ]
    return pl.pallas_call(
        body,
        out_shape=outs,
        in_specs=[pl.BlockSpec(memory_space=pltpu.SMEM)] * scalars
        + [pl.BlockSpec(memory_space=pltpu.HBM)] * far
        + [whole] * (len(args) - scalars - far),
        out_specs=jax.tree.map(lambda _: whole, outs),
        scratch_shapes=list(scratch),
        compiler_params=pltpu.CompilerParams(vmem_limit_bytes=VMEM_BYTES),
        cost_estimate=cost,
    )(*args)


def shards(
    load_cases,
    mass_diag,
    stiffness,
    block_cols,
    trace_dofs,
    penalty,
    cell_partials,
    cell_owner,
    cell_dof,
):
    cases, dofs = load_cases.shape
    count, blk, width = stiffness.shape
    cells = cell_partials.shape[1]
    slots = trace_dofs.shape[0]
    patches = lax.axis_size("patch")
    cap = 4 * cells // patches
    rows = cases + 8
    far_rows = cases + -(-(1 + 2 * (slots // cap)) // 8) * 8
    shape = jax.ShapeDtypeStruct
    field_shape = shape((cases, dofs), F32)
    slot_shape = shape((cases, slots), F32)
    mass = mass_diag.reshape(1, dofs)
    trace = trace_dofs.reshape(1, slots)
    pen = penalty.reshape(1, slots)
    cols = block_cols.T

    half = patches // 2
    pairs = [(i, (i + half) % patches) for i in range(patches)]
    packets = run(
        pack_cells,
        [shape((far_rows if by == half else rows, cap), F32) for by in range(patches)],
        (cell_partials, cell_owner.reshape(1, cells), cell_dof.reshape(1, cells), pen, trace),
        scratch=[
            pltpu.VMEM((cases, cells), F32),
            pltpu.VMEM((1, cells), jnp.int32),
            pltpu.VMEM((1, cells), jnp.int32),
            pltpu.VMEM((1, slots), F32),
            pltpu.VMEM((1, slots), jnp.int32),
            pltpu.SemaphoreType.DMA((5,)),
        ],
        far=5,
    )
    order = [0, 1, 2, half, *(by for by in range(3, patches) if by != half)]
    received = [packets[0]] + [
        lax.ppermute(packets[by], "patch", [(i, (i + by) % patches) for i in range(patches)])
        for by in order[1:]
    ]
    far, first = received[3], 5 * patches // 8
    base, stiff = run(
        early_cells,
        (field_shape, shape((count, 2 * blk, width), BF16)),
        (stiffness, load_cases, *received[:first]),
        scratch=[
            pltpu.VMEM((cases, dofs), F32),
            pltpu.VMEM(stiffness.shape, F32),
            pltpu.SemaphoreType.DMA((2,)),
        ],
        cost=pl.CostEstimate(flops=8 * stiffness.size, bytes_accessed=8 * stiffness.size, transcendentals=0),
        far=2,
    )
    late, base, stiff, cols, mass, trace = lax.optimization_barrier(
        (received[first:], base, stiff, cols, mass, trace)
    )

    spread = [pltpu.VMEM((dofs // blk, 2 * cases, LANES), BF16)] * 2
    strain_scratch = pltpu.VMEM((count, 2 * cases, LANES), BF16)
    sums = [pltpu.VMEM((dofs // blk, cases, LANES), F32)] * 2

    row_shape = shape((1, slots), F32)
    field, own, match_pen, match_trace = run(
        assemble, (field_shape, slot_shape, row_shape, row_shape), (base, trace, far, *late)
    )
    match = lax.ppermute(own, "patch", pairs)
    part, part_own = run(
        operator_body,
        (field_shape, slot_shape),
        (cols, field, mass, trace, stiff),
        scratch=[*spread, strain_scratch, *sums],
        scalars=1,
    )
    same = run(coincidence, shape((slots, slots), BF16), (trace, match_trace))
    part_own, same = lax.optimization_barrier((part_own, same))
    part_match = lax.ppermute(part_own, "patch", pairs)
    image, shift, gram, strain = run(
        first_image,
        (
            field_shape,
            slot_shape,
            shape((cases, 4 * cases), F32),
            shape((count, 2 * cases, LANES), BF16),
        ),
        (cols, field, part, own, match, pen, match_pen, trace, mass, same, stiff),
        scratch=spread,
        scalars=1,
    )
    gram, jump = run(
        gram_trace,
        (shape((cases, 4 * cases), F32), slot_shape),
        (gram, part_own, part_match, shift, pen, match_pen),
    )
    for stride, radix in reversed(digits(patches)):
        gram = sum_of(from_all(gram, "patch", stride, radix))
    stacked = run(
        second_image,
        shape((-(-6 * cases // LANES) * LANES, dofs), BF16),
        (cols, field, image, mass, stiff, strain, jump, trace),
        scratch=sums,
        scalars=1,
    )
    gram, stacked = lax.optimization_barrier((gram, stacked))
    comps = lax.axis_size("comp")
    grams = [gram] + [
        lax.ppermute(gram, "comp", [(i, i ^ by) for i in range(comps)]) for by in range(1, comps)
    ]
    grams = [grams[0], *grams[2::2], *grams[1::2]]
    return run(finish, (field_shape, field_shape), (*grams, field, stacked))


def solution(mesh):
    return jax.shard_map(
        shards,
        mesh=mesh,
        in_specs=(
            P(None, ("comp", "patch")),
            P(("comp", "patch")),
            P(("comp", "patch"), None, None),
            P(("comp", "patch"), None),
            P(("comp", "patch")),
            P(("comp", "patch")),
            P(None, ("comp", "patch")),
            P(("comp", "patch"), None),
            P(("comp", "patch")),
        ),
        out_specs=(P(None, ("comp", "patch")), P(None, ("comp", "patch"))),
        check_vma=False,
    )
```

```python
import jax
import jax.numpy as jnp
from jax import lax
from jax.experimental import pallas as pl
from jax.experimental.pallas import tpu as pltpu
from jax.sharding import PartitionSpec as P

F32 = jnp.float32
BF16 = jnp.bfloat16
WIDE = 256
LANES = 128
VMEM_BYTES = 32 * 1024 * 1024


def split2(x):
    high = x.astype(BF16)
    low = (x - high.astype(F32)).astype(BF16)
    return high, low


def stack2(x):
    return jnp.concatenate(split2(x), axis=0)


def dot_nn(a, b):
    return lax.dot_general(a, b, (((1,), (0,)), ((), ())), preferred_element_type=F32)


def dot_nt(a, b):
    return lax.dot_general(a, b, (((1,), (1,)), ((), ())), preferred_element_type=F32)


def iota(shape, axis):
    return lax.broadcasted_iota(jnp.int32, shape, axis)


def one_hot_low(low, width):
    return (iota((WIDE, width), 0) == low).astype(F32).astype(BF16)


def masked_groups(stacked, group, count):
    parts = []
    for g in range(count):
        mask = (group == g).astype(F32).astype(BF16)
        parts.append(stacked * jnp.broadcast_to(mask, stacked.shape))
    return jnp.concatenate(parts, axis=0)


def gather_slots(field, one_hot, group, groups):
    cases = field.shape[0]
    rows = jnp.concatenate(
        [stack2(field[:, g * WIDE:(g + 1) * WIDE]) for g in range(groups)], axis=0
    )
    found = dot_nn(rows, one_hot)
    total = jnp.zeros((cases, group.shape[1]), F32)
    for g in range(groups):
        base = g * 2 * cases
        both = found[base:base + cases] + found[base + cases:base + 2 * cases]
        total = jnp.where(group == g, both, total)
    return total


def pack_cells(*refs):
    sources, out_refs, targets, sems = refs[:5], refs[5:-6], refs[-6:-1], refs[-1]
    copies = [
        pltpu.make_async_copy(source, target, sems.at[i])
        for i, (source, target) in enumerate(zip(sources, targets))
    ]
    for copy in copies:
        copy.start()
    partials_ref, owner_ref, dof_ref, pen_ref, trace_ref = targets
    patches = len(out_refs)
    rows, cap = out_refs[0].shape
    cases, cells = partials_ref.shape
    me = lax.axis_index("patch")
    before = (iota((cells, cells), 0) < iota((cells, cells), 1)).astype(F32).astype(BF16)
    for copy in copies[1:]:
        copy.wait()
    shift = owner_ref[...] - me
    shift = jnp.where(shift < 0, shift + patches, shift)
    mine = (iota((patches, cells), 0) == shift).astype(F32)
    counts = dot_nn(mine.astype(BF16), before)
    rank = jnp.sum(mine * counts, axis=0, keepdims=True).astype(jnp.int32)
    extra = jnp.where(iota((rows - cases, cells), 0) == 0, dof_ref[...] + 1, 0).astype(F32)
    copies[0].wait()
    body = stack2(jnp.concatenate([partials_ref[...], extra], axis=0))
    for by, out_ref in enumerate(out_refs):
        key = jnp.where(shift == by, rank, -1)
        pick = (iota((cap, cells), 0) == key).astype(F32).astype(BF16)
        packed = dot_nt(body, pick)
        out_ref[:rows, :] = packed[:rows] + packed[rows:]
        if by == patches // 2:
            more = pen_ref.shape[1] // cap
            for i in range(more):
                at = cases + 1 + i
                out_ref[at:at + 1, :] = pen_ref[:, i * cap:(i + 1) * cap]
                out_ref[at + more:at + more + 1, :] = trace_ref[:, i * cap:(i + 1) * cap].astype(F32)


def add_cells(base, packet_refs):
    cases, dofs = base.shape
    groups = dofs // WIDE
    cells = jnp.concatenate([ref[:cases + 8, :] for ref in packet_refs], axis=1)
    slots = cells.shape[1]
    dof = cells[cases:cases + 1].astype(jnp.int32) - 1
    low = jnp.where(dof < 0, -1, dof & (WIDE - 1))
    return add_rows(base, cells[:cases], one_hot_low(low, slots), dof >> 8)


def early_cells(stiff_ref, load_ref, *refs):
    *packet_refs, field_ref, split_ref, load_copy_ref, wide_ref, sems = refs
    load_copy = pltpu.make_async_copy(load_ref, load_copy_ref, sems.at[0])
    load_copy.start()
    copy = pltpu.make_async_copy(stiff_ref, wide_ref, sems.at[1])
    copy.start()
    load_copy.wait()
    field_ref[...] = add_cells(load_copy_ref[...], packet_refs)
    copy.wait()
    blk = stiff_ref.shape[1]
    high, low = split2(wide_ref[...])
    split_ref[:, :blk, :] = high
    split_ref[:, blk:, :] = low


def assemble(base_ref, trace_ref, far_ref, *refs):
    *packet_refs, field_ref, own_ref, pen_ref, match_trace_ref = refs
    cases, dofs = base_ref.shape
    cap = far_ref.shape[1]
    more = pen_ref.shape[1] // cap
    for i in range(more):
        at = cases + 1 + i
        pen_ref[:, i * cap:(i + 1) * cap] = far_ref[at:at + 1, :]
        match_trace_ref[:, i * cap:(i + 1) * cap] = far_ref[at + more:at + more + 1, :]
    field = add_cells(base_ref[...], packet_refs)
    field_ref[...] = field
    trace = trace_ref[...]
    own_ref[...] = gather_slots(
        field, one_hot_low(trace & (WIDE - 1), trace.shape[1]), trace >> 8, dofs // WIDE
    )


def spread_blocks(field_ref, low_ref, high_ref):
    cases, dofs = field_ref.shape
    in_low = iota((cases, LANES), 1) < LANES // 2
    for j in range(dofs // LANES):
        tile = field_ref[:, j * LANES:(j + 1) * LANES]
        turned = pltpu.roll(tile, LANES // 2, 1)
        low_ref[2 * j] = stack2(jnp.where(in_low, tile, 0.0))
        high_ref[2 * j + 1] = stack2(jnp.where(in_low, 0.0, tile))
        low_ref[2 * j + 1] = stack2(jnp.where(in_low, turned, 0.0))
        high_ref[2 * j] = stack2(jnp.where(in_low, 0.0, turned))


def strain_rows(cols_ref, stiff_ref, low_ref, high_ref, strain_ref):
    count = stiff_ref.shape[0]
    cases = strain_ref.shape[1] // 2
    for n in range(count):
        c = [cols_ref[k, n] for k in range(4)]
        near = jnp.concatenate(
            [low_ref[c[0]] + high_ref[c[1]], low_ref[c[2]] + high_ref[c[3]]], axis=1
        )
        both = dot_nt(near, stiff_ref[n])
        both = both[:cases] + both[cases:]
        strain_ref[n] = stack2(both + pltpu.roll(both, LANES // 2, 1))


def transposed_sums(cols_ref, stiff_ref, strain_ref, sums):
    count = stiff_ref.shape[0]
    cases = strain_ref.shape[1] // 2
    for ref in sums:
        ref[...] = jnp.zeros_like(ref)
    for n in range(count):
        c = [cols_ref[k, n] for k in range(4)]
        both = dot_nn(strain_ref[n], stiff_ref[n])
        both = both[:cases] + both[cases:]
        left, right = both[:, :LANES], both[:, LANES:]
        sums[0][c[0]] += left
        sums[1][c[1]] += left
        sums[0][c[2]] += right
        sums[1][c[3]] += right


def folded_tile(sums, j):
    cases = sums[0].shape[1]
    in_low = iota((cases, LANES), 1) < LANES // 2
    even, odd = 2 * j, 2 * j + 1
    straight = jnp.where(in_low, sums[0][even], sums[1][odd])
    crossed = jnp.where(in_low, sums[0][odd], sums[1][even])
    return straight + pltpu.roll(crossed, LANES // 2, 1)


def operator_body(
    cols_ref, field_ref, mass_ref, trace_ref, stiff_ref, out_ref, own_ref, low_ref, high_ref, strain_ref, *sums
):
    spread_blocks(field_ref, low_ref, high_ref)
    strain_rows(cols_ref, stiff_ref, low_ref, high_ref, strain_ref)
    transposed_sums(cols_ref, stiff_ref, strain_ref, sums)
    dofs = field_ref.shape[1]
    for j in range(dofs // LANES):
        at = slice(j * LANES, (j + 1) * LANES)
        out_ref[:, at] = field_ref[:, at] * mass_ref[:, at] + folded_tile(sums, j)
    trace = trace_ref[...]
    own_ref[...] = gather_slots(
        out_ref[...], one_hot_low(trace & (WIDE - 1), trace.shape[1]), trace >> 8, dofs // WIDE
    )


def coincidence(trace_ref, match_trace_ref, out_ref):
    slots = trace_ref.shape[1]
    rows = [trace_ref[...].astype(F32), match_trace_ref[...]]
    for i in range(slots // LANES):
        at = slice(i * LANES, (i + 1) * LANES)
        total = jnp.zeros((LANES, slots), F32)
        for row in rows:
            column = jnp.broadcast_to(row[:, at], (LANES, LANES)).T
            total += (jnp.broadcast_to(column[:, :1], (LANES, slots)) == row).astype(F32)
        out_ref[at, :] = total.astype(BF16)


def add_rows(base, rows, one_hot, group):
    cases, dofs = base.shape
    groups = dofs // WIDE
    sums = dot_nt(masked_groups(stack2(rows), group, groups), one_hot)
    pieces = []
    for g in range(groups):
        row = g * 2 * cases
        pieces.append(
            base[:, g * WIDE:(g + 1) * WIDE]
            + (sums[row:row + cases] + sums[row + cases:row + 2 * cases])
        )
    return jnp.concatenate(pieces, axis=1)


def first_image(
    cols_ref, field_ref, part_ref, own_ref, match_ref, pen_ref, match_pen_ref, trace_ref, mass_ref, same_ref, stiff_ref,
    image_ref, shift_ref, gram_ref, strain_ref, low_ref, high_ref,
):
    cases, dofs = field_ref.shape
    trace = trace_ref[...]
    weight = pen_ref[...] * match_pen_ref[...]
    jump = weight * (own_ref[...] - match_ref[...])
    image_ref[...] = add_rows(
        part_ref[...], jump, one_hot_low(trace & (WIDE - 1), trace.shape[1]), trace >> 8
    )
    moved = dot_nn(stack2(jump), same_ref[...])
    shift_ref[...] = moved[:cases] + moved[cases:]
    spread_blocks(image_ref, low_ref, high_ref)
    strain_rows(cols_ref, stiff_ref, low_ref, high_ref, strain_ref)
    in_low = iota((2 * cases, LANES), 1) < LANES // 2
    strain = jnp.concatenate(
        [
            jnp.where(in_low, strain_ref[2 * j].astype(F32), strain_ref[2 * j + 1].astype(F32)).astype(BF16)
            for j in range(strain_ref.shape[0] // 2)
        ],
        axis=1,
    )
    image = image_ref[...]
    image_rows = stack2(image)
    rows = jnp.concatenate([stack2(field_ref[...]), image_rows], axis=0)
    every = dot_nt(rows, image_rows)
    every = every[:, :cases] + every[:, cases:]
    cross = every[:cases] + every[cases:2 * cases]
    square = every[2 * cases:3 * cases] + every[3 * cases:]
    start = dot_nt(rows[:2 * cases], rows[:2 * cases])
    start = start[:, :cases] + start[:, cases:]
    start = start[:cases] + start[cases:]
    last = dot_nt(image_rows, stack2(image * mass_ref[...])) + dot_nt(strain, strain)
    last = last[:, :cases] + last[:, cases:]
    last = last[:cases] + last[cases:]
    gram_ref[...] = jnp.concatenate([cross, start, square, last], axis=1)


def gram_trace(gram_ref, own_ref, match_ref, shift_ref, pen_ref, match_pen_ref, out_ref, jump_ref):
    cases = gram_ref.shape[0]
    apart = (own_ref[...] - match_ref[...]) + shift_ref[...]
    jump = (pen_ref[...] * match_pen_ref[...]) * apart
    jump_ref[...] = jump
    more = dot_nt(stack2(0.5 * apart), stack2(jump))
    more = more[:, :cases] + more[:, cases:]
    more = more[:cases] + more[cases:]
    zeros = jnp.zeros((cases, 3 * cases), F32)
    out_ref[...] = gram_ref[...] + jnp.concatenate([zeros, more], axis=1)


def second_image(
    cols_ref, field_ref, image_ref, mass_ref, stiff_ref, strain_ref, jump_ref, trace_ref, out_ref, *sums
):
    transposed_sums(cols_ref, stiff_ref, strain_ref, sums)
    trace = trace_ref[...]
    one_hot = one_hot_low(trace & (WIDE - 1), trace.shape[1])
    folded = jnp.concatenate(
        [folded_tile(sums, j) for j in range(image_ref.shape[1] // LANES)], axis=1
    )
    image = image_ref[...]
    rows = 2 * image.shape[0]
    second = add_rows(image * mass_ref[...] + folded, jump_ref[...], one_hot, trace >> 8)
    for i, part in enumerate((field_ref[...], image, second)):
        out_ref[i * rows:(i + 1) * rows, :] = stack2(part)
    out_ref[3 * rows:, :] = jnp.zeros((out_ref.shape[0] - 3 * rows, out_ref.shape[1]), BF16)


def eliminate(matrix, size, group=16):
    rows = iota(matrix.shape, 0)
    for first in range(0, size, group):
        columns = [
            jnp.broadcast_to(matrix[:, p:p + 1], matrix.shape) for p in range(first, first + group)
        ]
        for q in range(group):
            p = first + q
            column = columns[q]
            inverse = 1.0 / column[p:p + 1]
            row = matrix[p:p + 1] * inverse
            here = rows == p
            matrix = jnp.where(here, row, matrix - column * row)
            for r in range(q + 1, group):
                entry = column[first + r:first + r + 1] * inverse
                columns[r] = jnp.where(here, entry, columns[r] - column * entry)
    return matrix


def small_dot(a, b):
    return jnp.dot(a, b, precision=lax.Precision.HIGHEST, preferred_element_type=F32)


def finish(*refs):
    *gram_refs, field_ref, rows_ref, solution_ref, residual_ref = refs
    cases = field_ref.shape[0]
    gram = sum_of([ref[...] for ref in gram_refs])
    square = gram[:, 2 * cases:3 * cases]
    solved = eliminate(gram, cases)
    zeros = jnp.zeros((cases, 2 * cases), F32)
    given = jnp.concatenate([gram[:, 3 * cases:], gram[:, :cases]], axis=1)
    both = jnp.concatenate([solved[:, 2 * cases:3 * cases], solved[:, cases:2 * cases]], axis=1)
    second_part = eliminate(
        jnp.concatenate([given - small_dot(square, both), zeros], axis=1), cases
    )[:, cases:2 * cases]
    first_part = both[:, cases:] - small_dot(both[:, :cases], second_part)
    zero = jnp.zeros((cases, cases), F32)
    blocks = [[first_part, zero], [second_part, -first_part], [zero, -second_part], [zero, zero]]
    weights = [jnp.concatenate(block + [zero, zero], axis=1) for block in blocks]
    weights = jnp.concatenate([weights[i // 2] for i in range(8)], axis=0)
    weights = jnp.concatenate([weights[:LANES].T, weights[LANES:].T], axis=1)[:2 * cases]
    out = dot_nn(stack2(weights), rows_ref[...])
    out = out[:2 * cases] + out[2 * cases:]
    solution_ref[...] = out[:cases]
    residual_ref[...] = field_ref[...] + out[cases:]


def sum_of(terms):
    while len(terms) > 1:
        terms = [sum(terms[i:i + 2][1:], terms[i]) for i in range(0, len(terms), 2)]
    return terms[0]


def from_all(array, axis, stride=1, radix=None):
    count = lax.axis_size(axis)
    radix = radix or count
    span = stride * radix

    def target(i, by):
        digit = i // stride % radix
        return i // span * span + (digit + by) % radix * stride + i % stride

    return [array] + [
        lax.ppermute(array, axis, [(i, target(i, by)) for i in range(count)])
        for by in range(1, radix)
    ]


def digits(count):
    stages, stride = [], 1
    while stride < count:
        left = count // stride
        radix = 2 if stride == 1 and left % 2 == 0 else 4 if left % 4 == 0 else left
        stages.append((stride, radix))
        stride *= radix
    return stages


def run(body, outs, args, scratch=(), scalars=0, cost=None, far=0):
    whole = pl.BlockSpec(memory_space=pltpu.VMEM)
    args = [
        pltpu.with_memory_space_constraint(arg, pltpu.HBM) if scalars <= i < scalars + far else arg
        for i, arg in enumerate(args)
    ]
    return pl.pallas_call(
        body,
        out_shape=outs,
        in_specs=[pl.BlockSpec(memory_space=pltpu.SMEM)] * scalars
        + [pl.BlockSpec(memory_space=pltpu.HBM)] * far
        + [whole] * (len(args) - scalars - far),
        out_specs=jax.tree.map(lambda _: whole, outs),
        scratch_shapes=list(scratch),
        compiler_params=pltpu.CompilerParams(vmem_limit_bytes=VMEM_BYTES),
        cost_estimate=cost,
    )(*args)


def shards(
    load_cases,
    mass_diag,
    stiffness,
    block_cols,
    trace_dofs,
    penalty,
    cell_partials,
    cell_owner,
    cell_dof,
):
    cases, dofs = load_cases.shape
    count, blk, width = stiffness.shape
    cells = cell_partials.shape[1]
    slots = trace_dofs.shape[0]
    patches = lax.axis_size("patch")
    cap = 4 * cells // patches
    rows = cases + 8
    far_rows = cases + -(-(1 + 2 * (slots // cap)) // 8) * 8
    shape = jax.ShapeDtypeStruct
    field_shape = shape((cases, dofs), F32)
    slot_shape = shape((cases, slots), F32)
    mass = mass_diag.reshape(1, dofs)
    trace = trace_dofs.reshape(1, slots)
    pen = penalty.reshape(1, slots)
    cols = block_cols.T

    half = patches // 2
    pairs = [(i, (i + half) % patches) for i in range(patches)]
    packets = run(
        pack_cells,
        [shape((far_rows if by == half else rows, cap), F32) for by in range(patches)],
        (cell_partials, cell_owner.reshape(1, cells), cell_dof.reshape(1, cells), pen, trace),
        scratch=[
            pltpu.VMEM((cases, cells), F32),
            pltpu.VMEM((1, cells), jnp.int32),
            pltpu.VMEM((1, cells), jnp.int32),
            pltpu.VMEM((1, slots), F32),
            pltpu.VMEM((1, slots), jnp.int32),
            pltpu.SemaphoreType.DMA((5,)),
        ],
        far=5,
    )
    order = [0, 1, 2, half, *(by for by in range(3, patches) if by != half)]
    received = [packets[0]] + [
        lax.ppermute(packets[by], "patch", [(i, (i + by) % patches) for i in range(patches)])
        for by in order[1:]
    ]
    far, first = received[3], 5 * patches // 8
    base, stiff = run(
        early_cells,
        (field_shape, shape((count, 2 * blk, width), BF16)),
        (stiffness, load_cases, *received[:first]),
        scratch=[
            pltpu.VMEM((cases, dofs), F32),
            pltpu.VMEM(stiffness.shape, F32),
            pltpu.SemaphoreType.DMA((2,)),
        ],
        cost=pl.CostEstimate(flops=8 * stiffness.size, bytes_accessed=8 * stiffness.size, transcendentals=0),
        far=2,
    )
    late, base, stiff, cols, mass, trace = lax.optimization_barrier(
        (received[first:], base, stiff, cols, mass, trace)
    )

    spread = [pltpu.VMEM((dofs // blk, 2 * cases, LANES), BF16)] * 2
    strain_scratch = pltpu.VMEM((count, 2 * cases, LANES), BF16)
    sums = [pltpu.VMEM((dofs // blk, cases, LANES), F32)] * 2

    row_shape = shape((1, slots), F32)
    field, own, match_pen, match_trace = run(
        assemble, (field_shape, slot_shape, row_shape, row_shape), (base, trace, far, *late)
    )
    match = lax.ppermute(own, "patch", pairs)
    part, part_own = run(
        operator_body,
        (field_shape, slot_shape),
        (cols, field, mass, trace, stiff),
        scratch=[*spread, strain_scratch, *sums],
        scalars=1,
    )
    same = run(coincidence, shape((slots, slots), BF16), (trace, match_trace))
    part_own, same = lax.optimization_barrier((part_own, same))
    part_match = lax.ppermute(part_own, "patch", pairs)
    image, shift, gram, strain = run(
        first_image,
        (
            field_shape,
            slot_shape,
            shape((cases, 4 * cases), F32),
            shape((count, 2 * cases, LANES), BF16),
        ),
        (cols, field, part, own, match, pen, match_pen, trace, mass, same, stiff),
        scratch=spread,
        scalars=1,
    )
    gram, jump = run(
        gram_trace,
        (shape((cases, 4 * cases), F32), slot_shape),
        (gram, part_own, part_match, shift, pen, match_pen),
    )
    for stride, radix in reversed(digits(patches)):
        gram = sum_of(from_all(gram, "patch", stride, radix))
    stacked = run(
        second_image,
        shape((-(-6 * cases // LANES) * LANES, dofs), BF16),
        (cols, field, image, mass, stiff, strain, jump, trace),
        scratch=sums,
        scalars=1,
    )
    gram, stacked = lax.optimization_barrier((gram, stacked))
    grams = from_all(gram, "comp")
    grams = [grams[0], *grams[2::2], *grams[1::2]]
    return run(finish, (field_shape, field_shape), (*grams, field, stacked))


def solution(mesh):
    return jax.shard_map(
        shards,
        mesh=mesh,
        in_specs=(
            P(None, ("comp", "patch")),
            P(("comp", "patch")),
            P(("comp", "patch"), None, None),
            P(("comp", "patch"), None),
            P(("comp", "patch")),
            P(("comp", "patch")),
            P(None, ("comp", "patch")),
            P(("comp", "patch"), None),
            P(("comp", "patch")),
        ),
        out_specs=(P(None, ("comp", "patch")), P(None, ("comp", "patch"))),
        check_vma=False,
    )
```

```python
import jax
import jax.numpy as jnp
from jax import lax
from jax.experimental import pallas as pl
from jax.experimental.pallas import tpu as pltpu
from jax.sharding import PartitionSpec as P

F32 = jnp.float32
BF16 = jnp.bfloat16
WIDE = 256
LANES = 128
VMEM_BYTES = 32 * 1024 * 1024


def split2(x):
    high = x.astype(BF16)
    low = (x - high.astype(F32)).astype(BF16)
    return high, low


def stack2(x):
    return jnp.concatenate(split2(x), axis=0)


def dot_nn(a, b):
    return lax.dot_general(a, b, (((1,), (0,)), ((), ())), preferred_element_type=F32)


def dot_nt(a, b):
    return lax.dot_general(a, b, (((1,), (1,)), ((), ())), preferred_element_type=F32)


def iota(shape, axis):
    return lax.broadcasted_iota(jnp.int32, shape, axis)


def one_hot_low(low, width):
    return (iota((WIDE, width), 0) == low).astype(F32).astype(BF16)


def masked_groups(stacked, group, count):
    parts = []
    for g in range(count):
        mask = (group == g).astype(F32).astype(BF16)
        parts.append(stacked * jnp.broadcast_to(mask, stacked.shape))
    return jnp.concatenate(parts, axis=0)


def gather_slots(field, one_hot, group, groups):
    cases = field.shape[0]
    rows = jnp.concatenate(
        [stack2(field[:, g * WIDE:(g + 1) * WIDE]) for g in range(groups)], axis=0
    )
    found = dot_nn(rows, one_hot)
    total = jnp.zeros((cases, group.shape[1]), F32)
    for g in range(groups):
        base = g * 2 * cases
        both = found[base:base + cases] + found[base + cases:base + 2 * cases]
        total = jnp.where(group == g, both, total)
    return total


def pack_cells(*refs):
    sources, out_refs, targets, sems = refs[:5], refs[5:-6], refs[-6:-1], refs[-1]
    copies = [
        pltpu.make_async_copy(source, target, sems.at[i])
        for i, (source, target) in enumerate(zip(sources, targets))
    ]
    for copy in copies:
        copy.start()
    partials_ref, owner_ref, dof_ref, pen_ref, trace_ref = targets
    patches = len(out_refs)
    rows, cap = out_refs[0].shape
    cases, cells = partials_ref.shape
    me = lax.axis_index("patch")
    before = (iota((cells, cells), 0) < iota((cells, cells), 1)).astype(F32).astype(BF16)
    for copy in copies[1:]:
        copy.wait()
    shift = owner_ref[...] - me
    shift = jnp.where(shift < 0, shift + patches, shift)
    mine = (iota((patches, cells), 0) == shift).astype(F32)
    counts = dot_nn(mine.astype(BF16), before)
    rank = jnp.sum(mine * counts, axis=0, keepdims=True).astype(jnp.int32)
    extra = jnp.where(iota((rows - cases, cells), 0) == 0, dof_ref[...] + 1, 0).astype(F32)
    copies[0].wait()
    body = stack2(jnp.concatenate([partials_ref[...], extra], axis=0))
    for by, out_ref in enumerate(out_refs):
        key = jnp.where(shift == by, rank, -1)
        pick = (iota((cap, cells), 0) == key).astype(F32).astype(BF16)
        packed = dot_nt(body, pick)
        out_ref[:rows, :] = packed[:rows] + packed[rows:]
        if by == patches // 2:
            more = pen_ref.shape[1] // cap
            for i in range(more):
                at = cases + 1 + i
                out_ref[at:at + 1, :] = pen_ref[:, i * cap:(i + 1) * cap]
                out_ref[at + more:at + more + 1, :] = trace_ref[:, i * cap:(i + 1) * cap].astype(F32)


def add_cells(base, packet_refs):
    cases, dofs = base.shape
    groups = dofs // WIDE
    cells = jnp.concatenate([ref[:cases + 8, :] for ref in packet_refs], axis=1)
    slots = cells.shape[1]
    dof = cells[cases:cases + 1].astype(jnp.int32) - 1
    low = jnp.where(dof < 0, -1, dof & (WIDE - 1))
    return add_rows(base, cells[:cases], one_hot_low(low, slots), dof >> 8)


def early_cells(stiff_ref, load_ref, *refs):
    *packet_refs, field_ref, split_ref, load_copy_ref, wide_ref, sems = refs
    load_copy = pltpu.make_async_copy(load_ref, load_copy_ref, sems.at[0])
    load_copy.start()
    copy = pltpu.make_async_copy(stiff_ref, wide_ref, sems.at[1])
    copy.start()
    load_copy.wait()
    field_ref[...] = add_cells(load_copy_ref[...], packet_refs)
    copy.wait()
    blk = stiff_ref.shape[1]
    high, low = split2(wide_ref[...])
    split_ref[:, :blk, :] = high
    split_ref[:, blk:, :] = low


def assemble(base_ref, trace_ref, far_ref, *refs):
    *packet_refs, field_ref, own_ref, pen_ref, match_trace_ref = refs
    cases, dofs = base_ref.shape
    cap = far_ref.shape[1]
    more = pen_ref.shape[1] // cap
    for i in range(more):
        at = cases + 1 + i
        pen_ref[:, i * cap:(i + 1) * cap] = far_ref[at:at + 1, :]
        match_trace_ref[:, i * cap:(i + 1) * cap] = far_ref[at + more:at + more + 1, :]
    field = add_cells(base_ref[...], packet_refs)
    field_ref[...] = field
    trace = trace_ref[...]
    own_ref[...] = gather_slots(
        field, one_hot_low(trace & (WIDE - 1), trace.shape[1]), trace >> 8, dofs // WIDE
    )


def spread_blocks(field_ref, low_ref, high_ref):
    cases, dofs = field_ref.shape
    in_low = iota((cases, LANES), 1) < LANES // 2
    for j in range(dofs // LANES):
        tile = field_ref[:, j * LANES:(j + 1) * LANES]
        turned = pltpu.roll(tile, LANES // 2, 1)
        low_ref[2 * j] = stack2(jnp.where(in_low, tile, 0.0))
        high_ref[2 * j + 1] = stack2(jnp.where(in_low, 0.0, tile))
        low_ref[2 * j + 1] = stack2(jnp.where(in_low, turned, 0.0))
        high_ref[2 * j] = stack2(jnp.where(in_low, 0.0, turned))


def strain_rows(cols_ref, stiff_ref, low_ref, high_ref, strain_ref):
    count = stiff_ref.shape[0]
    cases = strain_ref.shape[1] // 2
    for n in range(count):
        c = [cols_ref[k, n] for k in range(4)]
        near = jnp.concatenate(
            [low_ref[c[0]] + high_ref[c[1]], low_ref[c[2]] + high_ref[c[3]]], axis=1
        )
        both = dot_nt(near, stiff_ref[n])
        both = both[:cases] + both[cases:]
        strain_ref[n] = stack2(both + pltpu.roll(both, LANES // 2, 1))


def transposed_sums(cols_ref, stiff_ref, strain_ref, sums):
    count = stiff_ref.shape[0]
    cases = strain_ref.shape[1] // 2
    for ref in sums:
        ref[...] = jnp.zeros_like(ref)
    for n in range(count):
        c = [cols_ref[k, n] for k in range(4)]
        both = dot_nn(strain_ref[n], stiff_ref[n])
        both = both[:cases] + both[cases:]
        left, right = both[:, :LANES], both[:, LANES:]
        sums[0][c[0]] += left
        sums[1][c[1]] += left
        sums[0][c[2]] += right
        sums[1][c[3]] += right


def folded_tile(sums, j):
    cases = sums[0].shape[1]
    in_low = iota((cases, LANES), 1) < LANES // 2
    even, odd = 2 * j, 2 * j + 1
    straight = jnp.where(in_low, sums[0][even], sums[1][odd])
    crossed = jnp.where(in_low, sums[0][odd], sums[1][even])
    return straight + pltpu.roll(crossed, LANES // 2, 1)


def operator_body(
    cols_ref, field_ref, mass_ref, trace_ref, stiff_ref, out_ref, own_ref, low_ref, high_ref, strain_ref, *sums
):
    spread_blocks(field_ref, low_ref, high_ref)
    strain_rows(cols_ref, stiff_ref, low_ref, high_ref, strain_ref)
    transposed_sums(cols_ref, stiff_ref, strain_ref, sums)
    dofs = field_ref.shape[1]
    for j in range(dofs // LANES):
        at = slice(j * LANES, (j + 1) * LANES)
        out_ref[:, at] = field_ref[:, at] * mass_ref[:, at] + folded_tile(sums, j)
    trace = trace_ref[...]
    own_ref[...] = gather_slots(
        out_ref[...], one_hot_low(trace & (WIDE - 1), trace.shape[1]), trace >> 8, dofs // WIDE
    )


def coincidence(trace_ref, match_trace_ref, out_ref):
    slots = trace_ref.shape[1]
    rows = [trace_ref[...].astype(F32), match_trace_ref[...]]
    for i in range(slots // LANES):
        at = slice(i * LANES, (i + 1) * LANES)
        total = jnp.zeros((LANES, slots), F32)
        for row in rows:
            column = jnp.broadcast_to(row[:, at], (LANES, LANES)).T
            total += (jnp.broadcast_to(column[:, :1], (LANES, slots)) == row).astype(F32)
        out_ref[at, :] = total.astype(BF16)


def add_rows(base, rows, one_hot, group):
    cases, dofs = base.shape
    groups = dofs // WIDE
    sums = dot_nt(masked_groups(stack2(rows), group, groups), one_hot)
    pieces = []
    for g in range(groups):
        row = g * 2 * cases
        pieces.append(
            base[:, g * WIDE:(g + 1) * WIDE]
            + (sums[row:row + cases] + sums[row + cases:row + 2 * cases])
        )
    return jnp.concatenate(pieces, axis=1)


def first_image(
    cols_ref, field_ref, part_ref, own_ref, match_ref, pen_ref, match_pen_ref, trace_ref, mass_ref, same_ref, stiff_ref,
    image_ref, shift_ref, gram_ref, strain_ref, low_ref, high_ref,
):
    cases, dofs = field_ref.shape
    trace = trace_ref[...]
    weight = pen_ref[...] * match_pen_ref[...]
    jump = weight * (own_ref[...] - match_ref[...])
    image_ref[...] = add_rows(
        part_ref[...], jump, one_hot_low(trace & (WIDE - 1), trace.shape[1]), trace >> 8
    )
    moved = dot_nn(stack2(jump), same_ref[...])
    shift_ref[...] = moved[:cases] + moved[cases:]
    spread_blocks(image_ref, low_ref, high_ref)
    strain_rows(cols_ref, stiff_ref, low_ref, high_ref, strain_ref)
    in_low = iota((2 * cases, LANES), 1) < LANES // 2
    strain = jnp.concatenate(
        [
            jnp.where(in_low, strain_ref[2 * j].astype(F32), strain_ref[2 * j + 1].astype(F32)).astype(BF16)
            for j in range(strain_ref.shape[0] // 2)
        ],
        axis=1,
    )
    image = image_ref[...]
    image_rows = stack2(image)
    rows = jnp.concatenate([stack2(field_ref[...]), image_rows], axis=0)
    every = dot_nt(rows, image_rows)
    every = every[:, :cases] + every[:, cases:]
    cross = every[:cases] + every[cases:2 * cases]
    square = every[2 * cases:3 * cases] + every[3 * cases:]
    start = dot_nt(rows[:2 * cases], rows[:2 * cases])
    start = start[:, :cases] + start[:, cases:]
    start = start[:cases] + start[cases:]
    last = dot_nt(image_rows, stack2(image * mass_ref[...])) + dot_nt(strain, strain)
    last = last[:, :cases] + last[:, cases:]
    last = last[:cases] + last[cases:]
    gram_ref[...] = jnp.concatenate([cross, start, square, last], axis=1)


def gram_trace(gram_ref, own_ref, match_ref, shift_ref, pen_ref, match_pen_ref, out_ref, jump_ref):
    cases = gram_ref.shape[0]
    apart = (own_ref[...] - match_ref[...]) + shift_ref[...]
    jump = (pen_ref[...] * match_pen_ref[...]) * apart
    jump_ref[...] = jump
    more = dot_nt(stack2(0.5 * apart), stack2(jump))
    more = more[:, :cases] + more[:, cases:]
    more = more[:cases] + more[cases:]
    zeros = jnp.zeros((cases, 3 * cases), F32)
    out_ref[...] = gram_ref[...] + jnp.concatenate([zeros, more], axis=1)


def second_image(
    cols_ref, field_ref, image_ref, mass_ref, stiff_ref, strain_ref, jump_ref, trace_ref, out_ref, *sums
):
    transposed_sums(cols_ref, stiff_ref, strain_ref, sums)
    trace = trace_ref[...]
    one_hot = one_hot_low(trace & (WIDE - 1), trace.shape[1])
    folded = jnp.concatenate(
        [folded_tile(sums, j) for j in range(image_ref.shape[1] // LANES)], axis=1
    )
    image = image_ref[...]
    rows = 2 * image.shape[0]
    second = add_rows(image * mass_ref[...] + folded, jump_ref[...], one_hot, trace >> 8)
    for i, part in enumerate((field_ref[...], image, second)):
        out_ref[i * rows:(i + 1) * rows, :] = stack2(part)
    out_ref[3 * rows:, :] = jnp.zeros((out_ref.shape[0] - 3 * rows, out_ref.shape[1]), BF16)


def eliminate(matrix, size, group=8):
    rows = iota(matrix.shape, 0)
    for first in range(0, size, group):
        columns = [
            jnp.broadcast_to(matrix[:, p:p + 1], matrix.shape) for p in range(first, first + group)
        ]
        for q in range(group):
            p = first + q
            column = columns[q]
            inverse = 1.0 / column[p:p + 1]
            row = matrix[p:p + 1] * inverse
            here = rows == p
            matrix = jnp.where(here, row, matrix - column * row)
            for r in range(q + 1, group):
                entry = column[first + r:first + r + 1] * inverse
                columns[r] = jnp.where(here, entry, columns[r] - column * entry)
    return matrix


def small_dot(a, b):
    return jnp.dot(a, b, precision=lax.Precision.HIGHEST, preferred_element_type=F32)


def finish(*refs):
    *gram_refs, field_ref, rows_ref, solution_ref, residual_ref = refs
    cases = field_ref.shape[0]
    gram = sum_of([ref[...] for ref in gram_refs])
    square = gram[:, 2 * cases:3 * cases]
    solved = eliminate(gram, cases)
    zeros = jnp.zeros((cases, 2 * cases), F32)
    given = jnp.concatenate([gram[:, 3 * cases:], gram[:, :cases]], axis=1)
    both = jnp.concatenate([solved[:, 2 * cases:3 * cases], solved[:, cases:2 * cases]], axis=1)
    second_part = eliminate(
        jnp.concatenate([given - small_dot(square, both), zeros], axis=1), cases
    )[:, cases:2 * cases]
    first_part = both[:, cases:] - small_dot(both[:, :cases], second_part)
    zero = jnp.zeros((cases, cases), F32)
    blocks = [[first_part, zero], [second_part, -first_part], [zero, -second_part], [zero, zero]]
    weights = [jnp.concatenate(block + [zero, zero], axis=1) for block in blocks]
    weights = jnp.concatenate([weights[i // 2] for i in range(8)], axis=0)
    weights = jnp.concatenate([weights[:LANES].T, weights[LANES:].T], axis=1)[:2 * cases]
    out = dot_nn(stack2(weights), rows_ref[...])
    out = out[:2 * cases] + out[2 * cases:]
    solution_ref[...] = out[:cases]
    residual_ref[...] = field_ref[...] + out[cases:]


def sum_of(terms):
    while len(terms) > 1:
        terms = [sum(terms[i:i + 2][1:], terms[i]) for i in range(0, len(terms), 2)]
    return terms[0]


def from_all(array, axis, stride=1, radix=None):
    count = lax.axis_size(axis)
    radix = radix or count
    span = stride * radix

    def target(i, by):
        digit = i // stride % radix
        return i // span * span + (digit + by) % radix * stride + i % stride

    return [array] + [
        lax.ppermute(array, axis, [(i, target(i, by)) for i in range(count)])
        for by in range(1, radix)
    ]


def digits(count):
    stages, stride = [], 1
    while stride < count:
        left = count // stride
        radix = 2 if stride == 1 and left % 2 == 0 else 4 if left % 4 == 0 else left
        stages.append((stride, radix))
        stride *= radix
    return stages


def run(body, outs, args, scratch=(), scalars=0, cost=None, far=0):
    whole = pl.BlockSpec(memory_space=pltpu.VMEM)
    args = [
        pltpu.with_memory_space_constraint(arg, pltpu.HBM) if scalars <= i < scalars + far else arg
        for i, arg in enumerate(args)
    ]
    return pl.pallas_call(
        body,
        out_shape=outs,
        in_specs=[pl.BlockSpec(memory_space=pltpu.SMEM)] * scalars
        + [pl.BlockSpec(memory_space=pltpu.HBM)] * far
        + [whole] * (len(args) - scalars - far),
        out_specs=jax.tree.map(lambda _: whole, outs),
        scratch_shapes=list(scratch),
        compiler_params=pltpu.CompilerParams(vmem_limit_bytes=VMEM_BYTES),
        cost_estimate=cost,
    )(*args)


def shards(
    load_cases,
    mass_diag,
    stiffness,
    block_cols,
    trace_dofs,
    penalty,
    cell_partials,
    cell_owner,
    cell_dof,
):
    cases, dofs = load_cases.shape
    count, blk, width = stiffness.shape
    cells = cell_partials.shape[1]
    slots = trace_dofs.shape[0]
    patches = lax.axis_size("patch")
    cap = 4 * cells // patches
    rows = cases + 8
    far_rows = cases + -(-(1 + 2 * (slots // cap)) // 8) * 8
    shape = jax.ShapeDtypeStruct
    field_shape = shape((cases, dofs), F32)
    slot_shape = shape((cases, slots), F32)
    mass = mass_diag.reshape(1, dofs)
    trace = trace_dofs.reshape(1, slots)
    pen = penalty.reshape(1, slots)
    cols = block_cols.T

    half = patches // 2
    pairs = [(i, (i + half) % patches) for i in range(patches)]
    packets = run(
        pack_cells,
        [shape((far_rows if by == half else rows, cap), F32) for by in range(patches)],
        (cell_partials, cell_owner.reshape(1, cells), cell_dof.reshape(1, cells), pen, trace),
        scratch=[
            pltpu.VMEM((cases, cells), F32),
            pltpu.VMEM((1, cells), jnp.int32),
            pltpu.VMEM((1, cells), jnp.int32),
            pltpu.VMEM((1, slots), F32),
            pltpu.VMEM((1, slots), jnp.int32),
            pltpu.SemaphoreType.DMA((5,)),
        ],
        far=5,
    )
    order = [0, 1, 2, half, *(by for by in range(3, patches) if by != half)]
    received = [packets[0]] + [
        lax.ppermute(packets[by], "patch", [(i, (i + by) % patches) for i in range(patches)])
        for by in order[1:]
    ]
    far, first = received[3], 5 * patches // 8
    base, stiff = run(
        early_cells,
        (field_shape, shape((count, 2 * blk, width), BF16)),
        (stiffness, load_cases, *received[:first]),
        scratch=[
            pltpu.VMEM((cases, dofs), F32),
            pltpu.VMEM(stiffness.shape, F32),
            pltpu.SemaphoreType.DMA((2,)),
        ],
        cost=pl.CostEstimate(flops=8 * stiffness.size, bytes_accessed=8 * stiffness.size, transcendentals=0),
        far=2,
    )
    late, base, stiff, cols, mass, trace = lax.optimization_barrier(
        (received[first:], base, stiff, cols, mass, trace)
    )

    spread = [pltpu.VMEM((dofs // blk, 2 * cases, LANES), BF16)] * 2
    strain_scratch = pltpu.VMEM((count, 2 * cases, LANES), BF16)
    sums = [pltpu.VMEM((dofs // blk, cases, LANES), F32)] * 2

    row_shape = shape((1, slots), F32)
    field, own, match_pen, match_trace = run(
        assemble, (field_shape, slot_shape, row_shape, row_shape), (base, trace, far, *late)
    )
    match = lax.ppermute(own, "patch", pairs)
    part, part_own = run(
        operator_body,
        (field_shape, slot_shape),
        (cols, field, mass, trace, stiff),
        scratch=[*spread, strain_scratch, *sums],
        scalars=1,
    )
    same = run(coincidence, shape((slots, slots), BF16), (trace, match_trace))
    part_own, same = lax.optimization_barrier((part_own, same))
    part_match = lax.ppermute(part_own, "patch", pairs)
    image, shift, gram, strain = run(
        first_image,
        (
            field_shape,
            slot_shape,
            shape((cases, 4 * cases), F32),
            shape((count, 2 * cases, LANES), BF16),
        ),
        (cols, field, part, own, match, pen, match_pen, trace, mass, same, stiff),
        scratch=spread,
        scalars=1,
    )
    gram, jump = run(
        gram_trace,
        (shape((cases, 4 * cases), F32), slot_shape),
        (gram, part_own, part_match, shift, pen, match_pen),
    )
    for stride, radix in reversed(digits(patches)):
        gram = sum_of(from_all(gram, "patch", stride, radix))
    stacked = run(
        second_image,
        shape((-(-6 * cases // LANES) * LANES, dofs), BF16),
        (cols, field, image, mass, stiff, strain, jump, trace),
        scratch=sums,
        scalars=1,
    )
    gram, stacked = lax.optimization_barrier((gram, stacked))
    grams = from_all(gram, "comp")
    grams = [grams[0], *grams[2::2], *grams[1::2][::-1]]
    return run(finish, (field_shape, field_shape), (*grams, field, stacked))


def solution(mesh):
    return jax.shard_map(
        shards,
        mesh=mesh,
        in_specs=(
            P(None, ("comp", "patch")),
            P(("comp", "patch")),
            P(("comp", "patch"), None, None),
            P(("comp", "patch"), None),
            P(("comp", "patch")),
            P(("comp", "patch")),
            P(None, ("comp", "patch")),
            P(("comp", "patch"), None),
            P(("comp", "patch")),
        ),
        out_specs=(P(None, ("comp", "patch")), P(None, ("comp", "patch"))),
        check_vma=False,
    )
```
